32 devices in a mesh: rows: 8 (over y, x, core), band: 4 (over z).
Axes of the slice: x: 2, y: 2, z: 4, core: 2. Of those that a mesh axis runs over, the one named last changes fastest.
Arguments:
- pan_image: float32 [384, 12288], P('rows', 'band'), may hold values from -1 to 17
- vnir_bands: float32 [8, 96, 3072], P('band', 'rows'), may hold values from -13 to 13
- swir_bands: float32 [8, 32, 1024], P('band', 'rows'), may hold values from -12 to 12
Outputs:
- joined_vnir: float32 [8, 384, 12288], P(None, 'rows', 'band')
- joined_swir: float32 [8, 96, 3072], P(None, 'rows', 'band')
The draws below stay inside these ranges and needn't reach their ends.
All inputs are finite; a program needn't handle non-finite values.
Results may differ from the reference program's by a relative error of at most 0.00023.
Values sent between devices are 32-bit elements; how exact they have to be, the bound alone decides.
No kernel may reach another device: no remote copies, remote signals or barrier semaphores. Data moves between devices by JAX's collectives and lax.ppermute only.
A program may use at most 192 MiB of HBM per device.

```python
import math
import jax
import jax.numpy as jnp
import numpy as np
from jax import lax

BANDS = 8
SWIR_BANDS = 8
RATIO_V = 4
RATIO_S = 3
TAPS_V = 17
TAPS_S = 13
WIDTH = 12288
HEIGHT = 384


def scene_field(key):
    base_key = jax.random.fold_in(key, 11)
    rough_part = jax.random.truncated_normal(jax.random.fold_in(base_key, 1), -3.0, 3.0, (HEIGHT, WIDTH), jnp.float32)
    coarse = jax.random.truncated_normal(jax.random.fold_in(base_key, 2), -3.0, 3.0, (HEIGHT // 4, WIDTH // 4), jnp.float32)
    smooth = jnp.repeat(jnp.repeat(coarse, 4, axis=0), 4, axis=1)
    row_pos = jnp.arange(HEIGHT, dtype=jnp.float32)[:, None] / max(HEIGHT - 1, 1)
    row_ramp = 1.0 + 2.0 * row_pos
    level = -1.0 + 2.0 * row_pos
    return level + row_ramp * (0.3 * rough_part + 0.3 * smooth)


def draw_pan_image(key, part):
    scene = scene_field(key)
    speckle = jax.random.truncated_normal(jax.random.fold_in(key, 31), -3.0, 3.0, (HEIGHT, WIDTH), jnp.float32)
    return 8.0 + scene + 0.3 * speckle


def draw_vnir_bands(key, part):
    scene = scene_field(key)
    factors = jax.random.uniform(jax.random.fold_in(key, 21), (BANDS,), jnp.float32, 0.5, 1.5)
    blocks = scene.reshape(HEIGHT // 4, 4, WIDTH // 4, 4).mean(axis=(1, 3))
    band_noise = jax.random.truncated_normal(jax.random.fold_in(key, 22), -3.0, 3.0, (BANDS, HEIGHT // 4, WIDTH // 4), jnp.float32)
    return factors[:, None, None] * blocks[None] + 0.5 * band_noise


def draw_swir_bands(key, part):
    scene = scene_field(key)
    factors = jax.random.uniform(jax.random.fold_in(key, 41), (SWIR_BANDS,), jnp.float32, 0.3, 1.5)
    blocks = scene.reshape(HEIGHT // 12, 12, WIDTH // 12, 12).mean(axis=(1, 3))
    band_noise = jax.random.truncated_normal(jax.random.fold_in(key, 42), -3.0, 3.0, (SWIR_BANDS, HEIGHT // 12, WIDTH // 12), jnp.float32)
    return factors[:, None, None] * blocks[None] + 0.3 * band_noise


def setup_inputs(seed: int = 0) -> dict:
    splits = jax.random.split(jax.random.key(seed), 4)
    return {
        "pan_image": draw_pan_image(jax.random.fold_in(splits[3], 71), 0),
        "vnir_bands": draw_vnir_bands(jax.random.fold_in(splits[3], 71), 0),
        "swir_bands": draw_swir_bands(jax.random.fold_in(splits[3], 71), 0),
    }


NYQUIST_GAIN = 0.29

def gauss_taps(upscale, kernel_len):
    spread = upscale * math.sqrt(-2.0 * math.log(NYQUIST_GAIN)) / math.pi
    radius = kernel_len // 2
    offsets = np.arange(-radius, radius + 1) * 1.0
    values = np.exp(-offsets ** 2 / (2.0 * spread ** 2))
    return values / values.sum()

def cubic_weight(distance):
    distance = abs(distance)
    if distance <= 1.0:
        return 1.5 * distance ** 3 - 2.5 * distance ** 2 + 1.0
    if distance < 2.0:
        return -0.5 * distance ** 3 + 2.5 * distance ** 2 - 4.0 * distance + 2.0
    return 0.0

def cubic_table(upscale):
    weights = np.zeros((5, upscale))
    for phase_index in range(upscale):
        centre = (phase_index + 0.5) / upscale - 0.5
        first_tap = math.floor(centre)
        fraction = centre - first_tap
        for tap_index in range(-1, 3):
            weights[first_tap + tap_index + 2, phase_index] += cubic_weight(tap_index - fraction)
    return weights

def pad_axis(field, along, margin):
    widths = [(0, 0)] * field.ndim
    widths[along] = (margin, margin)
    return jnp.pad(field, widths)

def filter_axis(padded, kernel, along):
    length = padded.shape[along] - len(kernel) + 1
    running = float(kernel[0]) * lax.slice_in_dim(padded, 0, length, axis=along)
    for offset in range(1, len(kernel)):
        running = running + float(kernel[offset]) * lax.slice_in_dim(padded, offset, offset + length, axis=along)
    return running

def upsample_axis(padded, upscale, along):
    weights = cubic_table(upscale)
    length = padded.shape[along] - 4
    phases = []
    for phase_index in range(upscale):
        running = float(weights[0, phase_index]) * lax.slice_in_dim(padded, 0, length, axis=along)
        for offset in range(1, 5):
            running = running + float(weights[offset, phase_index]) * lax.slice_in_dim(padded, offset, offset + length, axis=along)
        phases.append(running)
    stacked = jnp.stack(phases, axis=along + 1)
    new_shape = padded.shape[:along] + (length * upscale,) + padded.shape[along + 1:]
    return stacked.reshape(new_shape)

def moments(layers):
    flattened = layers.reshape(layers.shape[0], -1)
    products = jnp.dot(flattened.astype(jnp.float32), flattened.T.astype(jnp.float32), precision=lax.Precision.HIGHEST, preferred_element_type=jnp.float32)
    return (products, lax.optimization_barrier(jnp.sum(flattened, axis=1)))

def covariance(products, totals, pixels):
    averages = totals / pixels
    return products / pixels - averages[:, None] * averages[None, :]

def solve_spd(matrix, rhs):
    factor = jnp.linalg.cholesky(matrix)
    lower_sol = lax.linalg.triangular_solve(factor, rhs, left_side=True, lower=True)
    return lax.linalg.triangular_solve(factor, lower_sol, left_side=True, lower=True, transpose_a=True)

def first_gains(products, totals, pixels):
    cov_all = covariance(products, totals, pixels)
    inputs_cov = cov_all[:BANDS, :BANDS]
    cross_cov = cov_all[:BANDS, BANDS:]
    weights = solve_spd(inputs_cov, cross_cov)
    return cross_cov[:, 0] / jnp.sum(cross_cov[:, 0] * weights[:, 0])

def second_fit(products, totals, pixels):
    cov_all = covariance(products, totals, pixels)
    inputs_cov = cov_all[:BANDS, :BANDS]
    cross_cov = cov_all[:BANDS, BANDS:]
    target = lax.optimization_barrier(jnp.mean(cross_cov, axis=1, keepdims=True))
    weights = solve_spd(inputs_cov, target)[:, 0]
    numerators = lax.optimization_barrier(jnp.sum(weights[:, None] * cross_cov, axis=0))
    return (weights, numerators / jnp.sum(weights * target[:, 0]))

def reference(pan_image, vnir_bands, swir_bands):
    kernel_fine = gauss_taps(RATIO_V, TAPS_V)
    kernel_coarse = gauss_taps(RATIO_S, TAPS_S)
    padded = jnp.pad(pan_image, TAPS_V // 2)
    pan_low = filter_axis(filter_axis(padded, kernel_fine, 0), kernel_fine, 1)
    vnir_up = upsample_axis(pad_axis(upsample_axis(pad_axis(vnir_bands, 1, 2), RATIO_V, 1), 2, 2), RATIO_V, 2)
    products, totals = moments(jnp.concatenate([vnir_up, pan_low[None]], axis=0))
    gain_bands = first_gains(products, totals, HEIGHT * WIDTH)
    joined_vnir = vnir_up + gain_bands[:, None, None] * (pan_image - pan_low)[None]
    synthetic = joined_vnir.reshape(BANDS, HEIGHT // RATIO_V, RATIO_V, WIDTH // RATIO_V, RATIO_V).mean(axis=(2, 4))
    synth_pad = pad_axis(pad_axis(synthetic, 1, TAPS_S // 2), 2, TAPS_S // 2)
    synthetic_low = filter_axis(filter_axis(synth_pad, kernel_coarse, 1), kernel_coarse, 2)
    swir_up = upsample_axis(pad_axis(upsample_axis(pad_axis(swir_bands, 1, 2), RATIO_S, 1), 2, 2), RATIO_S, 2)
    products_two, totals_two = moments(jnp.concatenate([synthetic_low, swir_up], axis=0))
    weights, shares = second_fit(products_two, totals_two, HEIGHT // 4 * (WIDTH // 4))
    detail = jnp.einsum('b,bij->ij', weights, synthetic - synthetic_low, precision=lax.Precision.HIGHEST)
    joined_swir = swir_up + shares[:, None, None] * detail[None]
    return (joined_vnir, joined_swir)
```

```python
import math

import jax
import jax.numpy as jnp
import ml_dtypes
import numpy as np
from jax import lax
from jax.experimental import pallas as pl
from jax.experimental.pallas import tpu as pltpu
from jax.sharding import PartitionSpec as P

BANDS = 8
RATIO_V = 4
RATIO_S = 3
TAPS_V = 17
TAPS_S = 13
NYQUIST_GAIN = 0.29
LANES = 128
HALF = 64
HALO = 8
F32 = jnp.float32
BF16 = jnp.bfloat16
VMEM_BYTES = 48 * 1024 * 1024


def gauss_taps(upscale, kernel_len):
    spread = upscale * math.sqrt(-2.0 * math.log(NYQUIST_GAIN)) / math.pi
    radius = kernel_len // 2
    offsets = np.arange(-radius, radius + 1) * 1.0
    values = np.exp(-(offsets**2) / (2.0 * spread**2))
    return values / values.sum()


def cubic_weight(distance):
    distance = abs(distance)
    if distance <= 1.0:
        return 1.5 * distance**3 - 2.5 * distance**2 + 1.0
    if distance < 2.0:
        return -0.5 * distance**3 + 2.5 * distance**2 - 4.0 * distance + 2.0
    return 0.0


def cubic_table(upscale):
    weights = np.zeros((5, upscale))
    for phase_index in range(upscale):
        centre = (phase_index + 0.5) / upscale - 0.5
        first_tap = math.floor(centre)
        fraction = centre - first_tap
        for tap_index in range(-1, 3):
            weights[first_tap + tap_index + 2, phase_index] += cubic_weight(tap_index - fraction)
    return weights


KF = gauss_taps(RATIO_V, TAPS_V)
KC = gauss_taps(RATIO_S, TAPS_S)
C4 = cubic_table(RATIO_V)
C3 = cubic_table(RATIO_S)
MEAN4 = C4.mean(axis=1)


def split(table):
    high = np.asarray(table, np.float64).astype(np.float32).astype(ml_dtypes.bfloat16)
    low = (np.asarray(table, np.float64) - high.astype(np.float64)).astype(np.float32)
    return np.stack([high, low.astype(ml_dtypes.bfloat16)])


def band_matrix(size, taps):
    radius = len(taps) // 2
    out = np.zeros((size, size))
    for row in range(size):
        for tap in range(-radius, radius + 1):
            if 0 <= row + tap < size:
                out[row, row + tap] = taps[tap + radius]
    return out


def row_tables(h):
    hc = h // RATIO_V
    mean = np.zeros((3 * hc, 3 * h))
    for row in range(3 * hc):
        mean[row, RATIO_V * row : RATIO_V * (row + 1)] = 1.0 / RATIO_V
    fine = band_matrix(3 * h, KF)
    low = band_matrix(3 * hc, KC)
    mean_fine = mean @ fine
    pad = -(-hc // 8) * 8

    def part(matrix, rows, cols):
        return matrix[rows, :][:, cols]

    def stacked(rows, cols, filt):
        a = mean if filt is None else filt @ mean
        c = mean_fine if filt is None else filt @ mean_fine
        return np.concatenate([part(a, rows, cols), -part(c, rows, cols)], axis=1)

    own = slice(h, 2 * h)
    tables = []
    for variant in range(3):
        keep = np.ones(3 * hc)
        if variant == 1:
            keep[:hc] = 0.0
        if variant == 2:
            keep[2 * hc :] = 0.0
        masked = low * keep[None, :]
        rows = []
        for filt in (None, masked):
            block = np.zeros((pad, 2 * h))
            block[:hc] = stacked(slice(hc, 2 * hc), own, filt)
            rows.append(block)
        for filt in (None, low):
            rows.append(stacked(slice(hc, hc + HALO), slice(0, h), filt))
        for filt in (None, low):
            rows.append(stacked(slice(2 * hc - HALO, 2 * hc), slice(2 * h, 3 * h), filt))
        tables.append(np.concatenate(rows, axis=0))
    coarse_rows = np.stack(tables)
    fine_rows = np.concatenate(
        [fine[h : 2 * h, h : 2 * h], fine[h : h + HALO, 0:h], fine[2 * h - HALO : 2 * h, 2 * h : 3 * h]],
        axis=0,
    )
    return coarse_rows, fine_rows


def up_rows(hc):
    out = np.zeros((RATIO_V * hc, hc + 4))
    for m in range(hc):
        for p in range(RATIO_V):
            out[RATIO_V * m + p, m : m + 5] = C4[:, p]
    return out


def column_tables():
    n = LANES
    fine = np.zeros((2 * n, n))
    mean = np.zeros((5 * n, n))
    mean_fine = np.zeros((5 * n, n))
    low = np.zeros((2 * n, n))
    pair = np.zeros((3, 2 * n, 2 * n))
    up4 = np.zeros((2 * n, RATIO_V * n))
    up3 = np.zeros((2 * n, RATIO_S * n))
    for c in range(n):
        for t in range(-(TAPS_V // 2), TAPS_V // 2 + 1):
            fine[c + HALF + t, c] += KF[t + TAPS_V // 2]
            for q in range(RATIO_V):
                mean_fine[HALF + RATIO_V * c + q + t, c] += KF[t + TAPS_V // 2] / RATIO_V
        for q in range(RATIO_V):
            mean[HALF + RATIO_V * c + q, c] = 1.0 / RATIO_V
        for t in range(-(TAPS_S // 2), TAPS_S // 2 + 1):
            low[c + HALF + t, c] += KC[t + TAPS_S // 2]
            for s in range(-2, 3):
                value = KC[t + TAPS_S // 2] * MEAN4[s + 2]
                pair[0, c + HALF + t + s, n + c] += value
                if c + t >= 0:
                    pair[1, c + HALF + t + s, n + c] += value
                if c + t < n:
                    pair[2, c + HALF + t + s, n + c] += value
        for s in range(-2, 3):
            pair[:, c + HALF + s, c] += MEAN4[s + 2]
            for p in range(RATIO_V):
                up4[c + HALF + s, RATIO_V * c + p] += C4[s + 2, p]
            for p in range(RATIO_S):
                up3[c + HALF + s, RATIO_S * c + p] += C3[s + 2, p]
    return dict(fine=fine, mean=mean, mean_fine=mean_fine, low=low, pair=pair, up4=up4, up3=up3)


def parts2(x):
    high = x.astype(BF16)
    return high, (x - high.astype(F32)).astype(BF16)


def dot(a, b):
    return jnp.dot(a, b, preferred_element_type=F32)


def dot3(x, w):
    return dot(x[0], w[0]) + (dot(x[1], w[0]) + dot(x[0], w[1]))


def lanes_of(x, start, size):
    return tuple(part[:, start : start + size] for part in x)


def call(kernel, out_shape, scratch=(), out_specs=None, **cost):
    extra = {} if out_specs is None else dict(out_specs=out_specs)
    return pl.pallas_call(
        kernel,
        out_shape=out_shape,
        scratch_shapes=list(scratch),
        compiler_params=pltpu.CompilerParams(vmem_limit_bytes=VMEM_BYTES),
        cost_estimate=pl.CostEstimate(transcendentals=0, **cost) if cost else None,
        **extra,
    )


def local(pan_image, vnir_bands, swir_bands):
    groups = lax.axis_size("band")
    strips = lax.axis_size("rows")
    h, w = pan_image.shape
    nb, hc, _ = vnir_bands.shape
    _, hs, swir_width = swir_bands.shape
    wc = w // RATIO_V
    ws = wc // RATIO_S
    wf = wc + LANES
    sf = ws + LANES
    rb = -(-(hc + hs) // 8) * 8
    pad = -(-hc // 8) * 8
    fine_tiles = w // LANES
    coarse_tiles = wc // LANES
    swir_tiles = ws // LANES
    per_block = wf // LANES
    strip_blocks = -(-(h // 8) // per_block)
    fine_pixels = h * strips * w * groups

    def shape(*dims):
        return jax.ShapeDtypeStruct(dims, F32)

    coarse_rows, fine_rows = row_tables(h)
    cols = column_tables()
    lift = up_rows(hc)
    gram = lift.T @ lift
    rise = lift.sum(axis=0)

    def going(d):
        return (["right"] if d == 1 else []) + (["left"] if d == groups - 1 else [])

    chunk_rows = [nb * rb + 8 * strip_blocks * len(going(d)) for d in range(groups)]

    def strip_place(d, side):
        return nb * rb + 8 * strip_blocks * going(d).index(side)

    def pack(pan_ref, vnir_ref, swir_ref, *rest):
        outs, (wide, swide) = rest[:groups], rest[groups:]
        me = lax.axis_index("band")
        full = vnir_ref.shape[2]
        wide[:, :, 0:LANES] = jnp.zeros((nb, hc, LANES), F32)
        wide[:, :, LANES + full : 2 * LANES + full] = jnp.zeros((nb, hc, LANES), F32)
        wide[:, :, LANES : LANES + full] = vnir_ref[...]
        swide[:, :, 0:LANES] = jnp.zeros((nb, hs, LANES), F32)
        swide[:, :, LANES + swir_width : 2 * LANES + swir_width] = jnp.zeros((nb, hs, LANES), F32)
        swide[:, :, LANES : LANES + swir_width] = swir_ref[...]
        for d in range(groups):
            peer = lax.rem(me + d, groups)
            for j in range(nb):
                win = wide[j, :, pl.ds(pl.multiple_of(peer * wc, LANES), wc + 2 * LANES)]
                outs[d][j * rb : j * rb + hc, :] = win[:, HALF : HALF + wf]
                swin = swide[j, :, pl.ds(pl.multiple_of(peer * ws, LANES), ws + 2 * LANES)]
                outs[d][j * rb + hc : j * rb + hc + hs, 0:sf] = swin[:, HALF : HALF + sf]
            for side in going(d):
                first = strip_place(d, side)
                edge = pan_ref[:, w - LANES : w] if side == "right" else pan_ref[:, 0:LANES]
                for t in range(h // 8):
                    row = first + 8 * (t // per_block)
                    lane = LANES * (t % per_block)
                    outs[d][row : row + 8, lane : lane + LANES] = edge[8 * t : 8 * t + 8]

    chunks = call(
        pack,
        tuple(shape(chunk_rows[d], wf) for d in range(groups)),
        [
            pltpu.VMEM((nb, hc, vnir_bands.shape[2] + 2 * LANES), F32),
            pltpu.VMEM((nb, hs, swir_width + 2 * LANES), F32),
        ],
    )(pan_image, vnir_bands, swir_bands)
    got = [chunks[0]] + [
        lax.ppermute(chunks[d], "band", [(i, (i + d) % groups) for i in range(groups)])
        for d in range(1, groups)
    ]

    pan_blocks = -(-w // wc)
    send_rows = HALO + 3 + pan_blocks
    w_fine = split(cols["fine"])
    w_mean = split(cols["mean"])
    w_mean_fine = split(cols["mean_fine"])
    r_coarse = split(coarse_rows)
    r_fine = split(fine_rows)
    r_fine = np.concatenate([r_fine[0], r_fine[1], r_fine[0]], axis=1)

    def assemble(pan_ref, wf_ref, wm_ref, wmf_ref, rc_ref, rf_ref, *rest):
        ins = rest[:groups]
        x_out, s_out, up_out, down_out, d_out, ld_out, low_out, stage = rest[groups:]
        me = lax.axis_index("band")
        row_id = lax.axis_index("rows")
        for d in range(groups):
            source = lax.rem(me - d + groups, groups)
            block = ins[d][0 : nb * rb, :].reshape(nb, rb, wf)
            stage[pl.ds(source * nb, nb)] = block
        x_all = jnp.swapaxes(stage[...], 0, 1)
        x_out[...] = x_all[0:hc]
        s_out[...] = x_all[hc : hc + hs, :, 0:sf]
        up_out[0:HALO] = x_all[hc - HALO : hc]
        down_out[0:HALO] = x_all[0:HALO]
        for out, first in ((up_out, hc + hs - 2), (down_out, hc)):
            out[HALO, :, 0:sf] = x_all[first, :, 0:sf]
            out[HALO, :, wf - sf : wf] = x_all[first + 1, :, 0:sf]

        def strip(d, side, empty):
            first = strip_place(d, side)
            pieces = []
            for t in range(h // 8):
                row = first + 8 * (t // per_block)
                lane = LANES * (t % per_block)
                pieces.append(ins[d][row : row + 8, lane : lane + LANES])
            whole = jnp.concatenate(pieces, axis=0)
            return jnp.where(empty, 0.0, whole)

        left = strip(1, "right", me == 0)
        right = strip(groups - 1, "left", me == groups - 1)
        framed = jnp.concatenate([left[:, HALF:], pan_ref[...], right[:, :HALF]], axis=1)
        panes = parts2(framed)
        variant = jnp.where(row_id == 0, 1, jnp.where(row_id == strips - 1, 2, 0))
        rc = (rc_ref[0, variant], rc_ref[1, variant])
        for k in range(coarse_tiles + 1):
            start = RATIO_V * LANES * k - 2 * LANES
            skip = max(0, -start)
            stop = min(5 * LANES, w + LANES - start)
            piece = lanes_of(panes, start + skip, stop - skip)
            wm = wm_ref[0, skip:stop, :]
            wmf = (wmf_ref[0, skip:stop, :], wmf_ref[1, skip:stop, :])
            means = dot(piece[0], wm) + dot(piece[1], wm)
            fines = dot3(piece, wmf)
            both = parts2(jnp.concatenate([means, fines], axis=0))
            rows = dot(rc[0], both[0]) + (dot(rc[0], both[1]) + dot(rc[1], both[0]))
            at = slice(LANES * k, LANES * (k + 1))
            d_out[:, at] = rows[0:pad]
            ld_out[:, at] = rows[pad : 2 * pad]
            up_out[HALO + 1, :, at] = rows[2 * pad : 2 * pad + 8]
            up_out[HALO + 2, :, at] = rows[2 * pad + 8 : 2 * pad + 16]
            down_out[HALO + 1, :, at] = rows[2 * pad + 16 : 2 * pad + 24]
            down_out[HALO + 2, :, at] = rows[2 * pad + 24 : 2 * pad + 32]
        wfine = (wf_ref[0], wf_ref[1])
        rf = rf_ref[...]
        for k in range(fine_tiles):
            piece = lanes_of(panes, LANES * k, 2 * LANES)
            col = parts2(dot3(piece, wfine))
            rows = dot(rf, jnp.concatenate([col[0], col[0], col[1]], axis=0))
            low_out[:, LANES * k : LANES * (k + 1)] = rows[0:h]
            place = HALO + 3 + (LANES * k) // wc
            lane = (LANES * k) % wc
            up_out[place, :, lane : lane + LANES] = rows[h : h + HALO]
            down_out[place, :, lane : lane + LANES] = rows[h + HALO : h + 2 * HALO]

    x_loc, s_loc, up_send, down_send, d_own, ld_own, low_own = call(
        assemble,
        (
            shape(hc, BANDS, wf),
            shape(hs, BANDS, sf),
            shape(send_rows, BANDS, wf),
            shape(send_rows, BANDS, wf),
            shape(pad, wf),
            shape(pad, wf),
            shape(h, w),
        ),
        [pltpu.VMEM((BANDS, rb, wf), F32)],
    )(pan_image, w_fine, w_mean, w_mean_fine, r_coarse, r_fine, *got)
    from_low = lax.ppermute(up_send, "rows", [(i, i + 1) for i in range(strips - 1)])
    from_high = lax.ppermute(down_send, "rows", [(i + 1, i) for i in range(strips - 1)])

    w_low = split(cols["low"])
    w_pair = split(cols["pair"])
    w_up4 = split(cols["up4"])
    w_up3 = split(cols["up3"])
    r_adj = split(lift.T)
    r_adj = np.concatenate([r_adj[0], r_adj[0], r_adj[0], r_adj[1], r_adj[1]], axis=1)

    def moments(
        pan_ref, x_ref, s_ref, lo_ref, hi_ref, d_ref, ld_ref, low_ref,
        wl_ref, wp_ref, w4_ref, w3_ref, ra_ref,
        mom_out, y_out, diff_out, ugap_out, dgap_out, s_out,
        both, ulow, q_ref,
    ):
        me = lax.axis_index("band")
        row_id = lax.axis_index("rows")

        def x_row(r):
            if r < 0:
                return lo_ref[HALO + r]
            if r >= hc:
                return hi_ref[r - hc]
            return x_ref[r]

        frame = jnp.concatenate([x_row(r) for r in range(-2, hc + 2)], axis=0)
        frame = parts2(frame)
        w4 = (w4_ref[0], w4_ref[1])
        for k in range(coarse_tiles):
            up = dot3(lanes_of(frame, LANES * k, 2 * LANES), w4)
            for q in range(RATIO_V):
                y_out[RATIO_V * k + q] = up[:, LANES * q : LANES * (q + 1)]

        ra = ra_ref[...]
        psum = jnp.zeros((8, LANES), F32)
        psq = jnp.zeros((8, LANES), F32)
        for k in range(fine_tiles):
            at = slice(LANES * k, LANES * (k + 1))
            low = low_ref[:, at]
            place = HALO + 3 + (LANES * k) // wc
            lane = (LANES * k) % wc
            top = low[0:HALO] + lo_ref[place, :, lane : lane + LANES]
            end = low[h - HALO : h] + hi_ref[place, :, lane : lane + LANES]
            low = jnp.concatenate([top, low[HALO : h - HALO], end], axis=0)
            diff_out[k] = pan_ref[:, at] - low
            p1 = low.astype(BF16)
            rest = low - p1.astype(F32)
            p2 = rest.astype(BF16)
            p3 = (rest - p2.astype(F32)).astype(BF16)
            q_ref[k] = dot(ra, jnp.concatenate([p1, p2, p3, p1, p2], axis=0))
            for t in range(h // 8):
                tile = low[8 * t : 8 * t + 8]
                psum += tile
                psq += tile * tile

        def tile_step(k, carry):
            accs = list(carry[:BANDS])
            accp, accv = carry[BANDS], carry[BANDS + 1]
            ys = [y_out[k, pl.ds(8 * m, 8), :] for m in range(hc + 4)]
            for m in range(hc + 4):
                z = None
                for other in range(hc + 4):
                    if gram[m, other] != 0.0:
                        term = float(gram[m, other]) * ys[other]
                        z = term if z is None else z + term
                for i in range(BANDS):
                    accs[i] = accs[i] + z * y_out[k, pl.ds(8 * m + i, 1), :]
                accp = accp + ys[m] * q_ref[k, pl.ds(m, 1), :]
                accv = accv + float(rise[m]) * ys[m]
            return tuple(accs) + (accp, accv)

        zero = jnp.zeros((8, LANES), F32)
        first = lax.fori_loop(0, fine_tiles, tile_step, (zero,) * (BANDS + 2))

        below = jnp.where(row_id > 0, 1.0, 0.0).astype(F32)
        above = jnp.where(row_id < strips - 1, 1.0, 0.0).astype(F32)
        reach = TAPS_S // 2
        means = []
        for r in range(-reach, hc + reach):
            value = float(MEAN4[2]) * x_row(r)
            for t in (1, 2):
                value = value + float(MEAN4[2 + t]) * (x_row(r - t) + x_row(r + t))
            if r < 0:
                value = value * below
            if r >= hc:
                value = value * above
            means.append(value)
        lows = []
        for r in range(hc):
            centre = r + reach
            value = float(KC[reach]) * means[centre]
            for t in range(1, reach + 1):
                value = value + float(KC[reach + t]) * (means[centre - t] + means[centre + t])
            lows.append(value)
        u_rows = parts2(jnp.concatenate(means[reach : reach + hc], axis=0))
        l_rows = parts2(jnp.concatenate(lows, axis=0))
        left = jnp.where(me == 0, 1, 0)
        right = jnp.where(me == groups - 1, 2, 0)
        for k in range(coarse_tiles):
            which = left if k == 0 else (right if k == coarse_tiles - 1 else 0)
            wp = (wp_ref[0, which], wp_ref[1, which])
            mean_k = dot3(lanes_of(u_rows, LANES * k, 2 * LANES), tuple(p[:, :LANES] for p in wp))
            low_k = dot3(lanes_of(l_rows, LANES * k, 2 * LANES), tuple(p[:, LANES:] for p in wp))
            at = slice(LANES * k, LANES * (k + 1))
            ulow[:, at] = low_k
            ugap_out[:, at] = mean_k - low_k

        column = lax.broadcasted_iota(jnp.int32, (1, wf), 1) - HALF + me * wc
        inside = jnp.where((column >= 0) & (column < groups * wc), 1.0, 0.0).astype(F32)
        detail = []
        for index, ref in ((HALO + 1, d_ref), (HALO + 2, ld_ref)):
            both[...] = ref[...]
            both[0:HALO] = both[0:HALO] + lo_ref[index]
            both[hc - HALO : hc] = both[hc - HALO : hc] + hi_ref[index]
            detail.append(both[...])
        dlow_rows = parts2(detail[1] * inside)
        wl = (wl_ref[0], wl_ref[1])
        dlow = jnp.concatenate(
            [dot3(lanes_of(dlow_rows, LANES * k, 2 * LANES), wl) for k in range(coarse_tiles)], axis=1
        )
        dgap_out[...] = detail[0][:, HALF : HALF + wc] - dlow
        both[:, 0:wc] = dlow

        s_rows = [lo_ref[HALO, :, 0:sf], lo_ref[HALO, :, wf - sf : wf]]
        s_rows += [s_ref[r] for r in range(hs)]
        s_rows += [hi_ref[HALO, :, 0:sf], hi_ref[HALO, :, wf - sf : wf]]
        s_parts = parts2(jnp.concatenate(s_rows, axis=0))
        w3 = (w3_ref[0], w3_ref[1])
        s_cols = jnp.concatenate(
            [dot3(lanes_of(s_parts, LANES * k, 2 * LANES), w3) for k in range(swir_tiles)], axis=1
        )
        for m in range(hs):
            for p in range(RATIO_S):
                value = None
                for t in range(5):
                    if C3[t, p] != 0.0:
                        term = float(C3[t, p]) * s_cols[8 * (m + t) : 8 * (m + t) + 8]
                        value = term if value is None else value + term
                s_out[RATIO_S * m + p] = value

        ll = [zero] * BANDS
        cross = [zero] * BANDS
        ld = ls = sd = ss = dd = ds = zero
        for r in range(hc):
            for k in range(coarse_tiles):
                at = slice(LANES * k, LANES * (k + 1))
                u = ulow[8 * r : 8 * r + 8, at]
                s = s_out[r, :, at]
                dl = jnp.broadcast_to(both[r : r + 1, at], (8, LANES))
                for i in range(BANDS):
                    ll[i] = ll[i] + u * ulow[8 * r + i : 8 * r + i + 1, at]
                    cross[i] = cross[i] + u * s_out[r, i : i + 1, at]
                ld = ld + u * dl
                sd = sd + s * dl
                ls = ls + u
                ss = ss + s
                dd = dd + dl * dl
                ds = ds + dl

        lane = lax.broadcasted_iota(jnp.int32, (8, LANES), 1)
        columns = ll + cross + [ld, ls, sd, ss, dd, ds]
        columns += [zero] * (32 - len(columns))
        columns += list(first)
        table = zero
        for index, acc in enumerate(columns):
            if acc is not zero:
                table = jnp.where(lane == index, jnp.sum(acc, axis=1, keepdims=True), table)
        for index, acc in ((42, psq), (43, psum)):
            total = jnp.sum(jnp.sum(acc, axis=0, keepdims=True), axis=1, keepdims=True)
            table = jnp.where(lane == index, total, table)
        mom_out[...] = table

    mom, y_up, diff, ugap, dgap, s_up = call(
        moments,
        (
            shape(8, LANES),
            shape(fine_tiles, 8 * (hc + 4), LANES),
            shape(fine_tiles, h, LANES),
            shape(8 * hc, wc),
            shape(pad, wc),
            shape(hc, BANDS, wc),
        ),
        [
            pltpu.VMEM((pad, wf), F32),
            pltpu.VMEM((8 * hc, wc), F32),
            pltpu.VMEM((fine_tiles, hc + 4, LANES), F32),
        ],
    )(
        pan_image, x_loc, s_loc, from_low, from_high, d_own, ld_own, low_own,
        w_low, w_pair, w_up4, w_up3, r_adj,
    )
    devices = groups * strips
    spread = jnp.broadcast_to(mom[None], (devices,) + mom.shape)
    sums = lax.all_to_all(spread, ("rows", "band"), split_axis=0, concat_axis=0, tiled=True)

    def finish(sums_ref, y_ref, diff_ref, ugap_ref, dgap_ref, s_ref, vnir_out, swir_out, tiles, sems):
        lane = lax.broadcasted_iota(jnp.int32, (8, LANES), 1)
        sub = lax.broadcasted_iota(jnp.int32, (8, LANES), 0)
        eye = lane == sub
        total = sums_ref[0]
        for index in range(1, devices):
            total = total + sums_ref[index]

        def column(x, index):
            return jnp.broadcast_to(x[:, index : index + 1], (8, LANES))

        def across(col):
            return jnp.sum(jnp.where(eye, col, 0.0), axis=0, keepdims=True)

        def down(x):
            return jnp.sum(x, axis=0, keepdims=True)

        def solve(matrix, rhs):
            work = jnp.where(lane == 8, rhs, matrix)
            for k in range(BANDS):
                pivot_row = work[k : k + 1, :] / column(work, k)[k : k + 1, :]
                other = work - column(work, k) * pivot_row
                work = jnp.where(sub == k, pivot_row, other)
            return column(work, 8)

        n1 = float(fine_pixels)
        mean_v = column(total, 41) / n1
        mean_p = column(total, 43) / n1
        cov_v = pltpu.roll(total, LANES - 32, 1) / n1 - mean_v * across(mean_v)
        cov_p = column(total, 40) / n1 - mean_v * mean_p
        fit = solve(cov_v, cov_p)
        gain = cov_p / down(cov_p * fit)

        def tile_step(k, carry):
            for m in range(hc):
                ys = [y_ref[k, pl.ds(8 * (m + t), 8), :] for t in range(5)]
                for p in range(RATIO_V):
                    r = RATIO_V * m + p
                    value = gain * diff_ref[k, pl.ds(r, 1), :]
                    for t in range(5):
                        if C4[t, p] != 0.0:
                            value = value + float(C4[t, p]) * ys[t]
                    tiles[k, pl.ds(r, 8, stride=h), :] = value
            pltpu.make_async_copy(
                tiles.at[k], vnir_out.at[:, pl.ds(pl.multiple_of(LANES * k, LANES), LANES)], sems.at[k]
            ).start()
            return carry

        lax.fori_loop(0, fine_tiles, tile_step, 0)

        n2 = float(fine_pixels // (RATIO_V * RATIO_V))
        mean_l = column(total, 17) / n2
        mean_s = column(total, 19) / n2
        mean_d = column(total, 21) / n2
        cov_ll = total / n2 - mean_l * across(mean_l)
        cov_ls = pltpu.roll(total, LANES - 8, 1) / n2 - mean_l * across(mean_s)
        cov_ld = column(total, 16) / n2 - mean_l * mean_d
        cov_sd = column(total, 18) / n2 - mean_s * mean_d
        cov_dd = column(total, 20) / n2 - mean_d * mean_d
        gain_row = across(gain)
        a2 = cov_ll + gain * across(cov_ld) + cov_ld * gain_row + gain * gain_row * cov_dd
        b2 = cov_ls + gain * across(cov_sd)
        b2 = jnp.where(lane < BANDS, b2, 0.0)
        target = jnp.broadcast_to(jnp.sum(b2, axis=1, keepdims=True) / BANDS, (8, LANES))
        fit2 = solve(a2, target)
        numer = down(fit2 * b2)
        share_row = numer / down(fit2 * target)
        share = jnp.sum(jnp.where(eye, jnp.broadcast_to(share_row, (8, LANES)), 0.0), axis=1, keepdims=True)
        scale = down(fit2 * gain)[:, 0:1]
        fit_col = fit2[:, 0:1]
        for r in range(hc):
            seen = jnp.sum(fit_col * ugap_ref[8 * r : 8 * r + 8, :], axis=0, keepdims=True)
            seen = seen + scale * dgap_ref[r : r + 1, :]
            swir_out[:, r, :] = s_ref[r] + share * seen

        def drain(k, carry):
            pltpu.make_async_copy(
                tiles.at[k], vnir_out.at[:, pl.ds(pl.multiple_of(LANES * k, LANES), LANES)], sems.at[k]
            ).wait()
            return carry

        lax.fori_loop(0, fine_tiles, drain, 0)

    joined_vnir, joined_swir = call(
        finish,
        (shape(BANDS * h, w), shape(BANDS, hc, wc)),
        [pltpu.VMEM((fine_tiles, BANDS * h, LANES), F32), pltpu.SemaphoreType.DMA((fine_tiles,))],
        out_specs=(pl.BlockSpec(memory_space=pl.ANY), pl.BlockSpec(memory_space=pltpu.VMEM)),
    )(sums, y_up, diff, ugap, dgap, s_up)
    return joined_vnir.reshape(BANDS, h, w), joined_swir


def solution(mesh):
    return jax.shard_map(
        local,
        mesh=mesh,
        in_specs=(P("rows", "band"), P("band", "rows", None), P("band", "rows", None)),
        out_specs=(P(None, "rows", "band"), P(None, "rows", "band")),
        check_vma=False,
    )
```

```python
import math

import jax
import jax.numpy as jnp
import ml_dtypes
import numpy as np
from jax import lax
from jax.experimental import pallas as pl
from jax.experimental.pallas import tpu as pltpu
from jax.sharding import PartitionSpec as P

BANDS = 8
RATIO_V = 4
RATIO_S = 3
TAPS_V = 17
TAPS_S = 13
NYQUIST_GAIN = 0.29
LANES = 128
HALF = 64
REACH = 32
HALO = 8
F32 = jnp.float32
BF16 = jnp.bfloat16
VMEM_BYTES = 24 * 1024 * 1024
VMEM_MOST = 56 * 1024 * 1024


def gauss_taps(upscale, kernel_len):
    spread = upscale * math.sqrt(-2.0 * math.log(NYQUIST_GAIN)) / math.pi
    radius = kernel_len // 2
    offsets = np.arange(-radius, radius + 1) * 1.0
    values = np.exp(-(offsets**2) / (2.0 * spread**2))
    return values / values.sum()


def cubic_weight(distance):
    distance = abs(distance)
    if distance <= 1.0:
        return 1.5 * distance**3 - 2.5 * distance**2 + 1.0
    if distance < 2.0:
        return -0.5 * distance**3 + 2.5 * distance**2 - 4.0 * distance + 2.0
    return 0.0


def cubic_table(upscale):
    weights = np.zeros((5, upscale))
    for phase_index in range(upscale):
        centre = (phase_index + 0.5) / upscale - 0.5
        first_tap = math.floor(centre)
        fraction = centre - first_tap
        for tap_index in range(-1, 3):
            weights[first_tap + tap_index + 2, phase_index] += cubic_weight(tap_index - fraction)
    return weights


KF = gauss_taps(RATIO_V, TAPS_V)
KC = gauss_taps(RATIO_S, TAPS_S)
C4 = cubic_table(RATIO_V)
C3 = cubic_table(RATIO_S)
MEAN4 = C4.mean(axis=1)


def split(table):
    high = np.asarray(table, np.float64).astype(np.float32).astype(ml_dtypes.bfloat16)
    low = (np.asarray(table, np.float64) - high.astype(np.float64)).astype(np.float32)
    return np.stack([high, low.astype(ml_dtypes.bfloat16)])


def band_matrix(size, taps):
    radius = len(taps) // 2
    out = np.zeros((size, size))
    for row in range(size):
        for tap in range(-radius, radius + 1):
            if 0 <= row + tap < size:
                out[row, row + tap] = taps[tap + radius]
    return out


def row_tables(h):
    hc = h // RATIO_V
    mean = np.zeros((3 * hc, 3 * h))
    for row in range(3 * hc):
        mean[row, RATIO_V * row : RATIO_V * (row + 1)] = 1.0 / RATIO_V
    fine = band_matrix(3 * h, KF)
    low = band_matrix(3 * hc, KC)
    mean_fine = mean @ fine
    pad = -(-hc // 8) * 8

    def part(matrix, rows, cols):
        return matrix[rows, :][:, cols]

    def stacked(rows, cols, filt):
        a = mean if filt is None else filt @ mean
        c = mean_fine if filt is None else filt @ mean_fine
        return np.concatenate([part(a, rows, cols), -part(c, rows, cols)], axis=1)

    own = slice(h, 2 * h)
    tables = []
    for variant in range(3):
        keep = np.ones(3 * hc)
        if variant == 1:
            keep[:hc] = 0.0
        if variant == 2:
            keep[2 * hc :] = 0.0
        masked = low * keep[None, :]
        rows = []
        for filt in (None, masked):
            block = np.zeros((pad, 2 * h))
            block[:hc] = stacked(slice(hc, 2 * hc), own, filt)
            rows.append(block)
        for filt in (None, low):
            rows.append(stacked(slice(hc, hc + HALO), slice(0, h), filt))
        for filt in (None, low):
            rows.append(stacked(slice(2 * hc - HALO, 2 * hc), slice(2 * h, 3 * h), filt))
        tables.append(np.concatenate(rows, axis=0))
    coarse_rows = np.stack(tables)
    fine_rows = np.concatenate(
        [fine[h : 2 * h, h : 2 * h], fine[h : h + HALO, 0:h], fine[2 * h - HALO : 2 * h, 2 * h : 3 * h]],
        axis=0,
    )
    return coarse_rows, fine_rows


def up_rows(hc):
    out = np.zeros((RATIO_V * hc, hc + 4))
    for m in range(hc):
        for p in range(RATIO_V):
            out[RATIO_V * m + p, m : m + 5] = C4[:, p]
    return out


def column_tables():
    n = LANES
    fine = np.zeros((4 * n, 2 * n))
    mean = np.zeros((6 * n, n))
    mean_fine = np.zeros((6 * n, n))
    low = np.zeros((2 * n, n))
    pair = np.zeros((3, 2 * n, 2 * n))
    up4 = np.zeros((2 * n, RATIO_V * n))
    up3 = np.zeros((2 * n, RATIO_S * n))
    for c in range(2 * n):
        for t in range(-(TAPS_V // 2), TAPS_V // 2 + 1):
            fine[n + c + t, c] += KF[t + TAPS_V // 2]
    for c in range(n):
        for q in range(RATIO_V):
            mean[n + RATIO_V * c + q, c] = 1.0 / RATIO_V
            for t in range(-(TAPS_V // 2), TAPS_V // 2 + 1):
                mean_fine[n + RATIO_V * c + q + t, c] += KF[t + TAPS_V // 2] / RATIO_V
        for t in range(-(TAPS_S // 2), TAPS_S // 2 + 1):
            low[c + HALF + t, c] += KC[t + TAPS_S // 2]
            for s in range(-2, 3):
                value = KC[t + TAPS_S // 2] * MEAN4[s + 2]
                pair[0, c + HALF + t + s, n + c] += value
                if c + t >= 0:
                    pair[1, c + HALF + t + s, n + c] += value
                if c + t < n:
                    pair[2, c + HALF + t + s, n + c] += value
        for s in range(-2, 3):
            pair[:, c + HALF + s, c] += MEAN4[s + 2]
            for p in range(RATIO_V):
                up4[c + HALF + s, RATIO_V * c + p] += C4[s + 2, p]
            for p in range(RATIO_S):
                up3[c + HALF + s, RATIO_S * c + p] += C3[s + 2, p]
    return dict(fine=fine, mean=mean, mean_fine=mean_fine, low=low, pair=pair, up4=up4, up3=up3)


def stack_tables(tables):
    wide = 2 * LANES
    pieces, place, top = [], {}, 0
    for name, value in tables.items():
        stack = value.reshape((-1,) + value.shape[-2:])
        height, width = stack.shape[1:]
        starts = []
        for lane in range(0, width, wide):
            part = stack[:, :, lane : lane + wide]
            starts.append((top, part.shape[2]))
            piece = np.zeros((stack.shape[0] * height, wide), ml_dtypes.bfloat16)
            piece[:, : part.shape[2]] = part.reshape(-1, part.shape[2])
            pieces.append(piece)
            top += piece.shape[0]
        place[name] = (starts, height, width)
    return np.concatenate(pieces, axis=0), place


def parts2(x):
    high = x.astype(BF16)
    return high, (x - high.astype(F32)).astype(BF16)


def dot(a, b):
    return jnp.dot(a, b, preferred_element_type=F32)


def dot3(x, w):
    return dot(x[0], w[0]) + (dot(x[1], w[0]) + dot(x[0], w[1]))


def windows(x, starts, size):
    return tuple(jnp.concatenate([part[:, a : a + size] for a in starts], axis=0) for part in x)


def blocks(x, count):
    rows = x.shape[0] // count
    return jnp.concatenate([x[rows * k : rows * (k + 1)] for k in range(count)], axis=1)


def call(kernel, out_shape, scratch=(), cost=(0, 0), room=VMEM_BYTES, **specs):
    return pl.pallas_call(
        kernel,
        out_shape=out_shape,
        scratch_shapes=list(scratch),
        compiler_params=pltpu.CompilerParams(vmem_limit_bytes=room),
        cost_estimate=pl.CostEstimate(flops=cost[0], bytes_accessed=cost[1], transcendentals=0),
        **specs,
    )


ANY = pl.BlockSpec(memory_space=pl.ANY)
VMEM = pl.BlockSpec(memory_space=pltpu.VMEM)


def local(pan_image, vnir_bands, swir_bands):
    groups = lax.axis_size("band")
    strips = lax.axis_size("rows")
    h, w = pan_image.shape
    nb, hc, full = vnir_bands.shape
    _, hs, sfull = swir_bands.shape
    wc = w // RATIO_V
    ws = wc // RATIO_S
    wf = wc + LANES
    sf = ws + LANES
    pad = -(-hc // 8) * 8
    fine_tiles = w // LANES
    coarse_tiles = wc // LANES
    frame_tiles = coarse_tiles + 1
    swir_tiles = ws // LANES
    fine_pixels = h * strips * w * groups
    pairs = w // (2 * LANES)
    middle = frame_tiles - 2
    margin = RATIO_V * LANES

    def shape(*dims):
        return jax.ShapeDtypeStruct(dims, F32)

    coarse_rows, fine_rows = row_tables(h)
    cols = column_tables()
    lift = up_rows(hc)
    gram = lift.T @ lift
    rise = lift.sum(axis=0)

    swir_rows = -(-hs // RATIO_S)
    at_swir = hc
    at_edge = hc + swir_rows
    at_strip = at_edge + 1
    piece = REACH * (h // 8)
    per_row = wc // piece
    strip_rows = -(-(8 // nb) // per_row)

    def going(d):
        return (["right"] if d == 1 else []) + (["left"] if d == groups - 1 else [])

    def strip_place(d, side):
        return at_strip + strip_rows * going(d).index(side)

    chunk_rows = [at_strip + strip_rows * len(going(d)) for d in range(groups)]

    def pack(pan_ref, vnir_ref, swir_ref, *rest):
        outs, (wide, swide, edges, sems) = rest[:groups], rest[groups:]
        me = lax.axis_index("band")
        copies = [
            pltpu.make_async_copy(vnir_ref, wide.at[:, :, pl.ds(LANES, full)], sems.at[0]),
            pltpu.make_async_copy(swir_ref, swide.at[:, :, pl.ds(LANES, sfull)], sems.at[1]),
            pltpu.make_async_copy(pan_ref.at[:, pl.ds(0, LANES)], edges.at[0], sems.at[2]),
            pltpu.make_async_copy(pan_ref.at[:, pl.ds(w - LANES, LANES)], edges.at[1], sems.at[3]),
        ]
        for copy in copies:
            copy.start()
        wide[:, :, 0:LANES] = jnp.zeros((hc, nb, LANES), F32)
        wide[:, :, LANES + full : 2 * LANES + full] = jnp.zeros((hc, nb, LANES), F32)
        swide[:, :, 0:LANES] = jnp.zeros((nb, hs, LANES), F32)
        swide[:, :, LANES + sfull : 2 * LANES + sfull] = jnp.zeros((nb, hs, LANES), F32)
        for copy in copies:
            copy.wait()
        for d in range(groups):
            peer = lax.rem(me + d, groups)
            base = pl.multiple_of(peer * wc, LANES)
            sbase = pl.multiple_of(peer * ws, LANES)
            out = outs[d]
            out[0:hc] = wide[:, :, pl.ds(base + LANES, wc)]
            left = wide[:, :, pl.ds(base, LANES)]
            right = wide[:, :, pl.ds(base + LANES + wc, LANES)]
            borders = []
            for r in range(hc):
                borders += [left[r, :, LANES - HALO :], right[r, :, :HALO]]
            swin = swide[:, :, pl.ds(sbase, ws + 2 * LANES)]
            for q in range(hs):
                row = swin[:, q, :]
                lane = ws * (q % RATIO_S)
                out[at_swir + q // RATIO_S, :, lane : lane + ws] = row[:, LANES : LANES + ws]
                borders += [row[:, LANES - 2 : LANES], row[:, LANES + ws : LANES + ws + 2]]
            border = jnp.concatenate(borders, axis=1)
            out[at_edge, :, 0 : border.shape[1]] = border
            for side in going(d):
                first = strip_place(d, side)
                edge = edges[1, :, LANES - REACH :] if side == "right" else edges[0, :, :REACH]
                flat = jnp.concatenate([edge[8 * t : 8 * t + 8] for t in range(h // 8)], axis=1)
                for i in range(8 // nb):
                    lane = piece * (i % per_row)
                    out[first + i // per_row, :, lane : lane + piece] = flat[nb * i : nb * (i + 1)]

    chunks = call(
        pack,
        tuple(shape(chunk_rows[d], nb, wc) for d in range(groups)),
        [
            pltpu.VMEM((hc, nb, full + 2 * LANES), F32),
            pltpu.VMEM((nb, hs, sfull + 2 * LANES), F32),
            pltpu.VMEM((2, h, LANES), F32),
            pltpu.SemaphoreType.DMA((4,)),
        ],
        room=VMEM_MOST,
        in_specs=[ANY] * 3,
    )(pan_image, jnp.transpose(vnir_bands, (1, 0, 2)), swir_bands)
    got = [chunks[0]] + [
        lax.ppermute(chunks[d], "band", [(i, (i + d) % groups) for i in range(groups)])
        for d in range(1, groups)
    ]

    mean_parts, fine_parts = split(cols["mean"]), split(cols["mean_fine"])
    r_fine = split(fine_rows)
    r_adj = split(lift.T)
    table, place = stack_tables(
        dict(
            tall=np.concatenate([mean_parts[0], fine_parts[0]], axis=1),
            tall_low=fine_parts[1],
            fine=split(cols["fine"]),
            rows=split(coarse_rows),
            rows_fine=np.concatenate([r_fine[0], r_fine[1], r_fine[0]], axis=1),
            low=split(cols["low"]),
            pair=split(cols["pair"]),
            up4=split(cols["up4"]),
            up3=split(cols["up3"]),
            adjoint=np.concatenate([r_adj[0], r_adj[0], r_adj[0], r_adj[1], r_adj[1]], axis=1),
        )
    )

    def take(ref, name, index=0, rows=None):
        starts, height, width = place[name]
        first, height = (0, height) if rows is None else (rows[0], rows[1] - rows[0])
        pieces = []
        for start, part in starts:
            base = start + first
            if not isinstance(index, int) or index:
                base = pl.multiple_of(base + index * place[name][1], 16)
            pieces.append(ref[pl.ds(base, height), 0:part])
        return pieces[0] if len(pieces) == 1 else jnp.concatenate(pieces, axis=1)

    def both_parts(ref, name, index=0, stacked=1):
        return take(ref, name, index), take(ref, name, index + stacked)

    def shrink(panes, tall, low):
        both = dot(panes[0], tall) + dot(panes[1], tall)
        return both[:, :LANES], both[:, LANES:] + dot(panes[0], low)

    def along_rows(rc, means, fines):
        both = parts2(jnp.concatenate([means, fines], axis=0))
        return dot(rc[0], both[0]) + (dot(rc[0], both[1]) + dot(rc[1], both[0]))

    def filter_rows(rf, x):
        col = parts2(x)
        return dot(rf, jnp.concatenate([col[0], col[0], col[1]], axis=0))

    def row_variant():
        row_id = lax.axis_index("rows")
        return jnp.where(row_id == 0, 1, jnp.where(row_id == strips - 1, 2, 0))

    def early(pan_ref, table_ref, order_ref, coarse_out, fine_out):
        panes = parts2(pan_ref[...])
        starts = [margin * k - 3 * LANES for k in range(1, frame_tiles - 1)]
        means, fines = shrink(
            windows(panes, starts, 6 * LANES), take(table_ref, "tall"), take(table_ref, "tall_low")
        )
        rc = both_parts(table_ref, "rows", row_variant(), 3)
        coarse_out[...] = along_rows(rc, blocks(means, middle), blocks(fines, middle))
        starts = [2 * LANES * k - LANES for k in range(1, pairs - 1)]
        col = dot3(windows(panes, starts, 4 * LANES), both_parts(table_ref, "fine"))
        fine_out[...] = filter_rows(take(table_ref, "rows_fine"), blocks(col, pairs - 2))

    coarse_mid, fine_mid = call(
        early,
        (shape(2 * pad + 32, LANES * middle), shape(h + 2 * HALO, 2 * LANES * (pairs - 2))),
        cost=(2_000_000_000, 8_000_000),
        in_specs=[VMEM, VMEM, ANY],
    )(pan_image, table, chunks[0])

    at_s = HALO * frame_tiles
    at_ld = at_s + 2 * (sf // LANES)
    at_d = at_ld + frame_tiles
    at_low = at_d + -(-2 * frame_tiles // 8)
    sent = at_low + fine_tiles

    def assemble(pan_ref, table_ref, cm_ref, fm_ref, *rest):
        ins = rest[:groups]
        x_out, s_out, up_out, down_out, ce_out, fe_out = rest[groups:]
        me = lax.axis_index("band")

        def gather(row, lane, size):
            rows = [ins[(groups - i) % groups][row, :, lane : lane + size] for i in range(groups)]
            return pltpu.roll(jnp.concatenate(rows, axis=0), nb * me, 0)

        borders = gather(at_edge, 0, wc)
        zeros = jnp.zeros((8, HALF), F32)

        def framed(main, lane, reach):
            return jnp.concatenate(
                [
                    zeros[:, : HALF - reach],
                    borders[:, lane : lane + reach],
                    main,
                    borders[:, lane + reach : lane + 2 * reach],
                    zeros[:, : HALF - reach],
                ],
                axis=1,
            )

        for r in range(hc):
            row = framed(gather(r, 0, wc), 2 * HALO * r, HALO)
            x_out[r] = row
            for t in range(frame_tiles):
                tile = row[:, LANES * t : LANES * (t + 1)]
                if r >= hc - HALO:
                    up_out[frame_tiles * (r - hc + HALO) + t] = tile
                if r < HALO:
                    down_out[frame_tiles * r + t] = tile
        per = sf // LANES
        for q in range(hs):
            main = gather(at_swir + q // RATIO_S, ws * (q % RATIO_S), ws)
            row = framed(main, 2 * HALO * hc + 4 * q, 2)
            s_out[q] = row
            for t in range(per):
                tile = row[:, LANES * t : LANES * (t + 1)]
                if q >= hs - 2:
                    up_out[at_s + per * (q - hs + 2) + t] = tile
                if q < 2:
                    down_out[at_s + per * q + t] = tile

        def strip(d, side, empty):
            first = strip_place(d, side)
            rows = []
            for i in range(8 // nb):
                lane = piece * (i % per_row)
                rows.append(ins[d][first + i // per_row, :, lane : lane + piece])
            flat = jnp.where(empty, 0.0, jnp.concatenate(rows, axis=0))
            whole = [flat[:, REACH * t : REACH * (t + 1)] for t in range(h // 8)]
            return jnp.concatenate(whole, axis=0)

        blank = jnp.zeros((h, LANES - REACH), F32)
        left = jnp.concatenate([blank, strip(1, "right", me == 0), pan_ref[:, 0 : 3 * LANES]], axis=1)
        right = jnp.concatenate(
            [pan_ref[:, w - 3 * LANES : w], strip(groups - 1, "left", me == groups - 1), blank], axis=1
        )
        left, right = parts2(left), parts2(right)
        cut = 2 * LANES
        inner = (cut, 6 * LANES)
        lm, lf = shrink(left, take(table_ref, "tall", 0, inner), take(table_ref, "tall_low", 0, inner))
        inner = (0, 4 * LANES)
        rm, rfine = shrink(right, take(table_ref, "tall", 0, inner), take(table_ref, "tall_low", 0, inner))
        rc = both_parts(table_ref, "rows", row_variant(), 3)
        edge = along_rows(rc, jnp.concatenate([lm, rm], axis=1), jnp.concatenate([lf, rfine], axis=1))
        ce_out[...] = edge
        outer = tuple(jnp.concatenate([a, b], axis=0) for a, b in zip(left, right))
        fine_edge = filter_rows(
            take(table_ref, "rows_fine"), blocks(dot3(outer, both_parts(table_ref, "fine")), 2)
        )
        fe_out[...] = fine_edge

        def coarse(rows, k):
            if k == 0:
                return edge[rows, 0:LANES]
            if k == frame_tiles - 1:
                return edge[rows, LANES:]
            return cm_ref[rows, LANES * (k - 1) : LANES * k]

        first = 2 * pad
        for out, at, dead in ((up_out, first, 0), (down_out, first + 16, HALO - 2)):
            for k in range(frame_tiles):
                out[at_ld + k] = coarse(slice(at + 8, at + 16), k)
                small = coarse(slice(at, at + 8), k)[dead : dead + 2]
                out[at_d + k // 4, 2 * (k % 4) : 2 * (k % 4) + 2, :] = small
        for out, at in ((up_out, h), (down_out, h + HALO)):
            for k in range(fine_tiles):
                if k < 2:
                    tile = fine_edge[at : at + 8, LANES * k : LANES * (k + 1)]
                elif k >= fine_tiles - 2:
                    lane = LANES * (k - fine_tiles + 4)
                    tile = fine_edge[at : at + 8, lane : lane + LANES]
                else:
                    tile = fm_ref[at : at + 8, LANES * (k - 2) : LANES * (k - 1)]
                out[at_low + k] = tile

    x_loc, s_loc, up_send, down_send, coarse_edge, fine_edge = call(
        assemble,
        (
            shape(hc, BANDS, wf),
            shape(hs, BANDS, sf),
            shape(sent, 8, LANES),
            shape(sent, 8, LANES),
            shape(2 * pad + 32, 2 * LANES),
            shape(h + 2 * HALO, 4 * LANES),
        ),
        cost=(200_000_000, 3_000_000),
    )(pan_image, table, coarse_mid, fine_mid, *got)
    from_low = lax.ppermute(up_send, "rows", [(i, i + 1) for i in range(strips - 1)])
    from_high = lax.ppermute(down_send, "rows", [(i + 1, i) for i in range(strips - 1)])

    def moments(
        pan_ref, x_ref, s_ref, lo_ref, hi_ref, cm_ref, fm_ref, ce_ref, fe_ref,
        table_ref,
        mom_out, y_out, diff_out, ugap_out, dgap_out, s_out,
        both, ulow, q_ref,
    ):
        me = lax.axis_index("band")
        row_id = lax.axis_index("rows")

        def tiles(ref, first, number):
            return jnp.concatenate([ref[first + t] for t in range(number)], axis=1)

        def x_row(r):
            if r < 0:
                return tiles(lo_ref, frame_tiles * (HALO + r), frame_tiles)
            if r >= hc:
                return tiles(hi_ref, frame_tiles * (r - hc), frame_tiles)
            return x_ref[r]

        block_starts = [LANES * k for k in range(coarse_tiles)]
        frame = parts2(jnp.concatenate([x_row(r) for r in range(-2, hc + 2)], axis=0))
        up = dot3(windows(frame, block_starts, 2 * LANES), both_parts(table_ref, "up4"))
        size = 8 * (hc + 4)
        for k in range(coarse_tiles):
            for q in range(RATIO_V):
                y_out[RATIO_V * k + q] = up[size * k : size * (k + 1), LANES * q : LANES * (q + 1)]

        low = jnp.concatenate([fe_ref[0:h, 0 : 2 * LANES], fm_ref[0:h, :], fe_ref[0:h, 2 * LANES :]], axis=1)
        top = low[0:HALO] + tiles(lo_ref, at_low, fine_tiles)
        end = low[h - HALO : h] + tiles(hi_ref, at_low, fine_tiles)
        low = jnp.concatenate([top, low[HALO : h - HALO], end], axis=0)
        diff = pan_ref[...] - low
        p1 = low.astype(BF16)
        rest = low - p1.astype(F32)
        p2 = rest.astype(BF16)
        p3 = (rest - p2.astype(F32)).astype(BF16)
        adjoint = dot(take(table_ref, "adjoint"), jnp.concatenate([p1, p2, p3, p1, p2], axis=0))
        psum = jnp.zeros((8, LANES), F32)
        for k in range(fine_tiles):
            at = slice(LANES * k, LANES * (k + 1))
            diff_out[k] = diff[:, at]
            q_ref[k] = adjoint[:, at]
            for t in range(h // 8):
                psum = psum + low[8 * t : 8 * t + 8, at]

        zero = jnp.zeros((8, LANES), F32)
        turns = BANDS // 2 + 1

        def tile_step(k, carry):
            accs = list(carry[:turns])
            accp, accv = carry[turns], carry[turns + 1]
            ys = [y_out[k, pl.ds(8 * m, 8), :] for m in range(hc + 4)]
            for m in range(hc + 4):
                z = None
                for other in range(hc + 4):
                    if gram[m, other] != 0.0:
                        term = float(gram[m, other]) * ys[other]
                        z = term if z is None else z + term
                accs[0] = accs[0] + z * ys[m]
                for i in range(1, turns):
                    accs[i] = accs[i] + z * pltpu.roll(ys[m], i, 0)
                accp = accp + ys[m] * q_ref[k, pl.ds(m, 1), :]
                accv = accv + float(rise[m]) * ys[m]
            return tuple(accs) + (accp, accv)

        first = lax.fori_loop(0, fine_tiles, tile_step, (zero,) * (turns + 2))

        below = jnp.where(row_id > 0, 1.0, 0.0).astype(F32)
        above = jnp.where(row_id < strips - 1, 1.0, 0.0).astype(F32)
        reach = TAPS_S // 2
        means = []
        for r in range(-reach, hc + reach):
            value = float(MEAN4[2]) * x_row(r)
            for t in (1, 2):
                value = value + float(MEAN4[2 + t]) * (x_row(r - t) + x_row(r + t))
            if r < 0:
                value = value * below
            if r >= hc:
                value = value * above
            means.append(value)
        lows = []
        for r in range(hc):
            centre = r + reach
            value = float(KC[reach]) * means[centre]
            for t in range(1, reach + 1):
                value = value + float(KC[reach + t]) * (means[centre - t] + means[centre + t])
            lows.append(value)
        u_rows = windows(parts2(jnp.concatenate(means[reach : reach + hc], axis=0)), block_starts, 2 * LANES)
        l_rows = windows(parts2(jnp.concatenate(lows, axis=0)), block_starts, 2 * LANES)
        u_all = dot3(u_rows, tuple(x[:, :LANES] for x in both_parts(table_ref, "pair", 0, 3)))
        left = jnp.where(me == 0, 1, 0)
        right = jnp.where(me == groups - 1, 2, 0)
        size = 8 * hc
        last = coarse_tiles - 1
        for which, lo_k, hi_k in ((left, 0, 1), (0, 1, last), (right, last, last + 1)):
            if hi_k <= lo_k:
                continue
            wp = tuple(x[:, LANES:] for x in both_parts(table_ref, "pair", which, 3))
            part = dot3(tuple(x[size * lo_k : size * hi_k] for x in l_rows), wp)
            for k in range(lo_k, hi_k):
                at = slice(LANES * k, LANES * (k + 1))
                low_k = part[size * (k - lo_k) : size * (k - lo_k + 1)]
                ulow[:, at] = low_k
                ugap_out[:, at] = u_all[size * k : size * (k + 1)] - low_k

        column = lax.broadcasted_iota(jnp.int32, (1, wf), 1) - HALF + me * wc
        inside = jnp.where((column >= 0) & (column < groups * wc), 1.0, 0.0).astype(F32)

        def own(rows):
            return jnp.concatenate([ce_ref[rows, 0:LANES], cm_ref[rows, :], ce_ref[rows, LANES:]], axis=1)

        def small(ref):
            return jnp.concatenate(
                [ref[at_d + k // 4, 2 * (k % 4) : 2 * (k % 4) + 2, :] for k in range(frame_tiles)], axis=1
            )

        both[...] = own(slice(0, pad))
        both[0:2] = both[0:2] + small(lo_ref)
        both[hc - 2 : hc] = both[hc - 2 : hc] + small(hi_ref)
        detail = both[...]
        both[...] = own(slice(pad, 2 * pad))
        both[0:HALO] = both[0:HALO] + tiles(lo_ref, at_ld, frame_tiles)
        both[hc - HALO : hc] = both[hc - HALO : hc] + tiles(hi_ref, at_ld, frame_tiles)
        dlow_rows = windows(parts2(both[...] * inside), block_starts, 2 * LANES)
        dlow = blocks(dot3(dlow_rows, both_parts(table_ref, "low")), coarse_tiles)
        dgap_out[...] = detail[:, HALF : HALF + wc] - dlow
        both[:, 0:wc] = dlow

        per = sf // LANES
        s_rows = [tiles(lo_ref, at_s + per * q, per) for q in range(2)]
        s_rows += [s_ref[r] for r in range(hs)]
        s_rows += [tiles(hi_ref, at_s + per * q, per) for q in range(2)]
        s_parts = windows(parts2(jnp.concatenate(s_rows, axis=0)), block_starts[:swir_tiles], 2 * LANES)
        s_cols = blocks(dot3(s_parts, both_parts(table_ref, "up3")), swir_tiles)
        for m in range(hs):
            for p in range(RATIO_S):
                value = None
                for t in range(5):
                    if C3[t, p] != 0.0:
                        term = float(C3[t, p]) * s_cols[8 * (m + t) : 8 * (m + t) + 8]
                        value = term if value is None else value + term
                s_out[RATIO_S * m + p] = value

        ll = [zero] * turns
        cross = [zero] * BANDS
        ld = ls = sd = ss = dd = ds = zero
        for r in range(hc):
            for k in range(coarse_tiles):
                at = slice(LANES * k, LANES * (k + 1))
                u = ulow[8 * r : 8 * r + 8, at]
                s = s_out[r, :, at]
                dl = jnp.broadcast_to(both[r : r + 1, at], (8, LANES))
                ll[0] = ll[0] + u * u
                for i in range(1, turns):
                    ll[i] = ll[i] + u * pltpu.roll(u, i, 0)
                for i in range(BANDS):
                    cross[i] = cross[i] + u * s_out[r, i : i + 1, at]
                ld = ld + u * dl
                sd = sd + s * dl
                ls = ls + u
                ss = ss + s
                dd = dd + dl * dl
                ds = ds + dl

        lane = lax.broadcasted_iota(jnp.int32, (8, LANES), 1)
        sub = lax.broadcasted_iota(jnp.int32, (8, LANES), 0)

        def column_of(acc):
            return jnp.broadcast_to(jnp.sum(acc, axis=1, keepdims=True), (8, LANES))

        table = zero
        for base, accs in ((0, ll), (32, first[:turns])):
            for i in range(turns):
                col = column_of(accs[i])
                table = jnp.where(lane == base + lax.rem(sub + BANDS - i, BANDS), col, table)
                if 0 < i < BANDS // 2:
                    turned = pltpu.roll(col, BANDS - i, 0)
                    table = jnp.where(lane == base + lax.rem(sub + i, BANDS), turned, table)
        singles = [(8 + i, cross[i]) for i in range(BANDS)]
        singles += [(16, ld), (17, ls), (18, sd), (19, ss), (20, dd), (21, ds)]
        singles += [(40, first[turns]), (41, first[turns + 1])]
        for index, acc in singles:
            table = jnp.where(lane == index, column_of(acc), table)
        total = jnp.sum(jnp.sum(psum, axis=0, keepdims=True), axis=1, keepdims=True)
        table = jnp.where(lane == 43, total, table)
        turned = pltpu.roll(table, HALF, 1)
        mom_out[...] = jnp.where(lane[0:4] < HALF, table[0:4], turned[4:8])

    mom, y_up, diff, ugap, dgap, s_up = call(
        moments,
        (
            shape(4, LANES),
            shape(fine_tiles, 8 * (hc + 4), LANES),
            shape(fine_tiles, h, LANES),
            shape(8 * hc, wc),
            shape(pad, wc),
            shape(hc, BANDS, wc),
        ),
        [
            pltpu.VMEM((pad, wf), F32),
            pltpu.VMEM((8 * hc, wc), F32),
            pltpu.VMEM((fine_tiles, hc + 4, LANES), F32),
        ],
        cost=(1_000_000_000, 8_000_000),
    )(
        pan_image, x_loc, s_loc, from_low, from_high, coarse_mid, fine_mid, coarse_edge, fine_edge, table,
    )
    devices = groups * strips
    spread = jnp.broadcast_to(mom[None], (devices,) + mom.shape)
    sums = lax.all_to_all(spread, ("rows", "band"), split_axis=0, concat_axis=0, tiled=True)

    def finish(sums_ref, y_ref, diff_ref, ugap_ref, dgap_ref, s_ref, vnir_out, swir_out, tiles, sems):
        lane = lax.broadcasted_iota(jnp.int32, (8, LANES), 1)
        sub = lax.broadcasted_iota(jnp.int32, (8, LANES), 0)
        eye = lane == sub
        terms = [sums_ref[index] for index in range(devices)]
        while len(terms) > 1:
            terms = [sum(terms[i : i + 2][1:], terms[i]) for i in range(0, len(terms), 2)]
        total = jnp.concatenate([terms[0], pltpu.roll(terms[0], HALF, 1)], axis=0)
        def column(x, index):
            return jnp.broadcast_to(x[:, index : index + 1], (8, LANES))

        def across(col):
            return jnp.sum(jnp.where(eye, col, 0.0), axis=0, keepdims=True)

        def down(x):
            return jnp.sum(x, axis=0, keepdims=True)

        def solve(matrix, rhs):
            work = jnp.where(lane == 8, rhs, matrix)
            for k in range(BANDS):
                pivot_row = work[k : k + 1, :] / column(work, k)[k : k + 1, :]
                other = work - column(work, k) * pivot_row
                work = jnp.where(sub == k, pivot_row, other)
            return column(work, 8)

        n1 = float(fine_pixels)
        mean_v = column(total, 41) / n1
        mean_p = column(total, 43) / n1
        cov_v = pltpu.roll(total, LANES - 32, 1) / n1 - mean_v * across(mean_v)
        cov_p = column(total, 40) / n1 - mean_v * mean_p
        fit = solve(cov_v, cov_p)
        gain = cov_p / down(cov_p * fit)

        def tile_step(k, carry):
            for m in range(hc):
                ys = [y_ref[k, pl.ds(8 * (m + t), 8), :] for t in range(5)]
                for p in range(RATIO_V):
                    r = RATIO_V * m + p
                    value = gain * diff_ref[k, pl.ds(r, 1), :]
                    for t in range(5):
                        if C4[t, p] != 0.0:
                            value = value + float(C4[t, p]) * ys[t]
                    tiles[k, pl.ds(r, 8, stride=h), :] = value
            pltpu.make_async_copy(
                tiles.at[k], vnir_out.at[:, pl.ds(pl.multiple_of(LANES * k, LANES), LANES)], sems.at[k]
            ).start()
            return carry

        lax.fori_loop(0, fine_tiles, tile_step, 0)

        n2 = float(fine_pixels // (RATIO_V * RATIO_V))
        mean_l = column(total, 17) / n2
        mean_s = column(total, 19) / n2
        mean_d = column(total, 21) / n2
        cov_ll = total / n2 - mean_l * across(mean_l)
        cov_ls = pltpu.roll(total, LANES - 8, 1) / n2 - mean_l * across(mean_s)
        cov_ld = column(total, 16) / n2 - mean_l * mean_d
        cov_sd = column(total, 18) / n2 - mean_s * mean_d
        cov_dd = column(total, 20) / n2 - mean_d * mean_d
        gain_row = across(gain)
        a2 = cov_ll + gain * across(cov_ld) + cov_ld * gain_row + gain * gain_row * cov_dd
        b2 = cov_ls + gain * across(cov_sd)
        b2 = jnp.where(lane < BANDS, b2, 0.0)
        target = jnp.broadcast_to(jnp.sum(b2, axis=1, keepdims=True) / BANDS, (8, LANES))
        fit2 = solve(a2, target)
        numer = down(fit2 * b2)
        share_row = numer / down(fit2 * target)
        share = jnp.sum(jnp.where(eye, jnp.broadcast_to(share_row, (8, LANES)), 0.0), axis=1, keepdims=True)
        scale = down(fit2 * gain)[:, 0:1]
        fit_col = fit2[:, 0:1]
        for r in range(hc):
            seen = jnp.sum(fit_col * ugap_ref[8 * r : 8 * r + 8, :], axis=0, keepdims=True)
            seen = seen + scale * dgap_ref[r : r + 1, :]
            swir_out[r] = s_ref[r] + share * seen

        def drain(k, carry):
            pltpu.make_async_copy(
                tiles.at[k], vnir_out.at[:, pl.ds(pl.multiple_of(LANES * k, LANES), LANES)], sems.at[k]
            ).wait()
            return carry

        lax.fori_loop(0, fine_tiles, drain, 0)

    joined_vnir, joined_swir = call(
        finish,
        (shape(BANDS * h, w), shape(hc, BANDS, wc)),
        [pltpu.VMEM((fine_tiles, BANDS * h, LANES), F32), pltpu.SemaphoreType.DMA((fine_tiles,))],
        cost=(100_000_000, 8_000_000),
        out_specs=(ANY, VMEM),
    )(sums, y_up, diff, ugap, dgap, s_up)
    return joined_vnir.reshape(BANDS, h, w), jnp.transpose(joined_swir, (1, 0, 2))


def solution(mesh):
    return jax.shard_map(
        local,
        mesh=mesh,
        in_specs=(P("rows", "band"), P("band", "rows", None), P("band", "rows", None)),
        out_specs=(P(None, "rows", "band"), P(None, "rows", "band")),
        check_vma=False,
    )
```

```python
import math

import jax
import jax.numpy as jnp
import ml_dtypes
import numpy as np
from jax import lax
from jax.experimental import pallas as pl
from jax.experimental.pallas import tpu as pltpu
from jax.sharding import PartitionSpec as P

BANDS = 8
RATIO_V = 4
RATIO_S = 3
TAPS_V = 17
TAPS_S = 13
NYQUIST_GAIN = 0.29
LANES = 128
HALF = 64
REACH = 32
HALO = 8
F32 = jnp.float32
BF16 = jnp.bfloat16
VMEM_BYTES = 24 * 1024 * 1024
VMEM_MOST = 56 * 1024 * 1024


def gauss_taps(upscale, kernel_len):
    spread = upscale * math.sqrt(-2.0 * math.log(NYQUIST_GAIN)) / math.pi
    radius = kernel_len // 2
    offsets = np.arange(-radius, radius + 1) * 1.0
    values = np.exp(-(offsets**2) / (2.0 * spread**2))
    return values / values.sum()


def cubic_weight(distance):
    distance = abs(distance)
    if distance <= 1.0:
        return 1.5 * distance**3 - 2.5 * distance**2 + 1.0
    if distance < 2.0:
        return -0.5 * distance**3 + 2.5 * distance**2 - 4.0 * distance + 2.0
    return 0.0


def cubic_table(upscale):
    weights = np.zeros((5, upscale))
    for phase_index in range(upscale):
        centre = (phase_index + 0.5) / upscale - 0.5
        first_tap = math.floor(centre)
        fraction = centre - first_tap
        for tap_index in range(-1, 3):
            weights[first_tap + tap_index + 2, phase_index] += cubic_weight(tap_index - fraction)
    return weights


KF = gauss_taps(RATIO_V, TAPS_V)
KC = gauss_taps(RATIO_S, TAPS_S)
C4 = cubic_table(RATIO_V)
C3 = cubic_table(RATIO_S)
MEAN4 = C4.mean(axis=1)


def split(table):
    high = np.asarray(table, np.float64).astype(np.float32).astype(ml_dtypes.bfloat16)
    low = (np.asarray(table, np.float64) - high.astype(np.float64)).astype(np.float32)
    return np.stack([high, low.astype(ml_dtypes.bfloat16)])


def band_matrix(size, taps):
    radius = len(taps) // 2
    out = np.zeros((size, size))
    for row in range(size):
        for tap in range(-radius, radius + 1):
            if 0 <= row + tap < size:
                out[row, row + tap] = taps[tap + radius]
    return out


def row_tables(h):
    hc = h // RATIO_V
    mean = np.zeros((3 * hc, 3 * h))
    for row in range(3 * hc):
        mean[row, RATIO_V * row : RATIO_V * (row + 1)] = 1.0 / RATIO_V
    fine = band_matrix(3 * h, KF)
    low = band_matrix(3 * hc, KC)
    mean_fine = mean @ fine
    pad = -(-hc // 8) * 8

    def part(matrix, rows, cols):
        return matrix[rows, :][:, cols]

    def stacked(rows, cols, filt):
        a = mean if filt is None else filt @ mean
        c = mean_fine if filt is None else filt @ mean_fine
        return np.concatenate([part(a, rows, cols), -part(c, rows, cols)], axis=1)

    own = slice(h, 2 * h)
    tables = []
    for variant in range(3):
        keep = np.ones(3 * hc)
        if variant == 1:
            keep[:hc] = 0.0
        if variant == 2:
            keep[2 * hc :] = 0.0
        masked = low * keep[None, :]
        rows = []
        for filt in (None, masked):
            block = np.zeros((pad, 2 * h))
            block[:hc] = stacked(slice(hc, 2 * hc), own, filt)
            rows.append(block)
        for filt in (None, low):
            rows.append(stacked(slice(hc, hc + HALO), slice(0, h), filt))
        for filt in (None, low):
            rows.append(stacked(slice(2 * hc - HALO, 2 * hc), slice(2 * h, 3 * h), filt))
        tables.append(np.concatenate(rows, axis=0))
    coarse_rows = np.stack(tables)
    fine_rows = np.concatenate(
        [fine[h : 2 * h, h : 2 * h], fine[h : h + HALO, 0:h], fine[2 * h - HALO : 2 * h, 2 * h : 3 * h]],
        axis=0,
    )
    return coarse_rows, fine_rows


def up_rows(hc):
    out = np.zeros((RATIO_V * hc, hc + 4))
    for m in range(hc):
        for p in range(RATIO_V):
            out[RATIO_V * m + p, m : m + 5] = C4[:, p]
    return out


def column_tables():
    n = LANES
    fine = np.zeros((4 * n, 2 * n))
    mean = np.zeros((6 * n, n))
    mean_fine = np.zeros((6 * n, n))
    low = np.zeros((2 * n, n))
    pair = np.zeros((3, 2 * n, 2 * n))
    up4 = np.zeros((2 * n, RATIO_V * n))
    up3 = np.zeros((2 * n, RATIO_S * n))
    for c in range(2 * n):
        for t in range(-(TAPS_V // 2), TAPS_V // 2 + 1):
            fine[n + c + t, c] += KF[t + TAPS_V // 2]
    for c in range(n):
        for q in range(RATIO_V):
            mean[n + RATIO_V * c + q, c] = 1.0 / RATIO_V
            for t in range(-(TAPS_V // 2), TAPS_V // 2 + 1):
                mean_fine[n + RATIO_V * c + q + t, c] += KF[t + TAPS_V // 2] / RATIO_V
        for t in range(-(TAPS_S // 2), TAPS_S // 2 + 1):
            low[c + HALF + t, c] += KC[t + TAPS_S // 2]
            for s in range(-2, 3):
                value = KC[t + TAPS_S // 2] * MEAN4[s + 2]
                pair[0, c + HALF + t + s, n + c] += value
                if c + t >= 0:
                    pair[1, c + HALF + t + s, n + c] += value
                if c + t < n:
                    pair[2, c + HALF + t + s, n + c] += value
        for s in range(-2, 3):
            pair[:, c + HALF + s, c] += MEAN4[s + 2]
            for p in range(RATIO_V):
                up4[c + HALF + s, RATIO_V * c + p] += C4[s + 2, p]
            for p in range(RATIO_S):
                up3[c + HALF + s, RATIO_S * c + p] += C3[s + 2, p]
    return dict(fine=fine, mean=mean, mean_fine=mean_fine, low=low, pair=pair, up4=up4, up3=up3)


def stack_tables(tables):
    wide = 2 * LANES
    pieces, place, top = [], {}, 0
    for name, value in tables.items():
        stack = value.reshape((-1,) + value.shape[-2:])
        height, width = stack.shape[1:]
        starts = []
        for lane in range(0, width, wide):
            part = stack[:, :, lane : lane + wide]
            starts.append((top, part.shape[2]))
            piece = np.zeros((stack.shape[0] * height, wide), ml_dtypes.bfloat16)
            piece[:, : part.shape[2]] = part.reshape(-1, part.shape[2])
            pieces.append(piece)
            top += piece.shape[0]
        place[name] = (starts, height, width)
    return np.concatenate(pieces, axis=0), place


def parts2(x):
    high = x.astype(BF16)
    return high, (x - high.astype(F32)).astype(BF16)


def dot(a, b):
    return jnp.dot(a, b, preferred_element_type=F32)


def dot3(x, w):
    return dot(x[0], w[0]) + (dot(x[1], w[0]) + dot(x[0], w[1]))


def windows(x, starts, size):
    return tuple(jnp.concatenate([part[:, a : a + size] for a in starts], axis=0) for part in x)


def blocks(x, count):
    rows = x.shape[0] // count
    return jnp.concatenate([x[rows * k : rows * (k + 1)] for k in range(count)], axis=1)


def call(kernel, out_shape, scratch=(), cost=(0, 0), room=VMEM_BYTES, **specs):
    return pl.pallas_call(
        kernel,
        out_shape=out_shape,
        scratch_shapes=list(scratch),
        compiler_params=pltpu.CompilerParams(vmem_limit_bytes=room),
        cost_estimate=pl.CostEstimate(flops=cost[0], bytes_accessed=cost[1], transcendentals=0),
        **specs,
    )


ANY = pl.BlockSpec(memory_space=pl.ANY)
VMEM = pl.BlockSpec(memory_space=pltpu.VMEM)


def local(pan_image, vnir_bands, swir_bands):
    groups = lax.axis_size("band")
    strips = lax.axis_size("rows")
    h, w = pan_image.shape
    nb, hc, full = vnir_bands.shape
    _, hs, sfull = swir_bands.shape
    wc = w // RATIO_V
    ws = wc // RATIO_S
    wf = wc + LANES
    sf = ws + LANES
    pad = -(-hc // 8) * 8
    fine_tiles = w // LANES
    coarse_tiles = wc // LANES
    frame_tiles = coarse_tiles + 1
    swir_tiles = ws // LANES
    fine_pixels = h * strips * w * groups
    pairs = w // (2 * LANES)
    middle = frame_tiles - 2
    margin = RATIO_V * LANES

    def shape(*dims):
        return jax.ShapeDtypeStruct(dims, F32)

    coarse_rows, fine_rows = row_tables(h)
    cols = column_tables()
    lift = up_rows(hc)
    gram = lift.T @ lift
    rise = lift.sum(axis=0)

    swir_rows = -(-hs // RATIO_S)
    at_swir = hc
    edge_size = 2 * HALO * hc + 4 * hs
    edge_lane = ws * (hs % RATIO_S)
    shared = hs % RATIO_S and edge_lane + edge_size <= wc
    at_edge = hc + swir_rows - 1 if shared else hc + swir_rows
    edge_lane = edge_lane if shared else 0
    at_strip = at_edge + 1
    piece = REACH * (h // 8)
    per_row = wc // piece
    strip_rows = -(-(8 // nb) // per_row)

    def going(d):
        return (["right"] if d == 1 else []) + (["left"] if d == groups - 1 else [])

    def strip_place(d, side):
        return at_strip + strip_rows * going(d).index(side)

    chunk_rows = [at_strip + strip_rows * len(going(d)) for d in range(groups)]

    mean_parts, fine_parts = split(cols["mean"]), split(cols["mean_fine"])
    r_fine = split(fine_rows)
    r_adj = split(lift.T)
    table, place = stack_tables(
        dict(
            tall=np.concatenate([mean_parts[0], fine_parts[0]], axis=1),
            tall_low=fine_parts[1],
            fine=split(cols["fine"]),
            rows=split(coarse_rows),
            rows_fine=np.concatenate([r_fine[0], r_fine[1], r_fine[0]], axis=1),
            low=split(cols["low"]),
            pair=split(cols["pair"]),
            up4=split(cols["up4"]),
            up3=split(cols["up3"]),
            adjoint=np.concatenate([r_adj[0], r_adj[0], r_adj[0], r_adj[1], r_adj[1]], axis=1),
        )
    )

    sources = (pan_image, jnp.transpose(vnir_bands, (1, 0, 2)), swir_bands, jnp.asarray(table))

    def pack(pan_ref, vnir_ref, swir_ref, table_ref, *rest):
        outs, (pan_out, table_out, wide, swide, edges, sems) = rest[:groups], rest[groups:]
        me = lax.axis_index("band")
        copies = [
            pltpu.make_async_copy(vnir_ref, wide.at[:, :, pl.ds(LANES, full)], sems.at[0]),
            pltpu.make_async_copy(swir_ref, swide.at[:, :, pl.ds(LANES, sfull)], sems.at[1]),
            pltpu.make_async_copy(pan_ref.at[:, pl.ds(0, LANES)], edges.at[0], sems.at[2]),
            pltpu.make_async_copy(pan_ref.at[:, pl.ds(w - LANES, LANES)], edges.at[1], sems.at[3]),
            pltpu.make_async_copy(pan_ref, pan_out, sems.at[4]),
            pltpu.make_async_copy(table_ref, table_out, sems.at[5]),
        ]
        for copy in copies:
            copy.start()
        wide[:, :, 0:LANES] = jnp.zeros((hc, nb, LANES), F32)
        wide[:, :, LANES + full : 2 * LANES + full] = jnp.zeros((hc, nb, LANES), F32)
        swide[:, :, 0:LANES] = jnp.zeros((nb, hs, LANES), F32)
        swide[:, :, LANES + sfull : 2 * LANES + sfull] = jnp.zeros((nb, hs, LANES), F32)
        for copy in copies[:4]:
            copy.wait()
        for d in range(groups):
            peer = lax.rem(me + d, groups)
            base = pl.multiple_of(peer * wc, LANES)
            sbase = pl.multiple_of(peer * ws, LANES)
            out = outs[d]
            out[0:hc] = wide[:, :, pl.ds(base + LANES, wc)]
            left = wide[:, :, pl.ds(base, LANES)]
            right = wide[:, :, pl.ds(base + LANES + wc, LANES)]
            borders = []
            for r in range(hc):
                borders += [left[r, :, LANES - HALO :], right[r, :, :HALO]]
            swin = swide[:, :, pl.ds(sbase, ws + 2 * LANES)]
            for q in range(hs):
                row = swin[:, q, :]
                lane = ws * (q % RATIO_S)
                out[at_swir + q // RATIO_S, :, lane : lane + ws] = row[:, LANES : LANES + ws]
                borders += [row[:, LANES - 2 : LANES], row[:, LANES + ws : LANES + ws + 2]]
            border = jnp.concatenate(borders, axis=1)
            out[at_edge, :, edge_lane : edge_lane + edge_size] = border
            for side in going(d):
                first = strip_place(d, side)
                edge = edges[1, :, LANES - REACH :] if side == "right" else edges[0, :, :REACH]
                flat = jnp.concatenate([edge[8 * t : 8 * t + 8] for t in range(h // 8)], axis=1)
                for i in range(8 // nb):
                    lane = piece * (i % per_row)
                    out[first + i // per_row, :, lane : lane + piece] = flat[nb * i : nb * (i + 1)]
        for copy in copies[4:]:
            copy.wait()

    staged = call(
        pack,
        tuple(shape(chunk_rows[d], nb, wc) for d in range(groups))
        + (shape(h, w), jax.ShapeDtypeStruct(table.shape, BF16)),
        [
            pltpu.VMEM((hc, nb, full + 2 * LANES), F32),
            pltpu.VMEM((nb, hs, sfull + 2 * LANES), F32),
            pltpu.VMEM((2, h, LANES), F32),
            pltpu.SemaphoreType.DMA((6,)),
        ],
        cost=(0, 8_000_000),
        in_specs=[ANY] * 4,
    )(*(pltpu.with_memory_space_constraint(x, pltpu.HBM) for x in sources))
    chunks, pan_held, table_held = staged[:groups], staged[groups], staged[groups + 1]
    got = [chunks[0]] + [
        lax.ppermute(chunks[d], "band", [(i, (i + d) % groups) for i in range(groups)])
        for d in range(1, groups)
    ]

    def take(ref, name, index=0, rows=None):
        starts, height, width = place[name]
        first, height = (0, height) if rows is None else (rows[0], rows[1] - rows[0])
        pieces = []
        for start, part in starts:
            base = start + first
            if not isinstance(index, int) or index:
                base = pl.multiple_of(base + index * place[name][1], 16)
            pieces.append(ref[pl.ds(base, height), 0:part])
        return pieces[0] if len(pieces) == 1 else jnp.concatenate(pieces, axis=1)

    def both_parts(ref, name, index=0, stacked=1):
        return take(ref, name, index), take(ref, name, index + stacked)

    def shrink(panes, tall, low):
        both = dot(panes[0], tall) + dot(panes[1], tall)
        return both[:, :LANES], both[:, LANES:] + dot(panes[0], low)

    def along_rows(rc, means, fines):
        both = parts2(jnp.concatenate([means, fines], axis=0))
        return dot(rc[0], both[0]) + (dot(rc[0], both[1]) + dot(rc[1], both[0]))

    def filter_rows(rf, x):
        col = parts2(x)
        return dot(rf, jnp.concatenate([col[0], col[0], col[1]], axis=0))

    def row_variant():
        row_id = lax.axis_index("rows")
        return jnp.where(row_id == 0, 1, jnp.where(row_id == strips - 1, 2, 0))

    pairs_in = [(i, i ^ 1) for i in range(strips) if i ^ 1 < strips]
    pairs_out = [(i, i + 1) for i in range(1, strips - 1, 2)]
    pairs_out += [(j, i) for i, j in pairs_out]

    def is_even():
        return lax.rem(lax.axis_index("rows"), 2) == 0

    def put(outs, index, up, down):
        even = is_even()
        outs[0][index] = jnp.where(even, up, down)
        outs[1][index] = jnp.where(even, down, up)

    def arrived(refs, index, low):
        even = is_even()
        inner, outer = refs[0][index], refs[1][index]
        return jnp.where(even, outer, inner) if low else jnp.where(even, inner, outer)

    def trade(inner, outer):
        return lax.ppermute(inner, "rows", pairs_in), lax.ppermute(outer, "rows", pairs_out)

    at_up, at_down = 2 * pad, 2 * pad + 16

    def put_small(outs, first, ups, downs):
        blank = jnp.zeros((2, LANES), F32)
        for i in range(0, len(ups), 4):
            up = ups[i : i + 4] + [blank] * (4 - len(ups[i : i + 4]))
            down = downs[i : i + 4] + [blank] * (4 - len(downs[i : i + 4]))
            put(outs, first + i // 4, jnp.concatenate(up, axis=0), jnp.concatenate(down, axis=0))

    inner_fine = fine_tiles - 4
    mid_low = 0
    mid_sent = inner_fine

    def early(pan_ref, table_ref, coarse_out, fine_out, *outs):
        panes = parts2(pan_ref[...])
        starts = [margin * k - 3 * LANES for k in range(1, frame_tiles - 1)]
        means, fines = shrink(
            windows(panes, starts, 6 * LANES), take(table_ref, "tall"), take(table_ref, "tall_low")
        )
        rc = both_parts(table_ref, "rows", row_variant(), 3)
        rows = along_rows(rc, blocks(means, middle), blocks(fines, middle))
        coarse_out[...] = rows
        starts = [2 * LANES * k - LANES for k in range(1, pairs - 1)]
        col = dot3(windows(panes, starts, 4 * LANES), both_parts(table_ref, "fine"))
        rows = filter_rows(take(table_ref, "rows_fine"), blocks(col, pairs - 2))
        fine_out[...] = rows[0:h]
        for k in range(inner_fine):
            at = slice(LANES * k, LANES * (k + 1))
            put(outs, mid_low + k, rows[h : h + HALO, at], rows[h + HALO : h + 2 * HALO, at])

    coarse_mid, fine_mid, mid_in, mid_out = call(
        early,
        (
            shape(2 * pad + 32, LANES * middle),
            shape(h, LANES * inner_fine),
            shape(mid_sent, 8, LANES),
            shape(mid_sent, 8, LANES),
        ),
        cost=(2_000_000_000, 8_000_000),
    )(pan_held, table_held)
    mid_in, mid_out = trade(mid_in, mid_out)

    border_tiles = -(-edge_size // LANES)
    at_s = HALO * coarse_tiles
    at_h = at_s + 2 * swir_tiles
    at_ld = at_h + border_tiles
    at_d = at_ld + frame_tiles
    at_low = at_d + -(-frame_tiles // 4)
    sent = at_low + 4

    def framed(main, borders, lane, reach):
        blank = jnp.zeros((8, HALF - reach), F32)
        left = borders[:, lane : lane + reach]
        right = borders[:, lane + reach : lane + 2 * reach]
        return jnp.concatenate([blank, left, main, right, blank], axis=1)

    def assemble(pan_ref, table_ref, cm_ref, order_ref, order_too_ref, *rest):
        ins = rest[:groups]
        x_out, s_out, ce_out, fe_out = rest[groups : groups + 4]
        outs = rest[groups + 4 :]
        me = lax.axis_index("band")

        def gather(row, lane, size):
            rows = [ins[(groups - i) % groups][row, :, lane : lane + size] for i in range(groups)]
            return pltpu.roll(jnp.concatenate(rows, axis=0), nb * me, 0)

        def tile(x, t):
            return x[:, LANES * t : LANES * (t + 1)]

        borders = gather(at_edge, edge_lane, edge_size)
        blank = jnp.zeros((8, LANES * border_tiles - edge_size), F32)
        borders = jnp.concatenate([borders, blank], axis=1)
        for t in range(border_tiles):
            put(outs, at_h + t, tile(borders, t), tile(borders, t))
        mains = [gather(r, 0, wc) for r in range(hc)]
        for r in range(hc):
            x_out[r] = framed(mains[r], borders, 2 * HALO * r, HALO)
        for r in range(HALO):
            for t in range(coarse_tiles):
                put(outs, coarse_tiles * r + t, tile(mains[hc - HALO + r], t), tile(mains[r], t))
        shorts = [gather(at_swir + q // RATIO_S, ws * (q % RATIO_S), ws) for q in range(hs)]
        for q in range(hs):
            s_out[q] = framed(shorts[q], borders, 2 * HALO * hc + 4 * q, 2)
        for q in range(2):
            for t in range(swir_tiles):
                put(outs, at_s + swir_tiles * q + t, tile(shorts[hs - 2 + q], t), tile(shorts[q], t))

        def strip(d, side, empty):
            first = strip_place(d, side)
            rows = []
            for i in range(8 // nb):
                lane = piece * (i % per_row)
                rows.append(ins[d][first + i // per_row, :, lane : lane + piece])
            flat = jnp.where(empty, 0.0, jnp.concatenate(rows, axis=0))
            whole = [flat[:, REACH * t : REACH * (t + 1)] for t in range(h // 8)]
            return jnp.concatenate(whole, axis=0)

        blank = jnp.zeros((h, LANES - REACH), F32)
        left = jnp.concatenate([blank, strip(1, "right", me == 0), pan_ref[:, 0 : 3 * LANES]], axis=1)
        right = jnp.concatenate(
            [pan_ref[:, w - 3 * LANES : w], strip(groups - 1, "left", me == groups - 1), blank], axis=1
        )
        left, right = parts2(left), parts2(right)
        cut = 2 * LANES
        inner = (cut, 6 * LANES)
        lm, lf = shrink(left, take(table_ref, "tall", 0, inner), take(table_ref, "tall_low", 0, inner))
        inner = (0, 4 * LANES)
        rm, rfine = shrink(right, take(table_ref, "tall", 0, inner), take(table_ref, "tall_low", 0, inner))
        rc = both_parts(table_ref, "rows", row_variant(), 3)
        edge = along_rows(rc, jnp.concatenate([lm, rm], axis=1), jnp.concatenate([lf, rfine], axis=1))
        ce_out[...] = edge[0 : 2 * pad]
        outer = tuple(jnp.concatenate([a, b], axis=0) for a, b in zip(left, right))
        fine_edge = filter_rows(
            take(table_ref, "rows_fine"), blocks(dot3(outer, both_parts(table_ref, "fine")), 2)
        )
        fe_out[...] = fine_edge[0:h]
        sides = jnp.concatenate([edge[:, :LANES], cm_ref[...], edge[:, LANES:]], axis=1)
        ups, downs = [], []
        for k in range(frame_tiles):
            part = tile(sides, k)
            put(outs, at_ld + k, part[at_up + 8 : at_up + 16], part[at_down + 8 : at_down + 16])
            ups.append(part[at_up : at_up + 2])
            downs.append(part[at_down + HALO - 2 : at_down + HALO])
        put_small(outs, at_d, ups, downs)
        for k in range(4):
            at = slice(LANES * k, LANES * (k + 1))
            put(outs, at_low + k, fine_edge[h : h + HALO, at], fine_edge[h + HALO : h + 2 * HALO, at])

    x_loc, s_loc, coarse_edge, fine_edge, rest_in, rest_out = call(
        assemble,
        (
            shape(hc, BANDS, wf),
            shape(hs, BANDS, sf),
            shape(2 * pad, 2 * LANES),
            shape(h, 4 * LANES),
            shape(sent, 8, LANES),
            shape(sent, 8, LANES),
        ),
        cost=(200_000_000, 3_000_000),
        in_specs=[VMEM, VMEM, VMEM, ANY, ANY] + [VMEM] * groups,
    )(pan_held, table_held, coarse_mid, mid_in, mid_out, *got)
    rest_in, rest_out = trade(rest_in, rest_out)

    turns = BANDS // 2 + 1
    block_starts = [LANES * k for k in range(coarse_tiles)]
    own_rows = range(2, hc + 2)
    halo_rows = (0, 1, hc + 2, hc + 3)
    whole_rows = range(2, hc - 2)
    first_whole = RATIO_V * whole_rows[0]
    whole_count = RATIO_V * len(whole_rows)

    def lifted(rows, table_ref, store):
        stack = windows(parts2(jnp.concatenate(rows, axis=0)), block_starts, 2 * LANES)
        up = dot3(stack, both_parts(table_ref, "up4"))
        size = 8 * len(rows)
        for k in range(coarse_tiles):
            for q in range(RATIO_V):
                store(RATIO_V * k + q, up[size * k : size * (k + 1), LANES * q : LANES * (q + 1)])

    def weighted(pairs):
        value = None
        for weight, x in pairs:
            if weight != 0.0:
                value = float(weight) * x if value is None else value + float(weight) * x
        return value

    def adjoint_of(table_ref, low):
        p1 = low.astype(BF16)
        over = low - p1.astype(F32)
        p2 = over.astype(BF16)
        p3 = (over - p2.astype(F32)).astype(BF16)
        return dot(take(table_ref, "adjoint"), jnp.concatenate([p1, p2, p3, p1, p2], axis=0))

    def tile_sum(x):
        total = jnp.zeros((8, LANES), F32)
        for k in range(x.shape[1] // LANES):
            for t in range(x.shape[0] // 8):
                total = total + x[8 * t : 8 * t + 8, LANES * k : LANES * (k + 1)]
        return total

    def joined_low(low, top, end):
        return jnp.concatenate([low[0:HALO] + top, low[HALO : h - HALO], low[h - HALO : h] + end], axis=0)

    def inside(
        pan_ref, x_ref, s_ref, mid_in_ref, mid_out_ref, fm_ref, table_ref,
        y_out, v_out, acc_out, s_out, diff_out, q_out,
    ):
        def store(index, value):
            y_out[index] = value

        lifted([x_ref[r] for r in range(hc)], table_ref, store)
        rows = parts2(jnp.concatenate([s_ref[q] for q in range(hs)], axis=0))
        s_cols = dot3(windows(rows, block_starts[:swir_tiles], 2 * LANES), both_parts(table_ref, "up3"))
        s_out[...] = blocks(s_cols, swir_tiles)

        mid = (mid_in_ref, mid_out_ref)
        top, end = (
            jnp.concatenate([arrived(mid, mid_low + k, low) for k in range(inner_fine)], axis=1)
            for low in (True, False)
        )
        low = joined_low(fm_ref[...], top, end)
        diff = pan_ref[:, 2 * LANES : w - 2 * LANES] - low
        adjoint = adjoint_of(table_ref, low)
        for k in range(inner_fine):
            at = slice(LANES * k, LANES * (k + 1))
            diff_out[k] = diff[:, at]
            q_out[k] = adjoint[:, at]
        acc_out[turns + 1] = tile_sum(low)

        def tile_step(k, carry):
            accs, accv = list(carry[:turns]), carry[turns]
            ys = {m: y_out[k, pl.ds(8 * (m - 2), 8), :] for m in own_rows}
            for m in own_rows:
                z = weighted((gram[m, other], ys[other]) for other in own_rows)
                accs[0] = accs[0] + z * ys[m]
                for i in range(1, turns):
                    accs[i] = accs[i] + z * pltpu.roll(ys[m], i, 0)
                accv = accv + float(rise[m]) * ys[m]
            for m in whole_rows:
                for p in range(RATIO_V):
                    r = RATIO_V * m + p - first_whole
                    v_out[k, pl.ds(8 * r, 8), :] = weighted((C4[t, p], ys[m + t]) for t in range(5) if C4[t, p] != 0.0)
            return tuple(accs) + (accv,)

        zero = jnp.zeros((8, LANES), F32)
        first = lax.fori_loop(0, fine_tiles, tile_step, (zero,) * (turns + 1))
        for i in range(turns + 1):
            acc_out[i] = first[i]

    y_own, v_own, acc_own, s_own, diff_mid, q_mid = call(
        inside,
        (
            shape(fine_tiles, 8 * hc, LANES),
            shape(fine_tiles, 8 * whole_count, LANES),
            shape(turns + 2, 8, LANES),
            shape(8 * hs, wc),
            shape(inner_fine, h, LANES),
            shape(inner_fine, hc + 4, LANES),
        ),
        cost=(2_000_000_000, 8_000_000),
    )(pan_held, x_loc, s_loc, mid_in, mid_out, fine_mid, table_held)

    def moments(
        pan_ref, x_ref, y_ref, acc_ref, scol_ref, diff_ref, qmid_ref,
        rest_in_ref, rest_out_ref, cm_ref, ce_ref, fe_ref, table_ref,
        mom_out, y_out, diff_out, ugap_out, dgap_out, s_out,
        both, ulow, q_ref,
    ):
        me = lax.axis_index("band")
        row_id = lax.axis_index("rows")
        rest = (rest_in_ref, rest_out_ref)

        def tiles(refs, low, indices):
            return jnp.concatenate([arrived(refs, i, low) for i in indices], axis=1)

        def halo(first, per, reach, start, count):
            sides = []
            for low, base in ((True, start[0]), (False, start[1])):
                borders = tiles(rest, low, range(at_h, at_h + border_tiles))
                rows = []
                for r in range(count):
                    main = tiles(rest, low, range(first + per * r, first + per * (r + 1)))
                    rows.append(framed(main, borders, base + 2 * reach * r, reach))
                sides.append(rows)
            return sides

        x_low, x_high = halo(0, coarse_tiles, HALO, (2 * HALO * (hc - HALO), 0), HALO)

        def x_row(r):
            if r < 0:
                return x_low[HALO + r]
            if r >= hc:
                return x_high[r - hc]
            return x_ref[r]

        def store(index, value):
            y_out[index] = value

        lifted([x_row(r) for r in (-2, -1, hc, hc + 1)], table_ref, store)

        top, end = (tiles(rest, low, range(at_low, at_low + 4)) for low in (True, False))
        low = joined_low(fe_ref[...], top, end)
        diff = jnp.concatenate([pan_ref[:, : 2 * LANES], pan_ref[:, w - 2 * LANES :]], axis=1) - low
        adjoint = adjoint_of(table_ref, low)
        psum = acc_ref[turns + 1] + tile_sum(low)
        outer_tiles = (0, 1, fine_tiles - 2, fine_tiles - 1)
        for i, k in enumerate(outer_tiles):
            at = slice(LANES * i, LANES * (i + 1))
            diff_out[k] = diff[:, at]
            q_ref[k] = adjoint[:, at]
        for k in range(inner_fine):
            diff_out[k + 2] = diff_ref[k]
            q_ref[k + 2] = qmid_ref[k]

        zero = jnp.zeros((8, LANES), F32)

        def tile_step(k, carry):
            accs = list(carry[:turns])
            accp, accv = carry[turns], carry[turns + 1]
            ys = {m: y_ref[k, pl.ds(8 * (m - 2), 8), :] for m in own_rows}
            for i, m in enumerate(halo_rows):
                ys[m] = y_out[k, pl.ds(8 * i, 8), :]
            for m in halo_rows:
                near = weighted((gram[m, other], ys[other]) for other in own_rows)
                whole = near + weighted((gram[m, other], ys[other]) for other in halo_rows)
                accs[0] = accs[0] + ys[m] * (near + whole)
                for i in range(1, turns):
                    accs[i] = accs[i] + whole * pltpu.roll(ys[m], i, 0) + ys[m] * pltpu.roll(near, i, 0)
                accv = accv + float(rise[m]) * ys[m]
            for m in range(hc + 4):
                accp = accp + ys[m] * q_ref[k, pl.ds(m, 1), :]
            return tuple(accs) + (accp, accv)

        start = tuple(acc_ref[i] for i in range(turns)) + (zero, acc_ref[turns])
        first = lax.fori_loop(0, fine_tiles, tile_step, start)

        below = jnp.where(row_id > 0, 1.0, 0.0).astype(F32)
        above = jnp.where(row_id < strips - 1, 1.0, 0.0).astype(F32)
        reach = TAPS_S // 2
        means = []
        for r in range(-reach, hc + reach):
            value = float(MEAN4[2]) * x_row(r)
            for t in (1, 2):
                value = value + float(MEAN4[2 + t]) * (x_row(r - t) + x_row(r + t))
            if r < 0:
                value = value * below
            if r >= hc:
                value = value * above
            means.append(value)
        lows = []
        for r in range(hc):
            centre = r + reach
            value = float(KC[reach]) * means[centre]
            for t in range(1, reach + 1):
                value = value + float(KC[reach + t]) * (means[centre - t] + means[centre + t])
            lows.append(value)
        u_rows = windows(parts2(jnp.concatenate(means[reach : reach + hc], axis=0)), block_starts, 2 * LANES)
        l_rows = windows(parts2(jnp.concatenate(lows, axis=0)), block_starts, 2 * LANES)
        u_all = dot3(u_rows, tuple(x[:, :LANES] for x in both_parts(table_ref, "pair", 0, 3)))
        left = jnp.where(me == 0, 1, 0)
        right = jnp.where(me == groups - 1, 2, 0)
        size = 8 * hc
        last = coarse_tiles - 1
        for which, lo_k, hi_k in ((left, 0, 1), (0, 1, last), (right, last, last + 1)):
            if hi_k <= lo_k:
                continue
            wp = tuple(x[:, LANES:] for x in both_parts(table_ref, "pair", which, 3))
            part = dot3(tuple(x[size * lo_k : size * hi_k] for x in l_rows), wp)
            for k in range(lo_k, hi_k):
                at = slice(LANES * k, LANES * (k + 1))
                low_k = part[size * (k - lo_k) : size * (k - lo_k + 1)]
                ulow[:, at] = low_k
                ugap_out[:, at] = u_all[size * k : size * (k + 1)] - low_k

        column = lax.broadcasted_iota(jnp.int32, (1, wf), 1) - HALF + me * wc
        valid = jnp.where((column >= 0) & (column < groups * wc), 1.0, 0.0).astype(F32)

        def own(rows):
            return jnp.concatenate([ce_ref[rows, 0:LANES], cm_ref[rows, :], ce_ref[rows, LANES:]], axis=1)

        def small(low):
            rows = [arrived(rest, at_d + k // 4, low)[2 * (k % 4) : 2 * (k % 4) + 2] for k in range(frame_tiles)]
            return jnp.concatenate(rows, axis=1)

        both[...] = own(slice(0, pad))
        both[0:2] = both[0:2] + small(True)
        both[hc - 2 : hc] = both[hc - 2 : hc] + small(False)
        detail = both[...]
        both[...] = own(slice(pad, 2 * pad))
        both[0:HALO] = both[0:HALO] + tiles(rest, True, range(at_ld, at_ld + frame_tiles))
        both[hc - HALO : hc] = both[hc - HALO : hc] + tiles(rest, False, range(at_ld, at_ld + frame_tiles))
        dlow_rows = windows(parts2(both[...] * valid), block_starts, 2 * LANES)
        dlow = blocks(dot3(dlow_rows, both_parts(table_ref, "low")), coarse_tiles)
        dgap_out[...] = detail[:, HALF : HALF + wc] - dlow
        both[:, 0:wc] = dlow

        s_low, s_high = halo(at_s, swir_tiles, 2, (2 * HALO * hc + 4 * (hs - 2), 2 * HALO * hc), 2)
        s_parts = windows(parts2(jnp.concatenate(s_low + s_high, axis=0)), block_starts[:swir_tiles], 2 * LANES)
        s_around = blocks(dot3(s_parts, both_parts(table_ref, "up3")), swir_tiles)
        s_cols = jnp.concatenate([s_around[0:16], scol_ref[...], s_around[16:32]], axis=0)
        for m in range(hs):
            for p in range(RATIO_S):
                value = None
                for t in range(5):
                    if C3[t, p] != 0.0:
                        term = float(C3[t, p]) * s_cols[8 * (m + t) : 8 * (m + t) + 8]
                        value = term if value is None else value + term
                s_out[RATIO_S * m + p] = value

        ll = [zero] * turns
        cross = [zero] * BANDS
        ld = ls = sd = ss = dd = ds = zero
        for r in range(hc):
            for k in range(coarse_tiles):
                at = slice(LANES * k, LANES * (k + 1))
                u = ulow[8 * r : 8 * r + 8, at]
                s = s_out[r, :, at]
                dl = jnp.broadcast_to(both[r : r + 1, at], (8, LANES))
                ll[0] = ll[0] + u * u
                for i in range(1, turns):
                    ll[i] = ll[i] + u * pltpu.roll(u, i, 0)
                for i in range(BANDS):
                    cross[i] = cross[i] + u * s_out[r, i : i + 1, at]
                ld = ld + u * dl
                sd = sd + s * dl
                ls = ls + u
                ss = ss + s
                dd = dd + dl * dl
                ds = ds + dl

        lane = lax.broadcasted_iota(jnp.int32, (8, LANES), 1)
        sub = lax.broadcasted_iota(jnp.int32, (8, LANES), 0)

        def column_of(acc):
            return jnp.broadcast_to(jnp.sum(acc, axis=1, keepdims=True), (8, LANES))

        table = zero
        for base, accs in ((0, ll), (32, first[:turns])):
            for i in range(turns):
                col = column_of(accs[i])
                table = jnp.where(lane == base + lax.rem(sub + BANDS - i, BANDS), col, table)
                if 0 < i < BANDS // 2:
                    turned = pltpu.roll(col, BANDS - i, 0)
                    table = jnp.where(lane == base + lax.rem(sub + i, BANDS), turned, table)
        singles = [(8 + i, cross[i]) for i in range(BANDS)]
        singles += [(16, ld), (17, ls), (18, sd), (19, ss), (20, dd), (21, ds)]
        singles += [(40, first[turns]), (41, first[turns + 1])]
        for index, acc in singles:
            table = jnp.where(lane == index, column_of(acc), table)
        total = jnp.sum(jnp.sum(psum, axis=0, keepdims=True), axis=1, keepdims=True)
        table = jnp.where(lane == 43, total, table)
        turned = pltpu.roll(table, HALF, 1)
        mom_out[...] = jnp.where(lane[0:4] < HALF, table[0:4], turned[4:8])

    mom, y_halo, diff, ugap, dgap, s_up = call(
        moments,
        (
            shape(4, LANES),
            shape(fine_tiles, 32, LANES),
            shape(fine_tiles, h, LANES),
            shape(8 * hc, wc),
            shape(pad, wc),
            shape(hc, BANDS, wc),
        ),
        [
            pltpu.VMEM((pad, wf), F32),
            pltpu.VMEM((8 * hc, wc), F32),
            pltpu.VMEM((fine_tiles, hc + 4, LANES), F32),
        ],
        cost=(1_000_000_000, 8_000_000),
    )(
        pan_held, x_loc, y_own, acc_own, s_own, diff_mid, q_mid,
        rest_in, rest_out, coarse_mid, coarse_edge, fine_edge, table_held,
    )
    devices = groups * strips
    spread = jnp.broadcast_to(mom[None], (devices,) + mom.shape)
    sums = lax.all_to_all(spread, ("rows", "band"), split_axis=0, concat_axis=0, tiled=True)

    def finish(
        sums_ref, y_ref, yh_ref, v_ref, diff_ref, ugap_ref, dgap_ref, s_ref,
        vnir_out, swir_out, tiles, swir, sems,
    ):
        lane = lax.broadcasted_iota(jnp.int32, (8, LANES), 1)
        sub = lax.broadcasted_iota(jnp.int32, (8, LANES), 0)
        eye = lane == sub
        terms = [sums_ref[index] for index in range(devices)]
        while len(terms) > 1:
            terms = [sum(terms[i : i + 2][1:], terms[i]) for i in range(0, len(terms), 2)]
        total = jnp.concatenate([terms[0], pltpu.roll(terms[0], HALF, 1)], axis=0)

        def column(x, index):
            return jnp.broadcast_to(x[:, index : index + 1], (8, LANES))

        def across(col):
            return jnp.sum(jnp.where(eye, col, 0.0), axis=0, keepdims=True)

        def down(x):
            return jnp.sum(x, axis=0, keepdims=True)

        def solve(matrix, rhs):
            cols = [column(matrix, j) for j in range(BANDS)] + [rhs]
            inverse = jnp.zeros((8, LANES), F32)
            for k in range(BANDS):
                pivot = 1.0 / jnp.broadcast_to(cols[k][k : k + 1], (8, LANES))
                inverse = jnp.where(sub == k, pivot, inverse)
                factor = jnp.where(sub == k, 0.0, cols[k] * pivot)
                for j in range(k + 1, BANDS + 1):
                    cols[j] = cols[j] - factor * jnp.broadcast_to(cols[j][k : k + 1], (8, LANES))
            return cols[BANDS] * inverse

        n1 = float(fine_pixels)
        mean_v = column(total, 41) / n1
        mean_p = column(total, 43) / n1
        cov_v = pltpu.roll(total, LANES - 32, 1) / n1 - mean_v * across(mean_v)
        cov_p = column(total, 40) / n1 - mean_v * mean_p
        gain = cov_p / down(cov_p * solve(cov_v, cov_p))

        n2 = float(fine_pixels // (RATIO_V * RATIO_V))
        mean_l = column(total, 17) / n2
        mean_s = column(total, 19) / n2
        mean_d = column(total, 21) / n2
        cov_ll = total / n2 - mean_l * across(mean_l)
        cov_ls = pltpu.roll(total, LANES - 8, 1) / n2 - mean_l * across(mean_s)
        cov_ld = column(total, 16) / n2 - mean_l * mean_d
        cov_sd = column(total, 18) / n2 - mean_s * mean_d
        cov_dd = column(total, 20) / n2 - mean_d * mean_d
        gain_row = across(gain)
        a2 = cov_ll + gain * across(cov_ld) + cov_ld * gain_row + gain * gain_row * cov_dd
        b2 = jnp.where(lane < BANDS, cov_ls + gain * across(cov_sd), 0.0)
        target = jnp.broadcast_to(jnp.sum(b2, axis=1, keepdims=True) / BANDS, (8, LANES))

        def sent_tile(k):
            lanes = pl.ds(pl.multiple_of(LANES * k, LANES), LANES)
            return pltpu.make_async_copy(tiles.at[k], vnir_out.at[:, lanes], sems.at[k])

        def tile_step(k, carry):
            work, inverse = carry
            here = sub == k
            row = down(jnp.where(here, work, 0.0))
            col = jnp.sum(jnp.where(lane == k, work, 0.0), axis=1, keepdims=True)
            pivot = 1.0 / jnp.where(k < BANDS, down(jnp.where(here[:, 0:1], col, 0.0)), 1.0)
            inverse = jnp.where(here, pivot, inverse)
            work = work - jnp.where(here, 0.0, col * pivot) * row

            ys = {m: y_ref[k, pl.ds(8 * (m - 2), 8), :] for m in own_rows}
            for i, m in enumerate(halo_rows):
                ys[m] = yh_ref[k, pl.ds(8 * i, 8), :]
            for m in range(hc):
                for p in range(RATIO_V):
                    r = RATIO_V * m + p
                    if m in whole_rows:
                        value = v_ref[k, pl.ds(8 * (r - first_whole), 8), :]
                    else:
                        value = weighted((C4[t, p], ys[m + t]) for t in range(5) if C4[t, p] != 0.0)
                    value = value + gain * diff_ref[k, pl.ds(r, 1), :]
                    tiles[k, pl.ds(r, 8, stride=h), :] = value
            sent_tile(k).start()
            return work, inverse

        start = (jnp.where(lane == BANDS, target, a2), jnp.zeros((8, LANES), F32))
        work, inverse = lax.fori_loop(0, fine_tiles, tile_step, start)
        fit2 = column(work, BANDS) * inverse
        numer = down(fit2 * b2)
        share_row = numer / down(fit2 * target)
        share = jnp.sum(jnp.where(eye, jnp.broadcast_to(share_row, (8, LANES)), 0.0), axis=1, keepdims=True)
        scale = down(fit2 * gain)[:, 0:1]
        fit_col = fit2[:, 0:1]
        for r in range(hc):
            seen = jnp.sum(fit_col * ugap_ref[8 * r : 8 * r + 8, :], axis=0, keepdims=True)
            seen = seen + scale * dgap_ref[r : r + 1, :]
            swir[r] = s_ref[r] + share * seen
        last = pltpu.make_async_copy(swir, swir_out, sems.at[fine_tiles])
        last.start()

        def drain(k, carry):
            sent_tile(k).wait()
            return carry

        lax.fori_loop(0, fine_tiles, drain, 0)
        last.wait()

    joined_vnir, joined_swir = call(
        finish,
        (shape(BANDS * h, w), shape(hc, BANDS, wc)),
        [
            pltpu.VMEM((fine_tiles, BANDS * h, LANES), F32),
            pltpu.VMEM((hc, BANDS, wc), F32),
            pltpu.SemaphoreType.DMA((fine_tiles + 1,)),
        ],
        cost=(100_000_000, 8_000_000),
        out_specs=(ANY, ANY),
    )(sums, y_own, y_halo, v_own, diff, ugap, dgap, s_up)
    return joined_vnir.reshape(BANDS, h, w), jnp.transpose(joined_swir, (1, 0, 2))


def solution(mesh):
    return jax.shard_map(
        local,
        mesh=mesh,
        in_specs=(P("rows", "band"), P("band", "rows", None), P("band", "rows", None)),
        out_specs=(P(None, "rows", "band"), P(None, "rows", "band")),
        check_vma=False,
    )
```

```python
import math

import jax
import jax.numpy as jnp
import ml_dtypes
import numpy as np
from jax import lax
from jax.experimental import pallas as pl
from jax.experimental.pallas import tpu as pltpu
from jax.sharding import PartitionSpec as P

BANDS = 8
RATIO_V = 4
RATIO_S = 3
TAPS_V = 17
TAPS_S = 13
NYQUIST_GAIN = 0.29
LANES = 128
HALF = 64
REACH = 32
HALO = 8
F32 = jnp.float32
BF16 = jnp.bfloat16
VMEM_BYTES = 24 * 1024 * 1024
VMEM_MOST = 56 * 1024 * 1024


def gauss_taps(upscale, kernel_len):
    spread = upscale * math.sqrt(-2.0 * math.log(NYQUIST_GAIN)) / math.pi
    radius = kernel_len // 2
    offsets = np.arange(-radius, radius + 1) * 1.0
    values = np.exp(-(offsets**2) / (2.0 * spread**2))
    return values / values.sum()


def cubic_weight(distance):
    distance = abs(distance)
    if distance <= 1.0:
        return 1.5 * distance**3 - 2.5 * distance**2 + 1.0
    if distance < 2.0:
        return -0.5 * distance**3 + 2.5 * distance**2 - 4.0 * distance + 2.0
    return 0.0


def cubic_table(upscale):
    weights = np.zeros((5, upscale))
    for phase_index in range(upscale):
        centre = (phase_index + 0.5) / upscale - 0.5
        first_tap = math.floor(centre)
        fraction = centre - first_tap
        for tap_index in range(-1, 3):
            weights[first_tap + tap_index + 2, phase_index] += cubic_weight(tap_index - fraction)
    return weights


KF = gauss_taps(RATIO_V, TAPS_V)
KC = gauss_taps(RATIO_S, TAPS_S)
C4 = cubic_table(RATIO_V)
C3 = cubic_table(RATIO_S)
MEAN4 = C4.mean(axis=1)


def split(table):
    high = np.asarray(table, np.float64).astype(np.float32).astype(ml_dtypes.bfloat16)
    low = (np.asarray(table, np.float64) - high.astype(np.float64)).astype(np.float32)
    return np.stack([high, low.astype(ml_dtypes.bfloat16)])


def split3(table):
    high, middle = split(table)
    low = np.asarray(table, np.float64) - high.astype(np.float64) - middle.astype(np.float64)
    return high, middle, low.astype(np.float32).astype(ml_dtypes.bfloat16)


def band_matrix(size, taps):
    radius = len(taps) // 2
    out = np.zeros((size, size))
    for row in range(size):
        for tap in range(-radius, radius + 1):
            if 0 <= row + tap < size:
                out[row, row + tap] = taps[tap + radius]
    return out


def row_tables(h):
    hc = h // RATIO_V
    mean = np.zeros((3 * hc, 3 * h))
    for row in range(3 * hc):
        mean[row, RATIO_V * row : RATIO_V * (row + 1)] = 1.0 / RATIO_V
    fine = band_matrix(3 * h, KF)
    low = band_matrix(3 * hc, KC)
    mean_fine = mean @ fine
    pad = -(-hc // 8) * 8

    def part(matrix, rows, cols):
        return matrix[rows, :][:, cols]

    def stacked(rows, cols, filt):
        a = mean if filt is None else filt @ mean
        c = mean_fine if filt is None else filt @ mean_fine
        return np.concatenate([part(a, rows, cols), -part(c, rows, cols)], axis=1)

    own = slice(h, 2 * h)
    tables = []
    for variant in range(3):
        keep = np.ones(3 * hc)
        if variant == 1:
            keep[:hc] = 0.0
        if variant == 2:
            keep[2 * hc :] = 0.0
        masked = low * keep[None, :]
        rows = []
        for filt in (None, masked):
            block = np.zeros((pad, 2 * h))
            block[:hc] = stacked(slice(hc, 2 * hc), own, filt)
            rows.append(block)
        for filt in (None, low):
            rows.append(stacked(slice(hc, hc + HALO), slice(0, h), filt))
        for filt in (None, low):
            rows.append(stacked(slice(2 * hc - HALO, 2 * hc), slice(2 * h, 3 * h), filt))
        tables.append(np.concatenate(rows, axis=0))
    coarse_rows = np.stack(tables)
    fine_rows = np.concatenate(
        [fine[h : 2 * h, h : 2 * h], fine[h : h + HALO, 0:h], fine[2 * h - HALO : 2 * h, 2 * h : 3 * h]],
        axis=0,
    )
    return coarse_rows, fine_rows


def up_rows(hc):
    out = np.zeros((RATIO_V * hc, hc + 4))
    for m in range(hc):
        for p in range(RATIO_V):
            out[RATIO_V * m + p, m : m + 5] = C4[:, p]
    return out


def adjoint_rows(h):
    hc = h // RATIO_V
    reach = TAPS_V // 2
    size = h + 2 * reach
    lift = np.zeros((size, hc + 8))
    for r in range(size):
        m, p = divmod(r - reach, RATIO_V)
        lift[r, m + 2 : m + 7] = C4[:, p]
    fine = np.zeros((size, h))
    for r in range(size):
        for t in range(-reach, reach + 1):
            if 0 <= r - reach + t < h:
                fine[r, r - reach + t] = KF[t + reach]
    out = np.zeros((3, -(-(hc + 9) // 16) * 16, h))
    for variant in range(3):
        keep = np.ones((size, 1))
        if variant == 1:
            keep[:reach] = 0.0
        if variant == 2:
            keep[h + reach :] = 0.0
        out[variant, : hc + 8] = (lift * keep).T @ fine
        out[variant, hc + 8] = (fine * keep).sum(axis=0)
    return out


def column_tables():
    n = LANES
    fine = np.zeros((4 * n, 2 * n))
    mean = np.zeros((6 * n, n))
    mean_fine = np.zeros((6 * n, n))
    low = np.zeros((2 * n, n))
    pair = np.zeros((3, 2 * n, 2 * n))
    up4 = np.zeros((2 * n, RATIO_V * n))
    up3 = np.zeros((2 * n, RATIO_S * n))
    for c in range(2 * n):
        for t in range(-(TAPS_V // 2), TAPS_V // 2 + 1):
            fine[n + c + t, c] += KF[t + TAPS_V // 2]
    for c in range(n):
        for q in range(RATIO_V):
            mean[n + RATIO_V * c + q, c] = 1.0 / RATIO_V
            for t in range(-(TAPS_V // 2), TAPS_V // 2 + 1):
                mean_fine[n + RATIO_V * c + q + t, c] += KF[t + TAPS_V // 2] / RATIO_V
        for t in range(-(TAPS_S // 2), TAPS_S // 2 + 1):
            low[c + HALF + t, c] += KC[t + TAPS_S // 2]
            for s in range(-2, 3):
                value = KC[t + TAPS_S // 2] * MEAN4[s + 2]
                pair[0, c + HALF + t + s, n + c] += value
                if c + t >= 0:
                    pair[1, c + HALF + t + s, n + c] += value
                if c + t < n:
                    pair[2, c + HALF + t + s, n + c] += value
        for s in range(-2, 3):
            pair[:, c + HALF + s, c] += MEAN4[s + 2]
            for p in range(RATIO_V):
                up4[c + HALF + s, RATIO_V * c + p] += C4[s + 2, p]
            for p in range(RATIO_S):
                up3[c + HALF + s, RATIO_S * c + p] += C3[s + 2, p]
    return dict(fine=fine, mean=mean, mean_fine=mean_fine, low=low, pair=pair, up4=up4, up3=up3)


def stack_tables(tables):
    wide = 2 * LANES
    pieces, place, top = [], {}, 0
    for name, value in tables.items():
        stack = value.reshape((-1,) + value.shape[-2:])
        height, width = stack.shape[1:]
        starts = []
        for lane in range(0, width, wide):
            part = stack[:, :, lane : lane + wide]
            starts.append((top, part.shape[2]))
            piece = np.zeros((stack.shape[0] * height, wide), ml_dtypes.bfloat16)
            piece[:, : part.shape[2]] = part.reshape(-1, part.shape[2])
            pieces.append(piece)
            top += piece.shape[0]
        place[name] = (starts, height, width)
    return np.concatenate(pieces, axis=0), place


def parts2(x):
    high = x.astype(BF16)
    return high, (x - high.astype(F32)).astype(BF16)


def dot(a, b):
    return jnp.dot(a, b, preferred_element_type=F32)


def dot3(x, w):
    return dot(x[0], w[0]) + (dot(x[1], w[0]) + dot(x[0], w[1]))


def windows(x, starts, size):
    return tuple(jnp.concatenate([part[:, a : a + size] for a in starts], axis=0) for part in x)


def blocks(x, count):
    rows = x.shape[0] // count
    return jnp.concatenate([x[rows * k : rows * (k + 1)] for k in range(count)], axis=1)


def call(kernel, out_shape, scratch=(), cost=(0, 0), room=VMEM_BYTES, **specs):
    return pl.pallas_call(
        kernel,
        out_shape=out_shape,
        scratch_shapes=list(scratch),
        compiler_params=pltpu.CompilerParams(vmem_limit_bytes=room),
        cost_estimate=pl.CostEstimate(flops=cost[0], bytes_accessed=cost[1], transcendentals=0),
        **specs,
    )


ANY = pl.BlockSpec(memory_space=pl.ANY)
VMEM = pl.BlockSpec(memory_space=pltpu.VMEM)


def local(pan_image, vnir_bands, swir_bands):
    groups = lax.axis_size("band")
    strips = lax.axis_size("rows")
    h, w = pan_image.shape
    nb, hc, full = vnir_bands.shape
    _, hs, sfull = swir_bands.shape
    wc = w // RATIO_V
    ws = wc // RATIO_S
    wf = wc + LANES
    sf = ws + LANES
    pad = -(-hc // 8) * 8
    fine_tiles = w // LANES
    coarse_tiles = wc // LANES
    frame_tiles = coarse_tiles + 1
    swir_tiles = ws // LANES
    fine_pixels = h * strips * w * groups
    pairs = w // (2 * LANES)
    middle = frame_tiles - 2
    margin = RATIO_V * LANES

    def shape(*dims):
        return jax.ShapeDtypeStruct(dims, F32)

    coarse_rows, fine_rows = row_tables(h)
    cols = column_tables()
    lift = up_rows(hc)
    gram = lift.T @ lift
    rise = lift.sum(axis=0)

    swir_rows = -(-hs // RATIO_S)
    at_swir = hc
    edge_size = 2 * HALO * hc + 4 * hs
    edge_lane = ws * (hs % RATIO_S)
    shared = hs % RATIO_S and edge_lane + edge_size <= wc
    at_edge = hc + swir_rows - 1 if shared else hc + swir_rows
    edge_lane = edge_lane if shared else 0
    at_strip = at_edge + 1
    piece = REACH * (h // 8)
    per_row = wc // piece
    strip_rows = -(-(8 // nb) // per_row)

    def going(d):
        return (["right"] if d == 1 else []) + (["left"] if d == groups - 1 else [])

    def strip_place(d, side):
        return at_strip + strip_rows * going(d).index(side)

    chunk_rows = [at_strip + strip_rows * len(going(d)) for d in range(groups)]

    mean_parts, fine_parts = split(cols["mean"]), split(cols["mean_fine"])
    r_fine = split(fine_rows)
    r_adj = split3(adjoint_rows(h))
    table, place = stack_tables(
        dict(
            tall=np.concatenate([mean_parts[0], fine_parts[0]], axis=1),
            tall_low=fine_parts[1],
            fine=split(cols["fine"]),
            rows=split(coarse_rows),
            rows_fine=np.concatenate([r_fine[0], r_fine[1], r_fine[0]], axis=1),
            low=split(cols["low"]),
            pair=split(cols["pair"]),
            up4=split(cols["up4"]),
            up3=split(cols["up3"]),
            adjoint=np.concatenate([r_adj[i] for i in (0, 0, 0, 1, 1, 2)], axis=2),
        )
    )

    sources = (pan_image, jnp.transpose(vnir_bands, (1, 0, 2)), swir_bands, jnp.asarray(table))

    def pack(pan_ref, vnir_ref, swir_ref, table_ref, *rest):
        outs, (pan_out, table_out, wide, swide, edges, sems) = rest[:groups], rest[groups:]
        me = lax.axis_index("band")
        copies = [
            pltpu.make_async_copy(vnir_ref, wide.at[:, :, pl.ds(LANES, full)], sems.at[0]),
            pltpu.make_async_copy(swir_ref, swide.at[:, :, pl.ds(LANES, sfull)], sems.at[1]),
            pltpu.make_async_copy(pan_ref.at[:, pl.ds(0, LANES)], edges.at[0], sems.at[2]),
            pltpu.make_async_copy(pan_ref.at[:, pl.ds(w - LANES, LANES)], edges.at[1], sems.at[3]),
            pltpu.make_async_copy(pan_ref, pan_out, sems.at[4]),
            pltpu.make_async_copy(table_ref, table_out, sems.at[5]),
        ]
        for copy in copies:
            copy.start()
        wide[:, :, 0:LANES] = jnp.zeros((hc, nb, LANES), F32)
        wide[:, :, LANES + full : 2 * LANES + full] = jnp.zeros((hc, nb, LANES), F32)
        swide[:, :, 0:LANES] = jnp.zeros((nb, hs, LANES), F32)
        swide[:, :, LANES + sfull : 2 * LANES + sfull] = jnp.zeros((nb, hs, LANES), F32)
        for copy in copies[:4]:
            copy.wait()
        for d in range(groups):
            peer = lax.rem(me + d, groups)
            base = pl.multiple_of(peer * wc, LANES)
            sbase = pl.multiple_of(peer * ws, LANES)
            out = outs[d]
            out[0:hc] = wide[:, :, pl.ds(base + LANES, wc)]
            left = wide[:, :, pl.ds(base, LANES)]
            right = wide[:, :, pl.ds(base + LANES + wc, LANES)]
            borders = []
            for r in range(hc):
                borders += [left[r, :, LANES - HALO :], right[r, :, :HALO]]
            swin = swide[:, :, pl.ds(sbase, ws + 2 * LANES)]
            for q in range(hs):
                row = swin[:, q, :]
                lane = ws * (q % RATIO_S)
                out[at_swir + q // RATIO_S, :, lane : lane + ws] = row[:, LANES : LANES + ws]
                borders += [row[:, LANES - 2 : LANES], row[:, LANES + ws : LANES + ws + 2]]
            border = jnp.concatenate(borders, axis=1)
            out[at_edge, :, edge_lane : edge_lane + edge_size] = border
            for side in going(d):
                first = strip_place(d, side)
                edge = edges[1, :, LANES - REACH :] if side == "right" else edges[0, :, :REACH]
                flat = jnp.concatenate([edge[8 * t : 8 * t + 8] for t in range(h // 8)], axis=1)
                for i in range(8 // nb):
                    lane = piece * (i % per_row)
                    out[first + i // per_row, :, lane : lane + piece] = flat[nb * i : nb * (i + 1)]
        for copy in copies[4:]:
            copy.wait()

    staged = call(
        pack,
        tuple(shape(chunk_rows[d], nb, wc) for d in range(groups))
        + (shape(h, w), jax.ShapeDtypeStruct(table.shape, BF16)),
        [
            pltpu.VMEM((hc, nb, full + 2 * LANES), F32),
            pltpu.VMEM((nb, hs, sfull + 2 * LANES), F32),
            pltpu.VMEM((2, h, LANES), F32),
            pltpu.SemaphoreType.DMA((6,)),
        ],
        cost=(0, 8_000_000),
        in_specs=[ANY] * 4,
    )(*(pltpu.with_memory_space_constraint(x, pltpu.HBM) for x in sources))
    chunks, pan_held, table_held = staged[:groups], staged[groups], staged[groups + 1]
    got = [chunks[0]] + [
        lax.ppermute(chunks[d], "band", [(i, (i + d) % groups) for i in range(groups)])
        for d in range(1, groups)
    ]

    def take(ref, name, index=0, rows=None):
        starts, height, width = place[name]
        first, height = (0, height) if rows is None else (rows[0], rows[1] - rows[0])
        pieces = []
        for start, part in starts:
            base = start + first
            if not isinstance(index, int) or index:
                base = pl.multiple_of(base + index * place[name][1], 16)
            pieces.append(ref[pl.ds(base, height), 0:part])
        return pieces[0] if len(pieces) == 1 else jnp.concatenate(pieces, axis=1)

    def both_parts(ref, name, index=0, stacked=1):
        return take(ref, name, index), take(ref, name, index + stacked)

    def shrink(panes, tall, low):
        both = dot(panes[0], tall) + dot(panes[1], tall)
        return both[:, :LANES], both[:, LANES:] + dot(panes[0], low)

    def along_rows(rc, means, fines):
        both = parts2(jnp.concatenate([means, fines], axis=0))
        return dot(rc[0], both[0]) + (dot(rc[0], both[1]) + dot(rc[1], both[0]))

    def filter_rows(rf, x):
        col = parts2(x)
        return dot(rf, jnp.concatenate([col[0], col[0], col[1]], axis=0))

    def row_variant():
        row_id = lax.axis_index("rows")
        return jnp.where(row_id == 0, 1, jnp.where(row_id == strips - 1, 2, 0))

    pairs_in = [(i, i ^ 1) for i in range(strips) if i ^ 1 < strips]
    pairs_out = [(i, i + 1) for i in range(1, strips - 1, 2)]
    pairs_out += [(j, i) for i, j in pairs_out]

    def is_even():
        return lax.rem(lax.axis_index("rows"), 2) == 0

    def put(outs, index, up, down):
        even = is_even()
        outs[0][index] = jnp.where(even, up, down)
        outs[1][index] = jnp.where(even, down, up)

    def arrived(refs, index, low):
        even = is_even()
        inner, outer = refs[0][index], refs[1][index]
        return jnp.where(even, outer, inner) if low else jnp.where(even, inner, outer)

    def trade(inner, outer):
        outer = lax.ppermute(outer, "rows", pairs_out)
        return lax.ppermute(inner, "rows", pairs_in), outer

    at_up, at_down = 2 * pad, 2 * pad + 16

    def put_small(outs, first, ups, downs):
        blank = jnp.zeros((2, LANES), F32)
        for i in range(0, len(ups), 4):
            up = ups[i : i + 4] + [blank] * (4 - len(ups[i : i + 4]))
            down = downs[i : i + 4] + [blank] * (4 - len(downs[i : i + 4]))
            put(outs, first + i // 4, jnp.concatenate(up, axis=0), jnp.concatenate(down, axis=0))

    inner_fine = fine_tiles - 4

    def early(pan_ref, table_ref, coarse_out, fine_out, col_out):
        panes = parts2(pan_ref[...])
        starts = [margin * k - 3 * LANES for k in range(1, frame_tiles - 1)]
        means, fines = shrink(
            windows(panes, starts, 6 * LANES), take(table_ref, "tall"), take(table_ref, "tall_low")
        )
        rc = both_parts(table_ref, "rows", row_variant(), 3)
        coarse_out[...] = along_rows(rc, blocks(means, middle), blocks(fines, middle))
        starts = [2 * LANES * k - LANES for k in range(1, pairs - 1)]
        col = blocks(dot3(windows(panes, starts, 4 * LANES), both_parts(table_ref, "fine")), pairs - 2)
        col_out[...] = col
        fine_out[...] = filter_rows(take(table_ref, "rows_fine"), col)

    coarse_mid, fine_mid, col_mid = call(
        early,
        (
            shape(2 * pad + 32, LANES * middle),
            shape(h + 2 * HALO, LANES * inner_fine),
            shape(h, LANES * inner_fine),
        ),
        cost=(2_000_000_000, 8_000_000),
    )(pan_held, table_held)

    border_tiles = -(-edge_size // LANES)
    at_s = HALO * coarse_tiles
    at_h = at_s + 2 * swir_tiles
    at_ld = at_h + border_tiles
    at_d = at_ld + frame_tiles
    sent = at_d + -(-frame_tiles // 4)

    def framed(main, borders, lane, reach):
        blank = jnp.zeros((8, HALF - reach), F32)
        left = borders[:, lane : lane + reach]
        right = borders[:, lane + reach : lane + 2 * reach]
        return jnp.concatenate([blank, left, main, right, blank], axis=1)

    def assemble(pan_ref, table_ref, cm_ref, *rest):
        ins = rest[:groups]
        x_out, s_out, ce_out, fe_out, col_out = rest[groups : groups + 5]
        outs = rest[groups + 5 :]
        me = lax.axis_index("band")

        def gather(row, lane, size):
            rows = [ins[(groups - i) % groups][row, :, lane : lane + size] for i in range(groups)]
            return pltpu.roll(jnp.concatenate(rows, axis=0), nb * me, 0)

        def tile(x, t):
            return x[:, LANES * t : LANES * (t + 1)]

        borders = gather(at_edge, edge_lane, edge_size)
        blank = jnp.zeros((8, LANES * border_tiles - edge_size), F32)
        borders = jnp.concatenate([borders, blank], axis=1)
        for t in range(border_tiles):
            put(outs, at_h + t, tile(borders, t), tile(borders, t))
        mains = [gather(r, 0, wc) for r in range(hc)]
        for r in range(hc):
            x_out[r] = framed(mains[r], borders, 2 * HALO * r, HALO)
        for r in range(HALO):
            for t in range(coarse_tiles):
                put(outs, coarse_tiles * r + t, tile(mains[hc - HALO + r], t), tile(mains[r], t))
        shorts = [gather(at_swir + q // RATIO_S, ws * (q % RATIO_S), ws) for q in range(hs)]
        for q in range(hs):
            s_out[q] = framed(shorts[q], borders, 2 * HALO * hc + 4 * q, 2)
        for q in range(2):
            for t in range(swir_tiles):
                put(outs, at_s + swir_tiles * q + t, tile(shorts[hs - 2 + q], t), tile(shorts[q], t))

        def strip(d, side, empty):
            first = strip_place(d, side)
            rows = []
            for i in range(8 // nb):
                lane = piece * (i % per_row)
                rows.append(ins[d][first + i // per_row, :, lane : lane + piece])
            flat = jnp.where(empty, 0.0, jnp.concatenate(rows, axis=0))
            whole = [flat[:, REACH * t : REACH * (t + 1)] for t in range(h // 8)]
            return jnp.concatenate(whole, axis=0)

        blank = jnp.zeros((h, LANES - REACH), F32)
        left = jnp.concatenate([blank, strip(1, "right", me == 0), pan_ref[:, 0 : 3 * LANES]], axis=1)
        right = jnp.concatenate(
            [pan_ref[:, w - 3 * LANES : w], strip(groups - 1, "left", me == groups - 1), blank], axis=1
        )
        left, right = parts2(left), parts2(right)
        cut = 2 * LANES
        inner = (cut, 6 * LANES)
        lm, lf = shrink(left, take(table_ref, "tall", 0, inner), take(table_ref, "tall_low", 0, inner))
        inner = (0, 4 * LANES)
        rm, rfine = shrink(right, take(table_ref, "tall", 0, inner), take(table_ref, "tall_low", 0, inner))
        rc = both_parts(table_ref, "rows", row_variant(), 3)
        edge = along_rows(rc, jnp.concatenate([lm, rm], axis=1), jnp.concatenate([lf, rfine], axis=1))
        ce_out[...] = edge[0 : 2 * pad]
        outer = tuple(jnp.concatenate([a, b], axis=0) for a, b in zip(left, right))
        col = blocks(dot3(outer, both_parts(table_ref, "fine")), 2)
        col_out[...] = col
        fe_out[...] = filter_rows(take(table_ref, "rows_fine"), col)
        sides = jnp.concatenate([edge[:, :LANES], cm_ref[...], edge[:, LANES:]], axis=1)
        ups, downs = [], []
        for k in range(frame_tiles):
            part = tile(sides, k)
            put(outs, at_ld + k, part[at_up + 8 : at_up + 16], part[at_down + 8 : at_down + 16])
            ups.append(part[at_up : at_up + 2])
            downs.append(part[at_down + HALO - 2 : at_down + HALO])
        put_small(outs, at_d, ups, downs)

    x_loc, s_loc, coarse_edge, fine_edge, col_edge, rest_in, rest_out = call(
        assemble,
        (
            shape(hc, BANDS, wf),
            shape(hs, BANDS, sf),
            shape(2 * pad, 2 * LANES),
            shape(h + 2 * HALO, 4 * LANES),
            shape(h, 4 * LANES),
            shape(sent, 8, LANES),
            shape(sent, 8, LANES),
        ),
        cost=(200_000_000, 3_000_000),
        in_specs=[VMEM] * (groups + 3),
    )(pan_held, table_held, coarse_mid, *got)
    rest_in, rest_out = trade(rest_in, rest_out)

    turns = BANDS // 2 + 1
    block_starts = [LANES * k for k in range(coarse_tiles)]
    own_rows = range(2, hc + 2)
    halo_rows = (0, 1, hc + 2, hc + 3)
    around = (-2, -1) + halo_rows + (hc + 4, hc + 5)
    whole_rows = range(2, hc - 2)
    first_whole = RATIO_V * whole_rows[0]
    whole_count = RATIO_V * len(whole_rows)

    def lifted(rows, table_ref, store):
        stack = windows(parts2(jnp.concatenate(rows, axis=0)), block_starts, 2 * LANES)
        up = dot3(stack, both_parts(table_ref, "up4"))
        size = 8 * len(rows)
        for k in range(coarse_tiles):
            for q in range(RATIO_V):
                store(RATIO_V * k + q, up[size * k : size * (k + 1), LANES * q : LANES * (q + 1)])

    def weighted(pairs):
        value = None
        for weight, x in pairs:
            if weight != 0.0:
                value = float(weight) * x if value is None else value + float(weight) * x
        return value

    def adjoint_of(table_ref, col):
        p1 = col.astype(BF16)
        over = col - p1.astype(F32)
        p2 = over.astype(BF16)
        p3 = (over - p2.astype(F32)).astype(BF16)
        weights = take(table_ref, "adjoint", row_variant())
        return dot(weights, jnp.concatenate([p1, p2, p3, p1, p2, p1], axis=0))

    def inside(
        pan_ref, x_ref, s_ref, fm_ref, fe_ref, colm_ref, cole_ref, table_ref,
        y_out, v_out, acc_out, s_out, diff_out, q_out, *outs,
    ):
        def store(index, value):
            y_out[index] = value

        lifted([x_ref[r] for r in range(hc)], table_ref, store)
        rows = parts2(jnp.concatenate([s_ref[q] for q in range(hs)], axis=0))
        s_cols = dot3(windows(rows, block_starts[:swir_tiles], 2 * LANES), both_parts(table_ref, "up3"))
        s_out[...] = blocks(s_cols, swir_tiles)

        def joined(outer, inner):
            return jnp.concatenate([outer[:, : 2 * LANES], inner, outer[:, 2 * LANES :]], axis=1)

        low = joined(fe_ref[...], fm_ref[...])
        diff = pan_ref[...] - low[0:h]
        adjoint = adjoint_of(table_ref, joined(cole_ref[...], colm_ref[...]))
        total = jnp.zeros((1, LANES), F32)
        for k in range(fine_tiles):
            at = slice(LANES * k, LANES * (k + 1))
            diff_out[k] = diff[:, at]
            q_out[k] = adjoint[:, at]
            total = total + adjoint[hc + 8 : hc + 9, at]
            put(outs, k, low[h : h + HALO, at], low[h + HALO : h + 2 * HALO, at])
        acc_out[turns + 2] = jnp.concatenate([total, jnp.zeros((7, LANES), F32)], axis=0)

        def tile_step(k, carry):
            accs, accv, accp = list(carry[:turns]), carry[turns], carry[turns + 1]
            ys = {m: y_out[k, pl.ds(8 * (m - 2), 8), :] for m in own_rows}
            for m in own_rows:
                z = weighted((gram[m, other], ys[other]) for other in own_rows)
                accs[0] = accs[0] + z * ys[m]
                for i in range(1, turns):
                    accs[i] = accs[i] + z * pltpu.roll(ys[m], i, 0)
                accv = accv + float(rise[m]) * ys[m]
                accp = accp + ys[m] * q_out[k, pl.ds(m + 2, 1), :]
            for m in whole_rows:
                for p in range(RATIO_V):
                    r = RATIO_V * m + p - first_whole
                    v_out[k, pl.ds(8 * r, 8), :] = weighted((C4[t, p], ys[m + t]) for t in range(5) if C4[t, p] != 0.0)
            return tuple(accs) + (accv, accp)

        zero = jnp.zeros((8, LANES), F32)
        first = lax.fori_loop(0, fine_tiles, tile_step, (zero,) * (turns + 2))
        for i in range(turns + 2):
            acc_out[i] = first[i]

    q_rows = -(-(hc + 9) // 16) * 16
    y_own, v_own, acc_own, s_own, diff, q_own, low_in, low_out = call(
        inside,
        (
            shape(fine_tiles, 8 * hc, LANES),
            shape(fine_tiles, 8 * whole_count, LANES),
            shape(turns + 3, 8, LANES),
            shape(8 * hs, wc),
            shape(fine_tiles, h, LANES),
            shape(fine_tiles, q_rows, LANES),
            shape(fine_tiles, 8, LANES),
            shape(fine_tiles, 8, LANES),
        ),
        cost=(2_000_000_000, 8_000_000),
    )(pan_held, x_loc, s_loc, fine_mid, fine_edge, col_mid, col_edge, table_held)
    low_in, low_out = trade(low_in, low_out)

    def moments(
        x_ref, y_ref, acc_ref, scol_ref, q_ref, rest_in_ref, rest_out_ref, cm_ref, ce_ref, table_ref,
        mom_out, y_out, ugap_out, dgap_out, s_out,
        both, ulow,
    ):
        me = lax.axis_index("band")
        row_id = lax.axis_index("rows")
        rest = (rest_in_ref, rest_out_ref)

        def tiles(refs, low, indices):
            return jnp.concatenate([arrived(refs, i, low) for i in indices], axis=1)

        def halo(first, per, reach, start, count):
            sides = []
            for low, base in ((True, start[0]), (False, start[1])):
                borders = tiles(rest, low, range(at_h, at_h + border_tiles))
                rows = []
                for r in range(count):
                    main = tiles(rest, low, range(first + per * r, first + per * (r + 1)))
                    rows.append(framed(main, borders, base + 2 * reach * r, reach))
                sides.append(rows)
            return sides

        x_low, x_high = halo(0, coarse_tiles, HALO, (2 * HALO * (hc - HALO), 0), HALO)

        def x_row(r):
            if r < 0:
                return x_low[HALO + r]
            if r >= hc:
                return x_high[r - hc]
            return x_ref[r]

        def store(index, value):
            y_out[index] = value

        lifted([x_row(m - 2) for m in around], table_ref, store)

        zero = jnp.zeros((8, LANES), F32)

        def tile_step(k, carry):
            accs = list(carry[:turns])
            accp, accv = carry[turns], carry[turns + 1]
            ys = {m: y_ref[k, pl.ds(8 * (m - 2), 8), :] for m in own_rows}
            for i, m in enumerate(around):
                ys[m] = y_out[k, pl.ds(8 * i, 8), :]
            for m in halo_rows:
                near = weighted((gram[m, other], ys[other]) for other in own_rows)
                whole = near + weighted((gram[m, other], ys[other]) for other in halo_rows)
                accs[0] = accs[0] + ys[m] * (near + whole)
                for i in range(1, turns):
                    accs[i] = accs[i] + whole * pltpu.roll(ys[m], i, 0) + ys[m] * pltpu.roll(near, i, 0)
                accv = accv + float(rise[m]) * ys[m]
            for m in around:
                accp = accp + ys[m] * q_ref[k, pl.ds(m + 2, 1), :]
            return tuple(accs) + (accp, accv)

        start = tuple(acc_ref[i] for i in range(turns)) + (acc_ref[turns + 1], acc_ref[turns])
        first = lax.fori_loop(0, fine_tiles, tile_step, start)

        below = jnp.where(row_id > 0, 1.0, 0.0).astype(F32)
        above = jnp.where(row_id < strips - 1, 1.0, 0.0).astype(F32)
        reach = TAPS_S // 2
        means = []
        for r in range(-reach, hc + reach):
            value = float(MEAN4[2]) * x_row(r)
            for t in (1, 2):
                value = value + float(MEAN4[2 + t]) * (x_row(r - t) + x_row(r + t))
            if r < 0:
                value = value * below
            if r >= hc:
                value = value * above
            means.append(value)
        lows = []
        for r in range(hc):
            centre = r + reach
            value = float(KC[reach]) * means[centre]
            for t in range(1, reach + 1):
                value = value + float(KC[reach + t]) * (means[centre - t] + means[centre + t])
            lows.append(value)
        u_rows = windows(parts2(jnp.concatenate(means[reach : reach + hc], axis=0)), block_starts, 2 * LANES)
        l_rows = windows(parts2(jnp.concatenate(lows, axis=0)), block_starts, 2 * LANES)
        u_all = dot3(u_rows, tuple(x[:, :LANES] for x in both_parts(table_ref, "pair", 0, 3)))
        left = jnp.where(me == 0, 1, 0)
        right = jnp.where(me == groups - 1, 2, 0)
        size = 8 * hc
        last = coarse_tiles - 1
        for which, lo_k, hi_k in ((left, 0, 1), (0, 1, last), (right, last, last + 1)):
            if hi_k <= lo_k:
                continue
            wp = tuple(x[:, LANES:] for x in both_parts(table_ref, "pair", which, 3))
            part = dot3(tuple(x[size * lo_k : size * hi_k] for x in l_rows), wp)
            for k in range(lo_k, hi_k):
                at = slice(LANES * k, LANES * (k + 1))
                low_k = part[size * (k - lo_k) : size * (k - lo_k + 1)]
                ulow[:, at] = low_k
                ugap_out[:, at] = u_all[size * k : size * (k + 1)] - low_k

        column = lax.broadcasted_iota(jnp.int32, (1, wf), 1) - HALF + me * wc
        valid = jnp.where((column >= 0) & (column < groups * wc), 1.0, 0.0).astype(F32)

        def own(rows):
            return jnp.concatenate([ce_ref[rows, 0:LANES], cm_ref[rows, :], ce_ref[rows, LANES:]], axis=1)

        def small(low):
            rows = [arrived(rest, at_d + k // 4, low)[2 * (k % 4) : 2 * (k % 4) + 2] for k in range(frame_tiles)]
            return jnp.concatenate(rows, axis=1)

        both[...] = own(slice(0, pad))
        both[0:2] = both[0:2] + small(True)
        both[hc - 2 : hc] = both[hc - 2 : hc] + small(False)
        detail = both[...]
        both[...] = own(slice(pad, 2 * pad))
        both[0:HALO] = both[0:HALO] + tiles(rest, True, range(at_ld, at_ld + frame_tiles))
        both[hc - HALO : hc] = both[hc - HALO : hc] + tiles(rest, False, range(at_ld, at_ld + frame_tiles))
        dlow_rows = windows(parts2(both[...] * valid), block_starts, 2 * LANES)
        dlow = blocks(dot3(dlow_rows, both_parts(table_ref, "low")), coarse_tiles)
        dgap_out[...] = detail[:, HALF : HALF + wc] - dlow
        both[:, 0:wc] = dlow

        s_low, s_high = halo(at_s, swir_tiles, 2, (2 * HALO * hc + 4 * (hs - 2), 2 * HALO * hc), 2)
        s_parts = windows(parts2(jnp.concatenate(s_low + s_high, axis=0)), block_starts[:swir_tiles], 2 * LANES)
        s_around = blocks(dot3(s_parts, both_parts(table_ref, "up3")), swir_tiles)
        s_cols = jnp.concatenate([s_around[0:16], scol_ref[...], s_around[16:32]], axis=0)
        for m in range(hs):
            for p in range(RATIO_S):
                value = None
                for t in range(5):
                    if C3[t, p] != 0.0:
                        term = float(C3[t, p]) * s_cols[8 * (m + t) : 8 * (m + t) + 8]
                        value = term if value is None else value + term
                s_out[RATIO_S * m + p] = value

        ll = [zero] * turns
        cross = [zero] * BANDS
        ld = ls = sd = ss = dd = ds = zero
        for r in range(hc):
            for k in range(coarse_tiles):
                at = slice(LANES * k, LANES * (k + 1))
                u = ulow[8 * r : 8 * r + 8, at]
                s = s_out[r, :, at]
                dl = jnp.broadcast_to(both[r : r + 1, at], (8, LANES))
                ll[0] = ll[0] + u * u
                for i in range(1, turns):
                    ll[i] = ll[i] + u * pltpu.roll(u, i, 0)
                for i in range(BANDS):
                    cross[i] = cross[i] + u * s_out[r, i : i + 1, at]
                ld = ld + u * dl
                sd = sd + s * dl
                ls = ls + u
                ss = ss + s
                dd = dd + dl * dl
                ds = ds + dl

        lane = lax.broadcasted_iota(jnp.int32, (8, LANES), 1)
        sub = lax.broadcasted_iota(jnp.int32, (8, LANES), 0)

        def column_of(acc):
            return jnp.broadcast_to(jnp.sum(acc, axis=1, keepdims=True), (8, LANES))

        table = zero
        for base, accs in ((0, ll), (32, first[:turns])):
            for i in range(turns):
                col = column_of(accs[i])
                table = jnp.where(lane == base + lax.rem(sub + BANDS - i, BANDS), col, table)
                if 0 < i < BANDS // 2:
                    turned = pltpu.roll(col, BANDS - i, 0)
                    table = jnp.where(lane == base + lax.rem(sub + i, BANDS), turned, table)
        singles = [(8 + i, cross[i]) for i in range(BANDS)]
        singles += [(16, ld), (17, ls), (18, sd), (19, ss), (20, dd), (21, ds)]
        singles += [(40, first[turns]), (41, first[turns + 1])]
        for index, acc in singles:
            table = jnp.where(lane == index, column_of(acc), table)
        total = jnp.sum(jnp.sum(acc_ref[turns + 2], axis=0, keepdims=True), axis=1, keepdims=True)
        table = jnp.where(lane == 43, total, table)
        turned = pltpu.roll(table, HALF, 1)
        mom_out[...] = jnp.where(lane[0:4] < HALF, table[0:4], turned[4:8])

    mom, y_halo, ugap, dgap, s_up = call(
        moments,
        (
            shape(4, LANES),
            shape(fine_tiles, 8 * len(around), LANES),
            shape(8 * hc, wc),
            shape(pad, wc),
            shape(hc, BANDS, wc),
        ),
        [
            pltpu.VMEM((pad, wf), F32),
            pltpu.VMEM((8 * hc, wc), F32),
        ],
        cost=(1_000_000_000, 8_000_000),
    )(
        x_loc, y_own, acc_own, s_own, q_own, rest_in, rest_out, coarse_mid, coarse_edge, table_held,
    )
    devices = groups * strips
    mom, low_in, low_out = lax.optimization_barrier((mom, low_in, low_out))
    spread = jnp.broadcast_to(mom[None], (devices,) + mom.shape)
    sums = lax.all_to_all(spread, ("rows", "band"), split_axis=0, concat_axis=0, tiled=True)

    def finish(
        sums_ref, y_ref, yh_ref, v_ref, diff_ref, low_in_ref, low_out_ref, ugap_ref, dgap_ref, s_ref,
        vnir_out, swir_out, tiles, swir, ends, sems,
    ):
        lane = lax.broadcasted_iota(jnp.int32, (8, LANES), 1)
        sub = lax.broadcasted_iota(jnp.int32, (8, LANES), 0)
        eye = lane == sub
        terms = [sums_ref[index] for index in range(devices)]
        while len(terms) > 1:
            terms = [sum(terms[i : i + 2][1:], terms[i]) for i in range(0, len(terms), 2)]
        total = jnp.concatenate([terms[0], pltpu.roll(terms[0], HALF, 1)], axis=0)

        def column(x, index):
            return jnp.broadcast_to(x[:, index : index + 1], (8, LANES))

        def across(col):
            return jnp.sum(jnp.where(eye, col, 0.0), axis=0, keepdims=True)

        def down(x):
            return jnp.sum(x, axis=0, keepdims=True)

        def solve(matrix, rhs):
            cols = [column(matrix, j) for j in range(BANDS)] + [rhs]
            inverse = jnp.zeros((8, LANES), F32)
            for k in range(BANDS):
                pivot = 1.0 / jnp.broadcast_to(cols[k][k : k + 1], (8, LANES))
                inverse = jnp.where(sub == k, pivot, inverse)
                factor = jnp.where(sub == k, 0.0, cols[k] * pivot)
                for j in range(k + 1, BANDS + 1):
                    cols[j] = cols[j] - factor * jnp.broadcast_to(cols[j][k : k + 1], (8, LANES))
            return cols[BANDS] * inverse

        n1 = float(fine_pixels)
        mean_v = column(total, 41) / n1
        mean_p = column(total, 43) / n1
        cov_v = pltpu.roll(total, LANES - 32, 1) / n1 - mean_v * across(mean_v)
        cov_p = column(total, 40) / n1 - mean_v * mean_p
        gain = cov_p / down(cov_p * solve(cov_v, cov_p))

        n2 = float(fine_pixels // (RATIO_V * RATIO_V))
        mean_l = column(total, 17) / n2
        mean_s = column(total, 19) / n2
        mean_d = column(total, 21) / n2
        cov_ll = total / n2 - mean_l * across(mean_l)
        cov_ls = pltpu.roll(total, LANES - 8, 1) / n2 - mean_l * across(mean_s)
        cov_ld = column(total, 16) / n2 - mean_l * mean_d
        cov_sd = column(total, 18) / n2 - mean_s * mean_d
        cov_dd = column(total, 20) / n2 - mean_d * mean_d
        gain_row = across(gain)
        a2 = cov_ll + gain * across(cov_ld) + cov_ld * gain_row + gain * gain_row * cov_dd
        b2 = jnp.where(lane < BANDS, cov_ls + gain * across(cov_sd), 0.0)
        target = jnp.broadcast_to(jnp.sum(b2, axis=1, keepdims=True) / BANDS, (8, LANES))

        def sent_tile(k):
            lanes = pl.ds(pl.multiple_of(LANES * k, LANES), LANES)
            return pltpu.make_async_copy(tiles.at[k], vnir_out.at[:, lanes], sems.at[k])

        def tile_step(k, carry):
            work, inverse = carry
            here = sub == k
            row = down(jnp.where(here, work, 0.0))
            col = jnp.sum(jnp.where(lane == k, work, 0.0), axis=1, keepdims=True)
            pivot = 1.0 / jnp.where(k < BANDS, down(jnp.where(here[:, 0:1], col, 0.0)), 1.0)
            inverse = jnp.where(here, pivot, inverse)
            work = work - jnp.where(here, 0.0, col * pivot) * row

            ys = {m: y_ref[k, pl.ds(8 * (m - 2), 8), :] for m in own_rows}
            for i, m in enumerate(around):
                if m in halo_rows:
                    ys[m] = yh_ref[k, pl.ds(8 * i, 8), :]
            lows = (low_in_ref, low_out_ref)
            ends[k, 0:HALO, :] = diff_ref[k, 0:HALO, :] - arrived(lows, k, True)
            ends[k, HALO:, :] = diff_ref[k, h - HALO :, :] - arrived(lows, k, False)
            for m in range(hc):
                for p in range(RATIO_V):
                    r = RATIO_V * m + p
                    if m in whole_rows:
                        value = v_ref[k, pl.ds(8 * (r - first_whole), 8), :]
                    else:
                        value = weighted((C4[t, p], ys[m + t]) for t in range(5) if C4[t, p] != 0.0)
                    if r < HALO:
                        detail = ends[k, pl.ds(r, 1), :]
                    elif r >= h - HALO:
                        detail = ends[k, pl.ds(r - h + 2 * HALO, 1), :]
                    else:
                        detail = diff_ref[k, pl.ds(r, 1), :]
                    value = value + gain * detail
                    tiles[k, pl.ds(r, 8, stride=h), :] = value
            sent_tile(k).start()
            return work, inverse

        start = (jnp.where(lane == BANDS, target, a2), jnp.zeros((8, LANES), F32))
        work, inverse = lax.fori_loop(0, fine_tiles, tile_step, start)
        fit2 = column(work, BANDS) * inverse
        numer = down(fit2 * b2)
        share_row = numer / down(fit2 * target)
        share = jnp.sum(jnp.where(eye, jnp.broadcast_to(share_row, (8, LANES)), 0.0), axis=1, keepdims=True)
        scale = down(fit2 * gain)[:, 0:1]
        fit_col = fit2[:, 0:1]
        for r in range(hc):
            seen = jnp.sum(fit_col * ugap_ref[8 * r : 8 * r + 8, :], axis=0, keepdims=True)
            seen = seen + scale * dgap_ref[r : r + 1, :]
            swir[r] = s_ref[r] + share * seen
        last = pltpu.make_async_copy(swir, swir_out, sems.at[fine_tiles])
        last.start()

        def drain(k, carry):
            sent_tile(k).wait()
            return carry

        lax.fori_loop(0, fine_tiles, drain, 0)
        last.wait()

    joined_vnir, joined_swir = call(
        finish,
        (shape(BANDS * h, w), shape(hc, BANDS, wc)),
        [
            pltpu.VMEM((fine_tiles, BANDS * h, LANES), F32),
            pltpu.VMEM((hc, BANDS, wc), F32),
            pltpu.VMEM((fine_tiles, 2 * HALO, LANES), F32),
            pltpu.SemaphoreType.DMA((fine_tiles + 1,)),
        ],
        cost=(100_000_000, 8_000_000),
        out_specs=(ANY, ANY),
    )(sums, y_own, y_halo, v_own, diff, low_in, low_out, ugap, dgap, s_up)
    return joined_vnir.reshape(BANDS, h, w), jnp.transpose(joined_swir, (1, 0, 2))


def solution(mesh):
    return jax.shard_map(
        local,
        mesh=mesh,
        in_specs=(P("rows", "band"), P("band", "rows", None), P("band", "rows", None)),
        out_specs=(P(None, "rows", "band"), P(None, "rows", "band")),
        check_vma=False,
    )
```

```python
import math

import jax
import jax.numpy as jnp
import ml_dtypes
import numpy as np
from jax import lax
from jax.experimental import pallas as pl
from jax.experimental.pallas import tpu as pltpu
from jax.sharding import PartitionSpec as P

BANDS = 8
RATIO_V = 4
RATIO_S = 3
TAPS_V = 17
TAPS_S = 13
NYQUIST_GAIN = 0.29
LANES = 128
HALF = 64
REACH = 32
HALO = 8
F32 = jnp.float32
BF16 = jnp.bfloat16
VMEM_BYTES = 24 * 1024 * 1024
VMEM_MOST = 56 * 1024 * 1024


def gauss_taps(upscale, kernel_len):
    spread = upscale * math.sqrt(-2.0 * math.log(NYQUIST_GAIN)) / math.pi
    radius = kernel_len // 2
    offsets = np.arange(-radius, radius + 1) * 1.0
    values = np.exp(-(offsets**2) / (2.0 * spread**2))
    return values / values.sum()


def cubic_weight(distance):
    distance = abs(distance)
    if distance <= 1.0:
        return 1.5 * distance**3 - 2.5 * distance**2 + 1.0
    if distance < 2.0:
        return -0.5 * distance**3 + 2.5 * distance**2 - 4.0 * distance + 2.0
    return 0.0


def cubic_table(upscale):
    weights = np.zeros((5, upscale))
    for phase_index in range(upscale):
        centre = (phase_index + 0.5) / upscale - 0.5
        first_tap = math.floor(centre)
        fraction = centre - first_tap
        for tap_index in range(-1, 3):
            weights[first_tap + tap_index + 2, phase_index] += cubic_weight(tap_index - fraction)
    return weights


KF = gauss_taps(RATIO_V, TAPS_V)
KC = gauss_taps(RATIO_S, TAPS_S)
C4 = cubic_table(RATIO_V)
C3 = cubic_table(RATIO_S)
MEAN4 = C4.mean(axis=1)
WIDE = np.convolve(KC, MEAN4)


def split(table):
    high = np.asarray(table, np.float64).astype(np.float32).astype(ml_dtypes.bfloat16)
    low = (np.asarray(table, np.float64) - high.astype(np.float64)).astype(np.float32)
    return np.stack([high, low.astype(ml_dtypes.bfloat16)])


def split3(table):
    high, middle = split(table)
    low = np.asarray(table, np.float64) - high.astype(np.float64) - middle.astype(np.float64)
    return high, middle, low.astype(np.float32).astype(ml_dtypes.bfloat16)


def band_matrix(size, taps):
    radius = len(taps) // 2
    out = np.zeros((size, size))
    for row in range(size):
        for tap in range(-radius, radius + 1):
            if 0 <= row + tap < size:
                out[row, row + tap] = taps[tap + radius]
    return out


def row_tables(h):
    hc = h // RATIO_V
    mean = np.zeros((3 * hc, 3 * h))
    for row in range(3 * hc):
        mean[row, RATIO_V * row : RATIO_V * (row + 1)] = 1.0 / RATIO_V
    fine = band_matrix(3 * h, KF)
    low = band_matrix(3 * hc, KC)
    mean_fine = mean @ fine
    pad = -(-hc // 8) * 8

    def part(matrix, rows, cols):
        return matrix[rows, :][:, cols]

    def stacked(rows, cols, filt):
        a = mean if filt is None else filt @ mean
        c = mean_fine if filt is None else filt @ mean_fine
        return np.concatenate([part(a, rows, cols), -part(c, rows, cols)], axis=1)

    own = slice(h, 2 * h)
    tables = []
    for variant in range(3):
        keep = np.ones(3 * hc)
        if variant == 1:
            keep[:hc] = 0.0
        if variant == 2:
            keep[2 * hc :] = 0.0
        masked = low * keep[None, :]
        rows = []
        for filt in (None, masked):
            block = np.zeros((pad, 2 * h))
            block[:hc] = stacked(slice(hc, 2 * hc), own, filt)
            rows.append(block)
        for filt in (None, low):
            rows.append(stacked(slice(hc, hc + HALO), slice(0, h), filt))
        for filt in (None, low):
            rows.append(stacked(slice(2 * hc - HALO, 2 * hc), slice(2 * h, 3 * h), filt))
        tables.append(np.concatenate(rows, axis=0))
    coarse_rows = np.stack(tables)
    fine_rows = np.concatenate(
        [fine[h : 2 * h, h : 2 * h], fine[h : h + HALO, 0:h], fine[2 * h - HALO : 2 * h, 2 * h : 3 * h]],
        axis=0,
    )
    return coarse_rows, fine_rows


def up_rows(hc):
    out = np.zeros((RATIO_V * hc, hc + 4))
    for m in range(hc):
        for p in range(RATIO_V):
            out[RATIO_V * m + p, m : m + 5] = C4[:, p]
    return out


def adjoint_rows(h):
    hc = h // RATIO_V
    reach = TAPS_V // 2
    size = h + 2 * reach
    lift = np.zeros((size, hc + 8))
    for r in range(size):
        m, p = divmod(r - reach, RATIO_V)
        lift[r, m + 2 : m + 7] = C4[:, p]
    fine = np.zeros((size, h))
    for r in range(size):
        for t in range(-reach, reach + 1):
            if 0 <= r - reach + t < h:
                fine[r, r - reach + t] = KF[t + reach]
    out = np.zeros((3, -(-(hc + 9) // 16) * 16, h))
    for variant in range(3):
        keep = np.ones((size, 1))
        if variant == 1:
            keep[:reach] = 0.0
        if variant == 2:
            keep[h + reach :] = 0.0
        out[variant, : hc + 8] = (lift * keep).T @ fine
        out[variant, hc + 8] = (fine * keep).sum(axis=0)
    return out


def column_tables():
    n = LANES
    fine = np.zeros((4 * n, 2 * n))
    mean = np.zeros((6 * n, n))
    mean_fine = np.zeros((6 * n, n))
    low = np.zeros((2 * n, n))
    pair = np.zeros((3, 2 * n, 2 * n))
    up4 = np.zeros((2 * n, RATIO_V * n))
    up3 = np.zeros((2 * n, RATIO_S * n))
    for c in range(2 * n):
        for t in range(-(TAPS_V // 2), TAPS_V // 2 + 1):
            fine[n + c + t, c] += KF[t + TAPS_V // 2]
    for c in range(n):
        for q in range(RATIO_V):
            mean[n + RATIO_V * c + q, c] = 1.0 / RATIO_V
            for t in range(-(TAPS_V // 2), TAPS_V // 2 + 1):
                mean_fine[n + RATIO_V * c + q + t, c] += KF[t + TAPS_V // 2] / RATIO_V
        for t in range(-(TAPS_S // 2), TAPS_S // 2 + 1):
            low[c + HALF + t, c] += KC[t + TAPS_S // 2]
            for s in range(-2, 3):
                value = KC[t + TAPS_S // 2] * MEAN4[s + 2]
                pair[0, c + HALF + t + s, n + c] += value
                if c + t >= 0:
                    pair[1, c + HALF + t + s, n + c] += value
                if c + t < n:
                    pair[2, c + HALF + t + s, n + c] += value
        for s in range(-2, 3):
            pair[:, c + HALF + s, c] += MEAN4[s + 2]
            for p in range(RATIO_V):
                up4[c + HALF + s, RATIO_V * c + p] += C4[s + 2, p]
            for p in range(RATIO_S):
                up3[c + HALF + s, RATIO_S * c + p] += C3[s + 2, p]
    return dict(fine=fine, mean=mean, mean_fine=mean_fine, low=low, pair=pair, up4=up4, up3=up3)


def stack_tables(tables):
    wide = 2 * LANES
    pieces, place, top = [], {}, 0
    for name, value in tables.items():
        stack = value.reshape((-1,) + value.shape[-2:])
        height, width = stack.shape[1:]
        starts = []
        for lane in range(0, width, wide):
            part = stack[:, :, lane : lane + wide]
            starts.append((top, part.shape[2]))
            piece = np.zeros((stack.shape[0] * height, wide), ml_dtypes.bfloat16)
            piece[:, : part.shape[2]] = part.reshape(-1, part.shape[2])
            pieces.append(piece)
            top += piece.shape[0]
        place[name] = (starts, height, width)
    return np.concatenate(pieces, axis=0), place


def parts2(x):
    high = x.astype(BF16)
    return high, (x - high.astype(F32)).astype(BF16)


def dot(a, b):
    return jnp.dot(a, b, preferred_element_type=F32)


def dot3(x, w):
    return dot(x[0], w[0]) + (dot(x[1], w[0]) + dot(x[0], w[1]))


def windows(x, starts, size):
    return tuple(jnp.concatenate([part[:, a : a + size] for a in starts], axis=0) for part in x)


def blocks(x, count):
    rows = x.shape[0] // count
    return jnp.concatenate([x[rows * k : rows * (k + 1)] for k in range(count)], axis=1)


def call(kernel, out_shape, scratch=(), cost=(0, 0), room=VMEM_BYTES, **specs):
    return pl.pallas_call(
        kernel,
        out_shape=out_shape,
        scratch_shapes=list(scratch),
        compiler_params=pltpu.CompilerParams(vmem_limit_bytes=room),
        cost_estimate=pl.CostEstimate(flops=cost[0], bytes_accessed=cost[1], transcendentals=0),
        **specs,
    )


ANY = pl.BlockSpec(memory_space=pl.ANY)
VMEM = pl.BlockSpec(memory_space=pltpu.VMEM)


def local(pan_image, vnir_bands, swir_bands):
    groups = lax.axis_size("band")
    strips = lax.axis_size("rows")
    h, w = pan_image.shape
    nb, hc, full = vnir_bands.shape
    _, hs, sfull = swir_bands.shape
    wc = w // RATIO_V
    ws = wc // RATIO_S
    wf = wc + LANES
    sf = ws + LANES
    pad = -(-hc // 8) * 8
    fine_tiles = w // LANES
    coarse_tiles = wc // LANES
    frame_tiles = coarse_tiles + 1
    swir_tiles = ws // LANES
    fine_pixels = h * strips * w * groups
    pairs = w // (2 * LANES)
    middle = frame_tiles - 2
    margin = RATIO_V * LANES

    def shape(*dims):
        return jax.ShapeDtypeStruct(dims, F32)

    coarse_rows, fine_rows = row_tables(h)
    cols = column_tables()
    lift = up_rows(hc)
    gram = lift.T @ lift
    rise = lift.sum(axis=0)

    swir_rows = -(-hs // RATIO_S)
    at_swir = hc
    edge_size = 2 * HALO * hc + 4 * hs
    edge_lane = ws * (hs % RATIO_S)
    shared = hs % RATIO_S and edge_lane + edge_size <= wc
    at_edge = hc + swir_rows - 1 if shared else hc + swir_rows
    edge_lane = edge_lane if shared else 0
    at_strip = at_edge + 1
    piece = REACH * (h // 8)
    per_row = wc // piece
    strip_rows = -(-(8 // nb) // per_row)

    def going(d):
        return (["right"] if d == 1 else []) + (["left"] if d == groups - 1 else [])

    def strip_place(d, side):
        return at_strip + strip_rows * going(d).index(side)

    chunk_rows = [at_strip + strip_rows * len(going(d)) for d in range(groups)]

    mean_parts, fine_parts = split(cols["mean"]), split(cols["mean_fine"])
    r_fine = split(fine_rows)
    r_adj = split3(adjoint_rows(h))
    table, place = stack_tables(
        dict(
            tall=np.concatenate([mean_parts[0], fine_parts[0]], axis=1),
            tall_low=fine_parts[1],
            fine=split(cols["fine"]),
            rows=split(coarse_rows),
            rows_fine=np.concatenate([r_fine[0], r_fine[1], r_fine[0]], axis=1),
            low=split(cols["low"]),
            pair=split(cols["pair"]),
            up4=split(cols["up4"]),
            up3=split(cols["up3"]),
            adjoint=np.concatenate([r_adj[i] for i in (0, 0, 0, 1, 1, 2)], axis=2),
        )
    )

    def far(x):
        return pltpu.with_memory_space_constraint(x, pltpu.HBM)

    def pack(pan_ref, vnir_ref, swir_ref, *rest):
        outs, (wide, swide, edges, sems) = rest[:groups], rest[groups:]
        me = lax.axis_index("band")
        copies = [
            pltpu.make_async_copy(vnir_ref, wide.at[:, :, pl.ds(LANES, full)], sems.at[0]),
            pltpu.make_async_copy(swir_ref, swide.at[:, :, pl.ds(LANES, sfull)], sems.at[1]),
            pltpu.make_async_copy(pan_ref.at[:, pl.ds(0, LANES)], edges.at[0], sems.at[2]),
            pltpu.make_async_copy(pan_ref.at[:, pl.ds(w - LANES, LANES)], edges.at[1], sems.at[3]),
        ]
        for copy in copies:
            copy.start()
        wide[:, :, 0:LANES] = jnp.zeros((hc, nb, LANES), F32)
        wide[:, :, LANES + full : 2 * LANES + full] = jnp.zeros((hc, nb, LANES), F32)
        swide[:, :, 0:LANES] = jnp.zeros((nb, hs, LANES), F32)
        swide[:, :, LANES + sfull : 2 * LANES + sfull] = jnp.zeros((nb, hs, LANES), F32)
        for copy in copies:
            copy.wait()
        for d in range(groups):
            peer = lax.rem(me + d, groups)
            base = pl.multiple_of(peer * wc, LANES)
            sbase = pl.multiple_of(peer * ws, LANES)
            out = outs[d]
            out[0:hc] = wide[:, :, pl.ds(base + LANES, wc)]
            left = wide[:, :, pl.ds(base, LANES)]
            right = wide[:, :, pl.ds(base + LANES + wc, LANES)]
            borders = []
            for r in range(hc):
                borders += [left[r, :, LANES - HALO :], right[r, :, :HALO]]
            swin = swide[:, :, pl.ds(sbase, ws + 2 * LANES)]
            for q in range(hs):
                row = swin[:, q, :]
                lane = ws * (q % RATIO_S)
                out[at_swir + q // RATIO_S, :, lane : lane + ws] = row[:, LANES : LANES + ws]
                borders += [row[:, LANES - 2 : LANES], row[:, LANES + ws : LANES + ws + 2]]
            border = jnp.concatenate(borders, axis=1)
            out[at_edge, :, edge_lane : edge_lane + edge_size] = border
            for side in going(d):
                first = strip_place(d, side)
                edge = edges[1, :, LANES - REACH :] if side == "right" else edges[0, :, :REACH]
                flat = jnp.concatenate([edge[8 * t : 8 * t + 8] for t in range(h // 8)], axis=1)
                for i in range(8 // nb):
                    lane = piece * (i % per_row)
                    out[first + i // per_row, :, lane : lane + piece] = flat[nb * i : nb * (i + 1)]

    chunks = call(
        pack,
        tuple(shape(chunk_rows[d], nb, wc) for d in range(groups)),
        [
            pltpu.VMEM((hc, nb, full + 2 * LANES), F32),
            pltpu.VMEM((nb, hs, sfull + 2 * LANES), F32),
            pltpu.VMEM((2, h, LANES), F32),
            pltpu.SemaphoreType.DMA((4,)),
        ],
        cost=(0, 8_000_000),
        in_specs=[ANY] * 3,
    )(*(far(x) for x in (pan_image, jnp.transpose(vnir_bands, (1, 0, 2)), swir_bands)))
    *chunks, pan_late, table_late = lax.optimization_barrier((*chunks, pan_image, jnp.asarray(table)))
    got = [chunks[0]] + [
        lax.ppermute(chunks[d], "band", [(i, (i + d) % groups) for i in range(groups)])
        for d in range(1, groups)
    ]

    def take(ref, name, index=0, rows=None):
        starts, height, width = place[name]
        first, height = (0, height) if rows is None else (rows[0], rows[1] - rows[0])
        pieces = []
        for start, part in starts:
            base = start + first
            if not isinstance(index, int) or index:
                base = pl.multiple_of(base + index * place[name][1], 16)
            pieces.append(ref[pl.ds(base, height), 0:part])
        return pieces[0] if len(pieces) == 1 else jnp.concatenate(pieces, axis=1)

    def both_parts(ref, name, index=0, stacked=1):
        return take(ref, name, index), take(ref, name, index + stacked)

    def shrink(panes, tall, low):
        both = dot(panes[0], tall) + dot(panes[1], tall)
        return both[:, :LANES], both[:, LANES:] + dot(panes[0], low)

    def along_rows(rc, means, fines):
        both = parts2(jnp.concatenate([means, fines], axis=0))
        return dot(rc[0], both[0]) + (dot(rc[0], both[1]) + dot(rc[1], both[0]))

    def filter_rows(rf, x):
        col = parts2(x)
        return dot(rf, jnp.concatenate([col[0], col[0], col[1]], axis=0))

    def row_variant():
        row_id = lax.axis_index("rows")
        return jnp.where(row_id == 0, 1, jnp.where(row_id == strips - 1, 2, 0))

    pairs_in = [(i, i ^ 1) for i in range(strips) if i ^ 1 < strips]
    pairs_out = [(i, i + 1) for i in range(1, strips - 1, 2)]
    pairs_out += [(j, i) for i, j in pairs_out]

    def is_even():
        return lax.rem(lax.axis_index("rows"), 2) == 0

    def put(outs, index, up, down):
        even = is_even()
        outs[0][index] = jnp.where(even, up, down)
        outs[1][index] = jnp.where(even, down, up)

    def arrived(refs, index, low):
        even = is_even()
        inner, outer = refs[0][index], refs[1][index]
        return jnp.where(even, outer, inner) if low else jnp.where(even, inner, outer)

    def trade(inner, outer):
        outer = lax.ppermute(outer, "rows", pairs_out)
        return lax.ppermute(inner, "rows", pairs_in), outer

    at_up, at_down = 2 * pad, 2 * pad + 16

    def put_small(outs, first, ups, downs):
        blank = jnp.zeros((2, LANES), F32)
        for i in range(0, len(ups), 4):
            up = ups[i : i + 4] + [blank] * (4 - len(ups[i : i + 4]))
            down = downs[i : i + 4] + [blank] * (4 - len(downs[i : i + 4]))
            put(outs, first + i // 4, jnp.concatenate(up, axis=0), jnp.concatenate(down, axis=0))

    inner_fine = fine_tiles - 4

    def early(pan_far, table_far, pan_ref, table_ref, coarse_out, fine_out, col_out, sems):
        now = pl.ds(0, place["low"][0][0][0])
        later = pl.ds(now.size, table.shape[0] - now.size)
        copies = [
            pltpu.make_async_copy(pan_far, pan_ref, sems.at[0]),
            pltpu.make_async_copy(table_far.at[now], table_ref.at[now], sems.at[1]),
            pltpu.make_async_copy(table_far.at[later], table_ref.at[later], sems.at[2]),
        ]
        for copy in copies:
            copy.start()
        copies[0].wait()
        panes = parts2(pan_ref[...])
        copies[1].wait()
        starts = [margin * k - 3 * LANES for k in range(1, frame_tiles - 1)]
        means, fines = shrink(
            windows(panes, starts, 6 * LANES), take(table_ref, "tall"), take(table_ref, "tall_low")
        )
        rc = both_parts(table_ref, "rows", row_variant(), 3)
        coarse_out[...] = along_rows(rc, blocks(means, middle), blocks(fines, middle))
        starts = [2 * LANES * k - LANES for k in range(1, pairs - 1)]
        col = blocks(dot3(windows(panes, starts, 4 * LANES), both_parts(table_ref, "fine")), pairs - 2)
        col_out[...] = col
        fine_out[...] = filter_rows(take(table_ref, "rows_fine"), col)
        copies[2].wait()

    pan_held, table_held, coarse_mid, fine_mid, col_mid = call(
        early,
        (
            shape(h, w),
            jax.ShapeDtypeStruct(table.shape, BF16),
            shape(2 * pad + 32, LANES * middle),
            shape(h + 2 * HALO, LANES * inner_fine),
            shape(h, LANES * inner_fine),
        ),
        [pltpu.SemaphoreType.DMA((3,))],
        cost=(2_000_000_000, 8_000_000),
        in_specs=[ANY] * 2,
    )(far(pan_late), far(table_late))

    border_tiles = -(-edge_size // LANES)
    at_s = HALO * coarse_tiles
    at_h = at_s + 2 * swir_tiles
    at_ld = at_h + border_tiles
    at_d = at_ld + frame_tiles
    sent = at_d + -(-frame_tiles // 4)

    def framed(main, borders, lane, reach):
        blank = jnp.zeros((8, HALF - reach), F32)
        left = borders[:, lane : lane + reach]
        right = borders[:, lane + reach : lane + 2 * reach]
        return jnp.concatenate([blank, left, main, right, blank], axis=1)

    def assemble(pan_ref, table_ref, cm_ref, *rest):
        ins = rest[:groups]
        x_out, s_out, ce_out, fe_out, col_out = rest[groups : groups + 5]
        outs = rest[groups + 5 :]
        me = lax.axis_index("band")

        def gather(row, lane, size):
            rows = [ins[(groups - i) % groups][row, :, lane : lane + size] for i in range(groups)]
            return pltpu.roll(jnp.concatenate(rows, axis=0), nb * me, 0)

        def tile(x, t):
            return x[:, LANES * t : LANES * (t + 1)]

        borders = gather(at_edge, edge_lane, edge_size)
        blank = jnp.zeros((8, LANES * border_tiles - edge_size), F32)
        borders = jnp.concatenate([borders, blank], axis=1)
        for t in range(border_tiles):
            put(outs, at_h + t, tile(borders, t), tile(borders, t))
        mains = [gather(r, 0, wc) for r in range(hc)]
        for r in range(hc):
            x_out[r] = framed(mains[r], borders, 2 * HALO * r, HALO)
        for r in range(HALO):
            for t in range(coarse_tiles):
                put(outs, coarse_tiles * r + t, tile(mains[hc - HALO + r], t), tile(mains[r], t))
        shorts = [gather(at_swir + q // RATIO_S, ws * (q % RATIO_S), ws) for q in range(hs)]
        for q in range(hs):
            s_out[q] = framed(shorts[q], borders, 2 * HALO * hc + 4 * q, 2)
        for q in range(2):
            for t in range(swir_tiles):
                put(outs, at_s + swir_tiles * q + t, tile(shorts[hs - 2 + q], t), tile(shorts[q], t))

        def strip(d, side, empty):
            first = strip_place(d, side)
            rows = []
            for i in range(8 // nb):
                lane = piece * (i % per_row)
                rows.append(ins[d][first + i // per_row, :, lane : lane + piece])
            flat = jnp.where(empty, 0.0, jnp.concatenate(rows, axis=0))
            whole = [flat[:, REACH * t : REACH * (t + 1)] for t in range(h // 8)]
            return jnp.concatenate(whole, axis=0)

        blank = jnp.zeros((h, LANES - REACH), F32)
        left = jnp.concatenate([blank, strip(1, "right", me == 0), pan_ref[:, 0 : 3 * LANES]], axis=1)
        right = jnp.concatenate(
            [pan_ref[:, w - 3 * LANES : w], strip(groups - 1, "left", me == groups - 1), blank], axis=1
        )
        left, right = parts2(left), parts2(right)
        cut = 2 * LANES
        inner = (cut, 6 * LANES)
        lm, lf = shrink(left, take(table_ref, "tall", 0, inner), take(table_ref, "tall_low", 0, inner))
        inner = (0, 4 * LANES)
        rm, rfine = shrink(right, take(table_ref, "tall", 0, inner), take(table_ref, "tall_low", 0, inner))
        rc = both_parts(table_ref, "rows", row_variant(), 3)
        edge = along_rows(rc, jnp.concatenate([lm, rm], axis=1), jnp.concatenate([lf, rfine], axis=1))
        ce_out[...] = edge[0 : 2 * pad]
        outer = tuple(jnp.concatenate([a, b], axis=0) for a, b in zip(left, right))
        col = blocks(dot3(outer, both_parts(table_ref, "fine")), 2)
        col_out[...] = col
        fe_out[...] = filter_rows(take(table_ref, "rows_fine"), col)
        sides = jnp.concatenate([edge[:, :LANES], cm_ref[...], edge[:, LANES:]], axis=1)
        ups, downs = [], []
        for k in range(frame_tiles):
            part = tile(sides, k)
            put(outs, at_ld + k, part[at_up + 8 : at_up + 16], part[at_down + 8 : at_down + 16])
            ups.append(part[at_up : at_up + 2])
            downs.append(part[at_down + HALO - 2 : at_down + HALO])
        put_small(outs, at_d, ups, downs)

    x_loc, s_loc, coarse_edge, fine_edge, col_edge, rest_in, rest_out = call(
        assemble,
        (
            shape(hc, BANDS, wf),
            shape(hs, BANDS, sf),
            shape(2 * pad, 2 * LANES),
            shape(h + 2 * HALO, 4 * LANES),
            shape(h, 4 * LANES),
            shape(sent, 8, LANES),
            shape(sent, 8, LANES),
        ),
        cost=(200_000_000, 3_000_000),
        in_specs=[VMEM] * (groups + 3),
    )(pan_held, table_held, coarse_mid, *got)
    rest_in, rest_out = trade(rest_in, rest_out)

    turns = BANDS // 2 + 1
    block_starts = [LANES * k for k in range(coarse_tiles)]
    own_rows = range(2, hc + 2)
    halo_rows = (0, 1, hc + 2, hc + 3)
    around = (-2, -1) + halo_rows + (hc + 4, hc + 5)
    whole_rows = range(2, hc - 2)
    first_whole = RATIO_V * whole_rows[0]
    whole_count = RATIO_V * len(whole_rows)

    def lifted(rows, table_ref, store):
        stack = windows(parts2(jnp.concatenate(rows, axis=0)), block_starts, 2 * LANES)
        up = dot3(stack, both_parts(table_ref, "up4"))
        size = 8 * len(rows)
        for k in range(coarse_tiles):
            for q in range(RATIO_V):
                store(RATIO_V * k + q, up[size * k : size * (k + 1), LANES * q : LANES * (q + 1)])

    def weighted(pairs):
        value = None
        for weight, x in pairs:
            if weight != 0.0:
                value = float(weight) * x if value is None else value + float(weight) * x
        return value

    def adjoint_of(table_ref, col):
        p1 = col.astype(BF16)
        over = col - p1.astype(F32)
        p2 = over.astype(BF16)
        p3 = (over - p2.astype(F32)).astype(BF16)
        weights = take(table_ref, "adjoint", row_variant())
        return dot(weights, jnp.concatenate([p1, p2, p3, p1, p2, p1], axis=0))

    def inside(
        pan_ref, x_ref, s_ref, fm_ref, fe_ref, colm_ref, cole_ref, table_ref,
        y_out, v_out, acc_out, s_out, diff_out, q_out, edge_out, mean_out, lows_out, *outs,
    ):
        def store(index, value):
            y_out[index] = value

        lifted([x_ref[r] for r in range(hc)], table_ref, store)
        rows = parts2(jnp.concatenate([s_ref[q] for q in range(hs)], axis=0))
        s_cols = dot3(windows(rows, block_starts[:swir_tiles], 2 * LANES), both_parts(table_ref, "up3"))
        s_out[...] = blocks(s_cols, swir_tiles)

        def joined(outer, inner):
            return jnp.concatenate([outer[:, : 2 * LANES], inner, outer[:, 2 * LANES :]], axis=1)

        low = joined(fe_ref[...], fm_ref[...])
        diff = pan_ref[...] - low[0:h]
        adjoint = adjoint_of(table_ref, joined(cole_ref[...], colm_ref[...]))
        total = jnp.zeros((1, LANES), F32)
        for k in range(fine_tiles):
            at = slice(LANES * k, LANES * (k + 1))
            diff_out[k] = diff[:, at]
            q_out[k] = adjoint[:, at]
            total = total + adjoint[hc + 8 : hc + 9, at]
            put(outs, k, low[h : h + HALO, at], low[h + HALO : h + 2 * HALO, at])

        row_id = lax.axis_index("rows")
        below = jnp.where(row_id > 0, 1.0, 0.0).astype(F32)
        above = jnp.where(row_id < strips - 1, 1.0, 0.0).astype(F32)
        means = {}
        for r in range(-2, hc + 2):
            value = weighted((MEAN4[t + 2], x_ref[r + t]) for t in range(-2, 3) if 0 <= r + t < hc)
            means[r] = value * below if r < 0 else (value * above if r >= hc else value)
        for i, r in enumerate((0, 1, hc - 2, hc - 1)):
            edge_out[i] = means[r]
        rows = parts2(jnp.concatenate([means[r] for r in range(2, hc - 2)], axis=0))
        pair = tuple(x[:, :LANES] for x in both_parts(table_ref, "pair", 0, 3))
        mean_out[...] = blocks(dot3(windows(rows, block_starts, 2 * LANES), pair), coarse_tiles)
        reach = TAPS_S // 2
        for r in range(hc):
            lows_out[r] = weighted((KC[t + reach], means[r + t]) for t in range(-reach, reach + 1) if r + t in means)
        acc_out[turns + 2] = jnp.concatenate([total, jnp.zeros((7, LANES), F32)], axis=0)

        def tile_step(k, carry):
            accs, accv, accp = list(carry[:turns]), carry[turns], carry[turns + 1]
            ys = {m: y_out[k, pl.ds(8 * (m - 2), 8), :] for m in own_rows}
            for m in own_rows:
                z = weighted((gram[m, other], ys[other]) for other in own_rows)
                accs[0] = accs[0] + z * ys[m]
                for i in range(1, turns):
                    accs[i] = accs[i] + z * pltpu.roll(ys[m], i, 0)
                accv = accv + float(rise[m]) * ys[m]
                accp = accp + ys[m] * q_out[k, pl.ds(m + 2, 1), :]
            for m in whole_rows:
                for p in range(RATIO_V):
                    r = RATIO_V * m + p - first_whole
                    v_out[k, pl.ds(8 * r, 8), :] = weighted((C4[t, p], ys[m + t]) for t in range(5) if C4[t, p] != 0.0)
            return tuple(accs) + (accv, accp)

        zero = jnp.zeros((8, LANES), F32)
        first = lax.fori_loop(0, fine_tiles, tile_step, (zero,) * (turns + 2))
        for i in range(turns + 2):
            acc_out[i] = first[i]

    q_rows = -(-(hc + 9) // 16) * 16
    y_own, v_own, acc_own, s_own, diff, q_own, mean_edge, mean_own, lows_own, low_in, low_out = call(
        inside,
        (
            shape(fine_tiles, 8 * hc, LANES),
            shape(fine_tiles, 8 * whole_count, LANES),
            shape(turns + 3, 8, LANES),
            shape(8 * hs, wc),
            shape(fine_tiles, h, LANES),
            shape(fine_tiles, q_rows, LANES),
            shape(4, BANDS, wf),
            shape(8 * (hc - 4), wc),
            shape(hc, BANDS, wf),
            shape(fine_tiles, 8, LANES),
            shape(fine_tiles, 8, LANES),
        ),
        cost=(2_000_000_000, 8_000_000),
    )(pan_held, x_loc, s_loc, fine_mid, fine_edge, col_mid, col_edge, table_held)
    low_in, low_out = trade(low_in, low_out)

    def moments(
        x_ref, y_ref, acc_ref, scol_ref, q_ref, edge_ref, mean_ref, lows_ref,
        rest_in_ref, rest_out_ref, cm_ref, ce_ref, table_ref,
        mom_out, y_out, ugap_out, dgap_out, s_out,
        both, ulow,
    ):
        me = lax.axis_index("band")
        rest = (rest_in_ref, rest_out_ref)

        def tiles(refs, low, indices):
            return jnp.concatenate([arrived(refs, i, low) for i in indices], axis=1)

        def halo(first, per, reach, start, count):
            sides = []
            for low, base in ((True, start[0]), (False, start[1])):
                borders = tiles(rest, low, range(at_h, at_h + border_tiles))
                rows = []
                for r in range(count):
                    main = tiles(rest, low, range(first + per * r, first + per * (r + 1)))
                    rows.append(framed(main, borders, base + 2 * reach * r, reach))
                sides.append(rows)
            return sides

        x_low, x_high = halo(0, coarse_tiles, HALO, (2 * HALO * (hc - HALO), 0), HALO)

        def x_row(r):
            if r < 0:
                return x_low[HALO + r]
            if r >= hc:
                return x_high[r - hc]
            return x_ref[r]

        def store(index, value):
            y_out[index] = value

        lifted([x_row(m - 2) for m in around], table_ref, store)

        zero = jnp.zeros((8, LANES), F32)

        def tile_step(k, carry):
            accs = list(carry[:turns])
            accp, accv = carry[turns], carry[turns + 1]
            ys = {m: y_ref[k, pl.ds(8 * (m - 2), 8), :] for m in own_rows}
            for i, m in enumerate(around):
                ys[m] = y_out[k, pl.ds(8 * i, 8), :]
            for m in halo_rows:
                near = weighted((gram[m, other], ys[other]) for other in own_rows)
                whole = near + weighted((gram[m, other], ys[other]) for other in halo_rows)
                accs[0] = accs[0] + ys[m] * (near + whole)
                for i in range(1, turns):
                    accs[i] = accs[i] + whole * pltpu.roll(ys[m], i, 0) + ys[m] * pltpu.roll(near, i, 0)
                accv = accv + float(rise[m]) * ys[m]
            for m in around:
                accp = accp + ys[m] * q_ref[k, pl.ds(m + 2, 1), :]
            return tuple(accs) + (accp, accv)

        start = tuple(acc_ref[i] for i in range(turns)) + (acc_ref[turns + 1], acc_ref[turns])
        def two_tiles(k, carry):
            return tile_step(2 * k + 1, tile_step(2 * k, carry))

        first = lax.fori_loop(0, fine_tiles // 2, two_tiles, start)

        beyond = [r for r in range(-HALO, hc + HALO) if not 0 <= r < hc]
        edges = []
        for i, r in enumerate((0, 1, hc - 2, hc - 1)):
            more = weighted((MEAN4[a - r + 2], x_row(a)) for a in beyond if abs(a - r) <= 2)
            edges.append(edge_ref[i] + more)
        lows = []
        for r in range(hc):
            more = weighted((WIDE[a - r + HALO], x_row(a)) for a in beyond if abs(a - r) <= HALO)
            lows.append(lows_ref[r] + more)
        u_rows = windows(parts2(jnp.concatenate(edges, axis=0)), block_starts, 2 * LANES)
        l_rows = windows(parts2(jnp.concatenate(lows, axis=0)), block_starts, 2 * LANES)
        u_edge = dot3(u_rows, tuple(x[:, :LANES] for x in both_parts(table_ref, "pair", 0, 3)))
        left = jnp.where(me == 0, 1, 0)
        right = jnp.where(me == groups - 1, 2, 0)
        size = 8 * hc
        last = coarse_tiles - 1
        for which, lo_k, hi_k in ((left, 0, 1), (0, 1, last), (right, last, last + 1)):
            if hi_k <= lo_k:
                continue
            wp = tuple(x[:, LANES:] for x in both_parts(table_ref, "pair", which, 3))
            part = dot3(tuple(x[size * lo_k : size * hi_k] for x in l_rows), wp)
            for k in range(lo_k, hi_k):
                at = slice(LANES * k, LANES * (k + 1))
                low_k = part[size * (k - lo_k) : size * (k - lo_k + 1)]
                ulow[:, at] = low_k
                around_k = u_edge[32 * k : 32 * (k + 1)]
                u_k = jnp.concatenate([around_k[0:16], mean_ref[:, at], around_k[16:32]], axis=0)
                ugap_out[:, at] = u_k - low_k

        column = lax.broadcasted_iota(jnp.int32, (1, wf), 1) - HALF + me * wc
        valid = jnp.where((column >= 0) & (column < groups * wc), 1.0, 0.0).astype(F32)

        def own(rows):
            return jnp.concatenate([ce_ref[rows, 0:LANES], cm_ref[rows, :], ce_ref[rows, LANES:]], axis=1)

        def small(low):
            rows = [arrived(rest, at_d + k // 4, low)[2 * (k % 4) : 2 * (k % 4) + 2] for k in range(frame_tiles)]
            return jnp.concatenate(rows, axis=1)

        both[...] = own(slice(0, pad))
        both[0:2] = both[0:2] + small(True)
        both[hc - 2 : hc] = both[hc - 2 : hc] + small(False)
        detail = both[...]
        both[...] = own(slice(pad, 2 * pad))
        both[0:HALO] = both[0:HALO] + tiles(rest, True, range(at_ld, at_ld + frame_tiles))
        both[hc - HALO : hc] = both[hc - HALO : hc] + tiles(rest, False, range(at_ld, at_ld + frame_tiles))
        dlow_rows = windows(parts2(both[...] * valid), block_starts, 2 * LANES)
        dlow = blocks(dot3(dlow_rows, both_parts(table_ref, "low")), coarse_tiles)
        dgap_out[...] = detail[:, HALF : HALF + wc] - dlow
        both[:, 0:wc] = dlow

        s_low, s_high = halo(at_s, swir_tiles, 2, (2 * HALO * hc + 4 * (hs - 2), 2 * HALO * hc), 2)
        s_parts = windows(parts2(jnp.concatenate(s_low + s_high, axis=0)), block_starts[:swir_tiles], 2 * LANES)
        s_around = blocks(dot3(s_parts, both_parts(table_ref, "up3")), swir_tiles)
        s_cols = jnp.concatenate([s_around[0:16], scol_ref[...], s_around[16:32]], axis=0)
        for m in range(hs):
            for p in range(RATIO_S):
                value = None
                for t in range(5):
                    if C3[t, p] != 0.0:
                        term = float(C3[t, p]) * s_cols[8 * (m + t) : 8 * (m + t) + 8]
                        value = term if value is None else value + term
                s_out[RATIO_S * m + p] = value

        ll = [zero] * turns
        cross = [zero] * BANDS
        ld = ls = sd = ss = dd = ds = zero
        for r in range(hc):
            for k in range(coarse_tiles):
                at = slice(LANES * k, LANES * (k + 1))
                u = ulow[8 * r : 8 * r + 8, at]
                s = s_out[r, :, at]
                dl = jnp.broadcast_to(both[r : r + 1, at], (8, LANES))
                ll[0] = ll[0] + u * u
                for i in range(1, turns):
                    ll[i] = ll[i] + u * pltpu.roll(u, i, 0)
                for i in range(BANDS):
                    cross[i] = cross[i] + u * s_out[r, i : i + 1, at]
                ld = ld + u * dl
                sd = sd + s * dl
                ls = ls + u
                ss = ss + s
                dd = dd + dl * dl
                ds = ds + dl

        lane = lax.broadcasted_iota(jnp.int32, (8, LANES), 1)
        sub = lax.broadcasted_iota(jnp.int32, (8, LANES), 0)

        def column_of(acc):
            return jnp.broadcast_to(jnp.sum(acc, axis=1, keepdims=True), (8, LANES))

        table = zero
        for base, accs in ((0, ll), (32, first[:turns])):
            for i in range(turns):
                col = column_of(accs[i])
                table = jnp.where(lane == base + lax.rem(sub + BANDS - i, BANDS), col, table)
                if 0 < i < BANDS // 2:
                    turned = pltpu.roll(col, BANDS - i, 0)
                    table = jnp.where(lane == base + lax.rem(sub + i, BANDS), turned, table)
        singles = [(8 + i, cross[i]) for i in range(BANDS)]
        singles += [(16, ld), (17, ls), (18, sd), (19, ss), (20, dd), (21, ds)]
        singles += [(40, first[turns]), (41, first[turns + 1])]
        for index, acc in singles:
            table = jnp.where(lane == index, column_of(acc), table)
        total = jnp.sum(jnp.sum(acc_ref[turns + 2], axis=0, keepdims=True), axis=1, keepdims=True)
        table = jnp.where(lane == 43, total, table)
        turned = pltpu.roll(table, HALF, 1)
        mom_out[...] = jnp.where(lane[0:4] < HALF, table[0:4], turned[4:8])

    mom, y_halo, ugap, dgap, s_up = call(
        moments,
        (
            shape(4, LANES),
            shape(fine_tiles, 8 * len(around), LANES),
            shape(8 * hc, wc),
            shape(pad, wc),
            shape(hc, BANDS, wc),
        ),
        [
            pltpu.VMEM((pad, wf), F32),
            pltpu.VMEM((8 * hc, wc), F32),
        ],
        cost=(1_000_000_000, 8_000_000),
    )(
        x_loc, y_own, acc_own, s_own, q_own, mean_edge, mean_own, lows_own,
        rest_in, rest_out, coarse_mid, coarse_edge, table_held,
    )
    devices = groups * strips
    mom, low_in, low_out = lax.optimization_barrier((mom, low_in, low_out))
    spread = jnp.broadcast_to(mom[None], (devices,) + mom.shape)
    sums = lax.all_to_all(spread, ("rows", "band"), split_axis=0, concat_axis=0, tiled=True)

    def finish(
        sums_ref, y_ref, yh_ref, v_ref, diff_ref, low_in_ref, low_out_ref, ugap_ref, dgap_ref, s_ref,
        vnir_out, swir_out, tiles, swir, ends, sems,
    ):
        lane = lax.broadcasted_iota(jnp.int32, (8, LANES), 1)
        sub = lax.broadcasted_iota(jnp.int32, (8, LANES), 0)
        eye = lane == sub
        terms = [sums_ref[index] for index in range(devices)]
        while len(terms) > 1:
            terms = [sum(terms[i : i + 2][1:], terms[i]) for i in range(0, len(terms), 2)]
        total = jnp.concatenate([terms[0], pltpu.roll(terms[0], HALF, 1)], axis=0)

        def column(x, index):
            return jnp.broadcast_to(x[:, index : index + 1], (8, LANES))

        def across(col):
            return jnp.sum(jnp.where(eye, col, 0.0), axis=0, keepdims=True)

        def down(x):
            return jnp.sum(x, axis=0, keepdims=True)

        def solve(matrix, rhs):
            cols = [column(matrix, j) for j in range(BANDS)] + [rhs]
            inverse = jnp.zeros((8, LANES), F32)
            for k in range(BANDS):
                pivot = 1.0 / jnp.broadcast_to(cols[k][k : k + 1], (8, LANES))
                inverse = jnp.where(sub == k, pivot, inverse)
                factor = jnp.where(sub == k, 0.0, cols[k] * pivot)
                for j in range(k + 1, BANDS + 1):
                    cols[j] = cols[j] - factor * jnp.broadcast_to(cols[j][k : k + 1], (8, LANES))
            return cols[BANDS] * inverse

        n1 = float(fine_pixels)
        mean_v = column(total, 41) / n1
        mean_p = column(total, 43) / n1
        cov_v = pltpu.roll(total, LANES - 32, 1) / n1 - mean_v * across(mean_v)
        cov_p = column(total, 40) / n1 - mean_v * mean_p
        gain = cov_p / down(cov_p * solve(cov_v, cov_p))

        n2 = float(fine_pixels // (RATIO_V * RATIO_V))
        mean_l = column(total, 17) / n2
        mean_s = column(total, 19) / n2
        mean_d = column(total, 21) / n2
        cov_ll = total / n2 - mean_l * across(mean_l)
        cov_ls = pltpu.roll(total, LANES - 8, 1) / n2 - mean_l * across(mean_s)
        cov_ld = column(total, 16) / n2 - mean_l * mean_d
        cov_sd = column(total, 18) / n2 - mean_s * mean_d
        cov_dd = column(total, 20) / n2 - mean_d * mean_d
        gain_row = across(gain)
        a2 = cov_ll + gain * across(cov_ld) + cov_ld * gain_row + gain * gain_row * cov_dd
        b2 = jnp.where(lane < BANDS, cov_ls + gain * across(cov_sd), 0.0)
        target = jnp.broadcast_to(jnp.sum(b2, axis=1, keepdims=True) / BANDS, (8, LANES))

        def sent_tile(k):
            lanes = pl.ds(pl.multiple_of(LANES * k, LANES), LANES)
            return pltpu.make_async_copy(tiles.at[k], vnir_out.at[:, lanes], sems.at[k])

        def tile_step(k, carry):
            ys = {m: y_ref[k, pl.ds(8 * (m - 2), 8), :] for m in own_rows}
            for i, m in enumerate(around):
                if m in halo_rows:
                    ys[m] = yh_ref[k, pl.ds(8 * i, 8), :]
            lows = (low_in_ref, low_out_ref)
            ends[k, 0:HALO, :] = diff_ref[k, 0:HALO, :] - arrived(lows, k, True)
            ends[k, HALO:, :] = diff_ref[k, h - HALO :, :] - arrived(lows, k, False)
            for m in range(hc):
                for p in range(RATIO_V):
                    r = RATIO_V * m + p
                    if m in whole_rows:
                        value = v_ref[k, pl.ds(8 * (r - first_whole), 8), :]
                    else:
                        value = weighted((C4[t, p], ys[m + t]) for t in range(5) if C4[t, p] != 0.0)
                    if r < HALO:
                        detail = ends[k, pl.ds(r, 1), :]
                    elif r >= h - HALO:
                        detail = ends[k, pl.ds(r - h + 2 * HALO, 1), :]
                    else:
                        detail = diff_ref[k, pl.ds(r, 1), :]
                    value = value + gain * detail
                    tiles[k, pl.ds(r, 8, stride=h), :] = value
            sent_tile(k).start()
            return carry

        beside = fine_tiles // BANDS

        def solve_step(k, carry):
            work, inverse = carry
            here = sub == k
            row = down(jnp.where(here, work, 0.0))
            col = jnp.sum(jnp.where(lane == k, work, 0.0), axis=1, keepdims=True)
            pivot = 1.0 / down(jnp.where(here[:, 0:1], col, 0.0))
            inverse = jnp.where(here, pivot, inverse)
            work = work - jnp.where(here, 0.0, col * pivot) * row

            for i in range(beside):
                tile_step(beside * k + i, 0)
            return work, inverse

        start = (jnp.where(lane == BANDS, target, a2), jnp.zeros((8, LANES), F32))
        work, inverse = lax.fori_loop(0, BANDS, solve_step, start)
        lax.fori_loop(BANDS * beside, fine_tiles, tile_step, 0)
        fit2 = column(work, BANDS) * inverse
        numer = down(fit2 * b2)
        share_row = numer / down(fit2 * target)
        share = jnp.sum(jnp.where(eye, jnp.broadcast_to(share_row, (8, LANES)), 0.0), axis=1, keepdims=True)
        scale = down(fit2 * gain)[:, 0:1]
        fit_col = fit2[:, 0:1]
        for r in range(hc):
            seen = jnp.sum(fit_col * ugap_ref[8 * r : 8 * r + 8, :], axis=0, keepdims=True)
            seen = seen + scale * dgap_ref[r : r + 1, :]
            swir[r] = s_ref[r] + share * seen
        last = pltpu.make_async_copy(swir, swir_out, sems.at[fine_tiles])
        last.start()

        def drain(k, carry):
            sent_tile(k).wait()
            return carry

        lax.fori_loop(0, fine_tiles, drain, 0)
        last.wait()

    joined_vnir, joined_swir = call(
        finish,
        (shape(BANDS * h, w), shape(hc, BANDS, wc)),
        [
            pltpu.VMEM((fine_tiles, BANDS * h, LANES), F32),
            pltpu.VMEM((hc, BANDS, wc), F32),
            pltpu.VMEM((fine_tiles, 2 * HALO, LANES), F32),
            pltpu.SemaphoreType.DMA((fine_tiles + 1,)),
        ],
        cost=(100_000_000, 8_000_000),
        out_specs=(ANY, ANY),
    )(sums, y_own, y_halo, v_own, diff, low_in, low_out, ugap, dgap, s_up)
    return joined_vnir.reshape(BANDS, h, w), jnp.transpose(joined_swir, (1, 0, 2))


def solution(mesh):
    return jax.shard_map(
        local,
        mesh=mesh,
        in_specs=(P("rows", "band"), P("band", "rows", None), P("band", "rows", None)),
        out_specs=(P(None, "rows", "band"), P(None, "rows", "band")),
        check_vma=False,
    )
```

```python
import math

import jax
import jax.numpy as jnp
import ml_dtypes
import numpy as np
from jax import lax
from jax.experimental import pallas as pl
from jax.experimental.pallas import tpu as pltpu
from jax.sharding import PartitionSpec as P

BANDS = 8
RATIO_V = 4
RATIO_S = 3
TAPS_V = 17
TAPS_S = 13
NYQUIST_GAIN = 0.29
LANES = 128
HALF = 64
REACH = 32
HALO = 8
F32 = jnp.float32
BF16 = jnp.bfloat16
VMEM_BYTES = 24 * 1024 * 1024
VMEM_MOST = 56 * 1024 * 1024


def gauss_taps(upscale, kernel_len):
    spread = upscale * math.sqrt(-2.0 * math.log(NYQUIST_GAIN)) / math.pi
    radius = kernel_len // 2
    offsets = np.arange(-radius, radius + 1) * 1.0
    values = np.exp(-(offsets**2) / (2.0 * spread**2))
    return values / values.sum()


def cubic_weight(distance):
    distance = abs(distance)
    if distance <= 1.0:
        return 1.5 * distance**3 - 2.5 * distance**2 + 1.0
    if distance < 2.0:
        return -0.5 * distance**3 + 2.5 * distance**2 - 4.0 * distance + 2.0
    return 0.0


def cubic_table(upscale):
    weights = np.zeros((5, upscale))
    for phase_index in range(upscale):
        centre = (phase_index + 0.5) / upscale - 0.5
        first_tap = math.floor(centre)
        fraction = centre - first_tap
        for tap_index in range(-1, 3):
            weights[first_tap + tap_index + 2, phase_index] += cubic_weight(tap_index - fraction)
    return weights


KF = gauss_taps(RATIO_V, TAPS_V)
KC = gauss_taps(RATIO_S, TAPS_S)
C4 = cubic_table(RATIO_V)
C3 = cubic_table(RATIO_S)
MEAN4 = C4.mean(axis=1)
WIDE = np.convolve(KC, MEAN4)


def split(table):
    high = np.asarray(table, np.float64).astype(np.float32).astype(ml_dtypes.bfloat16)
    low = (np.asarray(table, np.float64) - high.astype(np.float64)).astype(np.float32)
    return np.stack([high, low.astype(ml_dtypes.bfloat16)])


def split3(table):
    high, middle = split(table)
    low = np.asarray(table, np.float64) - high.astype(np.float64) - middle.astype(np.float64)
    return high, middle, low.astype(np.float32).astype(ml_dtypes.bfloat16)


def band_matrix(size, taps):
    radius = len(taps) // 2
    out = np.zeros((size, size))
    for row in range(size):
        for tap in range(-radius, radius + 1):
            if 0 <= row + tap < size:
                out[row, row + tap] = taps[tap + radius]
    return out


def row_tables(h):
    hc = h // RATIO_V
    mean = np.zeros((3 * hc, 3 * h))
    for row in range(3 * hc):
        mean[row, RATIO_V * row : RATIO_V * (row + 1)] = 1.0 / RATIO_V
    fine = band_matrix(3 * h, KF)
    low = band_matrix(3 * hc, KC)
    mean_fine = mean @ fine
    pad = -(-hc // 8) * 8

    def part(matrix, rows, cols):
        return matrix[rows, :][:, cols]

    def stacked(rows, cols, filt):
        a = mean if filt is None else filt @ mean
        c = mean_fine if filt is None else filt @ mean_fine
        return np.concatenate([part(a, rows, cols), -part(c, rows, cols)], axis=1)

    own = slice(h, 2 * h)
    tables = []
    for variant in range(3):
        keep = np.ones(3 * hc)
        if variant == 1:
            keep[:hc] = 0.0
        if variant == 2:
            keep[2 * hc :] = 0.0
        masked = low * keep[None, :]
        rows = []
        for filt in (None, masked):
            block = np.zeros((pad, 2 * h))
            block[:hc] = stacked(slice(hc, 2 * hc), own, filt)
            rows.append(block)
        for filt in (None, low):
            rows.append(stacked(slice(hc, hc + HALO), slice(0, h), filt))
        for filt in (None, low):
            rows.append(stacked(slice(2 * hc - HALO, 2 * hc), slice(2 * h, 3 * h), filt))
        tables.append(np.concatenate(rows, axis=0))
    coarse_rows = np.stack(tables)
    fine_rows = np.concatenate(
        [fine[h : 2 * h, h : 2 * h], fine[h : h + HALO, 0:h], fine[2 * h - HALO : 2 * h, 2 * h : 3 * h]],
        axis=0,
    )
    return coarse_rows, fine_rows


def up_rows(hc):
    out = np.zeros((RATIO_V * hc, hc + 4))
    for m in range(hc):
        for p in range(RATIO_V):
            out[RATIO_V * m + p, m : m + 5] = C4[:, p]
    return out


def adjoint_rows(h):
    hc = h // RATIO_V
    reach = TAPS_V // 2
    size = h + 2 * reach
    lift = np.zeros((size, hc + 8))
    for r in range(size):
        m, p = divmod(r - reach, RATIO_V)
        lift[r, m + 2 : m + 7] = C4[:, p]
    fine = np.zeros((size, h))
    for r in range(size):
        for t in range(-reach, reach + 1):
            if 0 <= r - reach + t < h:
                fine[r, r - reach + t] = KF[t + reach]
    out = np.zeros((3, -(-(hc + 9) // 16) * 16, h))
    for variant in range(3):
        keep = np.ones((size, 1))
        if variant == 1:
            keep[:reach] = 0.0
        if variant == 2:
            keep[h + reach :] = 0.0
        out[variant, : hc + 8] = (lift * keep).T @ fine
        out[variant, hc + 8] = (fine * keep).sum(axis=0)
    return out


def column_tables():
    n = LANES
    fine = np.zeros((4 * n, 2 * n))
    mean = np.zeros((6 * n, n))
    mean_fine = np.zeros((6 * n, n))
    low = np.zeros((2 * n, n))
    pair = np.zeros((3, 2 * n, 2 * n))
    up4 = np.zeros((2 * n, RATIO_V * n))
    up3 = np.zeros((2 * n, RATIO_S * n))
    for c in range(2 * n):
        for t in range(-(TAPS_V // 2), TAPS_V // 2 + 1):
            fine[n + c + t, c] += KF[t + TAPS_V // 2]
    for c in range(n):
        for q in range(RATIO_V):
            mean[n + RATIO_V * c + q, c] = 1.0 / RATIO_V
            for t in range(-(TAPS_V // 2), TAPS_V // 2 + 1):
                mean_fine[n + RATIO_V * c + q + t, c] += KF[t + TAPS_V // 2] / RATIO_V
        for t in range(-(TAPS_S // 2), TAPS_S // 2 + 1):
            low[c + HALF + t, c] += KC[t + TAPS_S // 2]
            for s in range(-2, 3):
                value = KC[t + TAPS_S // 2] * MEAN4[s + 2]
                pair[0, c + HALF + t + s, n + c] += value
                if c + t >= 0:
                    pair[1, c + HALF + t + s, n + c] += value
                if c + t < n:
                    pair[2, c + HALF + t + s, n + c] += value
        for s in range(-2, 3):
            pair[:, c + HALF + s, c] += MEAN4[s + 2]
            for p in range(RATIO_V):
                up4[c + HALF + s, RATIO_V * c + p] += C4[s + 2, p]
            for p in range(RATIO_S):
                up3[c + HALF + s, RATIO_S * c + p] += C3[s + 2, p]
    return dict(fine=fine, mean=mean, mean_fine=mean_fine, low=low, pair=pair, up4=up4, up3=up3)


def stack_tables(tables):
    wide = 2 * LANES
    pieces, place, top = [], {}, 0
    for name, value in tables.items():
        stack = value.reshape((-1,) + value.shape[-2:])
        height, width = stack.shape[1:]
        starts = []
        for lane in range(0, width, wide):
            part = stack[:, :, lane : lane + wide]
            starts.append((top, part.shape[2]))
            piece = np.zeros((stack.shape[0] * height, wide), ml_dtypes.bfloat16)
            piece[:, : part.shape[2]] = part.reshape(-1, part.shape[2])
            pieces.append(piece)
            top += piece.shape[0]
        place[name] = (starts, height, width)
    return np.concatenate(pieces, axis=0), place


def parts2(x):
    high = x.astype(BF16)
    return high, (x - high.astype(F32)).astype(BF16)


def dot(a, b):
    return jnp.dot(a, b, preferred_element_type=F32)


def dot3(x, w):
    return dot(x[0], w[0]) + (dot(x[1], w[0]) + dot(x[0], w[1]))


def windows(x, starts, size):
    return tuple(jnp.concatenate([part[:, a : a + size] for a in starts], axis=0) for part in x)


def blocks(x, count):
    rows = x.shape[0] // count
    return jnp.concatenate([x[rows * k : rows * (k + 1)] for k in range(count)], axis=1)


def call(kernel, out_shape, scratch=(), cost=(0, 0), room=VMEM_BYTES, **specs):
    return pl.pallas_call(
        kernel,
        out_shape=out_shape,
        scratch_shapes=list(scratch),
        compiler_params=pltpu.CompilerParams(vmem_limit_bytes=room),
        cost_estimate=pl.CostEstimate(flops=cost[0], bytes_accessed=cost[1], transcendentals=0),
        **specs,
    )


ANY = pl.BlockSpec(memory_space=pl.ANY)
VMEM = pl.BlockSpec(memory_space=pltpu.VMEM)


def local(pan_image, vnir_bands, swir_bands):
    groups = lax.axis_size("band")
    strips = lax.axis_size("rows")
    h, w = pan_image.shape
    nb, hc, full = vnir_bands.shape
    _, hs, sfull = swir_bands.shape
    wc = w // RATIO_V
    ws = wc // RATIO_S
    wf = wc + LANES
    sf = ws + LANES
    pad = -(-hc // 8) * 8
    fine_tiles = w // LANES
    coarse_tiles = wc // LANES
    frame_tiles = coarse_tiles + 1
    swir_tiles = ws // LANES
    fine_pixels = h * strips * w * groups
    pairs = w // (2 * LANES)
    middle = frame_tiles - 2
    margin = RATIO_V * LANES

    def shape(*dims):
        return jax.ShapeDtypeStruct(dims, F32)

    coarse_rows, fine_rows = row_tables(h)
    cols = column_tables()
    lift = up_rows(hc)
    gram = lift.T @ lift
    rise = lift.sum(axis=0)

    swir_rows = -(-hs // RATIO_S)
    at_swir = hc
    edge_size = 2 * HALO * hc + 4 * hs
    edge_lane = ws * (hs % RATIO_S)
    shared = hs % RATIO_S and edge_lane + edge_size <= wc
    at_edge = hc + swir_rows - 1 if shared else hc + swir_rows
    edge_lane = edge_lane if shared else 0
    at_strip = at_edge + 1
    piece = REACH * (h // 8)
    per_row = wc // piece
    strip_rows = -(-(8 // nb) // per_row)

    def going(d):
        return (["right"] if d == 1 else []) + (["left"] if d == groups - 1 else [])

    def strip_place(d, side):
        return at_strip + strip_rows * going(d).index(side)

    chunk_rows = [at_strip + strip_rows * len(going(d)) for d in range(groups)]

    mean_parts, fine_parts = split(cols["mean"]), split(cols["mean_fine"])
    r_fine = split(fine_rows)
    r_adj = split3(adjoint_rows(h))
    table, place = stack_tables(
        dict(
            tall=np.concatenate([mean_parts[0], fine_parts[0]], axis=1),
            tall_low=fine_parts[1],
            fine=split(cols["fine"]),
            rows=split(coarse_rows),
            rows_fine=np.concatenate([r_fine[0], r_fine[1], r_fine[0]], axis=1),
            low=split(cols["low"]),
            pair=split(cols["pair"]),
            up4=split(cols["up4"]),
            up3=split(cols["up3"]),
            adjoint=np.concatenate([r_adj[i] for i in (0, 0, 0, 1, 1, 2)], axis=2),
        )
    )

    def far(x):
        return pltpu.with_memory_space_constraint(x, pltpu.HBM)

    def pack(pan_ref, vnir_ref, swir_ref, *rest):
        outs, (wide, swide, edges, sems) = rest[:groups], rest[groups:]
        me = lax.axis_index("band")
        copies = [
            pltpu.make_async_copy(vnir_ref, wide.at[:, :, pl.ds(LANES, full)], sems.at[0]),
            pltpu.make_async_copy(swir_ref, swide.at[:, :, pl.ds(LANES, sfull)], sems.at[1]),
            pltpu.make_async_copy(pan_ref.at[:, pl.ds(0, LANES)], edges.at[0], sems.at[2]),
            pltpu.make_async_copy(pan_ref.at[:, pl.ds(w - LANES, LANES)], edges.at[1], sems.at[3]),
        ]
        for copy in copies:
            copy.start()
        wide[:, :, 0:LANES] = jnp.zeros((hc, nb, LANES), F32)
        wide[:, :, LANES + full : 2 * LANES + full] = jnp.zeros((hc, nb, LANES), F32)
        swide[:, :, 0:LANES] = jnp.zeros((nb, hs, LANES), F32)
        swide[:, :, LANES + sfull : 2 * LANES + sfull] = jnp.zeros((nb, hs, LANES), F32)
        for copy in copies:
            copy.wait()
        for d in range(groups):
            peer = lax.rem(me + d, groups)
            base = pl.multiple_of(peer * wc, LANES)
            sbase = pl.multiple_of(peer * ws, LANES)
            out = outs[d]
            out[0:hc] = wide[:, :, pl.ds(base + LANES, wc)]
            left = wide[:, :, pl.ds(base, LANES)]
            right = wide[:, :, pl.ds(base + LANES + wc, LANES)]
            borders = []
            for r in range(hc):
                borders += [left[r, :, LANES - HALO :], right[r, :, :HALO]]
            swin = swide[:, :, pl.ds(sbase, ws + 2 * LANES)]
            for q in range(hs):
                row = swin[:, q, :]
                lane = ws * (q % RATIO_S)
                out[at_swir + q // RATIO_S, :, lane : lane + ws] = row[:, LANES : LANES + ws]
                borders += [row[:, LANES - 2 : LANES], row[:, LANES + ws : LANES + ws + 2]]
            border = jnp.concatenate(borders, axis=1)
            out[at_edge, :, edge_lane : edge_lane + edge_size] = border
            for side in going(d):
                first = strip_place(d, side)
                edge = edges[1, :, LANES - REACH :] if side == "right" else edges[0, :, :REACH]
                flat = jnp.concatenate([edge[8 * t : 8 * t + 8] for t in range(h // 8)], axis=1)
                for i in range(8 // nb):
                    lane = piece * (i % per_row)
                    out[first + i // per_row, :, lane : lane + piece] = flat[nb * i : nb * (i + 1)]

    chunks = call(
        pack,
        tuple(shape(chunk_rows[d], nb, wc) for d in range(groups)),
        [
            pltpu.VMEM((hc, nb, full + 2 * LANES), F32),
            pltpu.VMEM((nb, hs, sfull + 2 * LANES), F32),
            pltpu.VMEM((2, h, LANES), F32),
            pltpu.SemaphoreType.DMA((4,)),
        ],
        cost=(0, 8_000_000),
        in_specs=[ANY] * 3,
    )(*(far(x) for x in (pan_image, jnp.transpose(vnir_bands, (1, 0, 2)), swir_bands)))
    *chunks, pan_late, table_late = lax.optimization_barrier((*chunks, pan_image, jnp.asarray(table)))
    got = [chunks[0]] + [
        lax.ppermute(chunks[d], "band", [(i, (i + d) % groups) for i in range(groups)])
        for d in range(1, groups)
    ]

    def take(ref, name, index=0, rows=None):
        starts, height, width = place[name]
        first, height = (0, height) if rows is None else (rows[0], rows[1] - rows[0])
        pieces = []
        for start, part in starts:
            base = start + first
            if not isinstance(index, int) or index:
                base = pl.multiple_of(base + index * place[name][1], 16)
            pieces.append(ref[pl.ds(base, height), 0:part])
        return pieces[0] if len(pieces) == 1 else jnp.concatenate(pieces, axis=1)

    def both_parts(ref, name, index=0, stacked=1):
        return take(ref, name, index), take(ref, name, index + stacked)

    def shrink(panes, tall, low):
        both = dot(panes[0], tall) + dot(panes[1], tall)
        return both[:, :LANES], both[:, LANES:] + dot(panes[0], low)

    def along_rows(rc, means, fines):
        both = parts2(jnp.concatenate([means, fines], axis=0))
        return dot(rc[0], both[0]) + (dot(rc[0], both[1]) + dot(rc[1], both[0]))

    def filter_rows(rf, x):
        col = parts2(x)
        return dot(rf, jnp.concatenate([col[0], col[0], col[1]], axis=0))

    def row_variant():
        row_id = lax.axis_index("rows")
        return jnp.where(row_id == 0, 1, jnp.where(row_id == strips - 1, 2, 0))

    pairs_in = [(i, i ^ 1) for i in range(strips) if i ^ 1 < strips]
    pairs_out = [(i, i + 1) for i in range(1, strips - 1, 2)]
    pairs_out += [(j, i) for i, j in pairs_out]

    def is_even():
        return lax.rem(lax.axis_index("rows"), 2) == 0

    def put(outs, index, up, down):
        even = is_even()
        outs[0][index] = jnp.where(even, up, down)
        outs[1][index] = jnp.where(even, down, up)

    def arrived(refs, index, low):
        even = is_even()
        inner, outer = refs[0][index], refs[1][index]
        return jnp.where(even, outer, inner) if low else jnp.where(even, inner, outer)

    def trade(inner, outer):
        outer = lax.ppermute(outer, "rows", pairs_out)
        return lax.ppermute(inner, "rows", pairs_in), outer

    at_up, at_down = 2 * pad, 2 * pad + 16

    def put_small(outs, first, ups, downs):
        blank = jnp.zeros((2, LANES), F32)
        for i in range(0, len(ups), 4):
            up = ups[i : i + 4] + [blank] * (4 - len(ups[i : i + 4]))
            down = downs[i : i + 4] + [blank] * (4 - len(downs[i : i + 4]))
            put(outs, first + i // 4, jnp.concatenate(up, axis=0), jnp.concatenate(down, axis=0))

    inner_fine = fine_tiles - 4

    def early(pan_far, table_far, pan_ref, table_ref, coarse_out, fine_out, col_out, sems):
        now = pl.ds(0, place["low"][0][0][0])
        later = pl.ds(now.size, table.shape[0] - now.size)
        copies = [
            pltpu.make_async_copy(pan_far, pan_ref, sems.at[0]),
            pltpu.make_async_copy(table_far.at[now], table_ref.at[now], sems.at[1]),
            pltpu.make_async_copy(table_far.at[later], table_ref.at[later], sems.at[2]),
        ]
        for copy in copies:
            copy.start()
        copies[0].wait()
        panes = parts2(pan_ref[...])
        copies[1].wait()
        starts = [margin * k - 3 * LANES for k in range(1, frame_tiles - 1)]
        means, fines = shrink(
            windows(panes, starts, 6 * LANES), take(table_ref, "tall"), take(table_ref, "tall_low")
        )
        rc = both_parts(table_ref, "rows", row_variant(), 3)
        coarse_out[...] = along_rows(rc, blocks(means, middle), blocks(fines, middle))
        starts = [2 * LANES * k - LANES for k in range(1, pairs - 1)]
        col = blocks(dot3(windows(panes, starts, 4 * LANES), both_parts(table_ref, "fine")), pairs - 2)
        col_out[...] = col
        fine_out[...] = filter_rows(take(table_ref, "rows_fine"), col)
        copies[2].wait()

    pan_held, table_held, coarse_mid, fine_mid, col_mid = call(
        early,
        (
            shape(h, w),
            jax.ShapeDtypeStruct(table.shape, BF16),
            shape(2 * pad + 32, LANES * middle),
            shape(h + 2 * HALO, LANES * inner_fine),
            shape(h, LANES * inner_fine),
        ),
        [pltpu.SemaphoreType.DMA((3,))],
        cost=(2_000_000_000, 8_000_000),
        in_specs=[ANY] * 2,
    )(far(pan_late), far(table_late))

    border_tiles = -(-edge_size // LANES)
    at_s = HALO * coarse_tiles
    at_h = at_s + 2 * swir_tiles
    at_ld = at_h + border_tiles
    at_d = at_ld + frame_tiles
    sent = at_d + -(-frame_tiles // 4)

    def framed(main, borders, lane, reach):
        blank = jnp.zeros((8, HALF - reach), F32)
        left = borders[:, lane : lane + reach]
        right = borders[:, lane + reach : lane + 2 * reach]
        return jnp.concatenate([blank, left, main, right, blank], axis=1)

    def assemble(pan_ref, table_ref, cm_ref, *rest):
        ins = rest[:groups]
        x_out, s_out, ce_out, fe_out, col_out = rest[groups : groups + 5]
        outs = rest[groups + 5 :]
        me = lax.axis_index("band")

        def gather(row, lane, size):
            rows = [ins[(groups - i) % groups][row, :, lane : lane + size] for i in range(groups)]
            return pltpu.roll(jnp.concatenate(rows, axis=0), nb * me, 0)

        def tile(x, t):
            return x[:, LANES * t : LANES * (t + 1)]

        borders = gather(at_edge, edge_lane, edge_size)
        blank = jnp.zeros((8, LANES * border_tiles - edge_size), F32)
        borders = jnp.concatenate([borders, blank], axis=1)
        for t in range(border_tiles):
            put(outs, at_h + t, tile(borders, t), tile(borders, t))
        mains = [gather(r, 0, wc) for r in range(hc)]
        for r in range(hc):
            x_out[r] = framed(mains[r], borders, 2 * HALO * r, HALO)
        for r in range(HALO):
            for t in range(coarse_tiles):
                put(outs, coarse_tiles * r + t, tile(mains[hc - HALO + r], t), tile(mains[r], t))
        shorts = [gather(at_swir + q // RATIO_S, ws * (q % RATIO_S), ws) for q in range(hs)]
        for q in range(hs):
            s_out[q] = framed(shorts[q], borders, 2 * HALO * hc + 4 * q, 2)
        for q in range(2):
            for t in range(swir_tiles):
                put(outs, at_s + swir_tiles * q + t, tile(shorts[hs - 2 + q], t), tile(shorts[q], t))

        def strip(d, side, empty):
            first = strip_place(d, side)
            rows = []
            for i in range(8 // nb):
                lane = piece * (i % per_row)
                rows.append(ins[d][first + i // per_row, :, lane : lane + piece])
            flat = jnp.where(empty, 0.0, jnp.concatenate(rows, axis=0))
            whole = [flat[:, REACH * t : REACH * (t + 1)] for t in range(h // 8)]
            return jnp.concatenate(whole, axis=0)

        blank = jnp.zeros((h, LANES - REACH), F32)
        left = jnp.concatenate([blank, strip(1, "right", me == 0), pan_ref[:, 0 : 3 * LANES]], axis=1)
        right = jnp.concatenate(
            [pan_ref[:, w - 3 * LANES : w], strip(groups - 1, "left", me == groups - 1), blank], axis=1
        )
        left, right = parts2(left), parts2(right)
        cut = 2 * LANES
        inner = (cut, 6 * LANES)
        lm, lf = shrink(left, take(table_ref, "tall", 0, inner), take(table_ref, "tall_low", 0, inner))
        inner = (0, 4 * LANES)
        rm, rfine = shrink(right, take(table_ref, "tall", 0, inner), take(table_ref, "tall_low", 0, inner))
        rc = both_parts(table_ref, "rows", row_variant(), 3)
        edge = along_rows(rc, jnp.concatenate([lm, rm], axis=1), jnp.concatenate([lf, rfine], axis=1))
        ce_out[...] = edge[0 : 2 * pad]
        outer = tuple(jnp.concatenate([a, b], axis=0) for a, b in zip(left, right))
        col = blocks(dot3(outer, both_parts(table_ref, "fine")), 2)
        col_out[...] = col
        fe_out[...] = filter_rows(take(table_ref, "rows_fine"), col)
        sides = jnp.concatenate([edge[:, :LANES], cm_ref[...], edge[:, LANES:]], axis=1)
        ups, downs = [], []
        for k in range(frame_tiles):
            part = tile(sides, k)
            put(outs, at_ld + k, part[at_up + 8 : at_up + 16], part[at_down + 8 : at_down + 16])
            ups.append(part[at_up : at_up + 2])
            downs.append(part[at_down + HALO - 2 : at_down + HALO])
        put_small(outs, at_d, ups, downs)

    x_loc, s_loc, coarse_edge, fine_edge, col_edge, rest_in, rest_out = call(
        assemble,
        (
            shape(hc, BANDS, wf),
            shape(hs, BANDS, sf),
            shape(2 * pad, 2 * LANES),
            shape(h + 2 * HALO, 4 * LANES),
            shape(h, 4 * LANES),
            shape(sent, 8, LANES),
            shape(sent, 8, LANES),
        ),
        cost=(200_000_000, 3_000_000),
        in_specs=[VMEM] * (groups + 3),
    )(pan_held, table_held, coarse_mid, *got)
    rest_in, rest_out = trade(rest_in, rest_out)

    turns = BANDS // 2 + 1
    block_starts = [LANES * k for k in range(coarse_tiles)]
    own_rows = range(2, hc + 2)
    halo_rows = (0, 1, hc + 2, hc + 3)
    around = (-2, -1) + halo_rows + (hc + 4, hc + 5)

    def lifted(rows, table_ref, store):
        stack = windows(parts2(jnp.concatenate(rows, axis=0)), block_starts, 2 * LANES)
        up = dot3(stack, both_parts(table_ref, "up4"))
        size = 8 * len(rows)
        for k in range(coarse_tiles):
            for q in range(RATIO_V):
                store(RATIO_V * k + q, up[size * k : size * (k + 1), LANES * q : LANES * (q + 1)])

    def grouped(step, size):
        def body(k, carry):
            for i in range(size):
                carry = step(size * k + i, carry)
            return carry

        return body

    def weighted(pairs):
        value = None
        for weight, x in pairs:
            if weight != 0.0:
                value = float(weight) * x if value is None else value + float(weight) * x
        return value

    def adjoint_of(table_ref, col):
        p1 = col.astype(BF16)
        over = col - p1.astype(F32)
        p2 = over.astype(BF16)
        p3 = (over - p2.astype(F32)).astype(BF16)
        weights = take(table_ref, "adjoint", row_variant())
        return dot(weights, jnp.concatenate([p1, p2, p3, p1, p2, p1], axis=0))

    def inside(
        pan_ref, x_ref, s_ref, fm_ref, fe_ref, colm_ref, cole_ref, table_ref,
        y_out, v_out, acc_out, s_out, diff_out, q_out, edge_out, mean_out, lows_out, *outs,
    ):
        def store(index, value):
            y_out[index] = value

        lifted([x_ref[r] for r in range(hc)], table_ref, store)
        rows = parts2(jnp.concatenate([s_ref[q] for q in range(hs)], axis=0))
        s_cols = dot3(windows(rows, block_starts[:swir_tiles], 2 * LANES), both_parts(table_ref, "up3"))
        s_out[...] = blocks(s_cols, swir_tiles)

        def joined(outer, inner):
            return jnp.concatenate([outer[:, : 2 * LANES], inner, outer[:, 2 * LANES :]], axis=1)

        low = joined(fe_ref[...], fm_ref[...])
        diff = pan_ref[...] - low[0:h]
        adjoint = adjoint_of(table_ref, joined(cole_ref[...], colm_ref[...]))
        total = jnp.zeros((1, LANES), F32)
        for k in range(fine_tiles):
            at = slice(LANES * k, LANES * (k + 1))
            diff_out[k] = diff[:, at]
            q_out[k] = adjoint[:, at]
            total = total + adjoint[hc + 8 : hc + 9, at]
            put(outs, k, low[h : h + HALO, at], low[h + HALO : h + 2 * HALO, at])

        row_id = lax.axis_index("rows")
        below = jnp.where(row_id > 0, 1.0, 0.0).astype(F32)
        above = jnp.where(row_id < strips - 1, 1.0, 0.0).astype(F32)
        means = {}
        for r in range(-2, hc + 2):
            value = weighted((MEAN4[t + 2], x_ref[r + t]) for t in range(-2, 3) if 0 <= r + t < hc)
            means[r] = value * below if r < 0 else (value * above if r >= hc else value)
        for i, r in enumerate((0, 1, hc - 2, hc - 1)):
            edge_out[i] = means[r]
        rows = parts2(jnp.concatenate([means[r] for r in range(2, hc - 2)], axis=0))
        pair = tuple(x[:, :LANES] for x in both_parts(table_ref, "pair", 0, 3))
        mean_out[...] = blocks(dot3(windows(rows, block_starts, 2 * LANES), pair), coarse_tiles)
        reach = TAPS_S // 2
        for r in range(hc):
            lows_out[r] = weighted((KC[t + reach], means[r + t]) for t in range(-reach, reach + 1) if r + t in means)
        acc_out[turns + 2] = jnp.concatenate([total, jnp.zeros((7, LANES), F32)], axis=0)

        def tile_step(k, carry):
            accs, accv, accp = list(carry[:turns]), carry[turns], carry[turns + 1]
            ys = {m: y_out[k, pl.ds(8 * (m - 2), 8), :] for m in own_rows}
            for m in own_rows:
                z = weighted((gram[m, other], ys[other]) for other in own_rows)
                accs[0] = accs[0] + z * ys[m]
                for i in range(1, turns):
                    accs[i] = accs[i] + z * pltpu.roll(ys[m], i, 0)
                accv = accv + float(rise[m]) * ys[m]
                accp = accp + ys[m] * q_out[k, pl.ds(m + 2, 1), :]
            for m in range(hc):
                for p in range(RATIO_V):
                    r = RATIO_V * m + p
                    v_out[k, pl.ds(8 * r, 8), :] = weighted((C4[t, p], ys[m + t]) for t in range(5) if m + t in ys)
            return tuple(accs) + (accv, accp)

        zero = jnp.zeros((8, LANES), F32)
        first = lax.fori_loop(0, fine_tiles // 2, grouped(tile_step, 2), (zero,) * (turns + 2))
        for i in range(turns + 2):
            acc_out[i] = first[i]

    q_rows = -(-(hc + 9) // 16) * 16
    y_own, v_own, acc_own, s_own, diff, q_own, mean_edge, mean_own, lows_own, low_in, low_out = call(
        inside,
        (
            shape(fine_tiles, 8 * hc, LANES),
            shape(fine_tiles, 8 * h, LANES),
            shape(turns + 3, 8, LANES),
            shape(8 * hs, wc),
            shape(fine_tiles, h, LANES),
            shape(fine_tiles, q_rows, LANES),
            shape(4, BANDS, wf),
            shape(8 * (hc - 4), wc),
            shape(hc, BANDS, wf),
            shape(fine_tiles, 8, LANES),
            shape(fine_tiles, 8, LANES),
        ),
        cost=(2_000_000_000, 8_000_000),
    )(pan_held, x_loc, s_loc, fine_mid, fine_edge, col_mid, col_edge, table_held)
    low_in, low_out = trade(low_in, low_out)

    def moments(
        x_ref, y_ref, acc_ref, scol_ref, q_ref, edge_ref, mean_ref, lows_ref,
        rest_in_ref, rest_out_ref, cm_ref, ce_ref, table_ref,
        mom_out, y_out, ugap_out, dgap_out, s_out,
        both, ulow,
    ):
        me = lax.axis_index("band")
        rest = (rest_in_ref, rest_out_ref)

        def tiles(refs, low, indices):
            return jnp.concatenate([arrived(refs, i, low) for i in indices], axis=1)

        def halo(first, per, reach, start, count):
            sides = []
            for low, base in ((True, start[0]), (False, start[1])):
                borders = tiles(rest, low, range(at_h, at_h + border_tiles))
                rows = []
                for r in range(count):
                    main = tiles(rest, low, range(first + per * r, first + per * (r + 1)))
                    rows.append(framed(main, borders, base + 2 * reach * r, reach))
                sides.append(rows)
            return sides

        x_low, x_high = halo(0, coarse_tiles, HALO, (2 * HALO * (hc - HALO), 0), HALO)

        def x_row(r):
            if r < 0:
                return x_low[HALO + r]
            if r >= hc:
                return x_high[r - hc]
            return x_ref[r]

        def store(index, value):
            y_out[index] = value

        lifted([x_row(m - 2) for m in around], table_ref, store)

        zero = jnp.zeros((8, LANES), F32)

        def tile_step(k, carry):
            accs = list(carry[:turns])
            accp, accv = carry[turns], carry[turns + 1]
            ys = {m: y_ref[k, pl.ds(8 * (m - 2), 8), :] for m in own_rows}
            for i, m in enumerate(around):
                ys[m] = y_out[k, pl.ds(8 * i, 8), :]
            for m in halo_rows:
                near = weighted((gram[m, other], ys[other]) for other in own_rows)
                whole = near + weighted((gram[m, other], ys[other]) for other in halo_rows)
                accs[0] = accs[0] + ys[m] * (near + whole)
                for i in range(1, turns):
                    accs[i] = accs[i] + whole * pltpu.roll(ys[m], i, 0) + ys[m] * pltpu.roll(near, i, 0)
                accv = accv + float(rise[m]) * ys[m]
            for m in around:
                accp = accp + ys[m] * q_ref[k, pl.ds(m + 2, 1), :]
            return tuple(accs) + (accp, accv)

        start = tuple(acc_ref[i] for i in range(turns)) + (acc_ref[turns + 1], acc_ref[turns])
        first = lax.fori_loop(0, fine_tiles // 2, grouped(tile_step, 2), start)

        beyond = [r for r in range(-HALO, hc + HALO) if not 0 <= r < hc]
        edges = []
        for i, r in enumerate((0, 1, hc - 2, hc - 1)):
            more = weighted((MEAN4[a - r + 2], x_row(a)) for a in beyond if abs(a - r) <= 2)
            edges.append(edge_ref[i] + more)
        lows = []
        for r in range(hc):
            more = weighted((WIDE[a - r + HALO], x_row(a)) for a in beyond if abs(a - r) <= HALO)
            lows.append(lows_ref[r] + more)
        u_rows = windows(parts2(jnp.concatenate(edges, axis=0)), block_starts, 2 * LANES)
        l_rows = windows(parts2(jnp.concatenate(lows, axis=0)), block_starts, 2 * LANES)
        u_edge = dot3(u_rows, tuple(x[:, :LANES] for x in both_parts(table_ref, "pair", 0, 3)))
        left = jnp.where(me == 0, 1, 0)
        right = jnp.where(me == groups - 1, 2, 0)
        size = 8 * hc
        last = coarse_tiles - 1
        for which, lo_k, hi_k in ((left, 0, 1), (0, 1, last), (right, last, last + 1)):
            if hi_k <= lo_k:
                continue
            wp = tuple(x[:, LANES:] for x in both_parts(table_ref, "pair", which, 3))
            part = dot3(tuple(x[size * lo_k : size * hi_k] for x in l_rows), wp)
            for k in range(lo_k, hi_k):
                at = slice(LANES * k, LANES * (k + 1))
                low_k = part[size * (k - lo_k) : size * (k - lo_k + 1)]
                ulow[:, at] = low_k
                around_k = u_edge[32 * k : 32 * (k + 1)]
                u_k = jnp.concatenate([around_k[0:16], mean_ref[:, at], around_k[16:32]], axis=0)
                ugap_out[:, at] = u_k - low_k

        column = lax.broadcasted_iota(jnp.int32, (1, wf), 1) - HALF + me * wc
        valid = jnp.where((column >= 0) & (column < groups * wc), 1.0, 0.0).astype(F32)

        def own(rows):
            return jnp.concatenate([ce_ref[rows, 0:LANES], cm_ref[rows, :], ce_ref[rows, LANES:]], axis=1)

        def small(low):
            rows = [arrived(rest, at_d + k // 4, low)[2 * (k % 4) : 2 * (k % 4) + 2] for k in range(frame_tiles)]
            return jnp.concatenate(rows, axis=1)

        both[...] = own(slice(0, pad))
        both[0:2] = both[0:2] + small(True)
        both[hc - 2 : hc] = both[hc - 2 : hc] + small(False)
        detail = both[...]
        both[...] = own(slice(pad, 2 * pad))
        both[0:HALO] = both[0:HALO] + tiles(rest, True, range(at_ld, at_ld + frame_tiles))
        both[hc - HALO : hc] = both[hc - HALO : hc] + tiles(rest, False, range(at_ld, at_ld + frame_tiles))
        dlow_rows = windows(parts2(both[...] * valid), block_starts, 2 * LANES)
        dlow = blocks(dot3(dlow_rows, both_parts(table_ref, "low")), coarse_tiles)
        dgap_out[...] = detail[:, HALF : HALF + wc] - dlow
        both[:, 0:wc] = dlow

        s_low, s_high = halo(at_s, swir_tiles, 2, (2 * HALO * hc + 4 * (hs - 2), 2 * HALO * hc), 2)
        s_parts = windows(parts2(jnp.concatenate(s_low + s_high, axis=0)), block_starts[:swir_tiles], 2 * LANES)
        s_around = blocks(dot3(s_parts, both_parts(table_ref, "up3")), swir_tiles)
        s_cols = jnp.concatenate([s_around[0:16], scol_ref[...], s_around[16:32]], axis=0)
        for m in range(hs):
            for p in range(RATIO_S):
                value = None
                for t in range(5):
                    if C3[t, p] != 0.0:
                        term = float(C3[t, p]) * s_cols[8 * (m + t) : 8 * (m + t) + 8]
                        value = term if value is None else value + term
                s_out[RATIO_S * m + p] = value

        ll = [zero] * turns
        cross = [zero] * BANDS
        ld = ls = sd = ss = dd = ds = zero
        for r in range(hc):
            for k in range(coarse_tiles):
                at = slice(LANES * k, LANES * (k + 1))
                u = ulow[8 * r : 8 * r + 8, at]
                s = s_out[r, :, at]
                dl = jnp.broadcast_to(both[r : r + 1, at], (8, LANES))
                ll[0] = ll[0] + u * u
                for i in range(1, turns):
                    ll[i] = ll[i] + u * pltpu.roll(u, i, 0)
                for i in range(BANDS):
                    cross[i] = cross[i] + u * s_out[r, i : i + 1, at]
                ld = ld + u * dl
                sd = sd + s * dl
                ls = ls + u
                ss = ss + s
                dd = dd + dl * dl
                ds = ds + dl

        lane = lax.broadcasted_iota(jnp.int32, (8, LANES), 1)
        sub = lax.broadcasted_iota(jnp.int32, (8, LANES), 0)

        def column_of(acc):
            return jnp.broadcast_to(jnp.sum(acc, axis=1, keepdims=True), (8, LANES))

        table = zero
        for base, accs in ((0, ll), (32, first[:turns])):
            for i in range(turns):
                col = column_of(accs[i])
                table = jnp.where(lane == base + lax.rem(sub + BANDS - i, BANDS), col, table)
                if 0 < i < BANDS // 2:
                    turned = pltpu.roll(col, BANDS - i, 0)
                    table = jnp.where(lane == base + lax.rem(sub + i, BANDS), turned, table)
        singles = [(8 + i, cross[i]) for i in range(BANDS)]
        singles += [(16, ld), (17, ls), (18, sd), (19, ss), (20, dd), (21, ds)]
        singles += [(40, first[turns]), (41, first[turns + 1])]
        for index, acc in singles:
            table = jnp.where(lane == index, column_of(acc), table)
        total = jnp.sum(jnp.sum(acc_ref[turns + 2], axis=0, keepdims=True), axis=1, keepdims=True)
        table = jnp.where(lane == 43, total, table)
        turned = pltpu.roll(table, HALF, 1)
        mom_out[...] = jnp.where(lane[0:4] < HALF, table[0:4], turned[4:8])

    mom, y_halo, ugap, dgap, s_up = call(
        moments,
        (
            shape(4, LANES),
            shape(fine_tiles, 8 * len(around), LANES),
            shape(8 * hc, wc),
            shape(pad, wc),
            shape(hc, BANDS, wc),
        ),
        [
            pltpu.VMEM((pad, wf), F32),
            pltpu.VMEM((8 * hc, wc), F32),
        ],
        cost=(1_000_000_000, 8_000_000),
    )(
        x_loc, y_own, acc_own, s_own, q_own, mean_edge, mean_own, lows_own,
        rest_in, rest_out, coarse_mid, coarse_edge, table_held,
    )
    devices = groups * strips
    mom, low_in, low_out = lax.optimization_barrier((mom, low_in, low_out))
    spread = jnp.broadcast_to(mom[None], (devices,) + mom.shape)
    sums = lax.all_to_all(spread, ("rows", "band"), split_axis=0, concat_axis=0, tiled=True)

    apart_rows = h + 8

    def finish(
        sums_ref, yh_ref, v_ref, diff_ref, low_in_ref, low_out_ref, ugap_ref, dgap_ref, s_ref,
        vnir_out, swir_out, tiles, swir, ends, sems,
    ):
        lane = lax.broadcasted_iota(jnp.int32, (8, LANES), 1)
        sub = lax.broadcasted_iota(jnp.int32, (8, LANES), 0)
        eye = lane == sub
        terms = [sums_ref[index] for index in range(devices)]
        while len(terms) > 1:
            terms = [sum(terms[i : i + 2][1:], terms[i]) for i in range(0, len(terms), 2)]
        total = jnp.concatenate([terms[0], pltpu.roll(terms[0], HALF, 1)], axis=0)

        def column(x, index):
            return jnp.broadcast_to(x[:, index : index + 1], (8, LANES))

        def across(col):
            return jnp.sum(jnp.where(eye, col, 0.0), axis=0, keepdims=True)

        def down(x):
            return jnp.sum(x, axis=0, keepdims=True)

        def solve(matrix, rhs):
            cols = [column(matrix, j) for j in range(BANDS)] + [rhs]
            inverse = jnp.zeros((8, LANES), F32)
            for k in range(BANDS):
                pivot = 1.0 / jnp.broadcast_to(cols[k][k : k + 1], (8, LANES))
                inverse = jnp.where(sub == k, pivot, inverse)
                factor = jnp.where(sub == k, 0.0, cols[k] * pivot)
                for j in range(k + 1, BANDS + 1):
                    cols[j] = cols[j] - factor * jnp.broadcast_to(cols[j][k : k + 1], (8, LANES))
            return cols[BANDS] * inverse

        n1 = float(fine_pixels)
        mean_v = column(total, 41) / n1
        mean_p = column(total, 43) / n1
        cov_v = pltpu.roll(total, LANES - 32, 1) / n1 - mean_v * across(mean_v)
        cov_p = column(total, 40) / n1 - mean_v * mean_p
        gain = cov_p / down(cov_p * solve(cov_v, cov_p))

        n2 = float(fine_pixels // (RATIO_V * RATIO_V))
        mean_l = column(total, 17) / n2
        mean_s = column(total, 19) / n2
        mean_d = column(total, 21) / n2
        cov_ll = total / n2 - mean_l * across(mean_l)
        cov_ls = pltpu.roll(total, LANES - 8, 1) / n2 - mean_l * across(mean_s)
        cov_ld = column(total, 16) / n2 - mean_l * mean_d
        cov_sd = column(total, 18) / n2 - mean_s * mean_d
        cov_dd = column(total, 20) / n2 - mean_d * mean_d
        gain_row = across(gain)
        a2 = cov_ll + gain * across(cov_ld) + cov_ld * gain_row + gain * gain_row * cov_dd
        b2 = jnp.where(lane < BANDS, cov_ls + gain * across(cov_sd), 0.0)
        target = jnp.broadcast_to(jnp.sum(b2, axis=1, keepdims=True) / BANDS, (8, LANES))

        def sent_tile(k):
            lanes = pl.ds(pl.multiple_of(LANES * k, LANES), LANES)
            held = tiles.reshape(fine_tiles, BANDS, apart_rows, LANES).at[k, :, pl.ds(0, h), :]
            return pltpu.make_async_copy(held, vnir_out.at[:, :, lanes], sems.at[k])

        def tile_step(k, carry):
            ys = {m: yh_ref[k, pl.ds(8 * i, 8), :] for i, m in enumerate(around) if m in halo_rows}
            lows = (low_in_ref, low_out_ref)
            ends[k, 0:HALO, :] = diff_ref[k, 0:HALO, :] - arrived(lows, k, True)
            ends[k, HALO:, :] = diff_ref[k, h - HALO :, :] - arrived(lows, k, False)
            for m in range(hc):
                for p in range(RATIO_V):
                    r = RATIO_V * m + p
                    value = v_ref[k, pl.ds(8 * r, 8), :]
                    more = weighted((C4[t, p], ys[m + t]) for t in range(5) if m + t in ys)
                    if more is not None:
                        value = value + more
                    if r < HALO:
                        detail = ends[k, pl.ds(r, 1), :]
                    elif r >= h - HALO:
                        detail = ends[k, pl.ds(r - h + 2 * HALO, 1), :]
                    else:
                        detail = diff_ref[k, pl.ds(r, 1), :]
                    value = value + gain * detail
                    tiles[k, pl.ds(r, 8, stride=apart_rows), :] = value
            sent_tile(k).start()
            return carry

        beside = fine_tiles // BANDS

        def solve_step(k, carry):
            work, inverse = carry
            here = sub == k
            row = down(jnp.where(here, work, 0.0))
            col = jnp.sum(jnp.where(lane == k, work, 0.0), axis=1, keepdims=True)
            pivot = 1.0 / down(jnp.where(here[:, 0:1], col, 0.0))
            inverse = jnp.where(here, pivot, inverse)
            work = work - jnp.where(here, 0.0, col * pivot) * row

            for i in range(beside):
                tile_step(beside * k + i, 0)
            return work, inverse

        start = (jnp.where(lane == BANDS, target, a2), jnp.zeros((8, LANES), F32))
        work, inverse = lax.fori_loop(0, BANDS, solve_step, start)
        lax.fori_loop(BANDS * beside, fine_tiles, tile_step, 0)
        fit2 = column(work, BANDS) * inverse
        numer = down(fit2 * b2)
        share_row = numer / down(fit2 * target)
        share = jnp.sum(jnp.where(eye, jnp.broadcast_to(share_row, (8, LANES)), 0.0), axis=1, keepdims=True)
        scale = down(fit2 * gain)[:, 0:1]
        fit_col = fit2[:, 0:1]
        for r in range(hc):
            seen = jnp.sum(fit_col * ugap_ref[8 * r : 8 * r + 8, :], axis=0, keepdims=True)
            seen = seen + scale * dgap_ref[r : r + 1, :]
            swir[r] = s_ref[r] + share * seen
        last = pltpu.make_async_copy(swir, swir_out, sems.at[fine_tiles])
        last.start()

        def drain(k, carry):
            sent_tile(k).wait()
            return carry

        lax.fori_loop(0, fine_tiles, drain, 0)
        last.wait()

    joined_vnir, joined_swir = call(
        finish,
        (shape(BANDS, h, w), shape(hc, BANDS, wc)),
        [
            pltpu.VMEM((fine_tiles, BANDS * apart_rows, LANES), F32),
            pltpu.VMEM((hc, BANDS, wc), F32),
            pltpu.VMEM((fine_tiles, 2 * HALO, LANES), F32),
            pltpu.SemaphoreType.DMA((fine_tiles + 1,)),
        ],
        cost=(100_000_000, 8_000_000),
        out_specs=(ANY, ANY),
    )(sums, y_halo, v_own, diff, low_in, low_out, ugap, dgap, s_up)
    return joined_vnir, jnp.transpose(joined_swir, (1, 0, 2))


def solution(mesh):
    return jax.shard_map(
        local,
        mesh=mesh,
        in_specs=(P("rows", "band"), P("band", "rows", None), P("band", "rows", None)),
        out_specs=(P(None, "rows", "band"), P(None, "rows", "band")),
        check_vma=False,
    )
```

```python
import math

import jax
import jax.numpy as jnp
import ml_dtypes
import numpy as np
from jax import lax
from jax.experimental import pallas as pl
from jax.experimental.pallas import tpu as pltpu
from jax.sharding import PartitionSpec as P

BANDS = 8
RATIO_V = 4
RATIO_S = 3
TAPS_V = 17
TAPS_S = 13
NYQUIST_GAIN = 0.29
LANES = 128
HALF = 64
REACH = 32
HALO = 8
F32 = jnp.float32
BF16 = jnp.bfloat16
VMEM_BYTES = 24 * 1024 * 1024
VMEM_MOST = 56 * 1024 * 1024


def gauss_taps(upscale, kernel_len):
    spread = upscale * math.sqrt(-2.0 * math.log(NYQUIST_GAIN)) / math.pi
    radius = kernel_len // 2
    offsets = np.arange(-radius, radius + 1) * 1.0
    values = np.exp(-(offsets**2) / (2.0 * spread**2))
    return values / values.sum()


def cubic_weight(distance):
    distance = abs(distance)
    if distance <= 1.0:
        return 1.5 * distance**3 - 2.5 * distance**2 + 1.0
    if distance < 2.0:
        return -0.5 * distance**3 + 2.5 * distance**2 - 4.0 * distance + 2.0
    return 0.0


def cubic_table(upscale):
    weights = np.zeros((5, upscale))
    for phase_index in range(upscale):
        centre = (phase_index + 0.5) / upscale - 0.5
        first_tap = math.floor(centre)
        fraction = centre - first_tap
        for tap_index in range(-1, 3):
            weights[first_tap + tap_index + 2, phase_index] += cubic_weight(tap_index - fraction)
    return weights


KF = gauss_taps(RATIO_V, TAPS_V)
KC = gauss_taps(RATIO_S, TAPS_S)
C4 = cubic_table(RATIO_V)
C3 = cubic_table(RATIO_S)
MEAN4 = C4.mean(axis=1)
WIDE = np.convolve(KC, MEAN4)


def split(table):
    high = np.asarray(table, np.float64).astype(np.float32).astype(ml_dtypes.bfloat16)
    low = (np.asarray(table, np.float64) - high.astype(np.float64)).astype(np.float32)
    return np.stack([high, low.astype(ml_dtypes.bfloat16)])


def split3(table):
    high, middle = split(table)
    low = np.asarray(table, np.float64) - high.astype(np.float64) - middle.astype(np.float64)
    return high, middle, low.astype(np.float32).astype(ml_dtypes.bfloat16)


def band_matrix(size, taps):
    radius = len(taps) // 2
    out = np.zeros((size, size))
    for row in range(size):
        for tap in range(-radius, radius + 1):
            if 0 <= row + tap < size:
                out[row, row + tap] = taps[tap + radius]
    return out


def row_tables(h):
    hc = h // RATIO_V
    mean = np.zeros((3 * hc, 3 * h))
    for row in range(3 * hc):
        mean[row, RATIO_V * row : RATIO_V * (row + 1)] = 1.0 / RATIO_V
    fine = band_matrix(3 * h, KF)
    low = band_matrix(3 * hc, KC)
    mean_fine = mean @ fine
    pad = -(-hc // 8) * 8

    def part(matrix, rows, cols):
        return matrix[rows, :][:, cols]

    def stacked(rows, cols, filt):
        a = mean if filt is None else filt @ mean
        c = mean_fine if filt is None else filt @ mean_fine
        return np.concatenate([part(a, rows, cols), -part(c, rows, cols)], axis=1)

    own = slice(h, 2 * h)
    tables = []
    for variant in range(3):
        keep = np.ones(3 * hc)
        if variant == 1:
            keep[:hc] = 0.0
        if variant == 2:
            keep[2 * hc :] = 0.0
        masked = low * keep[None, :]
        rows = []
        for filt in (None, masked):
            block = np.zeros((pad, 2 * h))
            block[:hc] = stacked(slice(hc, 2 * hc), own, filt)
            rows.append(block)
        for filt in (None, low):
            rows.append(stacked(slice(hc, hc + HALO), slice(0, h), filt))
        for filt in (None, low):
            rows.append(stacked(slice(2 * hc - HALO, 2 * hc), slice(2 * h, 3 * h), filt))
        tables.append(np.concatenate(rows, axis=0))
    coarse_rows = np.stack(tables)
    fine_rows = np.concatenate(
        [fine[h : 2 * h, h : 2 * h], fine[h : h + HALO, 0:h], fine[2 * h - HALO : 2 * h, 2 * h : 3 * h]],
        axis=0,
    )
    return coarse_rows, fine_rows


def up_rows(hc):
    out = np.zeros((RATIO_V * hc, hc + 4))
    for m in range(hc):
        for p in range(RATIO_V):
            out[RATIO_V * m + p, m : m + 5] = C4[:, p]
    return out


def adjoint_rows(h):
    hc = h // RATIO_V
    reach = TAPS_V // 2
    size = h + 2 * reach
    lift = np.zeros((size, hc + 8))
    for r in range(size):
        m, p = divmod(r - reach, RATIO_V)
        lift[r, m + 2 : m + 7] = C4[:, p]
    fine = np.zeros((size, h))
    for r in range(size):
        for t in range(-reach, reach + 1):
            if 0 <= r - reach + t < h:
                fine[r, r - reach + t] = KF[t + reach]
    out = np.zeros((3, -(-(hc + 9) // 16) * 16, h))
    for variant in range(3):
        keep = np.ones((size, 1))
        if variant == 1:
            keep[:reach] = 0.0
        if variant == 2:
            keep[h + reach :] = 0.0
        out[variant, : hc + 8] = (lift * keep).T @ fine
        out[variant, hc + 8] = (fine * keep).sum(axis=0)
    return out


def column_tables():
    n = LANES
    fine = np.zeros((4 * n, 2 * n))
    mean = np.zeros((6 * n, n))
    mean_fine = np.zeros((6 * n, n))
    low = np.zeros((2 * n, n))
    pair = np.zeros((3, 2 * n, 2 * n))
    up4 = np.zeros((2 * n, RATIO_V * n))
    up3 = np.zeros((2 * n, RATIO_S * n))
    for c in range(2 * n):
        for t in range(-(TAPS_V // 2), TAPS_V // 2 + 1):
            fine[n + c + t, c] += KF[t + TAPS_V // 2]
    for c in range(n):
        for q in range(RATIO_V):
            mean[n + RATIO_V * c + q, c] = 1.0 / RATIO_V
            for t in range(-(TAPS_V // 2), TAPS_V // 2 + 1):
                mean_fine[n + RATIO_V * c + q + t, c] += KF[t + TAPS_V // 2] / RATIO_V
        for t in range(-(TAPS_S // 2), TAPS_S // 2 + 1):
            low[c + HALF + t, c] += KC[t + TAPS_S // 2]
            for s in range(-2, 3):
                value = KC[t + TAPS_S // 2] * MEAN4[s + 2]
                pair[0, c + HALF + t + s, n + c] += value
                if c + t >= 0:
                    pair[1, c + HALF + t + s, n + c] += value
                if c + t < n:
                    pair[2, c + HALF + t + s, n + c] += value
        for s in range(-2, 3):
            pair[:, c + HALF + s, c] += MEAN4[s + 2]
            for p in range(RATIO_V):
                up4[c + HALF + s, RATIO_V * c + p] += C4[s + 2, p]
            for p in range(RATIO_S):
                up3[c + HALF + s, RATIO_S * c + p] += C3[s + 2, p]
    return dict(fine=fine, mean=mean, mean_fine=mean_fine, low=low, pair=pair, up4=up4, up3=up3)


def stack_tables(tables):
    wide = 2 * LANES
    pieces, place, top = [], {}, 0
    for name, value in tables.items():
        stack = value.reshape((-1,) + value.shape[-2:])
        height, width = stack.shape[1:]
        starts = []
        for lane in range(0, width, wide):
            part = stack[:, :, lane : lane + wide]
            starts.append((top, part.shape[2]))
            piece = np.zeros((stack.shape[0] * height, wide), ml_dtypes.bfloat16)
            piece[:, : part.shape[2]] = part.reshape(-1, part.shape[2])
            pieces.append(piece)
            top += piece.shape[0]
        place[name] = (starts, height, width)
    return np.concatenate(pieces, axis=0), place


def parts2(x):
    high = x.astype(BF16)
    return high, (x - high.astype(F32)).astype(BF16)


def dot(a, b):
    return jnp.dot(a, b, preferred_element_type=F32)


def dot3(x, w):
    return dot(x[0], w[0]) + (dot(x[1], w[0]) + dot(x[0], w[1]))


def windows(x, starts, size):
    return tuple(jnp.concatenate([part[:, a : a + size] for a in starts], axis=0) for part in x)


def blocks(x, count):
    rows = x.shape[0] // count
    return jnp.concatenate([x[rows * k : rows * (k + 1)] for k in range(count)], axis=1)


def call(kernel, out_shape, scratch=(), cost=(0, 0), room=VMEM_BYTES, **specs):
    return pl.pallas_call(
        kernel,
        out_shape=out_shape,
        scratch_shapes=list(scratch),
        compiler_params=pltpu.CompilerParams(vmem_limit_bytes=room),
        cost_estimate=pl.CostEstimate(flops=cost[0], bytes_accessed=cost[1], transcendentals=0),
        **specs,
    )


ANY = pl.BlockSpec(memory_space=pl.ANY)
VMEM = pl.BlockSpec(memory_space=pltpu.VMEM)


def local(pan_image, vnir_bands, swir_bands):
    groups = lax.axis_size("band")
    strips = lax.axis_size("rows")
    h, w = pan_image.shape
    nb, hc, full = vnir_bands.shape
    _, hs, sfull = swir_bands.shape
    wc = w // RATIO_V
    ws = wc // RATIO_S
    wf = wc + LANES
    sf = ws + LANES
    pad = -(-hc // 8) * 8
    fine_tiles = w // LANES
    coarse_tiles = wc // LANES
    frame_tiles = coarse_tiles + 1
    swir_tiles = ws // LANES
    fine_pixels = h * strips * w * groups
    pairs = w // (2 * LANES)
    middle = frame_tiles - 2
    margin = RATIO_V * LANES

    def shape(*dims):
        return jax.ShapeDtypeStruct(dims, F32)

    coarse_rows, fine_rows = row_tables(h)
    cols = column_tables()
    lift = up_rows(hc)
    gram = lift.T @ lift
    rise = lift.sum(axis=0)

    swir_rows = -(-hs // RATIO_S)
    at_swir = hc
    edge_size = 2 * HALO * hc + 4 * hs
    edge_lane = ws * (hs % RATIO_S)
    shared = hs % RATIO_S and edge_lane + edge_size <= wc
    at_edge = hc + swir_rows - 1 if shared else hc + swir_rows
    edge_lane = edge_lane if shared else 0
    at_strip = at_edge + 1
    piece = REACH * (h // 8)
    per_row = wc // piece
    strip_rows = -(-(8 // nb) // per_row)

    def going(d):
        return (["right"] if d == 1 else []) + (["left"] if d == groups - 1 else [])

    def strip_place(d, side):
        return at_strip + strip_rows * going(d).index(side)

    chunk_rows = [at_strip + strip_rows * len(going(d)) for d in range(groups)]

    mean_parts, fine_parts = split(cols["mean"]), split(cols["mean_fine"])
    r_fine = split(fine_rows)
    r_adj = split3(adjoint_rows(h))
    table, place = stack_tables(
        dict(
            tall=np.concatenate([mean_parts[0], fine_parts[0]], axis=1),
            tall_low=fine_parts[1],
            fine=split(cols["fine"]),
            rows=split(coarse_rows),
            rows_fine=np.concatenate([r_fine[0], r_fine[1], r_fine[0]], axis=1),
            low=split(cols["low"]),
            pair=split(cols["pair"]),
            up4=split(cols["up4"]),
            up3=split(cols["up3"]),
            adjoint=np.concatenate([r_adj[i] for i in (0, 0, 0, 1, 1, 2)], axis=2),
        )
    )

    def far(x):
        return pltpu.with_memory_space_constraint(x, pltpu.HBM)

    def pack(pan_ref, vnir_ref, swir_ref, *rest):
        outs, (wide, swide, edges, sems) = rest[:groups], rest[groups:]
        me = lax.axis_index("band")
        copies = [
            pltpu.make_async_copy(vnir_ref, wide.at[:, :, pl.ds(LANES, full)], sems.at[0]),
            pltpu.make_async_copy(swir_ref, swide.at[:, :, pl.ds(LANES, sfull)], sems.at[1]),
            pltpu.make_async_copy(pan_ref.at[:, pl.ds(0, LANES)], edges.at[0], sems.at[2]),
            pltpu.make_async_copy(pan_ref.at[:, pl.ds(w - LANES, LANES)], edges.at[1], sems.at[3]),
        ]
        for copy in copies:
            copy.start()
        wide[:, :, 0:LANES] = jnp.zeros((hc, nb, LANES), F32)
        wide[:, :, LANES + full : 2 * LANES + full] = jnp.zeros((hc, nb, LANES), F32)
        swide[:, :, 0:LANES] = jnp.zeros((nb, hs, LANES), F32)
        swide[:, :, LANES + sfull : 2 * LANES + sfull] = jnp.zeros((nb, hs, LANES), F32)
        for copy in copies:
            copy.wait()
        for d in range(groups):
            peer = lax.rem(me + d, groups)
            base = pl.multiple_of(peer * wc, LANES)
            sbase = pl.multiple_of(peer * ws, LANES)
            out = outs[d]
            out[0:hc] = wide[:, :, pl.ds(base + LANES, wc)]
            left = wide[:, :, pl.ds(base, LANES)]
            right = wide[:, :, pl.ds(base + LANES + wc, LANES)]
            borders = []
            for r in range(hc):
                borders += [left[r, :, LANES - HALO :], right[r, :, :HALO]]
            swin = swide[:, :, pl.ds(sbase, ws + 2 * LANES)]
            for q in range(hs):
                row = swin[:, q, :]
                lane = ws * (q % RATIO_S)
                out[at_swir + q // RATIO_S, :, lane : lane + ws] = row[:, LANES : LANES + ws]
                borders += [row[:, LANES - 2 : LANES], row[:, LANES + ws : LANES + ws + 2]]
            border = jnp.concatenate(borders, axis=1)
            out[at_edge, :, edge_lane : edge_lane + edge_size] = border
            for side in going(d):
                first = strip_place(d, side)
                edge = edges[1, :, LANES - REACH :] if side == "right" else edges[0, :, :REACH]
                flat = jnp.concatenate([edge[8 * t : 8 * t + 8] for t in range(h // 8)], axis=1)
                for i in range(8 // nb):
                    lane = piece * (i % per_row)
                    out[first + i // per_row, :, lane : lane + piece] = flat[nb * i : nb * (i + 1)]

    chunks = call(
        pack,
        tuple(shape(chunk_rows[d], nb, wc) for d in range(groups)),
        [
            pltpu.VMEM((hc, nb, full + 2 * LANES), F32),
            pltpu.VMEM((nb, hs, sfull + 2 * LANES), F32),
            pltpu.VMEM((2, h, LANES), F32),
            pltpu.SemaphoreType.DMA((4,)),
        ],
        cost=(0, 8_000_000),
        in_specs=[ANY] * 3,
    )(*(far(x) for x in (pan_image, jnp.transpose(vnir_bands, (1, 0, 2)), swir_bands)))
    *chunks, pan_late, table_late = lax.optimization_barrier((*chunks, pan_image, jnp.asarray(table)))
    got = [chunks[0]] + [
        lax.ppermute(chunks[d], "band", [(i, (i + d) % groups) for i in range(groups)])
        for d in range(1, groups)
    ]

    def take(ref, name, index=0, rows=None):
        starts, height, width = place[name]
        first, height = (0, height) if rows is None else (rows[0], rows[1] - rows[0])
        pieces = []
        for start, part in starts:
            base = start + first
            if not isinstance(index, int) or index:
                base = pl.multiple_of(base + index * place[name][1], 16)
            pieces.append(ref[pl.ds(base, height), 0:part])
        return pieces[0] if len(pieces) == 1 else jnp.concatenate(pieces, axis=1)

    def both_parts(ref, name, index=0, stacked=1):
        return take(ref, name, index), take(ref, name, index + stacked)

    def shrink(panes, tall, low):
        both = dot(panes[0], tall) + dot(panes[1], tall)
        return both[:, :LANES], both[:, LANES:] + dot(panes[0], low)

    def along_rows(rc, means, fines):
        both = parts2(jnp.concatenate([means, fines], axis=0))
        return dot(rc[0], both[0]) + (dot(rc[0], both[1]) + dot(rc[1], both[0]))

    def filter_rows(rf, x):
        col = parts2(x)
        return dot(rf, jnp.concatenate([col[0], col[0], col[1]], axis=0))

    def row_variant():
        row_id = lax.axis_index("rows")
        return jnp.where(row_id == 0, 1, jnp.where(row_id == strips - 1, 2, 0))

    pairs_in = [(i, i ^ 1) for i in range(strips) if i ^ 1 < strips]
    pairs_out = [(i, i + 1) for i in range(1, strips - 1, 2)]
    pairs_out += [(j, i) for i, j in pairs_out]

    def is_even():
        return lax.rem(lax.axis_index("rows"), 2) == 0

    def put(outs, index, up, down):
        even = is_even()
        outs[0][index] = jnp.where(even, up, down)
        outs[1][index] = jnp.where(even, down, up)

    def arrived(refs, index, low):
        even = is_even()
        inner, outer = refs[0][index], refs[1][index]
        return jnp.where(even, outer, inner) if low else jnp.where(even, inner, outer)

    def trade(inner, outer):
        outer = lax.ppermute(outer, "rows", pairs_out)
        return lax.ppermute(inner, "rows", pairs_in), outer

    at_up, at_down = 2 * pad, 2 * pad + 16

    def put_small(outs, first, ups, downs):
        blank = jnp.zeros((2, LANES), F32)
        for i in range(0, len(ups), 4):
            up = ups[i : i + 4] + [blank] * (4 - len(ups[i : i + 4]))
            down = downs[i : i + 4] + [blank] * (4 - len(downs[i : i + 4]))
            put(outs, first + i // 4, jnp.concatenate(up, axis=0), jnp.concatenate(down, axis=0))

    def adjoint_of(table_ref, col):
        p1 = col.astype(BF16)
        over = col - p1.astype(F32)
        p2 = over.astype(BF16)
        p3 = (over - p2.astype(F32)).astype(BF16)
        weights = take(table_ref, "adjoint", row_variant())
        return dot(weights, jnp.concatenate([p1, p2, p3, p1, p2, p1], axis=0))

    inner_fine = fine_tiles - 4

    def early(pan_far, table_far, pan_ref, table_ref, coarse_out, fine_out, diff_out, q_out, sems):
        now = pl.ds(0, place["low"][0][0][0])
        later = pl.ds(now.size, table.shape[0] - now.size)
        copies = [
            pltpu.make_async_copy(pan_far, pan_ref, sems.at[0]),
            pltpu.make_async_copy(table_far.at[now], table_ref.at[now], sems.at[1]),
            pltpu.make_async_copy(table_far.at[later], table_ref.at[later], sems.at[2]),
        ]
        for copy in copies:
            copy.start()
        copies[0].wait()
        panes = parts2(pan_ref[...])
        copies[1].wait()
        starts = [margin * k - 3 * LANES for k in range(1, frame_tiles - 1)]
        means, fines = shrink(
            windows(panes, starts, 6 * LANES), take(table_ref, "tall"), take(table_ref, "tall_low")
        )
        rc = both_parts(table_ref, "rows", row_variant(), 3)
        coarse_out[...] = along_rows(rc, blocks(means, middle), blocks(fines, middle))
        starts = [2 * LANES * k - LANES for k in range(1, pairs - 1)]
        col = blocks(dot3(windows(panes, starts, 4 * LANES), both_parts(table_ref, "fine")), pairs - 2)
        rows = filter_rows(take(table_ref, "rows_fine"), col)
        fine_out[...] = rows[h:]
        diff = pan_ref[:, 2 * LANES : w - 2 * LANES] - rows[0:h]
        copies[2].wait()
        adjoint = adjoint_of(table_ref, col)
        for k in range(inner_fine):
            at = slice(LANES * k, LANES * (k + 1))
            diff_out[k + 2] = diff[:, at]
            q_out[k + 2] = adjoint[:, at]

    q_rows = -(-(hc + 9) // 16) * 16
    pan_held, table_held, coarse_mid, fine_mid, diff_mid, q_mid = call(
        early,
        (
            shape(h, w),
            jax.ShapeDtypeStruct(table.shape, BF16),
            shape(2 * pad + 32, LANES * middle),
            shape(2 * HALO, LANES * inner_fine),
            shape(fine_tiles, h, LANES),
            shape(fine_tiles, q_rows, LANES),
        ),
        [pltpu.SemaphoreType.DMA((3,))],
        cost=(2_000_000_000, 8_000_000),
        in_specs=[ANY] * 2,
    )(far(pan_late), far(table_late))

    border_tiles = -(-edge_size // LANES)
    at_s = HALO * coarse_tiles
    at_h = at_s + 2 * swir_tiles
    at_ld = at_h + border_tiles
    at_d = at_ld + frame_tiles
    sent = at_d + -(-frame_tiles // 4)

    def framed(main, borders, lane, reach):
        blank = jnp.zeros((8, HALF - reach), F32)
        left = borders[:, lane : lane + reach]
        right = borders[:, lane + reach : lane + 2 * reach]
        return jnp.concatenate([blank, left, main, right, blank], axis=1)

    def assemble(pan_ref, table_ref, cm_ref, *rest):
        ins = rest[:groups]
        x_out, s_out, ce_out, fe_out, col_out = rest[groups : groups + 5]
        outs = rest[groups + 5 :]
        me = lax.axis_index("band")

        def gather(row, lane, size):
            rows = [ins[(groups - i) % groups][row, :, lane : lane + size] for i in range(groups)]
            return pltpu.roll(jnp.concatenate(rows, axis=0), nb * me, 0)

        def tile(x, t):
            return x[:, LANES * t : LANES * (t + 1)]

        borders = gather(at_edge, edge_lane, edge_size)
        blank = jnp.zeros((8, LANES * border_tiles - edge_size), F32)
        borders = jnp.concatenate([borders, blank], axis=1)
        for t in range(border_tiles):
            put(outs, at_h + t, tile(borders, t), tile(borders, t))
        mains = [gather(r, 0, wc) for r in range(hc)]
        for r in range(hc):
            x_out[r] = framed(mains[r], borders, 2 * HALO * r, HALO)
        for r in range(HALO):
            for t in range(coarse_tiles):
                put(outs, coarse_tiles * r + t, tile(mains[hc - HALO + r], t), tile(mains[r], t))
        shorts = [gather(at_swir + q // RATIO_S, ws * (q % RATIO_S), ws) for q in range(hs)]
        for q in range(hs):
            s_out[q] = framed(shorts[q], borders, 2 * HALO * hc + 4 * q, 2)
        for q in range(2):
            for t in range(swir_tiles):
                put(outs, at_s + swir_tiles * q + t, tile(shorts[hs - 2 + q], t), tile(shorts[q], t))

        def strip(d, side, empty):
            first = strip_place(d, side)
            rows = []
            for i in range(8 // nb):
                lane = piece * (i % per_row)
                rows.append(ins[d][first + i // per_row, :, lane : lane + piece])
            flat = jnp.where(empty, 0.0, jnp.concatenate(rows, axis=0))
            whole = [flat[:, REACH * t : REACH * (t + 1)] for t in range(h // 8)]
            return jnp.concatenate(whole, axis=0)

        blank = jnp.zeros((h, LANES - REACH), F32)
        left = jnp.concatenate([blank, strip(1, "right", me == 0), pan_ref[:, 0 : 3 * LANES]], axis=1)
        right = jnp.concatenate(
            [pan_ref[:, w - 3 * LANES : w], strip(groups - 1, "left", me == groups - 1), blank], axis=1
        )
        left, right = parts2(left), parts2(right)
        cut = 2 * LANES
        inner = (cut, 6 * LANES)
        lm, lf = shrink(left, take(table_ref, "tall", 0, inner), take(table_ref, "tall_low", 0, inner))
        inner = (0, 4 * LANES)
        rm, rfine = shrink(right, take(table_ref, "tall", 0, inner), take(table_ref, "tall_low", 0, inner))
        rc = both_parts(table_ref, "rows", row_variant(), 3)
        edge = along_rows(rc, jnp.concatenate([lm, rm], axis=1), jnp.concatenate([lf, rfine], axis=1))
        ce_out[...] = edge[0 : 2 * pad]
        outer = tuple(jnp.concatenate([a, b], axis=0) for a, b in zip(left, right))
        col = blocks(dot3(outer, both_parts(table_ref, "fine")), 2)
        col_out[...] = col
        fe_out[...] = filter_rows(take(table_ref, "rows_fine"), col)
        sides = jnp.concatenate([edge[:, :LANES], cm_ref[...], edge[:, LANES:]], axis=1)
        ups, downs = [], []
        for k in range(frame_tiles):
            part = tile(sides, k)
            put(outs, at_ld + k, part[at_up + 8 : at_up + 16], part[at_down + 8 : at_down + 16])
            ups.append(part[at_up : at_up + 2])
            downs.append(part[at_down + HALO - 2 : at_down + HALO])
        put_small(outs, at_d, ups, downs)

    x_loc, s_loc, coarse_edge, fine_edge, col_edge, rest_in, rest_out = call(
        assemble,
        (
            shape(hc, BANDS, wf),
            shape(hs, BANDS, sf),
            shape(2 * pad, 2 * LANES),
            shape(h + 2 * HALO, 4 * LANES),
            shape(h, 4 * LANES),
            shape(sent, 8, LANES),
            shape(sent, 8, LANES),
        ),
        cost=(200_000_000, 3_000_000),
        in_specs=[VMEM] * (groups + 3),
    )(pan_held, table_held, coarse_mid, *got)
    rest_in, rest_out = trade(rest_in, rest_out)

    turns = BANDS // 2 + 1
    block_starts = [LANES * k for k in range(coarse_tiles)]
    own_rows = range(2, hc + 2)
    halo_rows = (0, 1, hc + 2, hc + 3)
    around = (-2, -1) + halo_rows + (hc + 4, hc + 5)

    def lifted(rows, table_ref, store):
        stack = windows(parts2(jnp.concatenate(rows, axis=0)), block_starts, 2 * LANES)
        up = dot3(stack, both_parts(table_ref, "up4"))
        size = 8 * len(rows)
        for k in range(coarse_tiles):
            for q in range(RATIO_V):
                store(RATIO_V * k + q, up[size * k : size * (k + 1), LANES * q : LANES * (q + 1)])

    def grouped(step, size):
        def body(k, carry):
            for i in range(size):
                carry = step(size * k + i, carry)
            return carry

        return body

    def weighted(pairs):
        value = None
        for weight, x in pairs:
            if weight != 0.0:
                value = float(weight) * x if value is None else value + float(weight) * x
        return value

    def inside(
        pan_ref, x_ref, s_ref, fm_ref, fe_ref, col_ref, table_ref, diff_in, q_in,
        y_out, v_out, acc_out, s_out, diff_out, q_out, edge_out, mean_out, lows_out, *outs,
    ):
        def store(index, value):
            y_out[index] = value

        lifted([x_ref[r] for r in range(hc)], table_ref, store)
        rows = parts2(jnp.concatenate([s_ref[q] for q in range(hs)], axis=0))
        s_cols = dot3(windows(rows, block_starts[:swir_tiles], 2 * LANES), both_parts(table_ref, "up3"))
        s_out[...] = blocks(s_cols, swir_tiles)

        diff = jnp.concatenate([pan_ref[:, : 2 * LANES], pan_ref[:, w - 2 * LANES :]], axis=1) - fe_ref[0:h, :]
        adjoint = adjoint_of(table_ref, col_ref[...])
        total = jnp.zeros((1, LANES), F32)
        for k in range(fine_tiles):
            if 2 <= k < fine_tiles - 2:
                at = slice(LANES * (k - 2), LANES * (k - 1))
                up, down = fm_ref[0:HALO, at], fm_ref[HALO:, at]
                total = total + q_in[k, hc + 8 : hc + 9, :]
            else:
                lane = LANES * (k % (fine_tiles - 4))
                at = slice(lane, lane + LANES)
                up, down = fe_ref[h : h + HALO, at], fe_ref[h + HALO :, at]
                diff_out[k] = diff[:, at]
                q_out[k] = adjoint[:, at]
                total = total + adjoint[hc + 8 : hc + 9, at]
            put(outs, k, up, down)

        row_id = lax.axis_index("rows")
        below = jnp.where(row_id > 0, 1.0, 0.0).astype(F32)
        above = jnp.where(row_id < strips - 1, 1.0, 0.0).astype(F32)
        means = {}
        for r in range(-2, hc + 2):
            value = weighted((MEAN4[t + 2], x_ref[r + t]) for t in range(-2, 3) if 0 <= r + t < hc)
            means[r] = value * below if r < 0 else (value * above if r >= hc else value)
        for i, r in enumerate((0, 1, hc - 2, hc - 1)):
            edge_out[i] = means[r]
        rows = parts2(jnp.concatenate([means[r] for r in range(2, hc - 2)], axis=0))
        pair = tuple(x[:, :LANES] for x in both_parts(table_ref, "pair", 0, 3))
        mean_out[...] = blocks(dot3(windows(rows, block_starts, 2 * LANES), pair), coarse_tiles)
        reach = TAPS_S // 2
        for r in range(hc):
            lows_out[r] = weighted((KC[t + reach], means[r + t]) for t in range(-reach, reach + 1) if r + t in means)
        acc_out[turns + 2] = jnp.concatenate([total, jnp.zeros((7, LANES), F32)], axis=0)

        def tile_step(k, carry):
            accs, accv, accp = list(carry[:turns]), carry[turns], carry[turns + 1]
            ys = {m: y_out[k, pl.ds(8 * (m - 2), 8), :] for m in own_rows}
            for m in own_rows:
                z = weighted((gram[m, other], ys[other]) for other in own_rows)
                accs[0] = accs[0] + z * ys[m]
                for i in range(1, turns):
                    accs[i] = accs[i] + z * pltpu.roll(ys[m], i, 0)
                accv = accv + float(rise[m]) * ys[m]
                accp = accp + ys[m] * q_out[k, pl.ds(m + 2, 1), :]
            for m in range(hc):
                for p in range(RATIO_V):
                    r = RATIO_V * m + p
                    v_out[k, pl.ds(8 * r, 8), :] = weighted((C4[t, p], ys[m + t]) for t in range(5) if m + t in ys)
            return tuple(accs) + (accv, accp)

        zero = jnp.zeros((8, LANES), F32)
        first = lax.fori_loop(0, fine_tiles // 2, grouped(tile_step, 2), (zero,) * (turns + 2))
        for i in range(turns + 2):
            acc_out[i] = first[i]

    y_own, v_own, acc_own, s_own, diff, q_own, mean_edge, mean_own, lows_own, low_in, low_out = call(
        inside,
        (
            shape(fine_tiles, 8 * hc, LANES),
            shape(fine_tiles, 8 * h, LANES),
            shape(turns + 3, 8, LANES),
            shape(8 * hs, wc),
            shape(fine_tiles, h, LANES),
            shape(fine_tiles, q_rows, LANES),
            shape(4, BANDS, wf),
            shape(8 * (hc - 4), wc),
            shape(hc, BANDS, wf),
            shape(fine_tiles, 8, LANES),
            shape(fine_tiles, 8, LANES),
        ),
        cost=(2_000_000_000, 8_000_000),
        input_output_aliases={7: 4, 8: 5},
    )(pan_held, x_loc, s_loc, fine_mid, fine_edge, col_edge, table_held, diff_mid, q_mid)
    low_in, low_out = trade(low_in, low_out)

    def moments(
        x_ref, y_ref, acc_ref, scol_ref, q_ref, edge_ref, mean_ref, lows_ref,
        rest_in_ref, rest_out_ref, cm_ref, ce_ref, table_ref,
        mom_out, y_out, ugap_out, dgap_out, s_out,
        both, ulow,
    ):
        me = lax.axis_index("band")
        rest = (rest_in_ref, rest_out_ref)

        def tiles(refs, low, indices):
            return jnp.concatenate([arrived(refs, i, low) for i in indices], axis=1)

        def halo(first, per, reach, start, count):
            sides = []
            for low, base in ((True, start[0]), (False, start[1])):
                borders = tiles(rest, low, range(at_h, at_h + border_tiles))
                rows = []
                for r in range(count):
                    main = tiles(rest, low, range(first + per * r, first + per * (r + 1)))
                    rows.append(framed(main, borders, base + 2 * reach * r, reach))
                sides.append(rows)
            return sides

        x_low, x_high = halo(0, coarse_tiles, HALO, (2 * HALO * (hc - HALO), 0), HALO)

        def x_row(r):
            if r < 0:
                return x_low[HALO + r]
            if r >= hc:
                return x_high[r - hc]
            return x_ref[r]

        def store(index, value):
            y_out[index] = value

        lifted([x_row(m - 2) for m in around], table_ref, store)

        zero = jnp.zeros((8, LANES), F32)

        def tile_step(k, carry):
            accs = list(carry[:turns])
            accp, accv = carry[turns], carry[turns + 1]
            ys = {m: y_ref[k, pl.ds(8 * (m - 2), 8), :] for m in own_rows}
            for i, m in enumerate(around):
                ys[m] = y_out[k, pl.ds(8 * i, 8), :]
            for m in halo_rows:
                near = weighted((gram[m, other], ys[other]) for other in own_rows)
                whole = near + weighted((gram[m, other], ys[other]) for other in halo_rows)
                accs[0] = accs[0] + ys[m] * (near + whole)
                for i in range(1, turns):
                    accs[i] = accs[i] + whole * pltpu.roll(ys[m], i, 0) + ys[m] * pltpu.roll(near, i, 0)
                accv = accv + float(rise[m]) * ys[m]
            for m in around:
                accp = accp + ys[m] * q_ref[k, pl.ds(m + 2, 1), :]
            return tuple(accs) + (accp, accv)

        start = tuple(acc_ref[i] for i in range(turns)) + (acc_ref[turns + 1], acc_ref[turns])
        first = start
        for k in range(fine_tiles):
            first = tile_step(k, first)

        beyond = [r for r in range(-HALO, hc + HALO) if not 0 <= r < hc]
        edges = []
        for i, r in enumerate((0, 1, hc - 2, hc - 1)):
            more = weighted((MEAN4[a - r + 2], x_row(a)) for a in beyond if abs(a - r) <= 2)
            edges.append(edge_ref[i] + more)
        lows = []
        for r in range(hc):
            more = weighted((WIDE[a - r + HALO], x_row(a)) for a in beyond if abs(a - r) <= HALO)
            lows.append(lows_ref[r] + more)
        u_rows = windows(parts2(jnp.concatenate(edges, axis=0)), block_starts, 2 * LANES)
        l_rows = windows(parts2(jnp.concatenate(lows, axis=0)), block_starts, 2 * LANES)
        u_edge = dot3(u_rows, tuple(x[:, :LANES] for x in both_parts(table_ref, "pair", 0, 3)))
        left = jnp.where(me == 0, 1, 0)
        right = jnp.where(me == groups - 1, 2, 0)
        size = 8 * hc
        last = coarse_tiles - 1
        for which, lo_k, hi_k in ((left, 0, 1), (0, 1, last), (right, last, last + 1)):
            if hi_k <= lo_k:
                continue
            wp = tuple(x[:, LANES:] for x in both_parts(table_ref, "pair", which, 3))
            part = dot3(tuple(x[size * lo_k : size * hi_k] for x in l_rows), wp)
            for k in range(lo_k, hi_k):
                at = slice(LANES * k, LANES * (k + 1))
                low_k = part[size * (k - lo_k) : size * (k - lo_k + 1)]
                ulow[:, at] = low_k
                around_k = u_edge[32 * k : 32 * (k + 1)]
                u_k = jnp.concatenate([around_k[0:16], mean_ref[:, at], around_k[16:32]], axis=0)
                ugap_out[:, at] = u_k - low_k

        column = lax.broadcasted_iota(jnp.int32, (1, wf), 1) - HALF + me * wc
        valid = jnp.where((column >= 0) & (column < groups * wc), 1.0, 0.0).astype(F32)

        def own(rows):
            return jnp.concatenate([ce_ref[rows, 0:LANES], cm_ref[rows, :], ce_ref[rows, LANES:]], axis=1)

        def small(low):
            rows = [arrived(rest, at_d + k // 4, low)[2 * (k % 4) : 2 * (k % 4) + 2] for k in range(frame_tiles)]
            return jnp.concatenate(rows, axis=1)

        both[...] = own(slice(0, pad))
        both[0:2] = both[0:2] + small(True)
        both[hc - 2 : hc] = both[hc - 2 : hc] + small(False)
        detail = both[...]
        both[...] = own(slice(pad, 2 * pad))
        both[0:HALO] = both[0:HALO] + tiles(rest, True, range(at_ld, at_ld + frame_tiles))
        both[hc - HALO : hc] = both[hc - HALO : hc] + tiles(rest, False, range(at_ld, at_ld + frame_tiles))
        dlow_rows = windows(parts2(both[...] * valid), block_starts, 2 * LANES)
        dlow = blocks(dot3(dlow_rows, both_parts(table_ref, "low")), coarse_tiles)
        dgap_out[...] = detail[:, HALF : HALF + wc] - dlow
        both[:, 0:wc] = dlow

        s_low, s_high = halo(at_s, swir_tiles, 2, (2 * HALO * hc + 4 * (hs - 2), 2 * HALO * hc), 2)
        s_parts = windows(parts2(jnp.concatenate(s_low + s_high, axis=0)), block_starts[:swir_tiles], 2 * LANES)
        s_around = blocks(dot3(s_parts, both_parts(table_ref, "up3")), swir_tiles)
        s_cols = jnp.concatenate([s_around[0:16], scol_ref[...], s_around[16:32]], axis=0)
        for m in range(hs):
            for p in range(RATIO_S):
                value = None
                for t in range(5):
                    if C3[t, p] != 0.0:
                        term = float(C3[t, p]) * s_cols[8 * (m + t) : 8 * (m + t) + 8]
                        value = term if value is None else value + term
                s_out[RATIO_S * m + p] = value

        ll = [zero] * turns
        cross = [zero] * BANDS
        ld = ls = sd = ss = dd = ds = zero
        for r in range(hc):
            for k in range(coarse_tiles):
                at = slice(LANES * k, LANES * (k + 1))
                u = ulow[8 * r : 8 * r + 8, at]
                s = s_out[r, :, at]
                dl = jnp.broadcast_to(both[r : r + 1, at], (8, LANES))
                ll[0] = ll[0] + u * u
                for i in range(1, turns):
                    ll[i] = ll[i] + u * pltpu.roll(u, i, 0)
                for i in range(BANDS):
                    cross[i] = cross[i] + u * s_out[r, i : i + 1, at]
                ld = ld + u * dl
                sd = sd + s * dl
                ls = ls + u
                ss = ss + s
                dd = dd + dl * dl
                ds = ds + dl

        lane = lax.broadcasted_iota(jnp.int32, (8, LANES), 1)
        sub = lax.broadcasted_iota(jnp.int32, (8, LANES), 0)

        def column_of(acc):
            return jnp.broadcast_to(jnp.sum(acc, axis=1, keepdims=True), (8, LANES))

        table = zero
        for base, accs in ((0, ll), (32, first[:turns])):
            for i in range(turns):
                col = column_of(accs[i])
                table = jnp.where(lane == base + lax.rem(sub + BANDS - i, BANDS), col, table)
                if 0 < i < BANDS // 2:
                    turned = pltpu.roll(col, BANDS - i, 0)
                    table = jnp.where(lane == base + lax.rem(sub + i, BANDS), turned, table)
        singles = [(8 + i, cross[i]) for i in range(BANDS)]
        singles += [(16, ld), (17, ls), (18, sd), (19, ss), (20, dd), (21, ds)]
        singles += [(40, first[turns]), (41, first[turns + 1])]
        for index, acc in singles:
            table = jnp.where(lane == index, column_of(acc), table)
        total = jnp.sum(jnp.sum(acc_ref[turns + 2], axis=0, keepdims=True), axis=1, keepdims=True)
        table = jnp.where(lane == 43, total, table)
        turned = pltpu.roll(table, HALF, 1)
        mom_out[...] = jnp.where(lane[0:4] < HALF, table[0:4], turned[4:8])

    mom, y_halo, ugap, dgap, s_up = call(
        moments,
        (
            shape(4, LANES),
            shape(fine_tiles, 8 * len(around), LANES),
            shape(8 * hc, wc),
            shape(pad, wc),
            shape(hc, BANDS, wc),
        ),
        [
            pltpu.VMEM((pad, wf), F32),
            pltpu.VMEM((8 * hc, wc), F32),
        ],
        cost=(1_000_000_000, 8_000_000),
    )(
        x_loc, y_own, acc_own, s_own, q_own, mean_edge, mean_own, lows_own,
        rest_in, rest_out, coarse_mid, coarse_edge, table_held,
    )
    devices = groups * strips
    mom, low_in, low_out = lax.optimization_barrier((mom, low_in, low_out))
    spread = jnp.broadcast_to(mom[None], (devices,) + mom.shape)
    sums = lax.all_to_all(spread, ("rows", "band"), split_axis=0, concat_axis=0, tiled=True)

    apart_rows = h + 8

    def finish(
        sums_ref, yh_ref, v_ref, diff_ref, low_in_ref, low_out_ref, ugap_ref, dgap_ref, s_ref,
        vnir_out, swir_out, tiles, swir, ends, sems,
    ):
        lane = lax.broadcasted_iota(jnp.int32, (8, LANES), 1)
        sub = lax.broadcasted_iota(jnp.int32, (8, LANES), 0)
        eye = lane == sub
        terms = [sums_ref[index] for index in range(devices)]
        while len(terms) > 1:
            terms = [sum(terms[i : i + 2][1:], terms[i]) for i in range(0, len(terms), 2)]
        total = jnp.concatenate([terms[0], pltpu.roll(terms[0], HALF, 1)], axis=0)

        def column(x, index):
            return jnp.broadcast_to(x[:, index : index + 1], (8, LANES))

        def across(col):
            return jnp.sum(jnp.where(eye, col, 0.0), axis=0, keepdims=True)

        def down(x):
            return jnp.sum(x, axis=0, keepdims=True)

        def solve(matrix, rhs):
            cols = [column(matrix, j) for j in range(BANDS)] + [rhs]
            inverse = jnp.zeros((8, LANES), F32)
            for k in range(BANDS):
                pivot = 1.0 / jnp.broadcast_to(cols[k][k : k + 1], (8, LANES))
                inverse = jnp.where(sub == k, pivot, inverse)
                factor = jnp.where(sub == k, 0.0, cols[k] * pivot)
                for j in range(k + 1, BANDS + 1):
                    cols[j] = cols[j] - factor * jnp.broadcast_to(cols[j][k : k + 1], (8, LANES))
            return cols[BANDS] * inverse

        n1 = 1.0 / fine_pixels
        mean_v = column(total, 41) * n1
        mean_p = column(total, 43) * n1
        cov_v = pltpu.roll(total, LANES - 32, 1) * n1 - mean_v * across(mean_v)
        cov_p = column(total, 40) * n1 - mean_v * mean_p
        gain = cov_p / down(cov_p * solve(cov_v, cov_p))

        n2 = RATIO_V * RATIO_V / fine_pixels
        mean_l = column(total, 17) * n2
        mean_s = column(total, 19) * n2
        mean_d = column(total, 21) * n2
        cov_ll = total * n2 - mean_l * across(mean_l)
        cov_ls = pltpu.roll(total, LANES - 8, 1) * n2 - mean_l * across(mean_s)
        cov_ld = column(total, 16) * n2 - mean_l * mean_d
        cov_sd = column(total, 18) * n2 - mean_s * mean_d
        cov_dd = column(total, 20) * n2 - mean_d * mean_d
        gain_row = across(gain)
        a2 = cov_ll + gain * across(cov_ld) + cov_ld * gain_row + gain * gain_row * cov_dd
        b2 = jnp.where(lane < BANDS, cov_ls + gain * across(cov_sd), 0.0)
        target = jnp.broadcast_to(jnp.sum(b2, axis=1, keepdims=True) / BANDS, (8, LANES))

        def sent_tile(k):
            lanes = pl.ds(pl.multiple_of(LANES * k, LANES), LANES)
            held = tiles.reshape(fine_tiles, BANDS, apart_rows, LANES).at[k, :, pl.ds(0, h), :]
            return pltpu.make_async_copy(held, vnir_out.at[:, :, lanes], sems.at[k])

        def tile_step(k, carry):
            ys = {m: yh_ref[k, pl.ds(8 * i, 8), :] for i, m in enumerate(around) if m in halo_rows}
            lows = (low_in_ref, low_out_ref)
            ends[k, 0:HALO, :] = diff_ref[k, 0:HALO, :] - arrived(lows, k, True)
            ends[k, HALO:, :] = diff_ref[k, h - HALO :, :] - arrived(lows, k, False)
            for m in range(hc):
                for p in range(RATIO_V):
                    r = RATIO_V * m + p
                    value = v_ref[k, pl.ds(8 * r, 8), :]
                    more = weighted((C4[t, p], ys[m + t]) for t in range(5) if m + t in ys)
                    if more is not None:
                        value = value + more
                    if r < HALO:
                        detail = ends[k, pl.ds(r, 1), :]
                    elif r >= h - HALO:
                        detail = ends[k, pl.ds(r - h + 2 * HALO, 1), :]
                    else:
                        detail = diff_ref[k, pl.ds(r, 1), :]
                    value = value + gain * detail
                    tiles[k, pl.ds(r, 8, stride=apart_rows), :] = value
            sent_tile(k).start()
            return carry

        beside = max(1, fine_tiles // (BANDS + BANDS // 2))

        def solve_step(k, carry):
            work, inverse = carry
            here = sub == k
            row = down(jnp.where(here, work, 0.0))
            col = jnp.sum(jnp.where(lane == k, work, 0.0), axis=1, keepdims=True)
            pivot = 1.0 / down(jnp.where(here[:, 0:1], col, 0.0))
            inverse = jnp.where(here, pivot, inverse)
            work = work - jnp.where(here, 0.0, col * pivot) * row

            for i in range(beside):
                tile_step(beside * k + i, 0)
            return work, inverse

        start = (jnp.where(lane == BANDS, target, a2), jnp.zeros((8, LANES), F32))
        work, inverse = lax.fori_loop(0, BANDS, solve_step, start)
        fit2 = column(work, BANDS) * inverse
        numer = down(fit2 * b2)
        share_row = numer / down(fit2 * target)
        share = jnp.sum(jnp.where(eye, jnp.broadcast_to(share_row, (8, LANES)), 0.0), axis=1, keepdims=True)
        scale = down(fit2 * gain)[:, 0:1]
        fit_col = fit2[:, 0:1]
        for r in range(hc):
            seen = jnp.sum(fit_col * ugap_ref[8 * r : 8 * r + 8, :], axis=0, keepdims=True)
            seen = seen + scale * dgap_ref[r : r + 1, :]
            swir[r] = s_ref[r] + share * seen
        last = pltpu.make_async_copy(swir, swir_out, sems.at[fine_tiles])
        last.start()

        lax.fori_loop(BANDS * beside, fine_tiles, tile_step, 0)

        def drain(k, carry):
            sent_tile(k).wait()
            return carry

        lax.fori_loop(0, fine_tiles, drain, 0)
        last.wait()

    joined_vnir, joined_swir = call(
        finish,
        (shape(BANDS, h, w), shape(hc, BANDS, wc)),
        [
            pltpu.VMEM((fine_tiles, BANDS * apart_rows, LANES), F32),
            pltpu.VMEM((hc, BANDS, wc), F32),
            pltpu.VMEM((fine_tiles, 2 * HALO, LANES), F32),
            pltpu.SemaphoreType.DMA((fine_tiles + 1,)),
        ],
        cost=(100_000_000, 8_000_000),
        out_specs=(ANY, ANY),
    )(sums, y_halo, v_own, diff, low_in, low_out, ugap, dgap, s_up)
    return joined_vnir, jnp.transpose(joined_swir, (1, 0, 2))


def solution(mesh):
    return jax.shard_map(
        local,
        mesh=mesh,
        in_specs=(P("rows", "band"), P("band", "rows", None), P("band", "rows", None)),
        out_specs=(P(None, "rows", "band"), P(None, "rows", "band")),
        check_vma=False,
    )
```

```python
import math

import jax
import jax.numpy as jnp
import ml_dtypes
import numpy as np
from jax import lax
from jax.experimental import pallas as pl
from jax.experimental.pallas import tpu as pltpu
from jax.sharding import PartitionSpec as P

BANDS = 8
RATIO_V = 4
RATIO_S = 3
TAPS_V = 17
TAPS_S = 13
NYQUIST_GAIN = 0.29
LANES = 128
HALF = 64
REACH = 32
HALO = 8
F32 = jnp.float32
BF16 = jnp.bfloat16
VMEM_BYTES = 24 * 1024 * 1024
VMEM_MOST = 56 * 1024 * 1024


def gauss_taps(upscale, kernel_len):
    spread = upscale * math.sqrt(-2.0 * math.log(NYQUIST_GAIN)) / math.pi
    radius = kernel_len // 2
    offsets = np.arange(-radius, radius + 1) * 1.0
    values = np.exp(-(offsets**2) / (2.0 * spread**2))
    return values / values.sum()


def cubic_weight(distance):
    distance = abs(distance)
    if distance <= 1.0:
        return 1.5 * distance**3 - 2.5 * distance**2 + 1.0
    if distance < 2.0:
        return -0.5 * distance**3 + 2.5 * distance**2 - 4.0 * distance + 2.0
    return 0.0


def cubic_table(upscale):
    weights = np.zeros((5, upscale))
    for phase_index in range(upscale):
        centre = (phase_index + 0.5) / upscale - 0.5
        first_tap = math.floor(centre)
        fraction = centre - first_tap
        for tap_index in range(-1, 3):
            weights[first_tap + tap_index + 2, phase_index] += cubic_weight(tap_index - fraction)
    return weights


KF = gauss_taps(RATIO_V, TAPS_V)
KC = gauss_taps(RATIO_S, TAPS_S)
C4 = cubic_table(RATIO_V)
C3 = cubic_table(RATIO_S)
MEAN4 = C4.mean(axis=1)
WIDE = np.convolve(KC, MEAN4)


def split(table):
    high = np.asarray(table, np.float64).astype(np.float32).astype(ml_dtypes.bfloat16)
    low = (np.asarray(table, np.float64) - high.astype(np.float64)).astype(np.float32)
    return np.stack([high, low.astype(ml_dtypes.bfloat16)])


def split3(table):
    high, middle = split(table)
    low = np.asarray(table, np.float64) - high.astype(np.float64) - middle.astype(np.float64)
    return high, middle, low.astype(np.float32).astype(ml_dtypes.bfloat16)


def band_matrix(size, taps):
    radius = len(taps) // 2
    out = np.zeros((size, size))
    for row in range(size):
        for tap in range(-radius, radius + 1):
            if 0 <= row + tap < size:
                out[row, row + tap] = taps[tap + radius]
    return out


def row_tables(h):
    hc = h // RATIO_V
    mean = np.zeros((3 * hc, 3 * h))
    for row in range(3 * hc):
        mean[row, RATIO_V * row : RATIO_V * (row + 1)] = 1.0 / RATIO_V
    fine = band_matrix(3 * h, KF)
    low = band_matrix(3 * hc, KC)
    mean_fine = mean @ fine
    pad = -(-hc // 8) * 8

    def part(matrix, rows, cols):
        return matrix[rows, :][:, cols]

    def stacked(rows, cols, filt):
        a = mean if filt is None else filt @ mean
        c = mean_fine if filt is None else filt @ mean_fine
        return np.concatenate([part(a, rows, cols), -part(c, rows, cols)], axis=1)

    own = slice(h, 2 * h)
    tables = []
    for variant in range(3):
        keep = np.ones(3 * hc)
        if variant == 1:
            keep[:hc] = 0.0
        if variant == 2:
            keep[2 * hc :] = 0.0
        masked = low * keep[None, :]
        rows = []
        for filt in (None, masked):
            block = np.zeros((pad, 2 * h))
            block[:hc] = stacked(slice(hc, 2 * hc), own, filt)
            rows.append(block)
        for filt in (None, low):
            rows.append(stacked(slice(hc, hc + HALO), slice(0, h), filt))
        for filt in (None, low):
            rows.append(stacked(slice(2 * hc - HALO, 2 * hc), slice(2 * h, 3 * h), filt))
        tables.append(np.concatenate(rows, axis=0))
    coarse_rows = np.stack(tables)
    fine_rows = np.concatenate(
        [fine[h : 2 * h, h : 2 * h], fine[h : h + HALO, 0:h], fine[2 * h - HALO : 2 * h, 2 * h : 3 * h]],
        axis=0,
    )
    return coarse_rows, fine_rows


def up_rows(hc):
    out = np.zeros((RATIO_V * hc, hc + 4))
    for m in range(hc):
        for p in range(RATIO_V):
            out[RATIO_V * m + p, m : m + 5] = C4[:, p]
    return out


def adjoint_rows(h):
    hc = h // RATIO_V
    reach = TAPS_V // 2
    size = h + 2 * reach
    lift = np.zeros((size, hc + 8))
    for r in range(size):
        m, p = divmod(r - reach, RATIO_V)
        lift[r, m + 2 : m + 7] = C4[:, p]
    fine = np.zeros((size, h))
    for r in range(size):
        for t in range(-reach, reach + 1):
            if 0 <= r - reach + t < h:
                fine[r, r - reach + t] = KF[t + reach]
    out = np.zeros((3, -(-(hc + 9) // 16) * 16, h))
    for variant in range(3):
        keep = np.ones((size, 1))
        if variant == 1:
            keep[:reach] = 0.0
        if variant == 2:
            keep[h + reach :] = 0.0
        out[variant, : hc + 8] = (lift * keep).T @ fine
        out[variant, hc + 8] = (fine * keep).sum(axis=0)
    return out


def column_tables():
    n = LANES
    fine = np.zeros((4 * n, 2 * n))
    mean = np.zeros((6 * n, n))
    mean_fine = np.zeros((6 * n, n))
    low = np.zeros((2 * n, n))
    pair = np.zeros((3, 2 * n, 2 * n))
    up4 = np.zeros((2 * n, RATIO_V * n))
    up3 = np.zeros((2 * n, RATIO_S * n))
    for c in range(2 * n):
        for t in range(-(TAPS_V // 2), TAPS_V // 2 + 1):
            fine[n + c + t, c] += KF[t + TAPS_V // 2]
    for c in range(n):
        for q in range(RATIO_V):
            mean[n + RATIO_V * c + q, c] = 1.0 / RATIO_V
            for t in range(-(TAPS_V // 2), TAPS_V // 2 + 1):
                mean_fine[n + RATIO_V * c + q + t, c] += KF[t + TAPS_V // 2] / RATIO_V
        for t in range(-(TAPS_S // 2), TAPS_S // 2 + 1):
            low[c + HALF + t, c] += KC[t + TAPS_S // 2]
            for s in range(-2, 3):
                value = KC[t + TAPS_S // 2] * MEAN4[s + 2]
                pair[0, c + HALF + t + s, n + c] += value
                if c + t >= 0:
                    pair[1, c + HALF + t + s, n + c] += value
                if c + t < n:
                    pair[2, c + HALF + t + s, n + c] += value
        for s in range(-2, 3):
            pair[:, c + HALF + s, c] += MEAN4[s + 2]
            for p in range(RATIO_V):
                up4[c + HALF + s, RATIO_V * c + p] += C4[s + 2, p]
            for p in range(RATIO_S):
                up3[c + HALF + s, RATIO_S * c + p] += C3[s + 2, p]
    return dict(fine=fine, mean=mean, mean_fine=mean_fine, low=low, pair=pair, up4=up4, up3=up3)


def stack_tables(tables):
    wide = 2 * LANES
    pieces, place, top = [], {}, 0
    for name, value in tables.items():
        stack = value.reshape((-1,) + value.shape[-2:])
        height, width = stack.shape[1:]
        starts = []
        for lane in range(0, width, wide):
            part = stack[:, :, lane : lane + wide]
            starts.append((top, part.shape[2]))
            piece = np.zeros((stack.shape[0] * height, wide), ml_dtypes.bfloat16)
            piece[:, : part.shape[2]] = part.reshape(-1, part.shape[2])
            pieces.append(piece)
            top += piece.shape[0]
        place[name] = (starts, height, width)
    return np.concatenate(pieces, axis=0), place


def parts2(x):
    high = x.astype(BF16)
    return high, (x - high.astype(F32)).astype(BF16)


def dot(a, b):
    return jnp.dot(a, b, preferred_element_type=F32)


def dot3(x, w):
    return dot(x[0], w[0]) + (dot(x[1], w[0]) + dot(x[0], w[1]))


def windows(x, starts, size):
    return tuple(jnp.concatenate([part[:, a : a + size] for a in starts], axis=0) for part in x)


def blocks(x, count):
    rows = x.shape[0] // count
    return jnp.concatenate([x[rows * k : rows * (k + 1)] for k in range(count)], axis=1)


def call(kernel, out_shape, scratch=(), cost=(0, 0), room=VMEM_BYTES, **specs):
    return pl.pallas_call(
        kernel,
        out_shape=out_shape,
        scratch_shapes=list(scratch),
        compiler_params=pltpu.CompilerParams(vmem_limit_bytes=room),
        cost_estimate=pl.CostEstimate(flops=cost[0], bytes_accessed=cost[1], transcendentals=0),
        **specs,
    )


ANY = pl.BlockSpec(memory_space=pl.ANY)
VMEM = pl.BlockSpec(memory_space=pltpu.VMEM)


def local(pan_image, vnir_bands, swir_bands):
    groups = lax.axis_size("band")
    strips = lax.axis_size("rows")
    h, w = pan_image.shape
    nb, hc, full = vnir_bands.shape
    _, hs, sfull = swir_bands.shape
    wc = w // RATIO_V
    ws = wc // RATIO_S
    wf = wc + LANES
    sf = ws + LANES
    pad = -(-hc // 8) * 8
    fine_tiles = w // LANES
    coarse_tiles = wc // LANES
    frame_tiles = coarse_tiles + 1
    swir_tiles = ws // LANES
    fine_pixels = h * strips * w * groups
    pairs = w // (2 * LANES)
    middle = frame_tiles - 2
    margin = RATIO_V * LANES

    def shape(*dims):
        return jax.ShapeDtypeStruct(dims, F32)

    coarse_rows, fine_rows = row_tables(h)
    cols = column_tables()
    lift = up_rows(hc)
    gram = lift.T @ lift
    rise = lift.sum(axis=0)

    swir_rows = -(-hs // RATIO_S)
    at_swir = hc
    edge_size = 2 * HALO * hc + 4 * hs
    edge_lane = ws * (hs % RATIO_S)
    shared = hs % RATIO_S and edge_lane + edge_size <= wc
    at_edge = hc + swir_rows - 1 if shared else hc + swir_rows
    edge_lane = edge_lane if shared else 0
    at_strip = at_edge + 1
    piece = REACH * (h // 8)
    per_row = wc // piece
    strip_rows = -(-(8 // nb) // per_row)

    def going(d):
        return (["right"] if d == 1 else []) + (["left"] if d == groups - 1 else [])

    def strip_place(d, side):
        return at_strip + strip_rows * going(d).index(side)

    chunk_rows = [at_strip + strip_rows * len(going(d)) for d in range(groups)]

    mean_parts, fine_parts = split(cols["mean"]), split(cols["mean_fine"])
    r_fine = split(fine_rows)
    r_adj = split3(adjoint_rows(h))
    table, place = stack_tables(
        dict(
            tall=np.concatenate([mean_parts[0], fine_parts[0]], axis=1),
            tall_low=fine_parts[1],
            fine=split(cols["fine"]),
            rows=split(coarse_rows),
            rows_fine=np.concatenate([r_fine[0], r_fine[1], r_fine[0]], axis=1),
            low=split(cols["low"]),
            pair=split(cols["pair"]),
            up4=split(cols["up4"]),
            up3=split(cols["up3"]),
            adjoint=np.concatenate([r_adj[i] for i in (0, 0, 0, 1, 1, 2)], axis=2),
        )
    )

    def far(x):
        return pltpu.with_memory_space_constraint(x, pltpu.HBM)

    def pack(pan_ref, vnir_ref, swir_ref, *rest):
        outs, (wide, swide, edges, sems) = rest[:groups], rest[groups:]
        me = lax.axis_index("band")
        copies = [
            pltpu.make_async_copy(vnir_ref, wide.at[:, :, pl.ds(LANES, full)], sems.at[0]),
            pltpu.make_async_copy(swir_ref, swide.at[:, :, pl.ds(LANES, sfull)], sems.at[1]),
            pltpu.make_async_copy(pan_ref.at[:, pl.ds(0, LANES)], edges.at[0], sems.at[2]),
            pltpu.make_async_copy(pan_ref.at[:, pl.ds(w - LANES, LANES)], edges.at[1], sems.at[3]),
        ]
        for copy in copies:
            copy.start()
        wide[:, :, 0:LANES] = jnp.zeros((hc, nb, LANES), F32)
        wide[:, :, LANES + full : 2 * LANES + full] = jnp.zeros((hc, nb, LANES), F32)
        swide[:, :, 0:LANES] = jnp.zeros((nb, hs, LANES), F32)
        swide[:, :, LANES + sfull : 2 * LANES + sfull] = jnp.zeros((nb, hs, LANES), F32)
        for copy in copies:
            copy.wait()
        for d in range(groups):
            peer = lax.rem(me + d, groups)
            base = pl.multiple_of(peer * wc, LANES)
            sbase = pl.multiple_of(peer * ws, LANES)
            out = outs[d]
            out[0:hc] = wide[:, :, pl.ds(base + LANES, wc)]
            left = wide[:, :, pl.ds(base, LANES)]
            right = wide[:, :, pl.ds(base + LANES + wc, LANES)]
            borders = []
            for r in range(hc):
                borders += [left[r, :, LANES - HALO :], right[r, :, :HALO]]
            swin = swide[:, :, pl.ds(sbase, ws + 2 * LANES)]
            for q in range(hs):
                row = swin[:, q, :]
                lane = ws * (q % RATIO_S)
                out[at_swir + q // RATIO_S, :, lane : lane + ws] = row[:, LANES : LANES + ws]
                borders += [row[:, LANES - 2 : LANES], row[:, LANES + ws : LANES + ws + 2]]
            border = jnp.concatenate(borders, axis=1)
            out[at_edge, :, edge_lane : edge_lane + edge_size] = border
            for side in going(d):
                first = strip_place(d, side)
                edge = edges[1, :, LANES - REACH :] if side == "right" else edges[0, :, :REACH]
                flat = jnp.concatenate([edge[8 * t : 8 * t + 8] for t in range(h // 8)], axis=1)
                for i in range(8 // nb):
                    lane = piece * (i % per_row)
                    out[first + i // per_row, :, lane : lane + piece] = flat[nb * i : nb * (i + 1)]

    chunks = call(
        pack,
        tuple(shape(chunk_rows[d], nb, wc) for d in range(groups)),
        [
            pltpu.VMEM((hc, nb, full + 2 * LANES), F32),
            pltpu.VMEM((nb, hs, sfull + 2 * LANES), F32),
            pltpu.VMEM((2, h, LANES), F32),
            pltpu.SemaphoreType.DMA((4,)),
        ],
        cost=(0, 8_000_000),
        in_specs=[ANY] * 3,
    )(*(far(x) for x in (pan_image, jnp.transpose(vnir_bands, (1, 0, 2)), swir_bands)))
    *chunks, pan_late, table_late = lax.optimization_barrier((*chunks, pan_image, jnp.asarray(table)))
    got = [chunks[0]] + [
        lax.ppermute(chunks[d], "band", [(i, (i + d) % groups) for i in range(groups)])
        for d in range(1, groups)
    ]

    def take(ref, name, index=0, rows=None):
        starts, height, width = place[name]
        first, height = (0, height) if rows is None else (rows[0], rows[1] - rows[0])
        pieces = []
        for start, part in starts:
            base = start + first
            if not isinstance(index, int) or index:
                base = pl.multiple_of(base + index * place[name][1], 16)
            pieces.append(ref[pl.ds(base, height), 0:part])
        return pieces[0] if len(pieces) == 1 else jnp.concatenate(pieces, axis=1)

    def both_parts(ref, name, index=0, stacked=1):
        return take(ref, name, index), take(ref, name, index + stacked)

    def shrink(panes, tall, low):
        both = dot(panes[0], tall) + dot(panes[1], tall)
        return both[:, :LANES], both[:, LANES:] + dot(panes[0], low)

    def along_rows(rc, means, fines):
        both = parts2(jnp.concatenate([means, fines], axis=0))
        return dot(rc[0], both[0]) + (dot(rc[0], both[1]) + dot(rc[1], both[0]))

    def filter_rows(rf, x):
        col = parts2(x)
        return dot(rf, jnp.concatenate([col[0], col[0], col[1]], axis=0))

    def row_variant():
        row_id = lax.axis_index("rows")
        return jnp.where(row_id == 0, 1, jnp.where(row_id == strips - 1, 2, 0))

    pairs_in = [(i, i ^ 1) for i in range(strips) if i ^ 1 < strips]
    pairs_out = [(i, i + 1) for i in range(1, strips - 1, 2)]
    pairs_out += [(j, i) for i, j in pairs_out]

    def is_even():
        return lax.rem(lax.axis_index("rows"), 2) == 0

    def put(outs, index, up, down):
        even = is_even()
        outs[0][index] = jnp.where(even, up, down)
        outs[1][index] = jnp.where(even, down, up)

    def arrived(refs, index, low):
        even = is_even()
        inner, outer = refs[0][index], refs[1][index]
        return jnp.where(even, outer, inner) if low else jnp.where(even, inner, outer)

    def trade(inner, outer):
        outer = lax.ppermute(outer, "rows", pairs_out)
        return lax.ppermute(inner, "rows", pairs_in), outer

    at_up, at_down = 2 * pad, 2 * pad + 16

    def put_small(outs, first, ups, downs):
        blank = jnp.zeros((2, LANES), F32)
        for i in range(0, len(ups), 4):
            up = ups[i : i + 4] + [blank] * (4 - len(ups[i : i + 4]))
            down = downs[i : i + 4] + [blank] * (4 - len(downs[i : i + 4]))
            put(outs, first + i // 4, jnp.concatenate(up, axis=0), jnp.concatenate(down, axis=0))

    def adjoint_of(table_ref, col):
        p1 = col.astype(BF16)
        over = col - p1.astype(F32)
        p2 = over.astype(BF16)
        p3 = (over - p2.astype(F32)).astype(BF16)
        weights = take(table_ref, "adjoint", row_variant())
        return dot(weights, jnp.concatenate([p1, p2, p3, p1, p2, p1], axis=0))

    inner_fine = fine_tiles - 4

    def early(pan_far, table_far, pan_ref, table_ref, coarse_out, fine_out, diff_out, q_out, sems):
        now = pl.ds(0, place["low"][0][0][0])
        later = pl.ds(now.size, table.shape[0] - now.size)
        copies = [
            pltpu.make_async_copy(pan_far, pan_ref, sems.at[0]),
            pltpu.make_async_copy(table_far.at[now], table_ref.at[now], sems.at[1]),
            pltpu.make_async_copy(table_far.at[later], table_ref.at[later], sems.at[2]),
        ]
        for copy in copies:
            copy.start()
        copies[0].wait()
        panes = parts2(pan_ref[...])
        copies[1].wait()
        starts = [margin * k - 3 * LANES for k in range(1, frame_tiles - 1)]
        means, fines = shrink(
            windows(panes, starts, 6 * LANES), take(table_ref, "tall"), take(table_ref, "tall_low")
        )
        rc = both_parts(table_ref, "rows", row_variant(), 3)
        coarse_out[...] = along_rows(rc, blocks(means, middle), blocks(fines, middle))
        starts = [2 * LANES * k - LANES for k in range(1, pairs - 1)]
        col = blocks(dot3(windows(panes, starts, 4 * LANES), both_parts(table_ref, "fine")), pairs - 2)
        rows = filter_rows(take(table_ref, "rows_fine"), col)
        fine_out[...] = rows[h:]
        diff = pan_ref[:, 2 * LANES : w - 2 * LANES] - rows[0:h]
        copies[2].wait()
        adjoint = adjoint_of(table_ref, col)
        for k in range(inner_fine):
            at = slice(LANES * k, LANES * (k + 1))
            diff_out[k + 2] = diff[:, at]
            q_out[k + 2] = adjoint[:, at]

    q_rows = -(-(hc + 9) // 16) * 16
    pan_held, table_held, coarse_mid, fine_mid, diff_mid, q_mid = call(
        early,
        (
            shape(h, w),
            jax.ShapeDtypeStruct(table.shape, BF16),
            shape(2 * pad + 32, LANES * middle),
            shape(2 * HALO, LANES * inner_fine),
            shape(fine_tiles, h, LANES),
            shape(fine_tiles, q_rows, LANES),
        ),
        [pltpu.SemaphoreType.DMA((3,))],
        cost=(2_000_000_000, 8_000_000),
        in_specs=[ANY] * 2,
    )(far(pan_late), far(table_late))

    border_tiles = -(-edge_size // LANES)
    at_s = HALO * coarse_tiles
    at_h = at_s + 2 * swir_tiles
    at_ld = at_h + border_tiles
    at_d = at_ld + frame_tiles
    sent = at_d + -(-frame_tiles // 4)

    def framed(main, borders, lane, reach):
        blank = jnp.zeros((8, HALF - reach), F32)
        left = borders[:, lane : lane + reach]
        right = borders[:, lane + reach : lane + 2 * reach]
        return jnp.concatenate([blank, left, main, right, blank], axis=1)

    def assemble(pan_ref, table_ref, cm_ref, *rest):
        ins = rest[:groups]
        x_out, s_out, ce_out, fe_out, col_out = rest[groups : groups + 5]
        outs = rest[groups + 5 :]
        me = lax.axis_index("band")

        def gather(row, lane, size):
            rows = [ins[(groups - i) % groups][row, :, lane : lane + size] for i in range(groups)]
            return pltpu.roll(jnp.concatenate(rows, axis=0), nb * me, 0)

        def tile(x, t):
            return x[:, LANES * t : LANES * (t + 1)]

        borders = gather(at_edge, edge_lane, edge_size)
        blank = jnp.zeros((8, LANES * border_tiles - edge_size), F32)
        borders = jnp.concatenate([borders, blank], axis=1)
        for t in range(border_tiles):
            put(outs, at_h + t, tile(borders, t), tile(borders, t))
        mains = [gather(r, 0, wc) for r in range(hc)]
        for r in range(hc):
            x_out[r] = framed(mains[r], borders, 2 * HALO * r, HALO)
        for r in range(HALO):
            for t in range(coarse_tiles):
                put(outs, coarse_tiles * r + t, tile(mains[hc - HALO + r], t), tile(mains[r], t))
        shorts = [gather(at_swir + q // RATIO_S, ws * (q % RATIO_S), ws) for q in range(hs)]
        for q in range(hs):
            s_out[q] = framed(shorts[q], borders, 2 * HALO * hc + 4 * q, 2)
        for q in range(2):
            for t in range(swir_tiles):
                put(outs, at_s + swir_tiles * q + t, tile(shorts[hs - 2 + q], t), tile(shorts[q], t))

        def strip(d, side, empty):
            first = strip_place(d, side)
            rows = []
            for i in range(8 // nb):
                lane = piece * (i % per_row)
                rows.append(ins[d][first + i // per_row, :, lane : lane + piece])
            flat = jnp.where(empty, 0.0, jnp.concatenate(rows, axis=0))
            whole = [flat[:, REACH * t : REACH * (t + 1)] for t in range(h // 8)]
            return jnp.concatenate(whole, axis=0)

        blank = jnp.zeros((h, LANES - REACH), F32)
        left = jnp.concatenate([blank, strip(1, "right", me == 0), pan_ref[:, 0 : 3 * LANES]], axis=1)
        right = jnp.concatenate(
            [pan_ref[:, w - 3 * LANES : w], strip(groups - 1, "left", me == groups - 1), blank], axis=1
        )
        left, right = parts2(left), parts2(right)
        cut = 2 * LANES
        inner = (cut, 6 * LANES)
        lm, lf = shrink(left, take(table_ref, "tall", 0, inner), take(table_ref, "tall_low", 0, inner))
        inner = (0, 4 * LANES)
        rm, rfine = shrink(right, take(table_ref, "tall", 0, inner), take(table_ref, "tall_low", 0, inner))
        rc = both_parts(table_ref, "rows", row_variant(), 3)
        edge = along_rows(rc, jnp.concatenate([lm, rm], axis=1), jnp.concatenate([lf, rfine], axis=1))
        ce_out[...] = edge[0 : 2 * pad]
        outer = tuple(jnp.concatenate([a, b], axis=0) for a, b in zip(left, right))
        col = blocks(dot3(outer, both_parts(table_ref, "fine")), 2)
        col_out[...] = col
        fe_out[...] = filter_rows(take(table_ref, "rows_fine"), col)
        sides = jnp.concatenate([edge[:, :LANES], cm_ref[...], edge[:, LANES:]], axis=1)
        ups, downs = [], []
        for k in range(frame_tiles):
            part = tile(sides, k)
            put(outs, at_ld + k, part[at_up + 8 : at_up + 16], part[at_down + 8 : at_down + 16])
            ups.append(part[at_up : at_up + 2])
            downs.append(part[at_down + HALO - 2 : at_down + HALO])
        put_small(outs, at_d, ups, downs)

    x_loc, s_loc, coarse_edge, fine_edge, col_edge, rest_in, rest_out = call(
        assemble,
        (
            shape(hc, BANDS, wf),
            shape(hs, BANDS, sf),
            shape(2 * pad, 2 * LANES),
            shape(h + 2 * HALO, 4 * LANES),
            shape(h, 4 * LANES),
            shape(sent, 8, LANES),
            shape(sent, 8, LANES),
        ),
        cost=(200_000_000, 3_000_000),
        in_specs=[VMEM] * (groups + 3),
    )(pan_held, table_held, coarse_mid, *got)
    rest_in, rest_out = trade(rest_in, rest_out)

    turns = BANDS // 2 + 1
    block_starts = [LANES * k for k in range(coarse_tiles)]
    own_rows = range(2, hc + 2)
    halo_rows = (0, 1, hc + 2, hc + 3)
    around = (-2, -1) + halo_rows + (hc + 4, hc + 5)

    def lifted(rows, table_ref, store):
        stack = windows(parts2(jnp.concatenate(rows, axis=0)), block_starts, 2 * LANES)
        up = dot3(stack, both_parts(table_ref, "up4"))
        size = 8 * len(rows)
        for k in range(coarse_tiles):
            for q in range(RATIO_V):
                store(RATIO_V * k + q, up[size * k : size * (k + 1), LANES * q : LANES * (q + 1)])

    def grouped(step, size):
        def body(k, carry):
            for i in range(size):
                carry = step(size * k + i, carry)
            return carry

        return body

    def weighted(pairs):
        value = None
        for weight, x in pairs:
            if weight != 0.0:
                value = float(weight) * x if value is None else value + float(weight) * x
        return value

    def inside(
        pan_ref, x_ref, s_ref, fm_ref, fe_ref, col_ref, table_ref, diff_in, q_in,
        y_out, v_out, acc_out, s_out, diff_out, q_out, edge_out, mean_out, lows_out, *outs,
    ):
        def store(index, value):
            y_out[index] = value

        lifted([x_ref[r] for r in range(hc)], table_ref, store)
        rows = parts2(jnp.concatenate([s_ref[q] for q in range(hs)], axis=0))
        s_cols = dot3(windows(rows, block_starts[:swir_tiles], 2 * LANES), both_parts(table_ref, "up3"))
        s_out[...] = blocks(s_cols, swir_tiles)

        diff = jnp.concatenate([pan_ref[:, : 2 * LANES], pan_ref[:, w - 2 * LANES :]], axis=1) - fe_ref[0:h, :]
        adjoint = adjoint_of(table_ref, col_ref[...])
        total = jnp.zeros((1, LANES), F32)
        for k in range(fine_tiles):
            if 2 <= k < fine_tiles - 2:
                at = slice(LANES * (k - 2), LANES * (k - 1))
                up, down = fm_ref[0:HALO, at], fm_ref[HALO:, at]
                total = total + q_in[k, hc + 8 : hc + 9, :]
            else:
                lane = LANES * (k % (fine_tiles - 4))
                at = slice(lane, lane + LANES)
                up, down = fe_ref[h : h + HALO, at], fe_ref[h + HALO :, at]
                diff_out[k] = diff[:, at]
                q_out[k] = adjoint[:, at]
                total = total + adjoint[hc + 8 : hc + 9, at]
            put(outs, k, up, down)

        row_id = lax.axis_index("rows")
        below = jnp.where(row_id > 0, 1.0, 0.0).astype(F32)
        above = jnp.where(row_id < strips - 1, 1.0, 0.0).astype(F32)
        means = {}
        for r in range(-2, hc + 2):
            value = weighted((MEAN4[t + 2], x_ref[r + t]) for t in range(-2, 3) if 0 <= r + t < hc)
            means[r] = value * below if r < 0 else (value * above if r >= hc else value)
        for i, r in enumerate((0, 1, hc - 2, hc - 1)):
            edge_out[i] = means[r]
        rows = parts2(jnp.concatenate([means[r] for r in range(2, hc - 2)], axis=0))
        pair = tuple(x[:, :LANES] for x in both_parts(table_ref, "pair", 0, 3))
        mean_out[...] = blocks(dot3(windows(rows, block_starts, 2 * LANES), pair), coarse_tiles)
        reach = TAPS_S // 2
        for r in range(hc):
            lows_out[r] = weighted((KC[t + reach], means[r + t]) for t in range(-reach, reach + 1) if r + t in means)
        acc_out[turns + 2] = jnp.concatenate([total, jnp.zeros((7, LANES), F32)], axis=0)

        def tile_step(k, carry):
            accs, accv, accp = list(carry[:turns]), carry[turns], carry[turns + 1]
            ys = {m: y_out[k, pl.ds(8 * (m - 2), 8), :] for m in own_rows}
            for m in own_rows:
                z = weighted((gram[m, other], ys[other]) for other in own_rows)
                accs[0] = accs[0] + z * ys[m]
                for i in range(1, turns):
                    accs[i] = accs[i] + z * pltpu.roll(ys[m], i, 0)
                accv = accv + float(rise[m]) * ys[m]
                accp = accp + ys[m] * q_out[k, pl.ds(m + 2, 1), :]
            for m in range(hc):
                for p in range(RATIO_V):
                    r = RATIO_V * m + p
                    v_out[k, pl.ds(8 * r, 8), :] = weighted((C4[t, p], ys[m + t]) for t in range(5) if m + t in ys)
            return tuple(accs) + (accv, accp)

        zero = jnp.zeros((8, LANES), F32)
        first = lax.fori_loop(0, fine_tiles // 2, grouped(tile_step, 2), (zero,) * (turns + 2))
        for i in range(turns + 2):
            acc_out[i] = first[i]

    y_own, v_own, acc_own, s_own, diff, q_own, mean_edge, mean_own, lows_own, low_in, low_out = call(
        inside,
        (
            shape(fine_tiles, 8 * hc, LANES),
            shape(fine_tiles, 8 * h, LANES),
            shape(turns + 3, 8, LANES),
            shape(8 * hs, wc),
            shape(fine_tiles, h, LANES),
            shape(fine_tiles, q_rows, LANES),
            shape(4, BANDS, wf),
            shape(8 * (hc - 4), wc),
            shape(hc, BANDS, wf),
            shape(fine_tiles, 8, LANES),
            shape(fine_tiles, 8, LANES),
        ),
        cost=(2_000_000_000, 8_000_000),
        input_output_aliases={7: 4, 8: 5},
    )(pan_held, x_loc, s_loc, fine_mid, fine_edge, col_edge, table_held, diff_mid, q_mid)
    low_in, low_out = trade(low_in, low_out)

    def moments(
        x_ref, y_ref, acc_ref, scol_ref, q_ref, edge_ref, mean_ref, lows_ref,
        rest_in_ref, rest_out_ref, cm_ref, ce_ref, table_ref,
        mom_out, y_out, ugap_out, dgap_out, s_out,
        both, ulow,
    ):
        me = lax.axis_index("band")
        rest = (rest_in_ref, rest_out_ref)

        def tiles(refs, low, indices):
            return jnp.concatenate([arrived(refs, i, low) for i in indices], axis=1)

        def halo(first, per, reach, start, count):
            sides = []
            for low, base in ((True, start[0]), (False, start[1])):
                borders = tiles(rest, low, range(at_h, at_h + border_tiles))
                rows = []
                for r in range(count):
                    main = tiles(rest, low, range(first + per * r, first + per * (r + 1)))
                    rows.append(framed(main, borders, base + 2 * reach * r, reach))
                sides.append(rows)
            return sides

        x_low, x_high = halo(0, coarse_tiles, HALO, (2 * HALO * (hc - HALO), 0), HALO)

        def x_row(r):
            if r < 0:
                return x_low[HALO + r]
            if r >= hc:
                return x_high[r - hc]
            return x_ref[r]

        def store(index, value):
            y_out[index] = value

        lifted([x_row(m - 2) for m in around], table_ref, store)

        zero = jnp.zeros((8, LANES), F32)

        def tile_step(k, carry):
            accs = list(carry[:turns])
            accp, accv = carry[turns], carry[turns + 1]
            ys = {m: y_ref[k, pl.ds(8 * (m - 2), 8), :] for m in own_rows}
            for i, m in enumerate(around):
                ys[m] = y_out[k, pl.ds(8 * i, 8), :]
            for m in halo_rows:
                near = weighted((gram[m, other], ys[other]) for other in own_rows)
                whole = near + weighted((gram[m, other], ys[other]) for other in halo_rows)
                accs[0] = accs[0] + ys[m] * (near + whole)
                for i in range(1, turns):
                    accs[i] = accs[i] + whole * pltpu.roll(ys[m], i, 0) + ys[m] * pltpu.roll(near, i, 0)
                accv = accv + float(rise[m]) * ys[m]
            for m in around:
                accp = accp + ys[m] * q_ref[k, pl.ds(m + 2, 1), :]
            return tuple(accs) + (accp, accv)

        start = tuple(acc_ref[i] for i in range(turns)) + (acc_ref[turns + 1], acc_ref[turns])
        first = start
        for k in range(fine_tiles):
            first = tile_step(k, first)

        beyond = [r for r in range(-HALO, hc + HALO) if not 0 <= r < hc]
        edges = []
        for i, r in enumerate((0, 1, hc - 2, hc - 1)):
            more = weighted((MEAN4[a - r + 2], x_row(a)) for a in beyond if abs(a - r) <= 2)
            edges.append(edge_ref[i] + more)
        lows = []
        for r in range(hc):
            more = weighted((WIDE[a - r + HALO], x_row(a)) for a in beyond if abs(a - r) <= HALO)
            lows.append(lows_ref[r] + more)
        u_rows = windows(parts2(jnp.concatenate(edges, axis=0)), block_starts, 2 * LANES)
        l_rows = windows(parts2(jnp.concatenate(lows, axis=0)), block_starts, 2 * LANES)
        u_edge = dot3(u_rows, tuple(x[:, :LANES] for x in both_parts(table_ref, "pair", 0, 3)))
        left = jnp.where(me == 0, 1, 0)
        right = jnp.where(me == groups - 1, 2, 0)
        size = 8 * hc
        last = coarse_tiles - 1
        for which, lo_k, hi_k in ((left, 0, 1), (0, 1, last), (right, last, last + 1)):
            if hi_k <= lo_k:
                continue
            wp = tuple(x[:, LANES:] for x in both_parts(table_ref, "pair", which, 3))
            part = dot3(tuple(x[size * lo_k : size * hi_k] for x in l_rows), wp)
            for k in range(lo_k, hi_k):
                at = slice(LANES * k, LANES * (k + 1))
                low_k = part[size * (k - lo_k) : size * (k - lo_k + 1)]
                ulow[:, at] = low_k
                around_k = u_edge[32 * k : 32 * (k + 1)]
                u_k = jnp.concatenate([around_k[0:16], mean_ref[:, at], around_k[16:32]], axis=0)
                ugap_out[:, at] = u_k - low_k

        column = lax.broadcasted_iota(jnp.int32, (1, wf), 1) - HALF + me * wc
        valid = jnp.where((column >= 0) & (column < groups * wc), 1.0, 0.0).astype(F32)

        def own(rows):
            return jnp.concatenate([ce_ref[rows, 0:LANES], cm_ref[rows, :], ce_ref[rows, LANES:]], axis=1)

        def small(low):
            rows = [arrived(rest, at_d + k // 4, low)[2 * (k % 4) : 2 * (k % 4) + 2] for k in range(frame_tiles)]
            return jnp.concatenate(rows, axis=1)

        both[...] = own(slice(0, pad))
        both[0:2] = both[0:2] + small(True)
        both[hc - 2 : hc] = both[hc - 2 : hc] + small(False)
        detail = both[...]
        both[...] = own(slice(pad, 2 * pad))
        both[0:HALO] = both[0:HALO] + tiles(rest, True, range(at_ld, at_ld + frame_tiles))
        both[hc - HALO : hc] = both[hc - HALO : hc] + tiles(rest, False, range(at_ld, at_ld + frame_tiles))
        dlow_rows = windows(parts2(both[...] * valid), block_starts, 2 * LANES)
        dlow = blocks(dot3(dlow_rows, both_parts(table_ref, "low")), coarse_tiles)
        dgap_out[...] = detail[:, HALF : HALF + wc] - dlow
        both[:, 0:wc] = dlow

        s_low, s_high = halo(at_s, swir_tiles, 2, (2 * HALO * hc + 4 * (hs - 2), 2 * HALO * hc), 2)
        s_parts = windows(parts2(jnp.concatenate(s_low + s_high, axis=0)), block_starts[:swir_tiles], 2 * LANES)
        s_around = blocks(dot3(s_parts, both_parts(table_ref, "up3")), swir_tiles)
        s_cols = jnp.concatenate([s_around[0:16], scol_ref[...], s_around[16:32]], axis=0)
        for m in range(hs):
            for p in range(RATIO_S):
                value = None
                for t in range(5):
                    if C3[t, p] != 0.0:
                        term = float(C3[t, p]) * s_cols[8 * (m + t) : 8 * (m + t) + 8]
                        value = term if value is None else value + term
                s_out[RATIO_S * m + p] = value

        ll = [zero] * turns
        cross = [zero] * BANDS
        ld = ls = sd = ss = dd = ds = zero
        for r in range(hc):
            for k in range(coarse_tiles):
                at = slice(LANES * k, LANES * (k + 1))
                u = ulow[8 * r : 8 * r + 8, at]
                s = s_out[r, :, at]
                dl = jnp.broadcast_to(both[r : r + 1, at], (8, LANES))
                ll[0] = ll[0] + u * u
                for i in range(1, turns):
                    ll[i] = ll[i] + u * pltpu.roll(u, i, 0)
                for i in range(BANDS):
                    cross[i] = cross[i] + u * s_out[r, i : i + 1, at]
                ld = ld + u * dl
                sd = sd + s * dl
                ls = ls + u
                ss = ss + s
                dd = dd + dl * dl
                ds = ds + dl

        lane = lax.broadcasted_iota(jnp.int32, (8, LANES), 1)
        sub = lax.broadcasted_iota(jnp.int32, (8, LANES), 0)

        def column_of(acc):
            return jnp.broadcast_to(jnp.sum(acc, axis=1, keepdims=True), (8, LANES))

        table = zero
        for base, accs in ((0, ll), (32, first[:turns])):
            for i in range(turns):
                col = column_of(accs[i])
                table = jnp.where(lane == base + lax.rem(sub + BANDS - i, BANDS), col, table)
                if 0 < i < BANDS // 2:
                    turned = pltpu.roll(col, BANDS - i, 0)
                    table = jnp.where(lane == base + lax.rem(sub + i, BANDS), turned, table)
        singles = [(8 + i, cross[i]) for i in range(BANDS)]
        singles += [(16, ld), (17, ls), (18, sd), (19, ss), (20, dd), (21, ds)]
        singles += [(40, first[turns]), (41, first[turns + 1])]
        for index, acc in singles:
            table = jnp.where(lane == index, column_of(acc), table)
        total = jnp.sum(jnp.sum(acc_ref[turns + 2], axis=0, keepdims=True), axis=1, keepdims=True)
        table = jnp.where(lane == 43, total, table)
        turned = pltpu.roll(table, HALF, 1)
        mom_out[...] = jnp.where(lane[0:4] < HALF, table[0:4], turned[4:8])

    mom, y_halo, ugap, dgap, s_up = call(
        moments,
        (
            shape(4, LANES),
            shape(fine_tiles, 8 * len(around), LANES),
            shape(8 * hc, wc),
            shape(pad, wc),
            shape(hc, BANDS, wc),
        ),
        [
            pltpu.VMEM((pad, wf), F32),
            pltpu.VMEM((8 * hc, wc), F32),
        ],
        cost=(1_000_000_000, 8_000_000),
    )(
        x_loc, y_own, acc_own, s_own, q_own, mean_edge, mean_own, lows_own,
        rest_in, rest_out, coarse_mid, coarse_edge, table_held,
    )
    devices = groups * strips
    mom, low_in, low_out = lax.optimization_barrier((mom, low_in, low_out))
    spread = jnp.broadcast_to(mom[None], (devices,) + mom.shape)
    sums = lax.all_to_all(spread, ("rows", "band"), split_axis=0, concat_axis=0, tiled=True)

    apart_rows = h + 8

    def finish(
        sums_ref, yh_ref, v_ref, diff_ref, low_in_ref, low_out_ref, ugap_ref, dgap_ref, s_ref,
        vnir_out, swir_out, tiles, swir, ends, sems,
    ):
        lane = lax.broadcasted_iota(jnp.int32, (8, LANES), 1)
        sub = lax.broadcasted_iota(jnp.int32, (8, LANES), 0)
        eye = lane == sub
        terms = [sums_ref[index] for index in range(devices)]
        while len(terms) > 1:
            terms = [sum(terms[i : i + 2][1:], terms[i]) for i in range(0, len(terms), 2)]
        total = jnp.concatenate([terms[0], pltpu.roll(terms[0], HALF, 1)], axis=0)

        def column(x, index):
            return jnp.broadcast_to(x[:, index : index + 1], (8, LANES))

        def across(col):
            return jnp.sum(jnp.where(eye, col, 0.0), axis=0, keepdims=True)

        def down(x):
            return jnp.sum(x, axis=0, keepdims=True)

        def solve(matrix, rhs):
            cols = [column(matrix, j) for j in range(BANDS)] + [rhs]
            inverse = jnp.zeros((8, LANES), F32)
            for k in range(BANDS):
                pivot = 1.0 / jnp.broadcast_to(cols[k][k : k + 1], (8, LANES))
                inverse = jnp.where(sub == k, pivot, inverse)
                factor = jnp.where(sub == k, 0.0, cols[k] * pivot)
                for j in range(k + 1, BANDS + 1):
                    cols[j] = cols[j] - factor * jnp.broadcast_to(cols[j][k : k + 1], (8, LANES))
            return cols[BANDS] * inverse

        n1 = 1.0 / fine_pixels
        mean_v = column(total, 41) * n1
        mean_p = column(total, 43) * n1
        cov_v = pltpu.roll(total, LANES - 32, 1) * n1 - mean_v * across(mean_v)
        cov_p = column(total, 40) * n1 - mean_v * mean_p
        gain = cov_p / down(cov_p * solve(cov_v, cov_p))

        n2 = RATIO_V * RATIO_V / fine_pixels
        mean_l = column(total, 17) * n2
        mean_s = column(total, 19) * n2
        mean_d = column(total, 21) * n2
        cov_ll = total * n2 - mean_l * across(mean_l)
        cov_ls = pltpu.roll(total, LANES - 8, 1) * n2 - mean_l * across(mean_s)
        cov_ld = column(total, 16) * n2 - mean_l * mean_d
        cov_sd = column(total, 18) * n2 - mean_s * mean_d
        cov_dd = column(total, 20) * n2 - mean_d * mean_d
        gain_row = across(gain)
        a2 = cov_ll + gain * across(cov_ld) + cov_ld * gain_row + gain * gain_row * cov_dd
        b2 = jnp.where(lane < BANDS, cov_ls + gain * across(cov_sd), 0.0)
        target = jnp.broadcast_to(jnp.sum(b2, axis=1, keepdims=True) / BANDS, (8, LANES))

        def sent_tile(k):
            lanes = pl.ds(pl.multiple_of(LANES * k, LANES), LANES)
            held = tiles.reshape(fine_tiles, BANDS + 1, apart_rows, LANES).at[k, pl.ds(0, BANDS), pl.ds(0, h), :]
            return pltpu.make_async_copy(held, vnir_out.at[:, :, lanes], sems.at[k])

        def tile_step(k, carry):
            ys = {m: yh_ref[k, pl.ds(8 * i, 8), :] for i, m in enumerate(around) if m in halo_rows}
            lows = (low_in_ref, low_out_ref)
            ends[k, 0:HALO, :] = diff_ref[k, 0:HALO, :] - arrived(lows, k, True)
            ends[k, HALO:, :] = diff_ref[k, h - HALO :, :] - arrived(lows, k, False)
            for m in range(hc):
                for p in range(RATIO_V):
                    r = RATIO_V * m + p
                    value = v_ref[k, pl.ds(8 * r, 8), :]
                    more = weighted((C4[t, p], ys[m + t]) for t in range(5) if m + t in ys)
                    if more is not None:
                        value = value + more
                    if r < HALO:
                        detail = ends[k, pl.ds(r, 1), :]
                    elif r >= h - HALO:
                        detail = ends[k, pl.ds(r - h + 2 * HALO, 1), :]
                    else:
                        detail = diff_ref[k, pl.ds(r, 1), :]
                    value = value + gain * detail
                    tiles[k, pl.ds(r, 8, stride=apart_rows), :] = value
            sent_tile(k).start()
            return carry

        beside = max(1, fine_tiles // (BANDS + BANDS // 2))

        def solve_step(k, carry):
            work, inverse = carry
            here = sub == k
            row = down(jnp.where(here, work, 0.0))
            col = jnp.sum(jnp.where(lane == k, work, 0.0), axis=1, keepdims=True)
            pivot = 1.0 / down(jnp.where(here[:, 0:1], col, 0.0))
            inverse = jnp.where(here, pivot, inverse)
            work = work - jnp.where(here, 0.0, col * pivot) * row

            for i in range(beside):
                tile_step(beside * k + i, 0)
            return work, inverse

        start = (jnp.where(lane == BANDS, target, a2), jnp.zeros((8, LANES), F32))
        work, inverse = lax.fori_loop(0, BANDS, solve_step, start)
        fit2 = column(work, BANDS) * inverse
        numer = down(fit2 * b2)
        share_row = numer / down(fit2 * target)
        share = jnp.sum(jnp.where(eye, jnp.broadcast_to(share_row, (8, LANES)), 0.0), axis=1, keepdims=True)
        scale = down(fit2 * gain)[:, 0:1]
        fit_col = fit2[:, 0:1]
        for r in range(hc):
            seen = jnp.sum(fit_col * ugap_ref[8 * r : 8 * r + 8, :], axis=0, keepdims=True)
            seen = seen + scale * dgap_ref[r : r + 1, :]
            swir[r] = s_ref[r] + share * seen
        last = pltpu.make_async_copy(swir, swir_out, sems.at[fine_tiles])
        last.start()

        lax.fori_loop(BANDS * beside, fine_tiles, tile_step, 0)

        def drain(k, carry):
            sent_tile(k).wait()
            return carry

        lax.fori_loop(0, fine_tiles, drain, 0)
        last.wait()

    joined_vnir, joined_swir = call(
        finish,
        (shape(BANDS, h, w), shape(hc, BANDS, wc)),
        [
            pltpu.VMEM((fine_tiles, (BANDS + 1) * apart_rows, LANES), F32),
            pltpu.VMEM((hc, BANDS, wc), F32),
            pltpu.VMEM((fine_tiles, 2 * HALO, LANES), F32),
            pltpu.SemaphoreType.DMA((fine_tiles + 1,)),
        ],
        cost=(100_000_000, 8_000_000),
        out_specs=(ANY, ANY),
    )(sums, y_halo, v_own, diff, low_in, low_out, ugap, dgap, s_up)
    return joined_vnir, jnp.transpose(joined_swir, (1, 0, 2))


def solution(mesh):
    return jax.shard_map(
        local,
        mesh=mesh,
        in_specs=(P("rows", "band"), P("band", "rows", None), P("band", "rows", None)),
        out_specs=(P(None, "rows", "band"), P(None, "rows", "band")),
        check_vma=False,
    )
```

```python
import math

import jax
import jax.numpy as jnp
import ml_dtypes
import numpy as np
from jax import lax
from jax.experimental import pallas as pl
from jax.experimental.pallas import tpu as pltpu
from jax.sharding import PartitionSpec as P

BANDS = 8
RATIO_V = 4
RATIO_S = 3
TAPS_V = 17
TAPS_S = 13
NYQUIST_GAIN = 0.29
LANES = 128
HALF = 64
REACH = 32
HALO = 8
F32 = jnp.float32
BF16 = jnp.bfloat16
VMEM_BYTES = 24 * 1024 * 1024
VMEM_MOST = 56 * 1024 * 1024


def gauss_taps(upscale, kernel_len):
    spread = upscale * math.sqrt(-2.0 * math.log(NYQUIST_GAIN)) / math.pi
    radius = kernel_len // 2
    offsets = np.arange(-radius, radius + 1) * 1.0
    values = np.exp(-(offsets**2) / (2.0 * spread**2))
    return values / values.sum()


def cubic_weight(distance):
    distance = abs(distance)
    if distance <= 1.0:
        return 1.5 * distance**3 - 2.5 * distance**2 + 1.0
    if distance < 2.0:
        return -0.5 * distance**3 + 2.5 * distance**2 - 4.0 * distance + 2.0
    return 0.0


def cubic_table(upscale):
    weights = np.zeros((5, upscale))
    for phase_index in range(upscale):
        centre = (phase_index + 0.5) / upscale - 0.5
        first_tap = math.floor(centre)
        fraction = centre - first_tap
        for tap_index in range(-1, 3):
            weights[first_tap + tap_index + 2, phase_index] += cubic_weight(tap_index - fraction)
    return weights


KF = gauss_taps(RATIO_V, TAPS_V)
KC = gauss_taps(RATIO_S, TAPS_S)
C4 = cubic_table(RATIO_V)
C3 = cubic_table(RATIO_S)
MEAN4 = C4.mean(axis=1)
WIDE = np.convolve(KC, MEAN4)


def split(table):
    high = np.asarray(table, np.float64).astype(np.float32).astype(ml_dtypes.bfloat16)
    low = (np.asarray(table, np.float64) - high.astype(np.float64)).astype(np.float32)
    return np.stack([high, low.astype(ml_dtypes.bfloat16)])


def split3(table):
    high, middle = split(table)
    low = np.asarray(table, np.float64) - high.astype(np.float64) - middle.astype(np.float64)
    return high, middle, low.astype(np.float32).astype(ml_dtypes.bfloat16)


def band_matrix(size, taps):
    radius = len(taps) // 2
    out = np.zeros((size, size))
    for row in range(size):
        for tap in range(-radius, radius + 1):
            if 0 <= row + tap < size:
                out[row, row + tap] = taps[tap + radius]
    return out


def row_tables(h):
    hc = h // RATIO_V
    mean = np.zeros((3 * hc, 3 * h))
    for row in range(3 * hc):
        mean[row, RATIO_V * row : RATIO_V * (row + 1)] = 1.0 / RATIO_V
    fine = band_matrix(3 * h, KF)
    low = band_matrix(3 * hc, KC)
    mean_fine = mean @ fine
    pad = -(-hc // 8) * 8

    def part(matrix, rows, cols):
        return matrix[rows, :][:, cols]

    def stacked(rows, cols, filt):
        a = mean if filt is None else filt @ mean
        c = mean_fine if filt is None else filt @ mean_fine
        return np.concatenate([part(a, rows, cols), -part(c, rows, cols)], axis=1)

    own = slice(h, 2 * h)
    tables = []
    for variant in range(3):
        keep = np.ones(3 * hc)
        if variant == 1:
            keep[:hc] = 0.0
        if variant == 2:
            keep[2 * hc :] = 0.0
        masked = low * keep[None, :]
        rows = []
        for filt in (None, masked):
            block = np.zeros((pad, 2 * h))
            block[:hc] = stacked(slice(hc, 2 * hc), own, filt)
            rows.append(block)
        for filt in (None, low):
            rows.append(stacked(slice(hc, hc + HALO), slice(0, h), filt))
        for filt in (None, low):
            rows.append(stacked(slice(2 * hc - HALO, 2 * hc), slice(2 * h, 3 * h), filt))
        tables.append(np.concatenate(rows, axis=0))
    coarse_rows = np.stack(tables)
    fine_rows = np.concatenate(
        [fine[h : 2 * h, h : 2 * h], fine[h : h + HALO, 0:h], fine[2 * h - HALO : 2 * h, 2 * h : 3 * h]],
        axis=0,
    )
    return coarse_rows, fine_rows


def up_rows(hc):
    out = np.zeros((RATIO_V * hc, hc + 4))
    for m in range(hc):
        for p in range(RATIO_V):
            out[RATIO_V * m + p, m : m + 5] = C4[:, p]
    return out


def adjoint_rows(h):
    hc = h // RATIO_V
    reach = TAPS_V // 2
    size = h + 2 * reach
    lift = np.zeros((size, hc + 8))
    for r in range(size):
        m, p = divmod(r - reach, RATIO_V)
        lift[r, m + 2 : m + 7] = C4[:, p]
    fine = np.zeros((size, h))
    for r in range(size):
        for t in range(-reach, reach + 1):
            if 0 <= r - reach + t < h:
                fine[r, r - reach + t] = KF[t + reach]
    out = np.zeros((3, -(-(hc + 9) // 16) * 16, h))
    for variant in range(3):
        keep = np.ones((size, 1))
        if variant == 1:
            keep[:reach] = 0.0
        if variant == 2:
            keep[h + reach :] = 0.0
        out[variant, : hc + 8] = (lift * keep).T @ fine
        out[variant, hc + 8] = (fine * keep).sum(axis=0)
    return out


def column_tables():
    n = LANES
    fine = np.zeros((4 * n, 2 * n))
    mean = np.zeros((6 * n, n))
    mean_fine = np.zeros((6 * n, n))
    low = np.zeros((2 * n, n))
    pair = np.zeros((3, 2 * n, 2 * n))
    up4 = np.zeros((2 * n, RATIO_V * n))
    up3 = np.zeros((2 * n, RATIO_S * n))
    for c in range(2 * n):
        for t in range(-(TAPS_V // 2), TAPS_V // 2 + 1):
            fine[n + c + t, c] += KF[t + TAPS_V // 2]
    for c in range(n):
        for q in range(RATIO_V):
            mean[n + RATIO_V * c + q, c] = 1.0 / RATIO_V
            for t in range(-(TAPS_V // 2), TAPS_V // 2 + 1):
                mean_fine[n + RATIO_V * c + q + t, c] += KF[t + TAPS_V // 2] / RATIO_V
        for t in range(-(TAPS_S // 2), TAPS_S // 2 + 1):
            low[c + HALF + t, c] += KC[t + TAPS_S // 2]
            for s in range(-2, 3):
                value = KC[t + TAPS_S // 2] * MEAN4[s + 2]
                pair[0, c + HALF + t + s, n + c] += value
                if c + t >= 0:
                    pair[1, c + HALF + t + s, n + c] += value
                if c + t < n:
                    pair[2, c + HALF + t + s, n + c] += value
        for s in range(-2, 3):
            pair[:, c + HALF + s, c] += MEAN4[s + 2]
            for p in range(RATIO_V):
                up4[c + HALF + s, RATIO_V * c + p] += C4[s + 2, p]
            for p in range(RATIO_S):
                up3[c + HALF + s, RATIO_S * c + p] += C3[s + 2, p]
    return dict(fine=fine, mean=mean, mean_fine=mean_fine, low=low, pair=pair, up4=up4, up3=up3)


def stack_tables(tables):
    wide = 2 * LANES
    pieces, place, top = [], {}, 0
    for name, value in tables.items():
        stack = value.reshape((-1,) + value.shape[-2:])
        height, width = stack.shape[1:]
        starts = []
        for lane in range(0, width, wide):
            part = stack[:, :, lane : lane + wide]
            starts.append((top, part.shape[2]))
            piece = np.zeros((stack.shape[0] * height, wide), ml_dtypes.bfloat16)
            piece[:, : part.shape[2]] = part.reshape(-1, part.shape[2])
            pieces.append(piece)
            top += piece.shape[0]
        place[name] = (starts, height, width)
    return np.concatenate(pieces, axis=0), place


def parts2(x):
    high = x.astype(BF16)
    return high, (x - high.astype(F32)).astype(BF16)


def dot(a, b):
    return jnp.dot(a, b, preferred_element_type=F32)


def dot3(x, w):
    return dot(x[0], w[0]) + (dot(x[1], w[0]) + dot(x[0], w[1]))


def windows(x, starts, size):
    return tuple(jnp.concatenate([part[:, a : a + size] for a in starts], axis=0) for part in x)


def blocks(x, count):
    rows = x.shape[0] // count
    return jnp.concatenate([x[rows * k : rows * (k + 1)] for k in range(count)], axis=1)


def call(kernel, out_shape, scratch=(), cost=(0, 0), room=VMEM_BYTES, **specs):
    return pl.pallas_call(
        kernel,
        out_shape=out_shape,
        scratch_shapes=list(scratch),
        compiler_params=pltpu.CompilerParams(vmem_limit_bytes=room),
        cost_estimate=pl.CostEstimate(flops=cost[0], bytes_accessed=cost[1], transcendentals=0),
        **specs,
    )


ANY = pl.BlockSpec(memory_space=pl.ANY)
VMEM = pl.BlockSpec(memory_space=pltpu.VMEM)


def local(pan_image, vnir_bands, swir_bands):
    groups = lax.axis_size("band")
    strips = lax.axis_size("rows")
    h, w = pan_image.shape
    nb, hc, full = vnir_bands.shape
    _, hs, sfull = swir_bands.shape
    wc = w // RATIO_V
    ws = wc // RATIO_S
    wf = wc + LANES
    sf = ws + LANES
    pad = -(-hc // 8) * 8
    fine_tiles = w // LANES
    coarse_tiles = wc // LANES
    frame_tiles = coarse_tiles + 1
    swir_tiles = ws // LANES
    fine_pixels = h * strips * w * groups
    pairs = w // (2 * LANES)
    middle = frame_tiles - 2
    margin = RATIO_V * LANES

    def shape(*dims):
        return jax.ShapeDtypeStruct(dims, F32)

    coarse_rows, fine_rows = row_tables(h)
    cols = column_tables()
    lift = up_rows(hc)
    gram = lift.T @ lift
    rise = lift.sum(axis=0)

    swir_rows = -(-hs // RATIO_S)
    at_swir = hc
    edge_size = 2 * HALO * hc + 4 * hs
    edge_lane = ws * (hs % RATIO_S)
    shared = hs % RATIO_S and edge_lane + edge_size <= wc
    at_edge = hc + swir_rows - 1 if shared else hc + swir_rows
    edge_lane = edge_lane if shared else 0
    at_strip = at_edge + 1
    piece = REACH * (h // 8)
    per_row = wc // piece
    strip_rows = -(-(8 // nb) // per_row)

    def going(d):
        return (["right"] if d == 1 else []) + (["left"] if d == groups - 1 else [])

    def strip_place(d, side):
        return at_strip + strip_rows * going(d).index(side)

    chunk_rows = [at_strip + strip_rows * len(going(d)) for d in range(groups)]

    mean_parts, fine_parts = split(cols["mean"]), split(cols["mean_fine"])
    r_fine = split(fine_rows)
    r_adj = split3(adjoint_rows(h))
    table, place = stack_tables(
        dict(
            tall=np.concatenate([mean_parts[0], fine_parts[0]], axis=1),
            tall_low=fine_parts[1],
            fine=split(cols["fine"]),
            rows=split(coarse_rows),
            rows_fine=np.concatenate([r_fine[0], r_fine[1], r_fine[0]], axis=1),
            low=split(cols["low"]),
            pair=split(cols["pair"]),
            up4=split(cols["up4"]),
            up3=split(cols["up3"]),
            adjoint=np.concatenate([r_adj[i] for i in (0, 0, 0, 1, 1, 2)], axis=2),
        )
    )

    def far(x):
        return pltpu.with_memory_space_constraint(x, pltpu.HBM)

    def pack(pan_ref, vnir_ref, swir_ref, *rest):
        outs, (wide, swide, edges, sems) = rest[:groups], rest[groups:]
        me = lax.axis_index("band")
        copies = [
            pltpu.make_async_copy(vnir_ref, wide.at[:, :, pl.ds(LANES, full)], sems.at[0]),
            pltpu.make_async_copy(swir_ref, swide.at[:, :, pl.ds(LANES, sfull)], sems.at[1]),
            pltpu.make_async_copy(pan_ref.at[:, pl.ds(0, LANES)], edges.at[0], sems.at[2]),
            pltpu.make_async_copy(pan_ref.at[:, pl.ds(w - LANES, LANES)], edges.at[1], sems.at[3]),
        ]
        for copy in copies:
            copy.start()
        wide[:, :, 0:LANES] = jnp.zeros((hc, nb, LANES), F32)
        wide[:, :, LANES + full : 2 * LANES + full] = jnp.zeros((hc, nb, LANES), F32)
        swide[:, :, 0:LANES] = jnp.zeros((nb, hs, LANES), F32)
        swide[:, :, LANES + sfull : 2 * LANES + sfull] = jnp.zeros((nb, hs, LANES), F32)
        for copy in copies:
            copy.wait()
        for d in range(groups):
            peer = lax.rem(me + d, groups)
            base = pl.multiple_of(peer * wc, LANES)
            sbase = pl.multiple_of(peer * ws, LANES)
            out = outs[d]
            out[0:hc] = wide[:, :, pl.ds(base + LANES, wc)]
            left = wide[:, :, pl.ds(base, LANES)]
            right = wide[:, :, pl.ds(base + LANES + wc, LANES)]
            borders = []
            for r in range(hc):
                borders += [left[r, :, LANES - HALO :], right[r, :, :HALO]]
            swin = swide[:, :, pl.ds(sbase, ws + 2 * LANES)]
            for q in range(hs):
                row = swin[:, q, :]
                lane = ws * (q % RATIO_S)
                out[at_swir + q // RATIO_S, :, lane : lane + ws] = row[:, LANES : LANES + ws]
                borders += [row[:, LANES - 2 : LANES], row[:, LANES + ws : LANES + ws + 2]]
            border = jnp.concatenate(borders, axis=1)
            out[at_edge, :, edge_lane : edge_lane + edge_size] = border
            for side in going(d):
                first = strip_place(d, side)
                edge = edges[1, :, LANES - REACH :] if side == "right" else edges[0, :, :REACH]
                flat = jnp.concatenate([edge[8 * t : 8 * t + 8] for t in range(h // 8)], axis=1)
                for i in range(8 // nb):
                    lane = piece * (i % per_row)
                    out[first + i // per_row, :, lane : lane + piece] = flat[nb * i : nb * (i + 1)]

    chunks = call(
        pack,
        tuple(shape(chunk_rows[d], nb, wc) for d in range(groups)),
        [
            pltpu.VMEM((hc, nb, full + 2 * LANES), F32),
            pltpu.VMEM((nb, hs, sfull + 2 * LANES), F32),
            pltpu.VMEM((2, h, LANES), F32),
            pltpu.SemaphoreType.DMA((4,)),
        ],
        cost=(0, 8_000_000),
        in_specs=[ANY] * 3,
    )(*(far(x) for x in (pan_image, jnp.transpose(vnir_bands, (1, 0, 2)), swir_bands)))
    *chunks, pan_late, table_late = lax.optimization_barrier((*chunks, pan_image, jnp.asarray(table)))
    got = [chunks[0]] + [
        lax.ppermute(chunks[d], "band", [(i, (i + d) % groups) for i in range(groups)])
        for d in range(1, groups)
    ]

    def take(ref, name, index=0, rows=None):
        starts, height, width = place[name]
        first, height = (0, height) if rows is None else (rows[0], rows[1] - rows[0])
        pieces = []
        for start, part in starts:
            base = start + first
            if not isinstance(index, int) or index:
                base = pl.multiple_of(base + index * place[name][1], 16)
            pieces.append(ref[pl.ds(base, height), 0:part])
        return pieces[0] if len(pieces) == 1 else jnp.concatenate(pieces, axis=1)

    def both_parts(ref, name, index=0, stacked=1):
        return take(ref, name, index), take(ref, name, index + stacked)

    def shrink(panes, tall, low):
        both = dot(panes[0], tall) + dot(panes[1], tall)
        return both[:, :LANES], both[:, LANES:] + dot(panes[0], low)

    def along_rows(rc, means, fines):
        both = parts2(jnp.concatenate([means, fines], axis=0))
        return dot(rc[0], both[0]) + (dot(rc[0], both[1]) + dot(rc[1], both[0]))

    def filter_rows(rf, x):
        col = parts2(x)
        return dot(rf, jnp.concatenate([col[0], col[0], col[1]], axis=0))

    def row_variant():
        row_id = lax.axis_index("rows")
        return jnp.where(row_id == 0, 1, jnp.where(row_id == strips - 1, 2, 0))

    pairs_in = [(i, i ^ 1) for i in range(strips) if i ^ 1 < strips]
    pairs_out = [(i, i + 1) for i in range(1, strips - 1, 2)]
    pairs_out += [(j, i) for i, j in pairs_out]

    def is_even():
        return lax.rem(lax.axis_index("rows"), 2) == 0

    def put(outs, index, up, down):
        even = is_even()
        outs[0][index] = jnp.where(even, up, down)
        outs[1][index] = jnp.where(even, down, up)

    def arrived(refs, index, low):
        even = is_even()
        inner, outer = refs[0][index], refs[1][index]
        return jnp.where(even, outer, inner) if low else jnp.where(even, inner, outer)

    def trade(inner, outer):
        outer = lax.ppermute(outer, "rows", pairs_out)
        return lax.ppermute(inner, "rows", pairs_in), outer

    at_up, at_down = 2 * pad, 2 * pad + 16

    def put_small(outs, first, ups, downs):
        blank = jnp.zeros((2, LANES), F32)
        for i in range(0, len(ups), 4):
            up = ups[i : i + 4] + [blank] * (4 - len(ups[i : i + 4]))
            down = downs[i : i + 4] + [blank] * (4 - len(downs[i : i + 4]))
            put(outs, first + i // 4, jnp.concatenate(up, axis=0), jnp.concatenate(down, axis=0))

    def adjoint_of(table_ref, col):
        p1 = col.astype(BF16)
        over = col - p1.astype(F32)
        p2 = over.astype(BF16)
        p3 = (over - p2.astype(F32)).astype(BF16)
        weights = take(table_ref, "adjoint", row_variant())
        return dot(weights, jnp.concatenate([p1, p2, p3, p1, p2, p1], axis=0))

    inner_fine = fine_tiles - 4

    def early(pan_far, table_far, pan_ref, table_ref, coarse_out, fine_out, diff_out, q_out, sems):
        now = pl.ds(0, place["low"][0][0][0])
        later = pl.ds(now.size, table.shape[0] - now.size)
        copies = [
            pltpu.make_async_copy(pan_far, pan_ref, sems.at[0]),
            pltpu.make_async_copy(table_far.at[now], table_ref.at[now], sems.at[1]),
            pltpu.make_async_copy(table_far.at[later], table_ref.at[later], sems.at[2]),
        ]
        for copy in copies:
            copy.start()
        copies[0].wait()
        panes = parts2(pan_ref[...])
        copies[1].wait()
        starts = [margin * k - 3 * LANES for k in range(1, frame_tiles - 1)]
        means, fines = shrink(
            windows(panes, starts, 6 * LANES), take(table_ref, "tall"), take(table_ref, "tall_low")
        )
        rc = both_parts(table_ref, "rows", row_variant(), 3)
        coarse_out[...] = along_rows(rc, blocks(means, middle), blocks(fines, middle))
        starts = [2 * LANES * k - LANES for k in range(1, pairs - 1)]
        col = blocks(dot3(windows(panes, starts, 4 * LANES), both_parts(table_ref, "fine")), pairs - 2)
        rows = filter_rows(take(table_ref, "rows_fine"), col)
        fine_out[...] = rows[h:]
        diff = pan_ref[:, 2 * LANES : w - 2 * LANES] - rows[0:h]
        copies[2].wait()
        adjoint = adjoint_of(table_ref, col)
        for k in range(inner_fine):
            at = slice(LANES * k, LANES * (k + 1))
            diff_out[k + 2] = diff[:, at]
            q_out[k + 2] = adjoint[:, at]

    q_rows = -(-(hc + 9) // 16) * 16
    pan_held, table_held, coarse_mid, fine_mid, diff_mid, q_mid = call(
        early,
        (
            shape(h, w),
            jax.ShapeDtypeStruct(table.shape, BF16),
            shape(2 * pad + 32, LANES * middle),
            shape(2 * HALO, LANES * inner_fine),
            shape(fine_tiles, h, LANES),
            shape(fine_tiles, q_rows, LANES),
        ),
        [pltpu.SemaphoreType.DMA((3,))],
        cost=(2_000_000_000, 8_000_000),
        in_specs=[ANY] * 2,
    )(far(pan_late), far(table_late))

    border_tiles = -(-edge_size // LANES)
    at_s = HALO * coarse_tiles
    at_h = at_s + 2 * swir_tiles
    at_ld = at_h + border_tiles
    at_d = at_ld + frame_tiles
    sent = at_d + -(-frame_tiles // 4)

    def framed(main, borders, lane, reach):
        blank = jnp.zeros((8, HALF - reach), F32)
        left = borders[:, lane : lane + reach]
        right = borders[:, lane + reach : lane + 2 * reach]
        return jnp.concatenate([blank, left, main, right, blank], axis=1)

    def assemble(pan_ref, table_ref, cm_ref, *rest):
        ins = rest[:groups]
        x_out, s_out, ce_out, fe_out, col_out = rest[groups : groups + 5]
        outs = rest[groups + 5 :]
        me = lax.axis_index("band")

        def gather(row, lane, size):
            rows = [ins[(groups - i) % groups][row, :, lane : lane + size] for i in range(groups)]
            return pltpu.roll(jnp.concatenate(rows, axis=0), nb * me, 0)

        def tile(x, t):
            return x[:, LANES * t : LANES * (t + 1)]

        borders = gather(at_edge, edge_lane, edge_size)
        blank = jnp.zeros((8, LANES * border_tiles - edge_size), F32)
        borders = jnp.concatenate([borders, blank], axis=1)
        for t in range(border_tiles):
            put(outs, at_h + t, tile(borders, t), tile(borders, t))
        mains = [gather(r, 0, wc) for r in range(hc)]
        for r in range(hc):
            x_out[r] = framed(mains[r], borders, 2 * HALO * r, HALO)
        for r in range(HALO):
            for t in range(coarse_tiles):
                put(outs, coarse_tiles * r + t, tile(mains[hc - HALO + r], t), tile(mains[r], t))
        shorts = [gather(at_swir + q // RATIO_S, ws * (q % RATIO_S), ws) for q in range(hs)]
        for q in range(hs):
            s_out[q] = framed(shorts[q], borders, 2 * HALO * hc + 4 * q, 2)
        for q in range(2):
            for t in range(swir_tiles):
                put(outs, at_s + swir_tiles * q + t, tile(shorts[hs - 2 + q], t), tile(shorts[q], t))

        def strip(d, side, empty):
            first = strip_place(d, side)
            rows = []
            for i in range(8 // nb):
                lane = piece * (i % per_row)
                rows.append(ins[d][first + i // per_row, :, lane : lane + piece])
            flat = jnp.where(empty, 0.0, jnp.concatenate(rows, axis=0))
            whole = [flat[:, REACH * t : REACH * (t + 1)] for t in range(h // 8)]
            return jnp.concatenate(whole, axis=0)

        blank = jnp.zeros((h, LANES - REACH), F32)
        left = jnp.concatenate([blank, strip(1, "right", me == 0), pan_ref[:, 0 : 3 * LANES]], axis=1)
        right = jnp.concatenate(
            [pan_ref[:, w - 3 * LANES : w], strip(groups - 1, "left", me == groups - 1), blank], axis=1
        )
        left, right = parts2(left), parts2(right)
        cut = 2 * LANES
        inner = (cut, 6 * LANES)
        lm, lf = shrink(left, take(table_ref, "tall", 0, inner), take(table_ref, "tall_low", 0, inner))
        inner = (0, 4 * LANES)
        rm, rfine = shrink(right, take(table_ref, "tall", 0, inner), take(table_ref, "tall_low", 0, inner))
        rc = both_parts(table_ref, "rows", row_variant(), 3)
        edge = along_rows(rc, jnp.concatenate([lm, rm], axis=1), jnp.concatenate([lf, rfine], axis=1))
        ce_out[...] = edge[0 : 2 * pad]
        outer = tuple(jnp.concatenate([a, b], axis=0) for a, b in zip(left, right))
        col = blocks(dot3(outer, both_parts(table_ref, "fine")), 2)
        col_out[...] = col
        fe_out[...] = filter_rows(take(table_ref, "rows_fine"), col)
        sides = jnp.concatenate([edge[:, :LANES], cm_ref[...], edge[:, LANES:]], axis=1)
        ups, downs = [], []
        for k in range(frame_tiles):
            part = tile(sides, k)
            put(outs, at_ld + k, part[at_up + 8 : at_up + 16], part[at_down + 8 : at_down + 16])
            ups.append(part[at_up : at_up + 2])
            downs.append(part[at_down + HALO - 2 : at_down + HALO])
        put_small(outs, at_d, ups, downs)

    x_loc, s_loc, coarse_edge, fine_edge, col_edge, rest_in, rest_out = call(
        assemble,
        (
            shape(hc, BANDS, wf),
            shape(hs, BANDS, sf),
            shape(2 * pad, 2 * LANES),
            shape(h + 2 * HALO, 4 * LANES),
            shape(h, 4 * LANES),
            shape(sent, 8, LANES),
            shape(sent, 8, LANES),
        ),
        cost=(200_000_000, 3_000_000),
        in_specs=[VMEM] * (groups + 3),
    )(pan_held, table_held, coarse_mid, *got)
    rest_in, rest_out = trade(rest_in, rest_out)

    turns = BANDS // 2 + 1
    block_starts = [LANES * k for k in range(coarse_tiles)]
    own_rows = range(2, hc + 2)
    halo_rows = (0, 1, hc + 2, hc + 3)
    around = (-2, -1) + halo_rows + (hc + 4, hc + 5)

    def lifted(rows, table_ref, store):
        stack = windows(parts2(jnp.concatenate(rows, axis=0)), block_starts, 2 * LANES)
        up = dot3(stack, both_parts(table_ref, "up4"))
        size = 8 * len(rows)
        for k in range(coarse_tiles):
            for q in range(RATIO_V):
                store(RATIO_V * k + q, up[size * k : size * (k + 1), LANES * q : LANES * (q + 1)])

    def grouped(step, size):
        def body(k, carry):
            for i in range(size):
                carry = step(size * k + i, carry)
            return carry

        return body

    def weighted(pairs):
        value = None
        for weight, x in pairs:
            if weight != 0.0:
                value = float(weight) * x if value is None else value + float(weight) * x
        return value

    def inside(
        pan_ref, x_ref, s_ref, fm_ref, fe_ref, col_ref, table_ref, diff_in, q_in,
        y_out, v_out, acc_out, s_out, diff_out, q_out, *outs,
    ):
        def store(index, value):
            y_out[index] = value

        lifted([x_ref[r] for r in range(hc)], table_ref, store)
        rows = parts2(jnp.concatenate([s_ref[q] for q in range(hs)], axis=0))
        s_cols = dot3(windows(rows, block_starts[:swir_tiles], 2 * LANES), both_parts(table_ref, "up3"))
        s_out[...] = blocks(s_cols, swir_tiles)

        diff = jnp.concatenate([pan_ref[:, : 2 * LANES], pan_ref[:, w - 2 * LANES :]], axis=1) - fe_ref[0:h, :]
        adjoint = adjoint_of(table_ref, col_ref[...])
        total = jnp.zeros((1, LANES), F32)
        for k in range(fine_tiles):
            if 2 <= k < fine_tiles - 2:
                at = slice(LANES * (k - 2), LANES * (k - 1))
                up, down = fm_ref[0:HALO, at], fm_ref[HALO:, at]
                total = total + q_in[k, hc + 8 : hc + 9, :]
            else:
                lane = LANES * (k % (fine_tiles - 4))
                at = slice(lane, lane + LANES)
                up, down = fe_ref[h : h + HALO, at], fe_ref[h + HALO :, at]
                diff_out[k] = diff[:, at]
                q_out[k] = adjoint[:, at]
                total = total + adjoint[hc + 8 : hc + 9, at]
            put(outs, k, up, down)

        acc_out[turns + 2] = jnp.concatenate([total, jnp.zeros((7, LANES), F32)], axis=0)

        def tile_step(k, carry):
            accs, accv, accp = list(carry[:turns]), carry[turns], carry[turns + 1]
            ys = {m: y_out[k, pl.ds(8 * (m - 2), 8), :] for m in own_rows}
            for m in own_rows:
                z = weighted((gram[m, other], ys[other]) for other in own_rows)
                accs[0] = accs[0] + z * ys[m]
                for i in range(1, turns):
                    accs[i] = accs[i] + z * pltpu.roll(ys[m], i, 0)
                accv = accv + float(rise[m]) * ys[m]
                accp = accp + ys[m] * q_out[k, pl.ds(m + 2, 1), :]
            for m in range(hc):
                for p in range(RATIO_V):
                    r = RATIO_V * m + p
                    v_out[k, pl.ds(8 * r, 8), :] = weighted((C4[t, p], ys[m + t]) for t in range(5) if m + t in ys)
            return tuple(accs) + (accv, accp)

        zero = jnp.zeros((8, LANES), F32)
        first = lax.fori_loop(0, fine_tiles // 2, grouped(tile_step, 2), (zero,) * (turns + 2))
        for i in range(turns + 2):
            acc_out[i] = first[i]

    y_own, v_own, acc_own, s_own, diff, q_own, low_in, low_out = call(
        inside,
        (
            shape(fine_tiles, 8 * hc, LANES),
            shape(fine_tiles, 8 * h, LANES),
            shape(turns + 3, 8, LANES),
            shape(8 * hs, wc),
            shape(fine_tiles, h, LANES),
            shape(fine_tiles, q_rows, LANES),
            shape(fine_tiles, 8, LANES),
            shape(fine_tiles, 8, LANES),
        ),
        cost=(2_000_000_000, 8_000_000),
        input_output_aliases={7: 4, 8: 5},
    )(pan_held, x_loc, s_loc, fine_mid, fine_edge, col_edge, table_held, diff_mid, q_mid)
    low_in, low_out = trade(low_in, low_out)

    def means_of(x_ref, table_ref, edge_out, mean_out, lows_out):
        row_id = lax.axis_index("rows")
        below = jnp.where(row_id > 0, 1.0, 0.0).astype(F32)
        above = jnp.where(row_id < strips - 1, 1.0, 0.0).astype(F32)
        means = {}
        for r in range(-2, hc + 2):
            value = weighted((MEAN4[t + 2], x_ref[r + t]) for t in range(-2, 3) if 0 <= r + t < hc)
            means[r] = value * below if r < 0 else (value * above if r >= hc else value)
        for i, r in enumerate((0, 1, hc - 2, hc - 1)):
            edge_out[i] = means[r]
        rows = parts2(jnp.concatenate([means[r] for r in range(2, hc - 2)], axis=0))
        pair = tuple(x[:, :LANES] for x in both_parts(table_ref, "pair", 0, 3))
        mean_out[...] = blocks(dot3(windows(rows, block_starts, 2 * LANES), pair), coarse_tiles)
        reach = TAPS_S // 2
        for r in range(hc):
            lows_out[r] = weighted((KC[t + reach], means[r + t]) for t in range(-reach, reach + 1) if r + t in means)

    mean_edge, mean_own, lows_own = call(
        means_of,
        (shape(4, BANDS, wf), shape(8 * (hc - 4), wc), shape(hc, BANDS, wf)),
        cost=(200_000_000, 3_000_000),
    )(x_loc, table_held)

    def moments(
        x_ref, y_ref, acc_ref, scol_ref, q_ref, edge_ref, mean_ref, lows_ref,
        rest_in_ref, rest_out_ref, cm_ref, ce_ref, table_ref,
        mom_out, y_out, ugap_out, dgap_out, s_out,
        both, ulow,
    ):
        me = lax.axis_index("band")
        rest = (rest_in_ref, rest_out_ref)

        def tiles(refs, low, indices):
            return jnp.concatenate([arrived(refs, i, low) for i in indices], axis=1)

        def halo(first, per, reach, start, count):
            sides = []
            for low, base in ((True, start[0]), (False, start[1])):
                borders = tiles(rest, low, range(at_h, at_h + border_tiles))
                rows = []
                for r in range(count):
                    main = tiles(rest, low, range(first + per * r, first + per * (r + 1)))
                    rows.append(framed(main, borders, base + 2 * reach * r, reach))
                sides.append(rows)
            return sides

        x_low, x_high = halo(0, coarse_tiles, HALO, (2 * HALO * (hc - HALO), 0), HALO)

        def x_row(r):
            if r < 0:
                return x_low[HALO + r]
            if r >= hc:
                return x_high[r - hc]
            return x_ref[r]

        def store(index, value):
            y_out[index] = value

        lifted([x_row(m - 2) for m in around], table_ref, store)

        zero = jnp.zeros((8, LANES), F32)

        def tile_step(k, carry):
            accs = list(carry[:turns])
            accp, accv = carry[turns], carry[turns + 1]
            ys = {m: y_ref[k, pl.ds(8 * (m - 2), 8), :] for m in own_rows}
            for i, m in enumerate(around):
                ys[m] = y_out[k, pl.ds(8 * i, 8), :]
            for m in halo_rows:
                near = weighted((gram[m, other], ys[other]) for other in own_rows)
                whole = near + weighted((gram[m, other], ys[other]) for other in halo_rows)
                accs[0] = accs[0] + ys[m] * (near + whole)
                for i in range(1, turns):
                    accs[i] = accs[i] + whole * pltpu.roll(ys[m], i, 0) + ys[m] * pltpu.roll(near, i, 0)
                accv = accv + float(rise[m]) * ys[m]
            for m in around:
                accp = accp + ys[m] * q_ref[k, pl.ds(m + 2, 1), :]
            return tuple(accs) + (accp, accv)

        start = tuple(acc_ref[i] for i in range(turns)) + (acc_ref[turns + 1], acc_ref[turns])
        first = start
        for k in range(fine_tiles):
            first = tile_step(k, first)

        beyond = [r for r in range(-HALO, hc + HALO) if not 0 <= r < hc]
        edges = []
        for i, r in enumerate((0, 1, hc - 2, hc - 1)):
            more = weighted((MEAN4[a - r + 2], x_row(a)) for a in beyond if abs(a - r) <= 2)
            edges.append(edge_ref[i] + more)
        lows = []
        for r in range(hc):
            more = weighted((WIDE[a - r + HALO], x_row(a)) for a in beyond if abs(a - r) <= HALO)
            lows.append(lows_ref[r] + more)
        u_rows = windows(parts2(jnp.concatenate(edges, axis=0)), block_starts, 2 * LANES)
        l_rows = windows(parts2(jnp.concatenate(lows, axis=0)), block_starts, 2 * LANES)
        u_edge = dot3(u_rows, tuple(x[:, :LANES] for x in both_parts(table_ref, "pair", 0, 3)))
        left = jnp.where(me == 0, 1, 0)
        right = jnp.where(me == groups - 1, 2, 0)
        size = 8 * hc
        last = coarse_tiles - 1
        for which, lo_k, hi_k in ((left, 0, 1), (0, 1, last), (right, last, last + 1)):
            if hi_k <= lo_k:
                continue
            wp = tuple(x[:, LANES:] for x in both_parts(table_ref, "pair", which, 3))
            part = dot3(tuple(x[size * lo_k : size * hi_k] for x in l_rows), wp)
            for k in range(lo_k, hi_k):
                at = slice(LANES * k, LANES * (k + 1))
                low_k = part[size * (k - lo_k) : size * (k - lo_k + 1)]
                ulow[:, at] = low_k
                around_k = u_edge[32 * k : 32 * (k + 1)]
                u_k = jnp.concatenate([around_k[0:16], mean_ref[:, at], around_k[16:32]], axis=0)
                ugap_out[:, at] = u_k - low_k

        column = lax.broadcasted_iota(jnp.int32, (1, wf), 1) - HALF + me * wc
        valid = jnp.where((column >= 0) & (column < groups * wc), 1.0, 0.0).astype(F32)

        def own(rows):
            return jnp.concatenate([ce_ref[rows, 0:LANES], cm_ref[rows, :], ce_ref[rows, LANES:]], axis=1)

        def small(low):
            rows = [arrived(rest, at_d + k // 4, low)[2 * (k % 4) : 2 * (k % 4) + 2] for k in range(frame_tiles)]
            return jnp.concatenate(rows, axis=1)

        both[...] = own(slice(0, pad))
        both[0:2] = both[0:2] + small(True)
        both[hc - 2 : hc] = both[hc - 2 : hc] + small(False)
        detail = both[...]
        both[...] = own(slice(pad, 2 * pad))
        both[0:HALO] = both[0:HALO] + tiles(rest, True, range(at_ld, at_ld + frame_tiles))
        both[hc - HALO : hc] = both[hc - HALO : hc] + tiles(rest, False, range(at_ld, at_ld + frame_tiles))
        dlow_rows = windows(parts2(both[...] * valid), block_starts, 2 * LANES)
        dlow = blocks(dot3(dlow_rows, both_parts(table_ref, "low")), coarse_tiles)
        dgap_out[...] = detail[:, HALF : HALF + wc] - dlow
        both[:, 0:wc] = dlow

        s_low, s_high = halo(at_s, swir_tiles, 2, (2 * HALO * hc + 4 * (hs - 2), 2 * HALO * hc), 2)
        s_parts = windows(parts2(jnp.concatenate(s_low + s_high, axis=0)), block_starts[:swir_tiles], 2 * LANES)
        s_around = blocks(dot3(s_parts, both_parts(table_ref, "up3")), swir_tiles)
        s_cols = jnp.concatenate([s_around[0:16], scol_ref[...], s_around[16:32]], axis=0)
        for m in range(hs):
            for p in range(RATIO_S):
                value = None
                for t in range(5):
                    if C3[t, p] != 0.0:
                        term = float(C3[t, p]) * s_cols[8 * (m + t) : 8 * (m + t) + 8]
                        value = term if value is None else value + term
                s_out[RATIO_S * m + p] = value

        ll = [zero] * turns
        cross = [zero] * BANDS
        ld = ls = sd = ss = dd = ds = zero
        for r in range(hc):
            for k in range(coarse_tiles):
                at = slice(LANES * k, LANES * (k + 1))
                u = ulow[8 * r : 8 * r + 8, at]
                s = s_out[r, :, at]
                dl = jnp.broadcast_to(both[r : r + 1, at], (8, LANES))
                ll[0] = ll[0] + u * u
                for i in range(1, turns):
                    ll[i] = ll[i] + u * pltpu.roll(u, i, 0)
                for i in range(BANDS):
                    cross[i] = cross[i] + u * s_out[r, i : i + 1, at]
                ld = ld + u * dl
                sd = sd + s * dl
                ls = ls + u
                ss = ss + s
                dd = dd + dl * dl
                ds = ds + dl

        lane = lax.broadcasted_iota(jnp.int32, (8, LANES), 1)
        sub = lax.broadcasted_iota(jnp.int32, (8, LANES), 0)

        def column_of(acc):
            return jnp.broadcast_to(jnp.sum(acc, axis=1, keepdims=True), (8, LANES))

        table = zero
        for base, accs in ((0, ll), (16, first[:turns])):
            for i in range(turns):
                col = column_of(accs[i])
                table = jnp.where(lane == base + lax.rem(sub + BANDS - i, BANDS), col, table)
                if 0 < i < BANDS // 2:
                    turned = pltpu.roll(col, BANDS - i, 0)
                    table = jnp.where(lane == base + lax.rem(sub + i, BANDS), turned, table)
        singles = [(8 + i, cross[i]) for i in range(BANDS)]
        singles += [(24, ld), (25, ls), (26, sd), (27, ss), (28, first[turns]), (29, first[turns + 1])]
        for index, acc in singles:
            table = jnp.where(lane == index, column_of(acc), table)
        total = jnp.sum(jnp.sum(acc_ref[turns + 2], axis=0, keepdims=True), axis=1, keepdims=True)
        rest_of = jnp.where(sub == 0, column_of(dd), jnp.where(sub == 1, column_of(ds), total))
        table = jnp.where(lane == 30, rest_of, table)
        packed = table[0:2]
        for q in range(1, 4):
            turned = pltpu.roll(table, 32 * q, 1)
            packed = jnp.where(lane[0:2] >= 32 * q, turned[2 * q : 2 * q + 2], packed)
        mom_out[...] = packed

    mom, y_halo, ugap, dgap, s_up = call(
        moments,
        (
            shape(2, LANES),
            shape(fine_tiles, 8 * len(around), LANES),
            shape(8 * hc, wc),
            shape(pad, wc),
            shape(hc, BANDS, wc),
        ),
        [
            pltpu.VMEM((pad, wf), F32),
            pltpu.VMEM((8 * hc, wc), F32),
        ],
        cost=(1_000_000_000, 8_000_000),
    )(
        x_loc, y_own, acc_own, s_own, q_own, mean_edge, mean_own, lows_own,
        rest_in, rest_out, coarse_mid, coarse_edge, table_held,
    )
    devices = groups * strips
    mom, low_in, low_out = lax.optimization_barrier((mom, low_in, low_out))
    spread = jnp.broadcast_to(mom[None], (devices,) + mom.shape)
    sums = lax.all_to_all(spread, ("rows", "band"), split_axis=0, concat_axis=0, tiled=True)

    apart_rows = h + 8

    def finish(
        sums_ref, yh_ref, v_ref, diff_ref, low_in_ref, low_out_ref, ugap_ref, dgap_ref, s_ref,
        vnir_out, swir_out, tiles, swir, ends, sems,
    ):
        lane = lax.broadcasted_iota(jnp.int32, (8, LANES), 1)
        sub = lax.broadcasted_iota(jnp.int32, (8, LANES), 0)
        eye = lane == sub
        terms = [sums_ref[index] for index in range(devices)]
        while len(terms) > 1:
            terms = [sum(terms[i : i + 2][1:], terms[i]) for i in range(0, len(terms), 2)]
        packed = jnp.concatenate([terms[0]] * 4, axis=0)
        total = packed
        for q in range(1, 4):
            total = jnp.where(sub >= 2 * q, pltpu.roll(packed, LANES - 32 * q, 1), total)

        def single(row):
            return jnp.broadcast_to(total[row : row + 1, 30:31], (8, LANES))


        def column(x, index):
            return jnp.broadcast_to(x[:, index : index + 1], (8, LANES))

        def across(col):
            return jnp.sum(jnp.where(eye, col, 0.0), axis=0, keepdims=True)

        def down(x):
            return jnp.sum(x, axis=0, keepdims=True)

        def solve(matrix, rhs):
            cols = [column(matrix, j) for j in range(BANDS)] + [rhs]
            inverse = jnp.zeros((8, LANES), F32)
            for k in range(BANDS):
                pivot = 1.0 / jnp.broadcast_to(cols[k][k : k + 1], (8, LANES))
                inverse = jnp.where(sub == k, pivot, inverse)
                factor = jnp.where(sub == k, 0.0, cols[k] * pivot)
                for j in range(k + 1, BANDS + 1):
                    cols[j] = cols[j] - factor * jnp.broadcast_to(cols[j][k : k + 1], (8, LANES))
            return cols[BANDS] * inverse

        n1 = 1.0 / fine_pixels
        mean_v = column(total, 29) * n1
        mean_p = single(2) * n1
        cov_v = pltpu.roll(total, LANES - 16, 1) * n1 - mean_v * across(mean_v)
        cov_p = column(total, 28) * n1 - mean_v * mean_p
        gain = cov_p / down(cov_p * solve(cov_v, cov_p))

        n2 = RATIO_V * RATIO_V / fine_pixels
        mean_l = column(total, 25) * n2
        mean_s = column(total, 27) * n2
        mean_d = single(1) * n2
        cov_ll = total * n2 - mean_l * across(mean_l)
        cov_ls = pltpu.roll(total, LANES - 8, 1) * n2 - mean_l * across(mean_s)
        cov_ld = column(total, 24) * n2 - mean_l * mean_d
        cov_sd = column(total, 26) * n2 - mean_s * mean_d
        cov_dd = single(0) * n2 - mean_d * mean_d
        gain_row = across(gain)
        a2 = cov_ll + gain * across(cov_ld) + cov_ld * gain_row + gain * gain_row * cov_dd
        b2 = jnp.where(lane < BANDS, cov_ls + gain * across(cov_sd), 0.0)
        target = jnp.broadcast_to(jnp.sum(b2, axis=1, keepdims=True) / BANDS, (8, LANES))

        def sent_tile(k):
            lanes = pl.ds(pl.multiple_of(LANES * k, LANES), LANES)
            held = tiles.reshape(fine_tiles, BANDS + 1, apart_rows, LANES).at[k, pl.ds(0, BANDS), pl.ds(0, h), :]
            return pltpu.make_async_copy(held, vnir_out.at[:, :, lanes], sems.at[k])

        def tile_step(k, carry):
            ys = {m: yh_ref[k, pl.ds(8 * i, 8), :] for i, m in enumerate(around) if m in halo_rows}
            lows = (low_in_ref, low_out_ref)
            ends[k, 0:HALO, :] = diff_ref[k, 0:HALO, :] - arrived(lows, k, True)
            ends[k, HALO:, :] = diff_ref[k, h - HALO :, :] - arrived(lows, k, False)
            for m in range(hc):
                for p in range(RATIO_V):
                    r = RATIO_V * m + p
                    value = v_ref[k, pl.ds(8 * r, 8), :]
                    more = weighted((C4[t, p], ys[m + t]) for t in range(5) if m + t in ys)
                    if more is not None:
                        value = value + more
                    if r < HALO:
                        detail = ends[k, pl.ds(r, 1), :]
                    elif r >= h - HALO:
                        detail = ends[k, pl.ds(r - h + 2 * HALO, 1), :]
                    else:
                        detail = diff_ref[k, pl.ds(r, 1), :]
                    value = value + gain * detail
                    tiles[k, pl.ds(r, 8, stride=apart_rows), :] = value
            sent_tile(k).start()
            return carry

        beside = max(1, fine_tiles // (BANDS + BANDS // 2))

        def solve_step(k, carry):
            work, inverse = carry
            here = sub == k
            row = down(jnp.where(here, work, 0.0))
            col = jnp.sum(jnp.where(lane == k, work, 0.0), axis=1, keepdims=True)
            pivot = 1.0 / down(jnp.where(here[:, 0:1], col, 0.0))
            inverse = jnp.where(here, pivot, inverse)
            work = work - jnp.where(here, 0.0, col * pivot) * row

            for i in range(beside):
                tile_step(beside * k + i, 0)
            return work, inverse

        start = (jnp.where(lane == BANDS, target, a2), jnp.zeros((8, LANES), F32))
        work, inverse = lax.fori_loop(0, BANDS, solve_step, start)
        fit2 = column(work, BANDS) * inverse
        numer = down(fit2 * b2)
        share_row = numer / down(fit2 * target)
        share = jnp.sum(jnp.where(eye, jnp.broadcast_to(share_row, (8, LANES)), 0.0), axis=1, keepdims=True)
        scale = down(fit2 * gain)[:, 0:1]
        fit_col = fit2[:, 0:1]
        for r in range(hc):
            seen = jnp.sum(fit_col * ugap_ref[8 * r : 8 * r + 8, :], axis=0, keepdims=True)
            seen = seen + scale * dgap_ref[r : r + 1, :]
            swir[r] = s_ref[r] + share * seen
        last = pltpu.make_async_copy(swir, swir_out, sems.at[fine_tiles])
        last.start()

        lax.fori_loop(BANDS * beside, fine_tiles, tile_step, 0)

        def drain(k, carry):
            sent_tile(k).wait()
            return carry

        lax.fori_loop(0, fine_tiles, drain, 0)
        last.wait()

    joined_vnir, joined_swir = call(
        finish,
        (shape(BANDS, h, w), shape(hc, BANDS, wc)),
        [
            pltpu.VMEM((fine_tiles, (BANDS + 1) * apart_rows, LANES), F32),
            pltpu.VMEM((hc, BANDS, wc), F32),
            pltpu.VMEM((fine_tiles, 2 * HALO, LANES), F32),
            pltpu.SemaphoreType.DMA((fine_tiles + 1,)),
        ],
        cost=(100_000_000, 8_000_000),
        out_specs=(ANY, ANY),
    )(sums, y_halo, v_own, diff, low_in, low_out, ugap, dgap, s_up)
    return joined_vnir, jnp.transpose(joined_swir, (1, 0, 2))


def solution(mesh):
    return jax.shard_map(
        local,
        mesh=mesh,
        in_specs=(P("rows", "band"), P("band", "rows", None), P("band", "rows", None)),
        out_specs=(P(None, "rows", "band"), P(None, "rows", "band")),
        check_vma=False,
    )
```

```python
import math

import jax
import jax.numpy as jnp
import ml_dtypes
import numpy as np
from jax import lax
from jax.experimental import pallas as pl
from jax.experimental.pallas import tpu as pltpu
from jax.sharding import PartitionSpec as P

BANDS = 8
RATIO_V = 4
RATIO_S = 3
TAPS_V = 17
TAPS_S = 13
NYQUIST_GAIN = 0.29
LANES = 128
HALF = 64
REACH = 32
HALO = 8
F32 = jnp.float32
BF16 = jnp.bfloat16
VMEM_BYTES = 24 * 1024 * 1024
VMEM_MOST = 56 * 1024 * 1024


def gauss_taps(upscale, kernel_len):
    spread = upscale * math.sqrt(-2.0 * math.log(NYQUIST_GAIN)) / math.pi
    radius = kernel_len // 2
    offsets = np.arange(-radius, radius + 1) * 1.0
    values = np.exp(-(offsets**2) / (2.0 * spread**2))
    return values / values.sum()


def cubic_weight(distance):
    distance = abs(distance)
    if distance <= 1.0:
        return 1.5 * distance**3 - 2.5 * distance**2 + 1.0
    if distance < 2.0:
        return -0.5 * distance**3 + 2.5 * distance**2 - 4.0 * distance + 2.0
    return 0.0


def cubic_table(upscale):
    weights = np.zeros((5, upscale))
    for phase_index in range(upscale):
        centre = (phase_index + 0.5) / upscale - 0.5
        first_tap = math.floor(centre)
        fraction = centre - first_tap
        for tap_index in range(-1, 3):
            weights[first_tap + tap_index + 2, phase_index] += cubic_weight(tap_index - fraction)
    return weights


KF = gauss_taps(RATIO_V, TAPS_V)
KC = gauss_taps(RATIO_S, TAPS_S)
C4 = cubic_table(RATIO_V)
C3 = cubic_table(RATIO_S)
MEAN4 = C4.mean(axis=1)
WIDE = np.convolve(KC, MEAN4)


def split(table):
    high = np.asarray(table, np.float64).astype(np.float32).astype(ml_dtypes.bfloat16)
    low = (np.asarray(table, np.float64) - high.astype(np.float64)).astype(np.float32)
    return np.stack([high, low.astype(ml_dtypes.bfloat16)])


def split3(table):
    high, middle = split(table)
    low = np.asarray(table, np.float64) - high.astype(np.float64) - middle.astype(np.float64)
    return high, middle, low.astype(np.float32).astype(ml_dtypes.bfloat16)


def band_matrix(size, taps):
    radius = len(taps) // 2
    out = np.zeros((size, size))
    for row in range(size):
        for tap in range(-radius, radius + 1):
            if 0 <= row + tap < size:
                out[row, row + tap] = taps[tap + radius]
    return out


def row_tables(h):
    hc = h // RATIO_V
    mean = np.zeros((3 * hc, 3 * h))
    for row in range(3 * hc):
        mean[row, RATIO_V * row : RATIO_V * (row + 1)] = 1.0 / RATIO_V
    fine = band_matrix(3 * h, KF)
    low = band_matrix(3 * hc, KC)
    mean_fine = mean @ fine
    pad = -(-hc // 8) * 8

    def part(matrix, rows, cols):
        return matrix[rows, :][:, cols]

    def stacked(rows, cols, filt):
        a = mean if filt is None else filt @ mean
        c = mean_fine if filt is None else filt @ mean_fine
        return np.concatenate([part(a, rows, cols), -part(c, rows, cols)], axis=1)

    own = slice(h, 2 * h)
    tables = []
    for variant in range(3):
        keep = np.ones(3 * hc)
        if variant == 1:
            keep[:hc] = 0.0
        if variant == 2:
            keep[2 * hc :] = 0.0
        masked = low * keep[None, :]
        rows = []
        for filt in (None, masked):
            block = np.zeros((pad, 2 * h))
            block[:hc] = stacked(slice(hc, 2 * hc), own, filt)
            rows.append(block)
        for filt in (None, low):
            rows.append(stacked(slice(hc, hc + HALO), slice(0, h), filt))
        for filt in (None, low):
            rows.append(stacked(slice(2 * hc - HALO, 2 * hc), slice(2 * h, 3 * h), filt))
        tables.append(np.concatenate(rows, axis=0))
    coarse_rows = np.stack(tables)
    fine_rows = np.concatenate(
        [fine[h : 2 * h, h : 2 * h], fine[h : h + HALO, 0:h], fine[2 * h - HALO : 2 * h, 2 * h : 3 * h]],
        axis=0,
    )
    return coarse_rows, fine_rows


def up_rows(hc):
    out = np.zeros((RATIO_V * hc, hc + 4))
    for m in range(hc):
        for p in range(RATIO_V):
            out[RATIO_V * m + p, m : m + 5] = C4[:, p]
    return out


def adjoint_rows(h):
    hc = h // RATIO_V
    reach = TAPS_V // 2
    size = h + 2 * reach
    lift = np.zeros((size, hc + 8))
    for r in range(size):
        m, p = divmod(r - reach, RATIO_V)
        lift[r, m + 2 : m + 7] = C4[:, p]
    fine = np.zeros((size, h))
    for r in range(size):
        for t in range(-reach, reach + 1):
            if 0 <= r - reach + t < h:
                fine[r, r - reach + t] = KF[t + reach]
    out = np.zeros((3, -(-(hc + 9) // 16) * 16, h))
    for variant in range(3):
        keep = np.ones((size, 1))
        if variant == 1:
            keep[:reach] = 0.0
        if variant == 2:
            keep[h + reach :] = 0.0
        out[variant, : hc + 8] = (lift * keep).T @ fine
        out[variant, hc + 8] = (fine * keep).sum(axis=0)
    return out


def column_tables():
    n = LANES
    fine = np.zeros((4 * n, 2 * n))
    mean = np.zeros((6 * n, n))
    mean_fine = np.zeros((6 * n, n))
    low = np.zeros((2 * n, n))
    pair = np.zeros((3, 2 * n, 2 * n))
    up4 = np.zeros((2 * n, RATIO_V * n))
    up3 = np.zeros((2 * n, RATIO_S * n))
    for c in range(2 * n):
        for t in range(-(TAPS_V // 2), TAPS_V // 2 + 1):
            fine[n + c + t, c] += KF[t + TAPS_V // 2]
    for c in range(n):
        for q in range(RATIO_V):
            mean[n + RATIO_V * c + q, c] = 1.0 / RATIO_V
            for t in range(-(TAPS_V // 2), TAPS_V // 2 + 1):
                mean_fine[n + RATIO_V * c + q + t, c] += KF[t + TAPS_V // 2] / RATIO_V
        for t in range(-(TAPS_S // 2), TAPS_S // 2 + 1):
            low[c + HALF + t, c] += KC[t + TAPS_S // 2]
            for s in range(-2, 3):
                value = KC[t + TAPS_S // 2] * MEAN4[s + 2]
                pair[0, c + HALF + t + s, n + c] += value
                if c + t >= 0:
                    pair[1, c + HALF + t + s, n + c] += value
                if c + t < n:
                    pair[2, c + HALF + t + s, n + c] += value
        for s in range(-2, 3):
            pair[:, c + HALF + s, c] += MEAN4[s + 2]
            for p in range(RATIO_V):
                up4[c + HALF + s, RATIO_V * c + p] += C4[s + 2, p]
            for p in range(RATIO_S):
                up3[c + HALF + s, RATIO_S * c + p] += C3[s + 2, p]
    return dict(fine=fine, mean=mean, mean_fine=mean_fine, low=low, pair=pair, up4=up4, up3=up3)


def stack_tables(tables):
    wide = 2 * LANES
    pieces, place, top = [], {}, 0
    for name, value in tables.items():
        stack = value.reshape((-1,) + value.shape[-2:])
        height, width = stack.shape[1:]
        starts = []
        for lane in range(0, width, wide):
            part = stack[:, :, lane : lane + wide]
            starts.append((top, part.shape[2]))
            piece = np.zeros((stack.shape[0] * height, wide), ml_dtypes.bfloat16)
            piece[:, : part.shape[2]] = part.reshape(-1, part.shape[2])
            pieces.append(piece)
            top += piece.shape[0]
        place[name] = (starts, height, width)
    return np.concatenate(pieces, axis=0), place


def parts2(x):
    high = x.astype(BF16)
    return high, (x - high.astype(F32)).astype(BF16)


def dot(a, b):
    return jnp.dot(a, b, preferred_element_type=F32)


def dot3(x, w):
    return dot(x[0], w[0]) + (dot(x[1], w[0]) + dot(x[0], w[1]))


def windows(x, starts, size):
    return tuple(jnp.concatenate([part[:, a : a + size] for a in starts], axis=0) for part in x)


def blocks(x, count):
    rows = x.shape[0] // count
    return jnp.concatenate([x[rows * k : rows * (k + 1)] for k in range(count)], axis=1)


def call(kernel, out_shape, scratch=(), cost=(0, 0), room=VMEM_BYTES, **specs):
    return pl.pallas_call(
        kernel,
        out_shape=out_shape,
        scratch_shapes=list(scratch),
        compiler_params=pltpu.CompilerParams(vmem_limit_bytes=room),
        cost_estimate=pl.CostEstimate(flops=cost[0], bytes_accessed=cost[1], transcendentals=0),
        **specs,
    )


ANY = pl.BlockSpec(memory_space=pl.ANY)
VMEM = pl.BlockSpec(memory_space=pltpu.VMEM)


def local(pan_image, vnir_bands, swir_bands):
    groups = lax.axis_size("band")
    strips = lax.axis_size("rows")
    h, w = pan_image.shape
    nb, hc, full = vnir_bands.shape
    _, hs, sfull = swir_bands.shape
    wc = w // RATIO_V
    ws = wc // RATIO_S
    wf = wc + LANES
    sf = ws + LANES
    pad = -(-hc // 8) * 8
    fine_tiles = w // LANES
    coarse_tiles = wc // LANES
    frame_tiles = coarse_tiles + 1
    swir_tiles = ws // LANES
    fine_pixels = h * strips * w * groups
    pairs = w // (2 * LANES)
    middle = frame_tiles - 2
    margin = RATIO_V * LANES

    def shape(*dims):
        return jax.ShapeDtypeStruct(dims, F32)

    coarse_rows, fine_rows = row_tables(h)
    cols = column_tables()
    lift = up_rows(hc)
    gram = lift.T @ lift
    rise = lift.sum(axis=0)

    swir_rows = -(-hs // RATIO_S)
    at_swir = hc
    edge_size = 2 * HALO * hc + 4 * hs
    edge_lane = ws * (hs % RATIO_S)
    shared = hs % RATIO_S and edge_lane + edge_size <= wc
    at_edge = hc + swir_rows - 1 if shared else hc + swir_rows
    edge_lane = edge_lane if shared else 0
    at_strip = at_edge + 1
    piece = REACH * (h // 8)
    per_row = wc // piece
    strip_rows = -(-(8 // nb) // per_row)

    def going(d):
        return (["right"] if d == 1 else []) + (["left"] if d == groups - 1 else [])

    def strip_place(d, side):
        return at_strip + strip_rows * going(d).index(side)

    chunk_rows = [at_strip + strip_rows * len(going(d)) for d in range(groups)]

    mean_parts, fine_parts = split(cols["mean"]), split(cols["mean_fine"])
    r_fine = split(fine_rows)
    r_adj = split3(adjoint_rows(h))
    table, place = stack_tables(
        dict(
            tall=np.concatenate([mean_parts[0], fine_parts[0]], axis=1),
            tall_low=fine_parts[1],
            fine=split(cols["fine"]),
            rows=split(coarse_rows),
            rows_fine=np.concatenate([r_fine[0], r_fine[1], r_fine[0]], axis=1),
            low=split(cols["low"]),
            pair=split(cols["pair"]),
            up4=split(cols["up4"]),
            up3=split(cols["up3"]),
            adjoint=np.concatenate([r_adj[i] for i in (0, 0, 0, 1, 1, 2)], axis=2),
        )
    )

    def far(x):
        return pltpu.with_memory_space_constraint(x, pltpu.HBM)

    def pack(pan_ref, vnir_ref, swir_ref, *rest):
        outs, (wide, swide, edges, sems) = rest[:groups], rest[groups:]
        me = lax.axis_index("band")
        copies = [
            pltpu.make_async_copy(vnir_ref, wide.at[:, :, pl.ds(LANES, full)], sems.at[0]),
            pltpu.make_async_copy(swir_ref, swide.at[:, :, pl.ds(LANES, sfull)], sems.at[1]),
            pltpu.make_async_copy(pan_ref.at[:, pl.ds(0, LANES)], edges.at[0], sems.at[2]),
            pltpu.make_async_copy(pan_ref.at[:, pl.ds(w - LANES, LANES)], edges.at[1], sems.at[3]),
        ]
        for copy in copies:
            copy.start()
        wide[:, :, 0:LANES] = jnp.zeros((hc, nb, LANES), F32)
        wide[:, :, LANES + full : 2 * LANES + full] = jnp.zeros((hc, nb, LANES), F32)
        swide[:, :, 0:LANES] = jnp.zeros((nb, hs, LANES), F32)
        swide[:, :, LANES + sfull : 2 * LANES + sfull] = jnp.zeros((nb, hs, LANES), F32)
        for copy in copies:
            copy.wait()
        for d in range(groups):
            peer = lax.rem(me + d, groups)
            base = pl.multiple_of(peer * wc, LANES)
            sbase = pl.multiple_of(peer * ws, LANES)
            out = outs[d]
            out[0:hc] = wide[:, :, pl.ds(base + LANES, wc)]
            left = wide[:, :, pl.ds(base, LANES)]
            right = wide[:, :, pl.ds(base + LANES + wc, LANES)]
            borders = []
            for r in range(hc):
                borders += [left[r, :, LANES - HALO :], right[r, :, :HALO]]
            swin = swide[:, :, pl.ds(sbase, ws + 2 * LANES)]
            for q in range(hs):
                row = swin[:, q, :]
                lane = ws * (q % RATIO_S)
                out[at_swir + q // RATIO_S, :, lane : lane + ws] = row[:, LANES : LANES + ws]
                borders += [row[:, LANES - 2 : LANES], row[:, LANES + ws : LANES + ws + 2]]
            border = jnp.concatenate(borders, axis=1)
            out[at_edge, :, edge_lane : edge_lane + edge_size] = border
            for side in going(d):
                first = strip_place(d, side)
                edge = edges[1, :, LANES - REACH :] if side == "right" else edges[0, :, :REACH]
                flat = jnp.concatenate([edge[8 * t : 8 * t + 8] for t in range(h // 8)], axis=1)
                for i in range(8 // nb):
                    lane = piece * (i % per_row)
                    out[first + i // per_row, :, lane : lane + piece] = flat[nb * i : nb * (i + 1)]

    chunks = call(
        pack,
        tuple(shape(chunk_rows[d], nb, wc) for d in range(groups)),
        [
            pltpu.VMEM((hc, nb, full + 2 * LANES), F32),
            pltpu.VMEM((nb, hs, sfull + 2 * LANES), F32),
            pltpu.VMEM((2, h, LANES), F32),
            pltpu.SemaphoreType.DMA((4,)),
        ],
        cost=(0, 8_000_000),
        in_specs=[ANY] * 3,
    )(*(far(x) for x in (pan_image, jnp.transpose(vnir_bands, (1, 0, 2)), swir_bands)))
    *chunks, pan_late, table_late = lax.optimization_barrier((*chunks, pan_image, jnp.asarray(table)))
    got = [chunks[0]] + [
        lax.ppermute(chunks[d], "band", [(i, (i + d) % groups) for i in range(groups)])
        for d in range(1, groups)
    ]

    def take(ref, name, index=0, rows=None):
        starts, height, width = place[name]
        first, height = (0, height) if rows is None else (rows[0], rows[1] - rows[0])
        pieces = []
        for start, part in starts:
            base = start + first
            if not isinstance(index, int) or index:
                base = pl.multiple_of(base + index * place[name][1], 16)
            pieces.append(ref[pl.ds(base, height), 0:part])
        return pieces[0] if len(pieces) == 1 else jnp.concatenate(pieces, axis=1)

    def both_parts(ref, name, index=0, stacked=1):
        return take(ref, name, index), take(ref, name, index + stacked)

    def shrink(panes, tall, low):
        both = dot(panes[0], tall) + dot(panes[1], tall)
        return both[:, :LANES], both[:, LANES:] + dot(panes[0], low)

    def along_rows(rc, means, fines):
        both = parts2(jnp.concatenate([means, fines], axis=0))
        return dot(rc[0], both[0]) + (dot(rc[0], both[1]) + dot(rc[1], both[0]))

    def filter_rows(rf, x):
        col = parts2(x)
        return dot(rf, jnp.concatenate([col[0], col[0], col[1]], axis=0))

    def row_variant():
        row_id = lax.axis_index("rows")
        return jnp.where(row_id == 0, 1, jnp.where(row_id == strips - 1, 2, 0))

    pairs_in = [(i, i ^ 1) for i in range(strips) if i ^ 1 < strips]
    pairs_out = [(i, i + 1) for i in range(1, strips - 1, 2)]
    pairs_out += [(j, i) for i, j in pairs_out]

    def is_even():
        return lax.rem(lax.axis_index("rows"), 2) == 0

    def put(outs, index, up, down):
        even = is_even()
        outs[0][index] = jnp.where(even, up, down)
        outs[1][index] = jnp.where(even, down, up)

    def arrived(refs, index, low):
        even = is_even()
        inner, outer = refs[0][index], refs[1][index]
        return jnp.where(even, outer, inner) if low else jnp.where(even, inner, outer)

    def trade(inner, outer):
        outer = lax.ppermute(outer, "rows", pairs_out)
        return lax.ppermute(inner, "rows", pairs_in), outer

    at_up, at_down = 2 * pad, 2 * pad + 16

    def put_small(outs, first, ups, downs):
        blank = jnp.zeros((2, LANES), F32)
        for i in range(0, len(ups), 4):
            up = ups[i : i + 4] + [blank] * (4 - len(ups[i : i + 4]))
            down = downs[i : i + 4] + [blank] * (4 - len(downs[i : i + 4]))
            put(outs, first + i // 4, jnp.concatenate(up, axis=0), jnp.concatenate(down, axis=0))

    def adjoint_of(table_ref, col):
        p1 = col.astype(BF16)
        over = col - p1.astype(F32)
        p2 = over.astype(BF16)
        p3 = (over - p2.astype(F32)).astype(BF16)
        weights = take(table_ref, "adjoint", row_variant())
        return dot(weights, jnp.concatenate([p1, p2, p3, p1, p2, p1], axis=0))

    inner_fine = fine_tiles - 4

    def early(pan_far, table_far, pan_ref, table_ref, coarse_out, fine_out, diff_out, q_out, sems):
        now = pl.ds(0, place["low"][0][0][0])
        later = pl.ds(now.size, table.shape[0] - now.size)
        copies = [
            pltpu.make_async_copy(pan_far, pan_ref, sems.at[0]),
            pltpu.make_async_copy(table_far.at[now], table_ref.at[now], sems.at[1]),
            pltpu.make_async_copy(table_far.at[later], table_ref.at[later], sems.at[2]),
        ]
        for copy in copies:
            copy.start()
        copies[0].wait()
        panes = parts2(pan_ref[...])
        copies[1].wait()
        starts = [margin * k - 3 * LANES for k in range(1, frame_tiles - 1)]
        means, fines = shrink(
            windows(panes, starts, 6 * LANES), take(table_ref, "tall"), take(table_ref, "tall_low")
        )
        rc = both_parts(table_ref, "rows", row_variant(), 3)
        coarse_out[...] = along_rows(rc, blocks(means, middle), blocks(fines, middle))
        starts = [2 * LANES * k - LANES for k in range(1, pairs - 1)]
        col = blocks(dot3(windows(panes, starts, 4 * LANES), both_parts(table_ref, "fine")), pairs - 2)
        rows = filter_rows(take(table_ref, "rows_fine"), col)
        fine_out[...] = rows[h:]
        diff = pan_ref[:, 2 * LANES : w - 2 * LANES] - rows[0:h]
        copies[2].wait()
        adjoint = adjoint_of(table_ref, col)
        for k in range(inner_fine):
            at = slice(LANES * k, LANES * (k + 1))
            diff_out[k + 2] = diff[:, at]
            q_out[k + 2] = adjoint[:, at]

    q_rows = -(-(hc + 9) // 16) * 16
    pan_held, table_held, coarse_mid, fine_mid, diff_mid, q_mid = call(
        early,
        (
            shape(h, w),
            jax.ShapeDtypeStruct(table.shape, BF16),
            shape(2 * pad + 32, LANES * middle),
            shape(2 * HALO, LANES * inner_fine),
            shape(fine_tiles, h, LANES),
            shape(fine_tiles, q_rows, LANES),
        ),
        [pltpu.SemaphoreType.DMA((3,))],
        cost=(2_000_000_000, 8_000_000),
        in_specs=[ANY] * 2,
    )(far(pan_late), far(table_late))

    border_tiles = -(-edge_size // LANES)
    at_s = HALO * coarse_tiles
    at_h = at_s + 2 * swir_tiles
    at_ld = at_h + border_tiles
    at_d = at_ld + frame_tiles
    sent = at_d + -(-frame_tiles // 4)

    def framed(main, borders, lane, reach):
        blank = jnp.zeros((8, HALF - reach), F32)
        left = borders[:, lane : lane + reach]
        right = borders[:, lane + reach : lane + 2 * reach]
        return jnp.concatenate([blank, left, main, right, blank], axis=1)

    def assemble(pan_ref, table_ref, cm_ref, *rest):
        ins = rest[:groups]
        x_out, s_out, ce_out, fe_out, col_out = rest[groups : groups + 5]
        outs = rest[groups + 5 :]
        me = lax.axis_index("band")

        def gather(row, lane, size):
            rows = [ins[(groups - i) % groups][row, :, lane : lane + size] for i in range(groups)]
            return pltpu.roll(jnp.concatenate(rows, axis=0), nb * me, 0)

        def tile(x, t):
            return x[:, LANES * t : LANES * (t + 1)]

        borders = gather(at_edge, edge_lane, edge_size)
        blank = jnp.zeros((8, LANES * border_tiles - edge_size), F32)
        borders = jnp.concatenate([borders, blank], axis=1)
        for t in range(border_tiles):
            put(outs, at_h + t, tile(borders, t), tile(borders, t))
        mains = [gather(r, 0, wc) for r in range(hc)]
        for r in range(hc):
            x_out[r] = framed(mains[r], borders, 2 * HALO * r, HALO)
        for r in range(HALO):
            for t in range(coarse_tiles):
                put(outs, coarse_tiles * r + t, tile(mains[hc - HALO + r], t), tile(mains[r], t))
        shorts = [gather(at_swir + q // RATIO_S, ws * (q % RATIO_S), ws) for q in range(hs)]
        for q in range(hs):
            s_out[q] = framed(shorts[q], borders, 2 * HALO * hc + 4 * q, 2)
        for q in range(2):
            for t in range(swir_tiles):
                put(outs, at_s + swir_tiles * q + t, tile(shorts[hs - 2 + q], t), tile(shorts[q], t))

        def strip(d, side, empty):
            first = strip_place(d, side)
            rows = []
            for i in range(8 // nb):
                lane = piece * (i % per_row)
                rows.append(ins[d][first + i // per_row, :, lane : lane + piece])
            flat = jnp.where(empty, 0.0, jnp.concatenate(rows, axis=0))
            whole = [flat[:, REACH * t : REACH * (t + 1)] for t in range(h // 8)]
            return jnp.concatenate(whole, axis=0)

        blank = jnp.zeros((h, LANES - REACH), F32)
        left = jnp.concatenate([blank, strip(1, "right", me == 0), pan_ref[:, 0 : 3 * LANES]], axis=1)
        right = jnp.concatenate(
            [pan_ref[:, w - 3 * LANES : w], strip(groups - 1, "left", me == groups - 1), blank], axis=1
        )
        left, right = parts2(left), parts2(right)
        cut = 2 * LANES
        inner = (cut, 6 * LANES)
        lm, lf = shrink(left, take(table_ref, "tall", 0, inner), take(table_ref, "tall_low", 0, inner))
        inner = (0, 4 * LANES)
        rm, rfine = shrink(right, take(table_ref, "tall", 0, inner), take(table_ref, "tall_low", 0, inner))
        rc = both_parts(table_ref, "rows", row_variant(), 3)
        edge = along_rows(rc, jnp.concatenate([lm, rm], axis=1), jnp.concatenate([lf, rfine], axis=1))
        ce_out[...] = edge[0 : 2 * pad]
        outer = tuple(jnp.concatenate([a, b], axis=0) for a, b in zip(left, right))
        col = blocks(dot3(outer, both_parts(table_ref, "fine")), 2)
        col_out[...] = col
        fe_out[...] = filter_rows(take(table_ref, "rows_fine"), col)
        sides = jnp.concatenate([edge[:, :LANES], cm_ref[...], edge[:, LANES:]], axis=1)
        ups, downs = [], []
        for k in range(frame_tiles):
            part = tile(sides, k)
            put(outs, at_ld + k, part[at_up + 8 : at_up + 16], part[at_down + 8 : at_down + 16])
            ups.append(part[at_up : at_up + 2])
            downs.append(part[at_down + HALO - 2 : at_down + HALO])
        put_small(outs, at_d, ups, downs)

    x_loc, s_loc, coarse_edge, fine_edge, col_edge, rest_in, rest_out = call(
        assemble,
        (
            shape(hc, BANDS, wf),
            shape(hs, BANDS, sf),
            shape(2 * pad, 2 * LANES),
            shape(h + 2 * HALO, 4 * LANES),
            shape(h, 4 * LANES),
            shape(sent, 8, LANES),
            shape(sent, 8, LANES),
        ),
        cost=(200_000_000, 3_000_000),
        in_specs=[VMEM] * (groups + 3),
    )(pan_held, table_held, coarse_mid, *got)
    rest_in, rest_out = trade(rest_in, rest_out)

    turns = BANDS // 2 + 1
    block_starts = [LANES * k for k in range(coarse_tiles)]
    own_rows = range(2, hc + 2)
    halo_rows = (0, 1, hc + 2, hc + 3)
    around = (-2, -1) + halo_rows + (hc + 4, hc + 5)

    def lifted(rows, table_ref, store):
        stack = windows(parts2(jnp.concatenate(rows, axis=0)), block_starts, 2 * LANES)
        up = dot3(stack, both_parts(table_ref, "up4"))
        size = 8 * len(rows)
        for k in range(coarse_tiles):
            for q in range(RATIO_V):
                store(RATIO_V * k + q, up[size * k : size * (k + 1), LANES * q : LANES * (q + 1)])

    def grouped(step, size):
        def body(k, carry):
            for i in range(size):
                carry = step(size * k + i, carry)
            return carry

        return body

    def weighted(pairs):
        value = None
        for weight, x in pairs:
            if weight != 0.0:
                value = float(weight) * x if value is None else value + float(weight) * x
        return value

    def inside(
        pan_ref, x_ref, s_ref, fm_ref, fe_ref, col_ref, table_ref, diff_in, q_in,
        y_out, v_out, acc_out, s_out, diff_out, q_out, *outs,
    ):
        def store(index, value):
            y_out[index] = value

        lifted([x_ref[r] for r in range(hc)], table_ref, store)
        rows = parts2(jnp.concatenate([s_ref[q] for q in range(hs)], axis=0))
        s_cols = dot3(windows(rows, block_starts[:swir_tiles], 2 * LANES), both_parts(table_ref, "up3"))
        s_out[...] = blocks(s_cols, swir_tiles)

        diff = jnp.concatenate([pan_ref[:, : 2 * LANES], pan_ref[:, w - 2 * LANES :]], axis=1) - fe_ref[0:h, :]
        adjoint = adjoint_of(table_ref, col_ref[...])
        total = jnp.zeros((1, LANES), F32)
        for k in range(fine_tiles):
            if 2 <= k < fine_tiles - 2:
                at = slice(LANES * (k - 2), LANES * (k - 1))
                up, down = fm_ref[0:HALO, at], fm_ref[HALO:, at]
                total = total + q_in[k, hc + 8 : hc + 9, :]
            else:
                lane = LANES * (k % (fine_tiles - 4))
                at = slice(lane, lane + LANES)
                up, down = fe_ref[h : h + HALO, at], fe_ref[h + HALO :, at]
                diff_out[k] = diff[:, at]
                q_out[k] = adjoint[:, at]
                total = total + adjoint[hc + 8 : hc + 9, at]
            put(outs, k, up, down)

        acc_out[turns + 2] = jnp.concatenate([total, jnp.zeros((7, LANES), F32)], axis=0)

        def tile_step(k, carry):
            accs, accv, accp = list(carry[:turns]), carry[turns], carry[turns + 1]
            ys = {m: y_out[k, pl.ds(8 * (m - 2), 8), :] for m in own_rows}
            for m in own_rows:
                z = weighted((gram[m, other], ys[other]) for other in own_rows)
                accs[0] = accs[0] + z * ys[m]
                for i in range(1, turns):
                    accs[i] = accs[i] + z * pltpu.roll(ys[m], i, 0)
                accv = accv + float(rise[m]) * ys[m]
                accp = accp + ys[m] * q_out[k, pl.ds(m + 2, 1), :]
            for m in range(hc):
                for p in range(RATIO_V):
                    r = RATIO_V * m + p
                    v_out[k, pl.ds(8 * r, 8), :] = weighted((C4[t, p], ys[m + t]) for t in range(5) if m + t in ys)
            return tuple(accs) + (accv, accp)

        zero = jnp.zeros((8, LANES), F32)
        first = (zero,) * (turns + 2)
        for k in range(fine_tiles):
            first = tile_step(k, first)
        for i in range(turns + 2):
            acc_out[i] = first[i]

    y_own, v_own, acc_own, s_own, diff, q_own, low_in, low_out = call(
        inside,
        (
            shape(fine_tiles, 8 * hc, LANES),
            shape(fine_tiles, 8 * h, LANES),
            shape(turns + 3, 8, LANES),
            shape(8 * hs, wc),
            shape(fine_tiles, h, LANES),
            shape(fine_tiles, q_rows, LANES),
            shape(fine_tiles, 8, LANES),
            shape(fine_tiles, 8, LANES),
        ),
        cost=(2_000_000_000, 8_000_000),
        input_output_aliases={7: 4, 8: 5},
    )(pan_held, x_loc, s_loc, fine_mid, fine_edge, col_edge, table_held, diff_mid, q_mid)
    low_in, low_out = trade(low_in, low_out)

    def means_of(x_ref, table_ref, edge_out, mean_out, lows_out):
        row_id = lax.axis_index("rows")
        below = jnp.where(row_id > 0, 1.0, 0.0).astype(F32)
        above = jnp.where(row_id < strips - 1, 1.0, 0.0).astype(F32)
        means = {}
        for r in range(-2, hc + 2):
            value = weighted((MEAN4[t + 2], x_ref[r + t]) for t in range(-2, 3) if 0 <= r + t < hc)
            means[r] = value * below if r < 0 else (value * above if r >= hc else value)
        for i, r in enumerate((0, 1, hc - 2, hc - 1)):
            edge_out[i] = means[r]
        rows = parts2(jnp.concatenate([means[r] for r in range(2, hc - 2)], axis=0))
        pair = tuple(x[:, :LANES] for x in both_parts(table_ref, "pair", 0, 3))
        mean_out[...] = blocks(dot3(windows(rows, block_starts, 2 * LANES), pair), coarse_tiles)
        reach = TAPS_S // 2
        for r in range(hc):
            lows_out[r] = weighted((KC[t + reach], means[r + t]) for t in range(-reach, reach + 1) if r + t in means)

    mean_edge, mean_own, lows_own = call(
        means_of,
        (shape(4, BANDS, wf), shape(8 * (hc - 4), wc), shape(hc, BANDS, wf)),
        cost=(200_000_000, 3_000_000),
    )(x_loc, table_held)

    def moments(
        x_ref, y_ref, acc_ref, scol_ref, q_ref, edge_ref, mean_ref, lows_ref,
        rest_in_ref, rest_out_ref, cm_ref, ce_ref, table_ref,
        mom_out, y_out, ugap_out, dgap_out, s_out,
        both, ulow,
    ):
        me = lax.axis_index("band")
        rest = (rest_in_ref, rest_out_ref)

        def tiles(refs, low, indices):
            return jnp.concatenate([arrived(refs, i, low) for i in indices], axis=1)

        def halo(first, per, reach, start, count):
            sides = []
            for low, base in ((True, start[0]), (False, start[1])):
                borders = tiles(rest, low, range(at_h, at_h + border_tiles))
                rows = []
                for r in range(count):
                    main = tiles(rest, low, range(first + per * r, first + per * (r + 1)))
                    rows.append(framed(main, borders, base + 2 * reach * r, reach))
                sides.append(rows)
            return sides

        x_low, x_high = halo(0, coarse_tiles, HALO, (2 * HALO * (hc - HALO), 0), HALO)

        def x_row(r):
            if r < 0:
                return x_low[HALO + r]
            if r >= hc:
                return x_high[r - hc]
            return x_ref[r]

        def store(index, value):
            y_out[index] = value

        lifted([x_row(m - 2) for m in around], table_ref, store)

        zero = jnp.zeros((8, LANES), F32)

        def tile_step(k, carry):
            accs = list(carry[:turns])
            accp, accv = carry[turns], carry[turns + 1]
            ys = {m: y_ref[k, pl.ds(8 * (m - 2), 8), :] for m in own_rows}
            for i, m in enumerate(around):
                ys[m] = y_out[k, pl.ds(8 * i, 8), :]
            for m in halo_rows:
                near = weighted((gram[m, other], ys[other]) for other in own_rows)
                whole = near + weighted((gram[m, other], ys[other]) for other in halo_rows)
                accs[0] = accs[0] + ys[m] * (near + whole)
                for i in range(1, turns):
                    accs[i] = accs[i] + whole * pltpu.roll(ys[m], i, 0) + ys[m] * pltpu.roll(near, i, 0)
                accv = accv + float(rise[m]) * ys[m]
            for m in around:
                accp = accp + ys[m] * q_ref[k, pl.ds(m + 2, 1), :]
            return tuple(accs) + (accp, accv)

        start = tuple(acc_ref[i] for i in range(turns)) + (acc_ref[turns + 1], acc_ref[turns])
        first = start
        for k in range(fine_tiles):
            first = tile_step(k, first)

        beyond = [r for r in range(-HALO, hc + HALO) if not 0 <= r < hc]
        edges = []
        for i, r in enumerate((0, 1, hc - 2, hc - 1)):
            more = weighted((MEAN4[a - r + 2], x_row(a)) for a in beyond if abs(a - r) <= 2)
            edges.append(edge_ref[i] + more)
        lows = []
        for r in range(hc):
            more = weighted((WIDE[a - r + HALO], x_row(a)) for a in beyond if abs(a - r) <= HALO)
            lows.append(lows_ref[r] + more)
        u_rows = windows(parts2(jnp.concatenate(edges, axis=0)), block_starts, 2 * LANES)
        l_rows = windows(parts2(jnp.concatenate(lows, axis=0)), block_starts, 2 * LANES)
        u_edge = dot3(u_rows, tuple(x[:, :LANES] for x in both_parts(table_ref, "pair", 0, 3)))
        left = jnp.where(me == 0, 1, 0)
        right = jnp.where(me == groups - 1, 2, 0)
        size = 8 * hc
        last = coarse_tiles - 1
        for which, lo_k, hi_k in ((left, 0, 1), (0, 1, last), (right, last, last + 1)):
            if hi_k <= lo_k:
                continue
            wp = tuple(x[:, LANES:] for x in both_parts(table_ref, "pair", which, 3))
            part = dot3(tuple(x[size * lo_k : size * hi_k] for x in l_rows), wp)
            for k in range(lo_k, hi_k):
                at = slice(LANES * k, LANES * (k + 1))
                low_k = part[size * (k - lo_k) : size * (k - lo_k + 1)]
                ulow[:, at] = low_k
                around_k = u_edge[32 * k : 32 * (k + 1)]
                u_k = jnp.concatenate([around_k[0:16], mean_ref[:, at], around_k[16:32]], axis=0)
                ugap_out[:, at] = u_k - low_k

        column = lax.broadcasted_iota(jnp.int32, (1, wf), 1) - HALF + me * wc
        valid = jnp.where((column >= 0) & (column < groups * wc), 1.0, 0.0).astype(F32)

        def own(rows):
            return jnp.concatenate([ce_ref[rows, 0:LANES], cm_ref[rows, :], ce_ref[rows, LANES:]], axis=1)

        def small(low):
            rows = [arrived(rest, at_d + k // 4, low)[2 * (k % 4) : 2 * (k % 4) + 2] for k in range(frame_tiles)]
            return jnp.concatenate(rows, axis=1)

        both[...] = own(slice(0, pad))
        both[0:2] = both[0:2] + small(True)
        both[hc - 2 : hc] = both[hc - 2 : hc] + small(False)
        detail = both[...]
        both[...] = own(slice(pad, 2 * pad))
        both[0:HALO] = both[0:HALO] + tiles(rest, True, range(at_ld, at_ld + frame_tiles))
        both[hc - HALO : hc] = both[hc - HALO : hc] + tiles(rest, False, range(at_ld, at_ld + frame_tiles))
        dlow_rows = windows(parts2(both[...] * valid), block_starts, 2 * LANES)
        dlow = blocks(dot3(dlow_rows, both_parts(table_ref, "low")), coarse_tiles)
        dgap_out[...] = detail[:, HALF : HALF + wc] - dlow
        both[:, 0:wc] = dlow

        s_low, s_high = halo(at_s, swir_tiles, 2, (2 * HALO * hc + 4 * (hs - 2), 2 * HALO * hc), 2)
        s_parts = windows(parts2(jnp.concatenate(s_low + s_high, axis=0)), block_starts[:swir_tiles], 2 * LANES)
        s_around = blocks(dot3(s_parts, both_parts(table_ref, "up3")), swir_tiles)
        s_cols = jnp.concatenate([s_around[0:16], scol_ref[...], s_around[16:32]], axis=0)
        for m in range(hs):
            for p in range(RATIO_S):
                value = None
                for t in range(5):
                    if C3[t, p] != 0.0:
                        term = float(C3[t, p]) * s_cols[8 * (m + t) : 8 * (m + t) + 8]
                        value = term if value is None else value + term
                s_out[RATIO_S * m + p] = value

        ll = [zero] * turns
        cross = [zero] * BANDS
        ld = ls = sd = ss = dd = ds = zero
        for r in range(hc):
            for k in range(coarse_tiles):
                at = slice(LANES * k, LANES * (k + 1))
                u = ulow[8 * r : 8 * r + 8, at]
                s = s_out[r, :, at]
                dl = jnp.broadcast_to(both[r : r + 1, at], (8, LANES))
                ll[0] = ll[0] + u * u
                for i in range(1, turns):
                    ll[i] = ll[i] + u * pltpu.roll(u, i, 0)
                for i in range(BANDS):
                    cross[i] = cross[i] + u * s_out[r, i : i + 1, at]
                ld = ld + u * dl
                sd = sd + s * dl
                ls = ls + u
                ss = ss + s
                dd = dd + dl * dl
                ds = ds + dl

        lane = lax.broadcasted_iota(jnp.int32, (8, LANES), 1)
        sub = lax.broadcasted_iota(jnp.int32, (8, LANES), 0)

        def column_of(acc):
            return jnp.broadcast_to(jnp.sum(acc, axis=1, keepdims=True), (8, LANES))

        table = zero
        for base, accs in ((0, ll), (16, first[:turns])):
            for i in range(turns):
                col = column_of(accs[i])
                table = jnp.where(lane == base + lax.rem(sub + BANDS - i, BANDS), col, table)
                if 0 < i < BANDS // 2:
                    turned = pltpu.roll(col, BANDS - i, 0)
                    table = jnp.where(lane == base + lax.rem(sub + i, BANDS), turned, table)
        singles = [(8 + i, cross[i]) for i in range(BANDS)]
        singles += [(24, ld), (25, ls), (26, sd), (27, ss), (28, first[turns]), (29, first[turns + 1])]
        for index, acc in singles:
            table = jnp.where(lane == index, column_of(acc), table)
        total = jnp.sum(jnp.sum(acc_ref[turns + 2], axis=0, keepdims=True), axis=1, keepdims=True)
        rest_of = jnp.where(sub == 0, column_of(dd), jnp.where(sub == 1, column_of(ds), total))
        table = jnp.where(lane == 30, rest_of, table)
        packed = table[0:2]
        for q in range(1, 4):
            turned = pltpu.roll(table, 32 * q, 1)
            packed = jnp.where(lane[0:2] >= 32 * q, turned[2 * q : 2 * q + 2], packed)
        mom_out[...] = packed

    mom, y_halo, ugap, dgap, s_up = call(
        moments,
        (
            shape(2, LANES),
            shape(fine_tiles, 8 * len(around), LANES),
            shape(8 * hc, wc),
            shape(pad, wc),
            shape(hc, BANDS, wc),
        ),
        [
            pltpu.VMEM((pad, wf), F32),
            pltpu.VMEM((8 * hc, wc), F32),
        ],
        cost=(1_000_000_000, 8_000_000),
    )(
        x_loc, y_own, acc_own, s_own, q_own, mean_edge, mean_own, lows_own,
        rest_in, rest_out, coarse_mid, coarse_edge, table_held,
    )
    devices = groups * strips
    mom, low_in, low_out = lax.optimization_barrier((mom, low_in, low_out))
    spread = jnp.broadcast_to(mom[None], (devices,) + mom.shape)
    sums = lax.all_to_all(spread, ("rows", "band"), split_axis=0, concat_axis=0, tiled=True)

    apart_rows = h + 8

    def finish(
        sums_ref, yh_ref, v_ref, diff_ref, low_in_ref, low_out_ref, ugap_ref, dgap_ref, s_ref,
        vnir_out, swir_out, tiles, swir, ends, sems,
    ):
        lane = lax.broadcasted_iota(jnp.int32, (8, LANES), 1)
        sub = lax.broadcasted_iota(jnp.int32, (8, LANES), 0)
        eye = lane == sub
        terms = [sums_ref[index] for index in range(devices)]
        while len(terms) > 1:
            terms = [sum(terms[i : i + 2][1:], terms[i]) for i in range(0, len(terms), 2)]
        packed = jnp.concatenate([terms[0]] * 4, axis=0)
        total = packed
        for q in range(1, 4):
            total = jnp.where(sub >= 2 * q, pltpu.roll(packed, LANES - 32 * q, 1), total)

        def single(row):
            return jnp.broadcast_to(total[row : row + 1, 30:31], (8, LANES))


        def column(x, index):
            return jnp.broadcast_to(x[:, index : index + 1], (8, LANES))

        def across(col):
            return jnp.sum(jnp.where(eye, col, 0.0), axis=0, keepdims=True)

        def down(x):
            return jnp.sum(x, axis=0, keepdims=True)

        def solve(matrix, rhs):
            cols = [column(matrix, j) for j in range(BANDS)] + [rhs]
            inverse = jnp.zeros((8, LANES), F32)
            for k in range(BANDS):
                pivot = 1.0 / jnp.broadcast_to(cols[k][k : k + 1], (8, LANES))
                inverse = jnp.where(sub == k, pivot, inverse)
                factor = jnp.where(sub == k, 0.0, cols[k] * pivot)
                for j in range(k + 1, BANDS + 1):
                    cols[j] = cols[j] - factor * jnp.broadcast_to(cols[j][k : k + 1], (8, LANES))
            return cols[BANDS] * inverse

        n1 = 1.0 / fine_pixels
        mean_v = column(total, 29) * n1
        mean_p = single(2) * n1
        cov_v = pltpu.roll(total, LANES - 16, 1) * n1 - mean_v * across(mean_v)
        cov_p = column(total, 28) * n1 - mean_v * mean_p
        gain = cov_p / down(cov_p * solve(cov_v, cov_p))

        n2 = RATIO_V * RATIO_V / fine_pixels
        mean_l = column(total, 25) * n2
        mean_s = column(total, 27) * n2
        mean_d = single(1) * n2
        cov_ll = total * n2 - mean_l * across(mean_l)
        cov_ls = pltpu.roll(total, LANES - 8, 1) * n2 - mean_l * across(mean_s)
        cov_ld = column(total, 24) * n2 - mean_l * mean_d
        cov_sd = column(total, 26) * n2 - mean_s * mean_d
        cov_dd = single(0) * n2 - mean_d * mean_d
        gain_row = across(gain)
        a2 = cov_ll + gain * across(cov_ld) + cov_ld * gain_row + gain * gain_row * cov_dd
        b2 = jnp.where(lane < BANDS, cov_ls + gain * across(cov_sd), 0.0)
        target = jnp.broadcast_to(jnp.sum(b2, axis=1, keepdims=True) / BANDS, (8, LANES))

        def sent_tile(k):
            lanes = pl.ds(pl.multiple_of(LANES * k, LANES), LANES)
            held = tiles.reshape(fine_tiles, BANDS + 1, apart_rows, LANES).at[k, pl.ds(0, BANDS), pl.ds(0, h), :]
            return pltpu.make_async_copy(held, vnir_out.at[:, :, lanes], sems.at[k])

        def tile_step(k, carry):
            ys = {m: yh_ref[k, pl.ds(8 * i, 8), :] for i, m in enumerate(around) if m in halo_rows}
            lows = (low_in_ref, low_out_ref)
            ends[k, 0:HALO, :] = diff_ref[k, 0:HALO, :] - arrived(lows, k, True)
            ends[k, HALO:, :] = diff_ref[k, h - HALO :, :] - arrived(lows, k, False)
            for m in range(hc):
                for p in range(RATIO_V):
                    r = RATIO_V * m + p
                    value = v_ref[k, pl.ds(8 * r, 8), :]
                    more = weighted((C4[t, p], ys[m + t]) for t in range(5) if m + t in ys)
                    if more is not None:
                        value = value + more
                    if r < HALO:
                        detail = ends[k, pl.ds(r, 1), :]
                    elif r >= h - HALO:
                        detail = ends[k, pl.ds(r - h + 2 * HALO, 1), :]
                    else:
                        detail = diff_ref[k, pl.ds(r, 1), :]
                    value = value + gain * detail
                    tiles[k, pl.ds(r, 8, stride=apart_rows), :] = value
            sent_tile(k).start()
            return carry

        beside = max(1, fine_tiles // (BANDS + BANDS // 2))

        def solve_step(k, carry):
            work, inverse = carry
            here = sub == k
            row = down(jnp.where(here, work, 0.0))
            col = jnp.sum(jnp.where(lane == k, work, 0.0), axis=1, keepdims=True)
            pivot = 1.0 / down(jnp.where(here[:, 0:1], col, 0.0))
            inverse = jnp.where(here, pivot, inverse)
            work = work - jnp.where(here, 0.0, col * pivot) * row

            for i in range(beside):
                tile_step(beside * k + i, 0)
            return work, inverse

        start = (jnp.where(lane == BANDS, target, a2), jnp.zeros((8, LANES), F32))
        work, inverse = lax.fori_loop(0, BANDS, solve_step, start)
        fit2 = column(work, BANDS) * inverse
        numer = down(fit2 * b2)
        share_row = numer / down(fit2 * target)
        share = jnp.sum(jnp.where(eye, jnp.broadcast_to(share_row, (8, LANES)), 0.0), axis=1, keepdims=True)
        scale = down(fit2 * gain)[:, 0:1]
        fit_col = fit2[:, 0:1]
        for r in range(hc):
            seen = jnp.sum(fit_col * ugap_ref[8 * r : 8 * r + 8, :], axis=0, keepdims=True)
            seen = seen + scale * dgap_ref[r : r + 1, :]
            swir[r] = s_ref[r] + share * seen
        last = pltpu.make_async_copy(swir, swir_out, sems.at[fine_tiles])
        last.start()

        lax.fori_loop(BANDS * beside, fine_tiles, tile_step, 0)

        def drain(k, carry):
            sent_tile(k).wait()
            return carry

        lax.fori_loop(0, fine_tiles, drain, 0)
        last.wait()

    joined_vnir, joined_swir = call(
        finish,
        (shape(BANDS, h, w), shape(hc, BANDS, wc)),
        [
            pltpu.VMEM((fine_tiles, (BANDS + 1) * apart_rows, LANES), F32),
            pltpu.VMEM((hc, BANDS, wc), F32),
            pltpu.VMEM((fine_tiles, 2 * HALO, LANES), F32),
            pltpu.SemaphoreType.DMA((fine_tiles + 1,)),
        ],
        cost=(100_000_000, 8_000_000),
        out_specs=(ANY, ANY),
    )(sums, y_halo, v_own, diff, low_in, low_out, ugap, dgap, s_up)
    return joined_vnir, jnp.transpose(joined_swir, (1, 0, 2))


def solution(mesh):
    return jax.shard_map(
        local,
        mesh=mesh,
        in_specs=(P("rows", "band"), P("band", "rows", None), P("band", "rows", None)),
        out_specs=(P(None, "rows", "band"), P(None, "rows", "band")),
        check_vma=False,
    )
```
